32 devices in a mesh: gx: 8 (over y, x, core), gy: 4 (over z).
Axes of the slice: x: 2, y: 2, z: 4, core: 2. Of those that a mesh axis runs over, the one named last changes fastest.
Arguments:
- fields: bfloat16 [2, 64, 16, 32, 128], P(None, None, 'gx', 'gy'), may hold values from -6 to 6
- depth_kernel: bfloat16 [64, 3, 3, 3], replicated, may hold values from -1.25 to 1.25
- point_in: bfloat16 [256, 64], replicated, may hold values from -0.75 to 0.75
- point_out: bfloat16 [64, 256], replicated, may hold values from -0.375 to 0.375
- down_kernel: bfloat16 [128, 64, 2, 2, 2], replicated, may hold values from -0.25 to 0.25
- cotangent: bfloat16 [8, 4, 1, 128, 2, 4, 64], P('gx', 'gy'), may hold values from -6 to 6
Outputs:
- coarse: bfloat16 [8, 4, 1, 128, 2, 4, 64], P('gx', 'gy')
- grad_fields: bfloat16 [2, 64, 16, 32, 128], P(None, None, 'gx', 'gy')
- grad_depth_kernel: float32 [64, 3, 3, 3], replicated
- grad_point_in: float32 [256, 64], replicated
- grad_point_out: float32 [64, 256], replicated
- grad_down_kernel: float32 [128, 64, 2, 2, 2], replicated
The draws below stay inside these ranges and needn't reach their ends.
All inputs are finite; a program needn't handle non-finite values.
Results may differ from the reference program's by a relative error of at most 0.0066.
Values may be sent and summed in bfloat16 or wider, within the bound.
No kernel may reach another device: no remote copies, remote signals or barrier semaphores. Data moves between devices by JAX's collectives and lax.ppermute only.
A program may use at most 192 MiB of HBM per device.

```python
import math
import jax
import jax.numpy as jnp
from jax import lax

C = 64
HID = 256
C2 = 128
GRIDC = 4
NZ = 128
BG = 1
SGX = 2
SGY = 1
SAMPLES = 2
NX = 16
NY = 32
XC = 2
YC = 4
ZC = 64
N_GX = 8
N_GY = 4


def levels(own_key, extent, cuts, least, largest):
    factor_of, own = 1.0, jax.random.fold_in(own_key, 6)
    for position, parts in cuts:
        heights = jnp.exp(jax.random.uniform(jax.random.fold_in(own, position), (parts,), jnp.float32, least / len(cuts), largest / len(cuts)))
        factor_of = factor_of * jnp.repeat(heights, extent[position] // parts).reshape([-1 if axis == position else 1 for axis in range(len(extent))])
    return factor_of


def noise(stream_key, dims, scale, bound, cuts=(), dtype=jnp.bfloat16):
    result = scale * jax.random.normal(stream_key, dims, jnp.float32)
    if cuts:
        result = result * levels(stream_key, dims, cuts, -0.22, 0.18)
    return jnp.clip(result, -bound, bound).astype(dtype)


def setup_inputs(seed: int = 0) -> dict:
    streams_of = jax.random.split(jax.random.key(seed), 7)
    fields = noise(streams_of[0], (SAMPLES, C, NX, NY, NZ), 1.0, 6.0, ((2, 8), (3, 4)))
    depth_kernel = noise(streams_of[1], (C, 3, 3, 3), 27 ** -0.5, 1.25)
    point_in = noise(streams_of[2], (HID, C), C ** -0.5, 0.75)
    point_out = noise(streams_of[3], (C, HID), HID ** -0.5, 0.375)
    down_kernel = noise(streams_of[4], (C2, C, 2, 2, 2), (8 * C) ** -0.5, 0.25)
    cotangent = noise(streams_of[5], (N_GX, N_GY, BG, C2, XC, YC, ZC), 1.0, 6.0, ((0, 8), (1, 4)))
    return {"fields": fields, "depth_kernel": depth_kernel, "point_in": point_in, "point_out": point_out, "down_kernel": down_kernel, "cotangent": cotangent}


def gelu_slope(values):
    outputs, pullback = jax.vjp(jax.nn.gelu, values)
    return pullback(jnp.ones_like(outputs))[0]

def depth_conv(padded, weights, span_x, span_y, span_z):
    summed = jnp.zeros(padded.shape[:-3] + (span_x, span_y, span_z), jnp.float32)
    for offset_x in range(3):
        for offset_y in range(3):
            for offset_z in range(3):
                factor = weights[:, offset_x, offset_y, offset_z].astype(jnp.float32)[:, None, None, None]
                window = padded[..., offset_x:offset_x + span_x, offset_y:offset_y + span_y, offset_z:offset_z + span_z]
                summed = summed + factor * window.astype(jnp.float32)
    return summed

def per_sample(sample_field, sample_grad, depth_kernel, point_in, point_out, down_kernel):
    padded = jnp.pad(sample_field, ((0, 0), (1, 1), (1, 1), (1, 1)))
    depth_out = depth_conv(padded, depth_kernel, NX, NY, NZ).astype(jnp.bfloat16)
    flat_depth = depth_out.reshape(C, -1)
    preact = jnp.dot(point_in, flat_depth, preferred_element_type=jnp.float32)
    active = jax.nn.gelu(preact).astype(jnp.bfloat16)
    merged = (sample_field.reshape(C, -1).astype(jnp.float32) + jnp.dot(point_out, active, preferred_element_type=jnp.float32)).astype(jnp.bfloat16)
    patches = merged.reshape(C, NX // 2, 2, NY // 2, 2, NZ // 2, 2).transpose(0, 2, 4, 6, 1, 3, 5).reshape(C * 8, -1)
    down_mat = down_kernel.reshape(C2, C * 8)
    reduced = jnp.dot(down_mat, patches, preferred_element_type=jnp.float32).astype(jnp.bfloat16)
    grad_down = sample_grad.reshape(C2, -1)
    grad_patch = jnp.dot(down_mat.T, grad_down, preferred_element_type=jnp.float32)
    grad_merged = grad_patch.reshape(C, 2, 2, 2, NX // 2, NY // 2, NZ // 2).transpose(0, 4, 1, 5, 2, 6, 3).reshape(C, -1).astype(jnp.bfloat16)
    grad_downw = jnp.dot(grad_down, patches.T, preferred_element_type=jnp.float32)
    grad_active = jnp.dot(point_out.T, grad_merged, preferred_element_type=jnp.float32)
    grad_pre = (grad_active * gelu_slope(preact)).astype(jnp.bfloat16)
    grad_outw = jnp.dot(grad_merged, active.T, preferred_element_type=jnp.float32)
    grad_inw = jnp.dot(grad_pre, flat_depth.T, preferred_element_type=jnp.float32)
    grad_depth = jnp.dot(point_in.T, grad_pre, preferred_element_type=jnp.float32).astype(jnp.bfloat16).reshape(C, NX, NY, NZ)
    grad_pad = jnp.pad(grad_depth, ((0, 0), (1, 1), (1, 1), (1, 1)))
    adjoint = depth_conv(grad_pad, depth_kernel[:, ::-1, ::-1, ::-1], NX, NY, NZ)
    grad_field = (grad_merged.reshape(C, NX, NY, NZ).astype(jnp.float32) + adjoint).astype(jnp.bfloat16)
    columns = []
    for offset_x in range(3):
        for offset_y in range(3):
            for offset_z in range(3):
                window = padded[:, offset_x:offset_x + NX, offset_y:offset_y + NY, offset_z:offset_z + NZ]
                columns.append(lax.optimization_barrier(jnp.sum(grad_depth.astype(jnp.float32) * window.astype(jnp.float32), axis=(1, 2, 3))))
    grad_depthw = jnp.stack(columns, axis=1).reshape(C, 3, 3, 3)
    return (reduced.reshape(C2, NX // 2, NY // 2, NZ // 2), grad_field, grad_depthw, grad_inw, grad_outw, grad_downw.reshape(C2, C, 2, 2, 2))

def reference(fields, depth_kernel, point_in, point_out, down_kernel, cotangent):
    fine_grad = cotangent.reshape(GRIDC, SGX, GRIDC, SGY, BG, C2, XC, YC, ZC).transpose(1, 3, 4, 5, 0, 6, 2, 7, 8).reshape(SAMPLES, C2, NX // 2, NY // 2, NZ // 2)

    def runner(inputs):
        return per_sample(inputs[0], inputs[1], depth_kernel, point_in, point_out, down_kernel)
    reduced, grad_fields, grad_depthw, grad_inw, grad_outw, grad_downw = lax.map(runner, (fields, fine_grad))
    norm_scale = 1.0 / math.sqrt(SAMPLES * NX * NY * NZ)
    coarse = reduced.reshape(SGX, SGY, BG, C2, GRIDC, XC, GRIDC, YC, ZC).transpose(4, 0, 6, 1, 2, 3, 5, 7, 8).reshape(N_GX, N_GY, BG, C2, XC, YC, ZC)
    return (coarse, grad_fields, lax.optimization_barrier(jnp.sum(grad_depthw, axis=0)) * norm_scale, lax.optimization_barrier(jnp.sum(grad_inw, axis=0)) * norm_scale, lax.optimization_barrier(jnp.sum(grad_outw, axis=0)) * norm_scale, lax.optimization_barrier(jnp.sum(grad_downw, axis=0)) * norm_scale)
```

```python
import functools
import math

import jax
import jax.numpy as jnp
from jax import lax
from jax.experimental import pallas as pl
from jax.experimental.pallas import tpu as pltpu
from jax.sharding import PartitionSpec as P

GRIDC = 4
F32 = jnp.float32
BF16 = jnp.bfloat16
VMEM_LIMIT = 40 * 1024 * 1024
CT = 8
GELU_C = math.sqrt(2.0 / math.pi)
GELU_A = 0.044715


def dot(a, b, ca, cb):
    return lax.dot_general(a, b, (((ca,), (cb,)), ((), ())), preferred_element_type=F32)


def write_edges(row, X, Y, ylo, yhi, corners):
    for x in range(X):
        ylo[0, x] = row(x, 0)
        yhi[0, x] = row(x, Y - 1)
    for i, x in enumerate((0, X - 1)):
        for j, y in enumerate((0, Y - 1)):
            corners[2 * i + j][0] = row(x, y)


def piece_shapes(S, X, Y, C, Z):
    return (
        [jax.ShapeDtypeStruct((S, Y, C, Z), BF16)] * X
        + [jax.ShapeDtypeStruct((S, X, C, Z), BF16)] * 2
        + [jax.ShapeDtypeStruct((S, C, Z), BF16)] * 4
    )


def piece_specs(X, Y, C, Z):
    return (
        [pl.BlockSpec((1, Y, C, Z), lambda s: (s, 0, 0, 0))] * X
        + [pl.BlockSpec((1, X, C, Z), lambda s: (s, 0, 0, 0))] * 2
        + [pl.BlockSpec((1, C, Z), lambda s: (s, 0, 0))] * 4
    )


def halo_specs(X, Y, C, Z):
    return (
        [pl.BlockSpec((1, Y, C, Z), lambda s: (s, 0, 0, 0))] * 2
        + [pl.BlockSpec((1, X, C, Z), lambda s: (s, 0, 0, 0))] * 2
        + [pl.BlockSpec((1, C, Z), lambda s: (s, 0, 0))] * 4
    )


def exchange_halo(pieces, X):
    planes, (ylo, yhi), corners = pieces[:X], pieces[X : X + 2], pieces[X + 2 :]
    nx, ny = lax.axis_size("gx"), lax.axis_size("gy")
    up_x = [(i, i + 1) for i in range(nx - 1)]
    up_y = [(i, i + 1) for i in range(ny - 1)]
    down_x = [(b, a) for a, b in up_x]
    down_y = [(b, a) for a, b in up_y]
    from_lo_x = lax.ppermute(planes[-1], "gx", up_x)
    from_hi_x = lax.ppermute(planes[0], "gx", down_x)
    from_lo_y = lax.ppermute(yhi, "gy", up_y)
    from_hi_y = lax.ppermute(ylo, "gy", down_y)
    got = []
    for i, dx in enumerate((-1, 1)):
        for j, dy in enumerate((-1, 1)):
            pairs = [
                ((x + dx) * ny + y + dy, x * ny + y)
                for x in range(nx)
                for y in range(ny)
                if 0 <= x + dx < nx and 0 <= y + dy < ny
            ]
            got.append(lax.ppermute(corners[2 * (1 - i) + (1 - j)], ("gx", "gy"), pairs))
    return [from_lo_x, from_hi_x, from_lo_y, from_hi_y] + got


def padded_rows(X, Y, planes, halo):
    xlo, xhi, ylo, yhi = halo[:4]
    corners = halo[4:]

    def row(x, y):
        ox, oy = (0 if x < 0 else 1 if x >= X else None), (0 if y < 0 else 1 if y >= Y else None)
        if ox is not None and oy is not None:
            return corners[2 * ox + oy][0]
        if ox is not None:
            return (xlo, xhi)[ox][0, y]
        if oy is not None:
            return (ylo, yhi)[oy][0, x]
        return planes[x][0, y]

    return row


def fill_taps(w_ref, wb, flip):
    C, Z = wb.shape[1:]
    for t in range(27):
        source = 26 - t if flip else t
        wb[t] = jnp.broadcast_to(w_ref[:, source : source + 1], (C, Z))


def fill_padded(row, Fs, X, Y):
    for x in range(-1, X + 1):
        for y in range(-1, Y + 1):
            Fs[(x + 1) * (Y + 2) + y + 1] = row(x, y).astype(F32)


def conv_tile(Fs, wb, channels, X, Y, lane, store):
    Z = Fs.shape[2]
    for x in range(X):
        for y in range(Y):
            acc = [None, None, None]
            for a in range(3):
                for b in range(3):
                    f = Fs[(x + a) * (Y + 2) + y + b, channels, :]
                    for e in range(3):
                        term = wb[(a * 3 + b) * 3 + e, channels, :] * f
                        acc[e] = term if acc[e] is None else acc[e] + term
            left = jnp.where(lane == 0, 0.0, pltpu.roll(acc[0], 1, 1))
            right = jnp.where(lane == Z - 1, 0.0, pltpu.roll(acc[2], Z - 1, 1))
            store(x, y, acc[1] + left + right)


def split_kernel(X, Y, C, Z, f_ref, *refs):
    planes, (ylo, yhi), corners = refs[:X], refs[X : X + 2], refs[X + 2 : X + 6]
    wide = refs[X + 6]
    wide[...] = f_ref[0].astype(F32)
    for x in range(X):
        for y in range(Y):
            planes[x][0, y] = wide[pl.ds(x * Y + y, C, stride=X * Y), :].astype(BF16)
    write_edges(lambda x, y: planes[x][0, y], X, Y, ylo, yhi, corners)


def main_kernel(dims, *refs):
    X, Y, C, Z, H, O = dims
    hx, NP = X // 2, Y // 4
    cells = X * Y * Z
    quarter = (Y // 2) * (Z // 2)
    planes, halo = refs[:X], refs[X : X + 8]
    gd_ref, w_ref, pinT_ref, pout_ref, wd_ref = refs[X + 8 : X + 13]
    outs = refs[X + 13 :]
    red_ref, gm_ref = outs[:2]
    d_planes, (d_ylo, d_yhi), d_corners = outs[2 : X + 2], outs[X + 2 : X + 4], outs[X + 4 : X + 8]
    packed_ref = outs[X + 8]
    Fs, wb, Ds, GMs, Mb, Pt, G1, adw, adown, aout, ain, pin, poutT = outs[X + 9 :]
    step = pl.program_id(0)

    @pl.when(step == 0)
    def _():
        fill_taps(w_ref, wb, False)
        adw[...] = jnp.zeros_like(adw)
        adown[...] = jnp.zeros_like(adown)
        aout[...] = jnp.zeros_like(aout)
        ain[...] = jnp.zeros_like(ain)
        pin[...] = pinT_ref[...].astype(F32).T.astype(BF16)
        poutT[...] = pout_ref[...].astype(F32).T.astype(BF16)

    fill_padded(padded_rows(X, Y, planes, halo), Fs, X, Y)
    lane = lax.broadcasted_iota(jnp.int32, (CT, Z), 1)

    fine = lax.broadcasted_iota(jnp.int32, (2 * Z, 2 * Z), 0)
    coarse = lax.broadcasted_iota(jnp.int32, (2 * Z, 2 * Z), 1)
    goes = (coarse // Z) * 1 + ((coarse % Z) % (Z // 2)) * 2 + ((coarse % Z) // (Z // 2)) * Z
    perm = jnp.where(fine == goes, 1.0, 0.0).astype(BF16)

    for X0 in range(hx):
        gp = dot(wd_ref[...], gd_ref[0, X0], 1, 1).astype(BF16)
        for a in range(2):
            for b in range(2):
                for p in range(NP):
                    src = ((a * 2 + b) * 2) * C
                    dst = ((a * 2 + b) * NP + p) * C
                    for e in range(2):
                        Mb[dst : dst + C, e * Z : (e + 1) * Z] = gp[
                            src + e * C : src + (e + 1) * C, p * Z : (p + 1) * Z
                        ]
        gm = dot(Mb[...], perm, 1, 1).astype(BF16)
        for a in range(2):
            for b in range(2):
                for p in range(NP):
                    src = ((a * 2 + b) * NP + p) * C
                    for q in range(2):
                        x, y = 2 * X0 + a, 2 * (2 * p + q) + b
                        value = gm[src : src + C, q * Z : (q + 1) * Z]
                        gm_ref[0, x, y] = value
                        r = x * Y + y
                        GMs[:, r * Z : (r + 1) * Z] = value

    def conv_body(i, carry):
        channels = pl.ds(pl.multiple_of(i * CT, CT), CT)

        def store(x, y, value):
            r = x * Y + y
            Ds[channels, r * Z : (r + 1) * Z] = value

        conv_tile(Fs, wb, channels, X, Y, lane, store)
        return carry

    lax.fori_loop(0, C // CT, conv_body, 0)

    width = 4 * Z

    for X0 in range(hx):

        def chunk_body(i, carry):
            a, p = i // NP, i % NP
            x = 2 * X0 + a
            columns = pl.ds(pl.multiple_of((x * NP + p) * width, width), width)
            depth = Ds[:, columns].astype(BF16)
            gm = GMs[:, columns]
            pre = dot(pin[...], depth, 1, 0)
            sq = pre * pre
            t = jnp.tanh(pre * (GELU_C + (GELU_C * GELU_A) * sq))
            h = 0.5 + 0.5 * t
            act = pre * h
            slope = h + act * (1.0 - h) * (2.0 * GELU_C + (6.0 * GELU_C * GELU_A) * sq)
            active = act.astype(BF16)
            branch = dot(pout_ref[...], active, 1, 0)
            for j in range(4):
                row = (x + 1) * (Y + 2) + 4 * p + j + 1
                merged = (Fs[row] + branch[:, j * Z : (j + 1) * Z]).astype(BF16)
                start = pl.multiple_of(((a * 2 + j % 2) * NP + p) * C, C)
                Mb[pl.ds(start, C), (j // 2) * Z : (j // 2 + 1) * Z] = merged
            grad_pre = (dot(poutT[...], gm, 1, 0) * slope).astype(BF16)
            grad_depth = dot(pinT_ref[...], grad_pre, 1, 0).astype(BF16).astype(F32)
            for j in range(4):
                G1[x * Y + 4 * p + j] = grad_depth[:, j * Z : (j + 1) * Z]
            aout[...] += dot(gm, active, 1, 1)
            ain[...] += dot(depth, grad_pre, 1, 1)
            return carry

        lax.fori_loop(0, 2 * NP, chunk_body, 0)

        pt = dot(Mb[...], perm, 1, 0).astype(BF16)
        for a in range(2):
            for b in range(2):
                for p in range(NP):
                    src = ((a * 2 + b) * NP + p) * C
                    for e in range(2):
                        dst = ((a * 2 + b) * 2 + e) * C
                        Pt[dst : dst + C, p * Z : (p + 1) * Z] = pt[
                            src : src + C, e * Z : (e + 1) * Z
                        ]
        red_ref[0, X0] = dot(Pt[...], wd_ref[...], 0, 0).astype(BF16)
        adown[...] += dot(Pt[...], gd_ref[0, X0], 1, 0)

    def grad_row(x, y):
        return G1[x * Y + y].astype(BF16)

    for x in range(X):
        for y in range(Y):
            d_planes[x][0, y] = grad_row(x, y)
    write_edges(grad_row, X, Y, d_ylo, d_yhi, d_corners)

    def tap_body(i, carry):
        channels = pl.ds(pl.multiple_of(i * CT, CT), CT)
        sums = [None] * 27
        for x in range(X):
            for y in range(Y):
                g = G1[x * Y + y, channels, :]
                gs = (
                    jnp.where(lane == Z - 1, 0.0, pltpu.roll(g, Z - 1, 1)),
                    g,
                    jnp.where(lane == 0, 0.0, pltpu.roll(g, 1, 1)),
                )
                for a in range(3):
                    for b in range(3):
                        f = Fs[(x + a) * (Y + 2) + y + b, channels, :]
                        for e in range(3):
                            t = (a * 3 + b) * 3 + e
                            term = gs[e] * f
                            sums[t] = term if sums[t] is None else sums[t] + term
        for t in range(27):
            adw[t, channels, :] += sums[t]
        return carry

    lax.fori_loop(0, C // CT, tap_body, 0)

    @pl.when(step == pl.num_programs(0) - 1)
    def _():
        columns = lax.broadcasted_iota(jnp.int32, (C, Z), 1)
        taps = jnp.zeros((C, Z), F32)
        for t in range(27):
            taps = jnp.where(columns == t, jnp.sum(adw[t], axis=1, keepdims=True), taps)
        at = 0
        for block in (
            [adown[...]]
            + [aout[:, k : k + Z] for k in range(0, H, Z)]
            + [ain[:, k : k + Z] for k in range(0, H, Z)]
            + [taps]
        ):
            packed_ref[at : at + block.shape[0], :] = block.astype(BF16)
            at += block.shape[0]
        if at < packed_ref.shape[0]:
            rest = packed_ref.shape[0] - at
            packed_ref[at:, :] = jnp.zeros((rest, Z), BF16)


def adjoint_kernel(X, Y, C, Z, *refs):
    planes, halo = refs[:X], refs[X : X + 8]
    gm_ref, w_ref, out_ref, Fs, wb, wide = refs[X + 8 :]

    @pl.when(pl.program_id(0) == 0)
    def _():
        fill_taps(w_ref, wb, True)

    fill_padded(padded_rows(X, Y, planes, halo), Fs, X, Y)
    lane = lax.broadcasted_iota(jnp.int32, (CT, Z), 1)
    rows = X * Y

    def conv_body(i, carry):
        first = pl.multiple_of(i * CT, CT)
        channels = pl.ds(first, CT)

        def store(x, y, value):
            r = x * Y + y
            total = value + gm_ref[0, x, y, channels, :].astype(F32)
            wide[pl.ds(first * rows + r, CT, stride=rows), :] = total

        conv_tile(Fs, wb, channels, X, Y, lane, store)
        return carry

    lax.fori_loop(0, C // CT, conv_body, 0)
    out_ref[0] = wide[...].astype(BF16)


def swap_in_group(blocks, axis):
    g = blocks.shape[0]
    if g == 1:
        return blocks
    n = lax.axis_size(axis)
    member = lax.axis_index(axis) % g
    got = [lax.dynamic_index_in_dim(blocks, member, 0, keepdims=False)]
    for k in range(1, g):
        out = lax.dynamic_index_in_dim(blocks, (member + k) % g, 0, keepdims=False)
        pairs = [(i, i - i % g + (i + k) % g) for i in range(n)]
        got.append(lax.ppermute(out, axis, pairs))
    if g == 2:
        first = member == 0
        return jnp.stack([jnp.where(first, got[0], got[1]), jnp.where(first, got[1], got[0])])
    got = jnp.stack(got)
    return jnp.take(got, (member - jnp.arange(g, dtype=jnp.int32)) % g, axis=0)


def sum_over_devices(packed, devices):
    axes = ("gx", "gy")
    lanes = packed.shape[1]
    mine = lax.all_to_all(packed.reshape(devices, -1, lanes), axes, 0, 0)
    total = jnp.sum(mine.astype(F32), axis=0).astype(BF16)
    every = lax.all_to_all(jnp.broadcast_to(total[None], (devices,) + total.shape), axes, 0, 0)
    return every.reshape(-1, lanes).astype(F32)


def per_device(fields, depth_kernel, point_in, point_out, down_kernel, cotangent):
    S, C, X, Y, Z = fields.shape
    H, O = point_in.shape[0], down_kernel.shape[0]
    hx, hy, hz = X // 2, Y // 2, Z // 2
    nx, ny = lax.axis_size("gx"), lax.axis_size("gy")
    devices = nx * ny
    gx, gy = nx // GRIDC, ny // GRIDC
    per_group = S // (gx * gy)
    params = pltpu.CompilerParams(
        dimension_semantics=("arbitrary",), vmem_limit_bytes=VMEM_LIMIT
    )

    pieces = pl.pallas_call(
        functools.partial(split_kernel, X, Y, C, Z),
        grid=(S,),
        in_specs=[pl.BlockSpec((1, C * X * Y, Z), lambda s: (s, 0, 0))],
        out_specs=piece_specs(X, Y, C, Z),
        out_shape=piece_shapes(S, X, Y, C, Z),
        scratch_shapes=[pltpu.VMEM((C * X * Y, Z), F32)],
        compiler_params=params,
        name="split_fields",
    )(fields.reshape(S, C * X * Y, Z))

    halo = exchange_halo(pieces, X)

    moved = cotangent[0, 0].transpose(0, 2, 3, 4, 1)
    moved = moved.reshape(per_group, gx * hx, gy, hy * hz, O).transpose(2, 0, 1, 3, 4)
    moved = swap_in_group(moved, "gy").reshape(gy * per_group, gx, hx, hy * hz, O)
    moved = swap_in_group(moved.transpose(1, 0, 2, 3, 4), "gx")
    grad_down = moved.reshape(S, hx, hy * hz, O)

    wd = down_kernel.transpose(2, 3, 4, 1, 0).reshape(8 * C, O)
    taps = depth_kernel.reshape(C, 27).astype(F32)

    rows = 8 * C + 2 * C * (H // Z) + C
    chunk = -(-rows // (16 * devices)) * 16
    cells = X * Y * Z
    whole = lambda shape: pl.BlockSpec(shape, lambda s: (0,) * len(shape))
    flops = S * cells * (2 * 6 * C * H + 2 * 3 * C * O + 2 * 2 * 27 * C)
    out = pl.pallas_call(
        functools.partial(main_kernel, (X, Y, C, Z, H, O)),
        grid=(S,),
        in_specs=[pl.BlockSpec((1, Y, C, Z), lambda s: (s, 0, 0, 0))] * X
        + halo_specs(X, Y, C, Z)
        + [
            pl.BlockSpec((1, hx, hy * hz, O), lambda s: (s, 0, 0, 0)),
            whole((C, 27)),
            whole((C, H)),
            whole((C, H)),
            whole((8 * C, O)),
        ],
        out_specs=[
            pl.BlockSpec((1, hx, hy * hz, O), lambda s: (s, 0, 0, 0)),
            pl.BlockSpec((1, X, Y, C, Z), lambda s: (s, 0, 0, 0, 0)),
        ]
        + piece_specs(X, Y, C, Z)
        + [whole((devices * chunk, Z))],
        out_shape=[
            jax.ShapeDtypeStruct((S, hx, hy * hz, O), BF16),
            jax.ShapeDtypeStruct((S, X, Y, C, Z), BF16),
        ]
        + piece_shapes(S, X, Y, C, Z)
        + [jax.ShapeDtypeStruct((devices * chunk, Z), BF16)],
        scratch_shapes=[
            pltpu.VMEM(((X + 2) * (Y + 2), C, Z), F32),
            pltpu.VMEM((27, C, Z), F32),
            pltpu.VMEM((C, cells), F32),
            pltpu.VMEM((C, cells), BF16),
            pltpu.VMEM((Y * C, 2 * Z), BF16),
            pltpu.VMEM((8 * C, hy * hz), BF16),
            pltpu.VMEM((X * Y, C, Z), F32),
            pltpu.VMEM((27, C, Z), F32),
            pltpu.VMEM((8 * C, O), F32),
            pltpu.VMEM((C, H), F32),
            pltpu.VMEM((C, H), F32),
            pltpu.VMEM((H, C), BF16),
            pltpu.VMEM((H, C), BF16),
        ],
        compiler_params=params,
        cost_estimate=pl.CostEstimate(
            flops=flops, bytes_accessed=8 * S * cells * C, transcendentals=S * cells * H
        ),
        name="main",
    )(*pieces[:X], *halo, grad_down, taps, point_in.T, point_out, wd)
    reduced, grad_merged = out[:2]
    grad_pieces = out[2 : X + 8]
    packed = out[X + 8]

    grad_halo = exchange_halo(grad_pieces, X)

    total = sum_over_devices(packed, devices)

    grad_fields = pl.pallas_call(
        functools.partial(adjoint_kernel, X, Y, C, Z),
        grid=(S,),
        in_specs=[pl.BlockSpec((1, Y, C, Z), lambda s: (s, 0, 0, 0))] * X
        + halo_specs(X, Y, C, Z)
        + [pl.BlockSpec((1, X, Y, C, Z), lambda s: (s, 0, 0, 0, 0)), whole((C, 27))],
        out_specs=pl.BlockSpec((1, C * X * Y, Z), lambda s: (s, 0, 0)),
        out_shape=jax.ShapeDtypeStruct((S, C * X * Y, Z), BF16),
        scratch_shapes=[
            pltpu.VMEM(((X + 2) * (Y + 2), C, Z), F32),
            pltpu.VMEM((27, C, Z), F32),
            pltpu.VMEM((C * X * Y, Z), F32),
        ],
        compiler_params=params,
        cost_estimate=pl.CostEstimate(
            flops=S * cells * 2 * 27 * C, bytes_accessed=8 * S * cells * C, transcendentals=0
        ),
        name="adjoint",
    )(*grad_pieces[:X], *grad_halo, grad_merged, taps).reshape(S, C, X, Y, Z)

    moved = swap_in_group(reduced.reshape(gx, S // gx, hx, hy * hz, O), "gx")
    moved = moved.transpose(1, 0, 2, 3, 4).reshape(gy, per_group, gx * hx, hy * hz, O)
    moved = swap_in_group(moved, "gy").transpose(1, 2, 0, 3, 4)
    coarse = moved.reshape(per_group, gx * hx, gy * hy, hz, O).transpose(0, 4, 1, 2, 3)[None, None]

    total = total * (1.0 / math.sqrt(S * cells * devices))
    at = 8 * C
    grad_down_kernel = total[:at].reshape(2, 2, 2, C, O).transpose(4, 3, 0, 1, 2)
    wide = C * (H // Z)
    halves = total[at : at + 2 * wide].reshape(2, H // Z, C, Z).transpose(0, 2, 1, 3)
    halves = halves.reshape(2, C, H)
    grad_depth_kernel = total[at + 2 * wide : rows, :27].reshape(C, 3, 3, 3)
    return (
        coarse,
        grad_fields,
        grad_depth_kernel,
        halves[1].T,
        halves[0],
        grad_down_kernel,
    )


def solution(mesh):
    placed = (
        P(None, None, "gx", "gy", None),
        P(),
        P(),
        P(),
        P(),
        P("gx", "gy", None, None, None, None, None),
    )
    return jax.shard_map(
        per_device,
        mesh=mesh,
        in_specs=placed,
        out_specs=(
            P("gx", "gy", None, None, None, None, None),
            P(None, None, "gx", "gy", None),
            P(),
            P(),
            P(),
            P(),
        ),
        check_vma=False,
    )
```

```python
import functools
import math

import jax
import jax.numpy as jnp
from jax import lax
from jax.experimental import pallas as pl
from jax.experimental.pallas import tpu as pltpu
from jax.sharding import PartitionSpec as P

GRIDC = 4
F32 = jnp.float32
BF16 = jnp.bfloat16
VMEM_LIMIT = 40 * 1024 * 1024
CT = 8
GELU_C = math.sqrt(2.0 / math.pi)
GELU_A = 0.044715


def dot(a, b, ca, cb):
    return lax.dot_general(a, b, (((ca,), (cb,)), ((), ())), preferred_element_type=F32)


def sides():
    p, q = lax.axis_index("gx") % 2, lax.axis_index("gy") % 2
    return p, q


def write_pieces(row, Y, near, far, first, second):
    p, q = sides()
    for k, (x, plane) in enumerate(((1 - p, near), (p, far))):
        for y in range(Y):
            plane[0, y + 1] = row(x, y)
        first[0, k] = row(x, (1 - q) * (Y - 1))
        second[0, k] = row(x, q * (Y - 1))


def piece_shapes(S, Y, C, Z):
    return [jax.ShapeDtypeStruct((S, Y + 2, C, Z), BF16)] * 2 + [
        jax.ShapeDtypeStruct((S, 2, C, Z), BF16)
    ] * 2


def piece_specs(Y, C, Z):
    return [pl.BlockSpec((1, Y + 2, C, Z), lambda s: (s, 0, 0, 0))] * 2 + [
        pl.BlockSpec((1, 2, C, Z), lambda s: (s, 0, 0, 0))
    ] * 2


def plane_specs(Y, C, Z):
    return [pl.BlockSpec((1, Y + 2, C, Z), lambda s: (s, 0, 0, 0))] * 4


def swap_pairs(n, start):
    return [pair for i in range(start, n - 1, 2) for pair in ((i, i + 1), (i + 1, i))]


def exchange_halo(pieces, Y):
    near, far, first, second = pieces
    nx, ny = lax.axis_size("gx"), lax.axis_size("gy")
    _, q = sides()
    first = lax.ppermute(first, "gy", swap_pairs(ny, 0))
    second = lax.ppermute(second, "gy", swap_pairs(ny, 1))
    planes = []
    for k, plane in enumerate((near, far)):
        plane = lax.dynamic_update_slice_in_dim(
            plane, first[:, k : k + 1], (1 - q) * (Y + 1), axis=1
        )
        plane = lax.dynamic_update_slice_in_dim(plane, second[:, k : k + 1], q * (Y + 1), axis=1)
        planes.append(plane)
    from_near = lax.ppermute(planes[0], "gx", swap_pairs(nx, 0))
    from_far = lax.ppermute(planes[1], "gx", swap_pairs(nx, 1))
    return [*planes, from_near, from_far]


def fill_taps(w_ref, wb, flip):
    C, Z = wb.shape[1:]
    for t in range(27):
        source = 26 - t if flip else t
        wb[t] = jnp.broadcast_to(w_ref[:, source : source + 1], (C, Z))


def fill_padded(planes, Fs):
    p, _ = sides()
    rows = planes[0].shape[1]
    for x, plane in zip((2 - p, 1 + p, 3 * (1 - p), 3 * p), planes):
        for y in range(rows):
            Fs[x * rows + y] = plane[0, y].astype(F32)


def conv_tile(Fs, wb, channels, X, Y, lane, store):
    Z = Fs.shape[2]
    for x in range(X):
        for y in range(Y):
            acc = [None, None, None]
            for a in range(3):
                for b in range(3):
                    f = Fs[(x + a) * (Y + 2) + y + b, channels, :]
                    for e in range(3):
                        term = wb[(a * 3 + b) * 3 + e, channels, :] * f
                        acc[e] = term if acc[e] is None else acc[e] + term
            left = jnp.where(lane == 0, 0.0, pltpu.roll(acc[0], 1, 1))
            right = jnp.where(lane == Z - 1, 0.0, pltpu.roll(acc[2], Z - 1, 1))
            store(x, y, acc[1] + left + right)


def split_kernel(X, Y, C, Z, f_ref, near, far, first, second, wide):
    wide[...] = f_ref[0].astype(F32)

    def row(x, y):
        return wide[pl.ds(x * Y + y, C, stride=X * Y), :].astype(BF16)

    write_pieces(row, Y, near, far, first, second)


def main_kernel(dims, *refs):
    X, Y, C, Z, H, O = dims
    hx, NP = X // 2, Y // 4
    cells = X * Y * Z
    quarter = (Y // 2) * (Z // 2)
    planes = refs[:4]
    gd_ref, w_ref, pinT_ref, pout_ref, wd_ref, red_ref, gm_ref = refs[4:11]
    pieces, packed_ref = refs[11:15], refs[15]
    Fs, wb, Ds, GMs, Mb, Pt, G1, adw, adown, aout, ain, pin, poutT = refs[16:]
    step = pl.program_id(0)

    @pl.when(step == 0)
    def _():
        fill_taps(w_ref, wb, False)
        adw[...] = jnp.zeros_like(adw)
        adown[...] = jnp.zeros_like(adown)
        aout[...] = jnp.zeros_like(aout)
        ain[...] = jnp.zeros_like(ain)
        pin[...] = pinT_ref[...].astype(F32).T.astype(BF16)
        poutT[...] = pout_ref[...].astype(F32).T.astype(BF16)

    fill_padded(planes, Fs)
    lane = lax.broadcasted_iota(jnp.int32, (CT, Z), 1)

    fine = lax.broadcasted_iota(jnp.int32, (2 * Z, 2 * Z), 0)
    coarse = lax.broadcasted_iota(jnp.int32, (2 * Z, 2 * Z), 1)
    goes = (coarse // Z) * 1 + ((coarse % Z) % (Z // 2)) * 2 + ((coarse % Z) // (Z // 2)) * Z
    perm = jnp.where(fine == goes, 1.0, 0.0).astype(BF16)

    for X0 in range(hx):
        gp = dot(wd_ref[...], gd_ref[0, X0], 1, 1).astype(BF16)
        for a in range(2):
            for b in range(2):
                for p in range(NP):
                    src = ((a * 2 + b) * 2) * C
                    dst = ((a * 2 + b) * NP + p) * C
                    for e in range(2):
                        Mb[dst : dst + C, e * Z : (e + 1) * Z] = gp[
                            src + e * C : src + (e + 1) * C, p * Z : (p + 1) * Z
                        ]
        gm = dot(Mb[...], perm, 1, 1).astype(BF16)
        for a in range(2):
            for b in range(2):
                for p in range(NP):
                    src = ((a * 2 + b) * NP + p) * C
                    for q in range(2):
                        x, y = 2 * X0 + a, 2 * (2 * p + q) + b
                        value = gm[src : src + C, q * Z : (q + 1) * Z]
                        gm_ref[0, x, y] = value
                        r = x * Y + y
                        GMs[:, r * Z : (r + 1) * Z] = value

    def conv_body(i, carry):
        channels = pl.ds(pl.multiple_of(i * CT, CT), CT)

        def store(x, y, value):
            r = x * Y + y
            Ds[channels, r * Z : (r + 1) * Z] = value

        conv_tile(Fs, wb, channels, X, Y, lane, store)
        return carry

    lax.fori_loop(0, C // CT, conv_body, 0)

    width = 4 * Z

    for X0 in range(hx):

        def chunk_body(i, carry):
            a, p = i // NP, i % NP
            x = 2 * X0 + a
            columns = pl.ds(pl.multiple_of((x * NP + p) * width, width), width)
            depth = Ds[:, columns].astype(BF16)
            gm = GMs[:, columns]
            pre = dot(pin[...], depth, 1, 0)
            sq = pre * pre
            t = jnp.tanh(pre * (GELU_C + (GELU_C * GELU_A) * sq))
            h = 0.5 + 0.5 * t
            act = pre * h
            slope = h + act * (1.0 - h) * (2.0 * GELU_C + (6.0 * GELU_C * GELU_A) * sq)
            active = act.astype(BF16)
            branch = dot(pout_ref[...], active, 1, 0)
            for j in range(4):
                row = (x + 1) * (Y + 2) + 4 * p + j + 1
                merged = (Fs[row] + branch[:, j * Z : (j + 1) * Z]).astype(BF16)
                start = pl.multiple_of(((a * 2 + j % 2) * NP + p) * C, C)
                Mb[pl.ds(start, C), (j // 2) * Z : (j // 2 + 1) * Z] = merged
            grad_pre = (dot(poutT[...], gm, 1, 0) * slope).astype(BF16)
            grad_depth = dot(pinT_ref[...], grad_pre, 1, 0).astype(BF16).astype(F32)
            for j in range(4):
                G1[x * Y + 4 * p + j] = grad_depth[:, j * Z : (j + 1) * Z]
            aout[...] += dot(gm, active, 1, 1)
            ain[...] += dot(depth, grad_pre, 1, 1)
            return carry

        lax.fori_loop(0, 2 * NP, chunk_body, 0)

        pt = dot(Mb[...], perm, 1, 0).astype(BF16)
        for a in range(2):
            for b in range(2):
                for p in range(NP):
                    src = ((a * 2 + b) * NP + p) * C
                    for e in range(2):
                        dst = ((a * 2 + b) * 2 + e) * C
                        Pt[dst : dst + C, p * Z : (p + 1) * Z] = pt[
                            src : src + C, e * Z : (e + 1) * Z
                        ]
        red_ref[0, X0] = dot(Pt[...], wd_ref[...], 0, 0).astype(BF16)
        adown[...] += dot(Pt[...], gd_ref[0, X0], 1, 0)

    write_pieces(lambda x, y: G1[x * Y + y].astype(BF16), Y, *pieces)

    def tap_body(i, carry):
        channels = pl.ds(pl.multiple_of(i * CT, CT), CT)
        sums = [None] * 27
        for x in range(X):
            for y in range(Y):
                g = G1[x * Y + y, channels, :]
                gs = (
                    jnp.where(lane == Z - 1, 0.0, pltpu.roll(g, Z - 1, 1)),
                    g,
                    jnp.where(lane == 0, 0.0, pltpu.roll(g, 1, 1)),
                )
                for a in range(3):
                    for b in range(3):
                        f = Fs[(x + a) * (Y + 2) + y + b, channels, :]
                        for e in range(3):
                            t = (a * 3 + b) * 3 + e
                            term = gs[e] * f
                            sums[t] = term if sums[t] is None else sums[t] + term
        for t in range(27):
            adw[t, channels, :] += sums[t]
        return carry

    lax.fori_loop(0, C // CT, tap_body, 0)

    @pl.when(step == pl.num_programs(0) - 1)
    def _():
        columns = lax.broadcasted_iota(jnp.int32, (C, Z), 1)
        taps = jnp.zeros((C, Z), F32)
        for t in range(27):
            taps = jnp.where(columns == t, jnp.sum(adw[t], axis=1, keepdims=True), taps)
        at = 0
        for block in (
            [adown[...]]
            + [aout[:, k : k + Z] for k in range(0, H, Z)]
            + [ain[:, k : k + Z] for k in range(0, H, Z)]
            + [taps]
        ):
            packed_ref[at : at + block.shape[0], :] = block.astype(BF16)
            at += block.shape[0]
        if at < packed_ref.shape[0]:
            rest = packed_ref.shape[0] - at
            packed_ref[at:, :] = jnp.zeros((rest, Z), BF16)


def adjoint_kernel(X, Y, C, Z, *refs):
    planes = refs[:4]
    gm_ref, w_ref, out_ref, Fs, wb, wide = refs[4:]

    @pl.when(pl.program_id(0) == 0)
    def _():
        fill_taps(w_ref, wb, True)

    fill_padded(planes, Fs)
    lane = lax.broadcasted_iota(jnp.int32, (CT, Z), 1)
    rows = X * Y

    def conv_body(i, carry):
        first = pl.multiple_of(i * CT, CT)
        channels = pl.ds(first, CT)

        def store(x, y, value):
            r = x * Y + y
            total = value + gm_ref[0, x, y, channels, :].astype(F32)
            wide[pl.ds(first * rows + r, CT, stride=rows), :] = total

        conv_tile(Fs, wb, channels, X, Y, lane, store)
        return carry

    lax.fori_loop(0, C // CT, conv_body, 0)
    out_ref[0] = wide[...].astype(BF16)


def swap_in_group(blocks, axis):
    g = blocks.shape[0]
    if g == 1:
        return blocks
    n = lax.axis_size(axis)
    member = lax.axis_index(axis) % g
    got = [lax.dynamic_index_in_dim(blocks, member, 0, keepdims=False)]
    for k in range(1, g):
        out = lax.dynamic_index_in_dim(blocks, (member + k) % g, 0, keepdims=False)
        pairs = [(i, i - i % g + (i + k) % g) for i in range(n)]
        got.append(lax.ppermute(out, axis, pairs))
    if g == 2:
        first = member == 0
        return jnp.stack([jnp.where(first, got[0], got[1]), jnp.where(first, got[1], got[0])])
    got = jnp.stack(got)
    return jnp.take(got, (member - jnp.arange(g, dtype=jnp.int32)) % g, axis=0)


def sum_share(packed, devices):
    blocks = packed.reshape(devices, -1, packed.shape[1])
    mine = lax.all_to_all(blocks, ("gx", "gy"), 0, 0)
    return jnp.sum(mine.astype(F32), axis=0).astype(BF16)


def gather_shares(share, devices):
    every = jnp.broadcast_to(share[None], (devices,) + share.shape)
    every = lax.all_to_all(every, ("gx", "gy"), 0, 0)
    return every.reshape(-1, share.shape[1]).astype(F32)


def per_device(fields, depth_kernel, point_in, point_out, down_kernel, cotangent):
    S, C, X, Y, Z = fields.shape
    assert X == 2 and Y % 4 == 0
    H, O = point_in.shape[0], down_kernel.shape[0]
    hx, hy, hz = X // 2, Y // 2, Z // 2
    nx, ny = lax.axis_size("gx"), lax.axis_size("gy")
    devices = nx * ny
    gx, gy = nx // GRIDC, ny // GRIDC
    per_group = S // (gx * gy)
    params = pltpu.CompilerParams(
        dimension_semantics=("arbitrary",), vmem_limit_bytes=VMEM_LIMIT
    )

    pieces = pl.pallas_call(
        functools.partial(split_kernel, X, Y, C, Z),
        grid=(S,),
        in_specs=[pl.BlockSpec((1, C * X * Y, Z), lambda s: (s, 0, 0))],
        out_specs=piece_specs(Y, C, Z),
        out_shape=piece_shapes(S, Y, C, Z),
        scratch_shapes=[pltpu.VMEM((C * X * Y, Z), F32)],
        compiler_params=params,
        name="split_fields",
    )(fields.reshape(S, C * X * Y, Z))

    planes = exchange_halo(pieces, Y)

    moved = cotangent[0, 0].transpose(0, 2, 3, 4, 1)
    moved = moved.reshape(per_group, gx * hx, gy, hy * hz, O).transpose(2, 0, 1, 3, 4)
    moved = swap_in_group(moved, "gy").reshape(gy * per_group, gx, hx, hy * hz, O)
    moved = swap_in_group(moved.transpose(1, 0, 2, 3, 4), "gx")
    grad_down = moved.reshape(S, hx, hy * hz, O)

    wd = down_kernel.transpose(2, 3, 4, 1, 0).reshape(8 * C, O)
    taps = depth_kernel.reshape(C, 27).astype(F32)

    rows = 8 * C + 2 * C * (H // Z) + C
    chunk = -(-rows // (16 * devices)) * 16
    cells = X * Y * Z
    whole = lambda shape: pl.BlockSpec(shape, lambda s: (0,) * len(shape))
    flops = S * cells * (2 * 6 * C * H + 2 * 3 * C * O + 2 * 2 * 27 * C)
    out = pl.pallas_call(
        functools.partial(main_kernel, (X, Y, C, Z, H, O)),
        grid=(S,),
        in_specs=plane_specs(Y, C, Z)
        + [
            pl.BlockSpec((1, hx, hy * hz, O), lambda s: (s, 0, 0, 0)),
            whole((C, 27)),
            whole((C, H)),
            whole((C, H)),
            whole((8 * C, O)),
        ],
        out_specs=[
            pl.BlockSpec((1, hx, hy * hz, O), lambda s: (s, 0, 0, 0)),
            pl.BlockSpec((1, X, Y, C, Z), lambda s: (s, 0, 0, 0, 0)),
        ]
        + piece_specs(Y, C, Z)
        + [whole((devices * chunk, Z))],
        out_shape=[
            jax.ShapeDtypeStruct((S, hx, hy * hz, O), BF16),
            jax.ShapeDtypeStruct((S, X, Y, C, Z), BF16),
        ]
        + piece_shapes(S, Y, C, Z)
        + [jax.ShapeDtypeStruct((devices * chunk, Z), BF16)],
        scratch_shapes=[
            pltpu.VMEM(((X + 2) * (Y + 2), C, Z), F32),
            pltpu.VMEM((27, C, Z), F32),
            pltpu.VMEM((C, cells), F32),
            pltpu.VMEM((C, cells), BF16),
            pltpu.VMEM((Y * C, 2 * Z), BF16),
            pltpu.VMEM((8 * C, hy * hz), BF16),
            pltpu.VMEM((X * Y, C, Z), F32),
            pltpu.VMEM((27, C, Z), F32),
            pltpu.VMEM((8 * C, O), F32),
            pltpu.VMEM((C, H), F32),
            pltpu.VMEM((C, H), F32),
            pltpu.VMEM((H, C), BF16),
            pltpu.VMEM((H, C), BF16),
        ],
        compiler_params=params,
        cost_estimate=pl.CostEstimate(
            flops=flops, bytes_accessed=8 * S * cells * C, transcendentals=S * cells * H
        ),
        name="main",
    )(*planes, grad_down, taps, point_in.T, point_out, wd)
    reduced, grad_merged = out[:2]
    grad_pieces, packed = out[2:6], out[6]

    grad_planes = exchange_halo(grad_pieces, Y)

    total = sum_share(packed, devices)
    total, *grad_planes = lax.optimization_barrier((total, *grad_planes))
    total = gather_shares(total, devices)

    grad_fields = pl.pallas_call(
        functools.partial(adjoint_kernel, X, Y, C, Z),
        grid=(S,),
        in_specs=plane_specs(Y, C, Z)
        + [pl.BlockSpec((1, X, Y, C, Z), lambda s: (s, 0, 0, 0, 0)), whole((C, 27))],
        out_specs=pl.BlockSpec((1, C * X * Y, Z), lambda s: (s, 0, 0)),
        out_shape=jax.ShapeDtypeStruct((S, C * X * Y, Z), BF16),
        scratch_shapes=[
            pltpu.VMEM(((X + 2) * (Y + 2), C, Z), F32),
            pltpu.VMEM((27, C, Z), F32),
            pltpu.VMEM((C * X * Y, Z), F32),
        ],
        compiler_params=params,
        cost_estimate=pl.CostEstimate(
            flops=S * cells * 2 * 27 * C, bytes_accessed=8 * S * cells * C, transcendentals=0
        ),
        name="adjoint",
    )(*grad_planes, grad_merged, taps).reshape(S, C, X, Y, Z)

    moved = swap_in_group(reduced.reshape(gx, S // gx, hx, hy * hz, O), "gx")
    moved = moved.transpose(1, 0, 2, 3, 4).reshape(gy, per_group, gx * hx, hy * hz, O)
    moved = swap_in_group(moved, "gy").transpose(1, 2, 0, 3, 4)
    coarse = moved.reshape(per_group, gx * hx, gy * hy, hz, O).transpose(0, 4, 1, 2, 3)[None, None]

    total = total * (1.0 / math.sqrt(S * cells * devices))
    at = 8 * C
    grad_down_kernel = total[:at].reshape(2, 2, 2, C, O).transpose(4, 3, 0, 1, 2)
    wide = C * (H // Z)
    halves = total[at : at + 2 * wide].reshape(2, H // Z, C, Z).transpose(0, 2, 1, 3)
    halves = halves.reshape(2, C, H)
    grad_depth_kernel = total[at + 2 * wide : rows, :27].reshape(C, 3, 3, 3)
    return (
        coarse,
        grad_fields,
        grad_depth_kernel,
        halves[1].T,
        halves[0],
        grad_down_kernel,
    )


def solution(mesh):
    placed = (
        P(None, None, "gx", "gy", None),
        P(),
        P(),
        P(),
        P(),
        P("gx", "gy", None, None, None, None, None),
    )
    return jax.shard_map(
        per_device,
        mesh=mesh,
        in_specs=placed,
        out_specs=(
            P("gx", "gy", None, None, None, None, None),
            P(None, None, "gx", "gy", None),
            P(),
            P(),
            P(),
            P(),
        ),
        check_vma=False,
    )
```

```python
import functools
import math

import jax
import jax.numpy as jnp
from jax import lax
from jax.experimental import pallas as pl
from jax.experimental.pallas import tpu as pltpu
from jax.sharding import PartitionSpec as P

GRIDC = 4
F32 = jnp.float32
BF16 = jnp.bfloat16
VMEM_LIMIT = 40 * 1024 * 1024
CT = 8
GELU_C = math.sqrt(2.0 / math.pi)
GELU_A = 0.044715


def dot(a, b, ca, cb):
    return lax.dot_general(a, b, (((ca,), (cb,)), ((), ())), preferred_element_type=F32)


def sides():
    return lax.axis_index("gx") % 2, lax.axis_index("gy") % 2


def write_pieces(row, Y, near, far, first, second):
    p, q = sides()
    for k, (x, plane) in enumerate(((1 - p, near), (p, far))):
        for y in range(Y):
            plane[0, y] = row(x, y)
        first[k, 0] = row(x, (1 - q) * (Y - 1))
        second[k, 0] = row(x, q * (Y - 1))


def piece_shapes(S, Y, C, Z):
    return [jax.ShapeDtypeStruct((S, Y, C, Z), BF16)] * 2 + [
        jax.ShapeDtypeStruct((2, S, C, Z), BF16)
    ] * 2


def piece_specs(Y, C, Z):
    return [pl.BlockSpec((1, Y, C, Z), lambda s: (s, 0, 0, 0))] * 2 + [
        pl.BlockSpec((2, 1, C, Z), lambda s: (0, s, 0, 0))
    ] * 2


def widened_specs(Y, C, Z):
    return [pl.BlockSpec((1, Y, C, Z), lambda s: (s, 0, 0, 0))] * 4 + [
        pl.BlockSpec((2, 1, C, Z), lambda s: (0, s, 0, 0))
    ] * 4


def swap_pairs(n, start):
    return [pair for i in range(start, n - 1, 2) for pair in ((i, i + 1), (i + 1, i))]


def exchange_halo(pieces):
    near, far, first, second = pieces
    nx, ny = lax.axis_size("gx"), lax.axis_size("gy")
    from_far = lax.ppermute(far, "gx", swap_pairs(nx, 1))
    first = lax.ppermute(first, "gy", swap_pairs(ny, 0))
    second = lax.ppermute(second, "gy", swap_pairs(ny, 1))
    from_near = lax.ppermute(near, "gx", swap_pairs(nx, 0))
    corners = [jnp.stack([first[k], second[k]]) for k in range(2)]
    corner_far = lax.ppermute(corners[1], "gx", swap_pairs(nx, 1))
    corner_near = lax.ppermute(corners[0], "gx", swap_pairs(nx, 0))
    return [near, far, from_near, from_far, first, second, corner_near, corner_far]


def fill_taps(w_ref, wb, flip):
    C, Z = wb.shape[1:]
    for t in range(27):
        source = 26 - t if flip else t
        wb[t] = jnp.broadcast_to(w_ref[:, source : source + 1], (C, Z))


def fill_padded(pieces, Fs):
    near, far, from_near, from_far, first, second, corner_near, corner_far = pieces
    p, q = sides()
    Y = near.shape[1]
    places = (2 - p, 1 + p, 3 * (1 - p), 3 * p)
    rims = ((first, 0), (second, 0)), ((first, 1), (second, 1))
    rims += ((corner_near, 0), (corner_near, 1)), ((corner_far, 0), (corner_far, 1))
    for x, plane, ((r0, k0), (r1, k1)) in zip(places, (near, far, from_near, from_far), rims):
        for y in range(Y):
            Fs[x * (Y + 2) + y + 1] = plane[0, y].astype(F32)
        Fs[x * (Y + 2) + (1 - q) * (Y + 1)] = r0[k0, 0].astype(F32)
        Fs[x * (Y + 2) + q * (Y + 1)] = r1[k1, 0].astype(F32)


def conv_tile(Fs, wb, channels, X, Y, lane, store):
    Z = Fs.shape[2]
    weights = [wb[t, channels, :] for t in range(27)]
    for x in range(X):
        for y in range(Y):
            acc = [None, None, None]
            for a in range(3):
                for b in range(3):
                    f = Fs[(x + a) * (Y + 2) + y + b, channels, :]
                    for e in range(3):
                        term = weights[(a * 3 + b) * 3 + e] * f
                        acc[e] = term if acc[e] is None else acc[e] + term
            left = jnp.where(lane == 0, 0.0, pltpu.roll(acc[0], 1, 1))
            right = jnp.where(lane == Z - 1, 0.0, pltpu.roll(acc[2], Z - 1, 1))
            store(x, y, acc[1] + left + right)


def split_kernel(X, Y, C, Z, f_ref, near, far, first, second, wide):
    wide[...] = f_ref[0].astype(F32)

    def row(x, y):
        return wide[pl.ds(x * Y + y, C, stride=X * Y), :].astype(BF16)

    write_pieces(row, Y, near, far, first, second)


def main_kernel(dims, *refs):
    X, Y, C, Z, H, O = dims
    hx, NP = X // 2, Y // 4
    cells = X * Y * Z
    quarter = (Y // 2) * (Z // 2)
    widened = refs[:8]
    gd_ref, w_ref, pinT_ref, pout_ref, wd_ref, red_ref, gm_ref = refs[8:15]
    pieces, packed_ref = refs[15:19], refs[19]
    Fs, wb, Ds, GMs, Mb, Pt, G1, adw, adown, aout, ain, pin, poutT = refs[20:33]
    pre_s, ga_s, act_s, gp_s = refs[33:]
    step = pl.program_id(0)

    @pl.when(step == 0)
    def _():
        fill_taps(w_ref, wb, False)
        adw[...] = jnp.zeros_like(adw)
        adown[...] = jnp.zeros_like(adown)
        aout[...] = jnp.zeros_like(aout)
        ain[...] = jnp.zeros_like(ain)
        pin[...] = pinT_ref[...].astype(F32).T.astype(BF16)
        poutT[...] = pout_ref[...].astype(F32).T.astype(BF16)

    fill_padded(widened, Fs)
    lane = lax.broadcasted_iota(jnp.int32, (CT, Z), 1)

    fine = lax.broadcasted_iota(jnp.int32, (2 * Z, 2 * Z), 0)
    coarse = lax.broadcasted_iota(jnp.int32, (2 * Z, 2 * Z), 1)
    goes = (coarse // Z) * 1 + ((coarse % Z) % (Z // 2)) * 2 + ((coarse % Z) // (Z // 2)) * Z
    perm = jnp.where(fine == goes, 1.0, 0.0).astype(BF16)

    for X0 in range(hx):
        gp = dot(wd_ref[...], gd_ref[0, X0], 1, 1).astype(BF16)
        for a in range(2):
            for b in range(2):
                for p in range(NP):
                    src = ((a * 2 + b) * 2) * C
                    dst = ((a * 2 + b) * NP + p) * C
                    for e in range(2):
                        Mb[dst : dst + C, e * Z : (e + 1) * Z] = gp[
                            src + e * C : src + (e + 1) * C, p * Z : (p + 1) * Z
                        ]
        gm = dot(Mb[...], perm, 1, 1).astype(BF16)
        for a in range(2):
            for b in range(2):
                for p in range(NP):
                    src = ((a * 2 + b) * NP + p) * C
                    for q in range(2):
                        x, y = 2 * X0 + a, 2 * (2 * p + q) + b
                        value = gm[src : src + C, q * Z : (q + 1) * Z]
                        gm_ref[0, x, y] = value
                        r = x * Y + y
                        GMs[:, r * Z : (r + 1) * Z] = value

    def conv_body(i, carry):
        channels = pl.ds(pl.multiple_of(i * CT, CT), CT)

        def store(x, y, value):
            r = x * Y + y
            Ds[channels, r * Z : (r + 1) * Z] = value

        conv_tile(Fs, wb, channels, X, Y, lane, store)
        return carry

    lax.fori_loop(0, C // CT, conv_body, 0)

    width = 4 * Z

    for X0 in range(hx):

        for i in range(2 * NP):
            a, p = i // NP, i % NP
            x = 2 * X0 + a
            columns = slice((x * NP + p) * width, (x * NP + p + 1) * width)
            depth = Ds[:, columns].astype(BF16)
            gm = GMs[:, columns]
            pre_s[i] = dot(pin[...], depth, 1, 0)
            ga_s[i] = dot(poutT[...], gm, 1, 0)
            for h0 in range(0, H, 16):
                hs = slice(h0, h0 + 16)
                pre = pre_s[i, hs, :]
                sq = pre * pre
                t = jnp.tanh(pre * (GELU_C + (GELU_C * GELU_A) * sq))
                h = 0.5 + 0.5 * t
                act = pre * h
                slope = h + act * (1.0 - h) * (2.0 * GELU_C + (6.0 * GELU_C * GELU_A) * sq)
                act_s[i, hs, :] = act.astype(BF16)
                gp_s[i, hs, :] = (ga_s[i, hs, :] * slope).astype(BF16)
            active, grad_pre = act_s[i], gp_s[i]
            branch = dot(pout_ref[...], active, 1, 0)
            for j in range(4):
                row = (x + 1) * (Y + 2) + 4 * p + j + 1
                merged = (Fs[row] + branch[:, j * Z : (j + 1) * Z]).astype(BF16)
                start = ((a * 2 + j % 2) * NP + p) * C
                Mb[start : start + C, (j // 2) * Z : (j // 2 + 1) * Z] = merged
            grad_depth = dot(pinT_ref[...], grad_pre, 1, 0).astype(BF16).astype(F32)
            for j in range(4):
                G1[x * Y + 4 * p + j] = grad_depth[:, j * Z : (j + 1) * Z]
            aout[...] += dot(gm, active, 1, 1)
            ain[...] += dot(depth, grad_pre, 1, 1)

        pt = dot(Mb[...], perm, 1, 0).astype(BF16)
        for a in range(2):
            for b in range(2):
                for p in range(NP):
                    src = ((a * 2 + b) * NP + p) * C
                    for e in range(2):
                        dst = ((a * 2 + b) * 2 + e) * C
                        Pt[dst : dst + C, p * Z : (p + 1) * Z] = pt[
                            src : src + C, e * Z : (e + 1) * Z
                        ]
        red_ref[0, X0] = dot(Pt[...], wd_ref[...], 0, 0).astype(BF16)
        adown[...] += dot(Pt[...], gd_ref[0, X0], 1, 0)

    write_pieces(lambda x, y: G1[x * Y + y].astype(BF16), Y, *pieces)

    def tap_body(i, carry):
        channels = pl.ds(pl.multiple_of(i * CT, CT), CT)
        sums = [None] * 27
        for x in range(X):
            for y in range(Y):
                g = G1[x * Y + y, channels, :]
                gs = (
                    jnp.where(lane == Z - 1, 0.0, pltpu.roll(g, Z - 1, 1)),
                    g,
                    jnp.where(lane == 0, 0.0, pltpu.roll(g, 1, 1)),
                )
                for a in range(3):
                    for b in range(3):
                        f = Fs[(x + a) * (Y + 2) + y + b, channels, :]
                        for e in range(3):
                            t = (a * 3 + b) * 3 + e
                            term = gs[e] * f
                            sums[t] = term if sums[t] is None else sums[t] + term
        for t in range(27):
            adw[t, channels, :] += sums[t]
        return carry

    lax.fori_loop(0, C // CT, tap_body, 0)

    @pl.when(step == pl.num_programs(0) - 1)
    def _():
        columns = lax.broadcasted_iota(jnp.int32, (C, Z), 1)
        taps = jnp.zeros((C, Z), F32)
        for t in range(27):
            taps = jnp.where(columns == t, jnp.sum(adw[t], axis=1, keepdims=True), taps)
        at = 0
        for block in (
            [adown[...]]
            + [aout[:, k : k + Z] for k in range(0, H, Z)]
            + [ain[:, k : k + Z] for k in range(0, H, Z)]
            + [taps]
        ):
            packed_ref[at : at + block.shape[0], :] = block.astype(BF16)
            at += block.shape[0]
        if at < packed_ref.shape[0]:
            rest = packed_ref.shape[0] - at
            packed_ref[at:, :] = jnp.zeros((rest, Z), BF16)


def adjoint_kernel(X, Y, C, Z, *refs):
    widened = refs[:8]
    gm_ref, w_ref, out_ref, Fs, wb, wide = refs[8:]

    @pl.when(pl.program_id(0) == 0)
    def _():
        fill_taps(w_ref, wb, True)

    fill_padded(widened, Fs)
    lane = lax.broadcasted_iota(jnp.int32, (CT, Z), 1)
    rows = X * Y

    def conv_body(i, carry):
        first = pl.multiple_of(i * CT, CT)
        channels = pl.ds(first, CT)

        def store(x, y, value):
            r = x * Y + y
            total = value + gm_ref[0, x, y, channels, :].astype(F32)
            wide[pl.ds(first * rows + r, CT, stride=rows), :] = total

        conv_tile(Fs, wb, channels, X, Y, lane, store)
        return carry

    lax.fori_loop(0, C // CT, conv_body, 0)
    out_ref[0] = wide[...].astype(BF16)


def swap_in_group(blocks, axis):
    g = blocks.shape[0]
    if g == 1:
        return blocks
    n = lax.axis_size(axis)
    member = lax.axis_index(axis) % g
    got = [lax.dynamic_index_in_dim(blocks, member, 0, keepdims=False)]
    for k in range(1, g):
        out = lax.dynamic_index_in_dim(blocks, (member + k) % g, 0, keepdims=False)
        pairs = [(i, i - i % g + (i + k) % g) for i in range(n)]
        got.append(lax.ppermute(out, axis, pairs))
    if g == 2:
        first = member == 0
        return jnp.stack([jnp.where(first, got[0], got[1]), jnp.where(first, got[1], got[0])])
    got = jnp.stack(got)
    return jnp.take(got, (member - jnp.arange(g, dtype=jnp.int32)) % g, axis=0)


def sum_share(packed, devices):
    blocks = packed.reshape(devices, -1, packed.shape[1])
    mine = lax.all_to_all(blocks, ("gx", "gy"), 0, 0)
    return jnp.sum(mine.astype(F32), axis=0).astype(BF16)


def gather_shares(share, devices):
    every = jnp.broadcast_to(share[None], (devices,) + share.shape)
    every = lax.all_to_all(every, ("gx", "gy"), 0, 0)
    return every.reshape(-1, share.shape[1]).astype(F32)


def per_device(fields, depth_kernel, point_in, point_out, down_kernel, cotangent):
    S, C, X, Y, Z = fields.shape
    assert X == 2 and Y % 4 == 0
    H, O = point_in.shape[0], down_kernel.shape[0]
    hx, hy, hz = X // 2, Y // 2, Z // 2
    nx, ny = lax.axis_size("gx"), lax.axis_size("gy")
    devices = nx * ny
    gx, gy = nx // GRIDC, ny // GRIDC
    per_group = S // (gx * gy)
    params = pltpu.CompilerParams(
        dimension_semantics=("arbitrary",), vmem_limit_bytes=VMEM_LIMIT
    )

    pieces = pl.pallas_call(
        functools.partial(split_kernel, X, Y, C, Z),
        grid=(S,),
        in_specs=[pl.BlockSpec((1, C * X * Y, Z), lambda s: (s, 0, 0))],
        out_specs=piece_specs(Y, C, Z),
        out_shape=piece_shapes(S, Y, C, Z),
        scratch_shapes=[pltpu.VMEM((C * X * Y, Z), F32)],
        compiler_params=params,
        name="split_fields",
    )(fields.reshape(S, C * X * Y, Z))

    widened = exchange_halo(pieces)

    moved = cotangent[0, 0].transpose(0, 2, 3, 4, 1)
    moved = moved.reshape(per_group, gx * hx, gy, hy * hz, O).transpose(2, 0, 1, 3, 4)
    moved = swap_in_group(moved, "gy").reshape(gy * per_group, gx, hx, hy * hz, O)
    moved = swap_in_group(moved.transpose(1, 0, 2, 3, 4), "gx")
    grad_down = moved.reshape(S, hx, hy * hz, O)

    wd = down_kernel.transpose(2, 3, 4, 1, 0).reshape(8 * C, O)
    taps = depth_kernel.reshape(C, 27).astype(F32)

    rows = 8 * C + 2 * C * (H // Z) + C
    chunk = -(-rows // (16 * devices)) * 16
    cells = X * Y * Z
    whole = lambda shape: pl.BlockSpec(shape, lambda s: (0,) * len(shape))
    flops = S * cells * (2 * 6 * C * H + 2 * 3 * C * O + 2 * 2 * 27 * C)
    out = pl.pallas_call(
        functools.partial(main_kernel, (X, Y, C, Z, H, O)),
        grid=(S,),
        in_specs=widened_specs(Y, C, Z)
        + [
            pl.BlockSpec((1, hx, hy * hz, O), lambda s: (s, 0, 0, 0)),
            whole((C, 27)),
            whole((C, H)),
            whole((C, H)),
            whole((8 * C, O)),
        ],
        out_specs=[
            pl.BlockSpec((1, hx, hy * hz, O), lambda s: (s, 0, 0, 0)),
            pl.BlockSpec((1, X, Y, C, Z), lambda s: (s, 0, 0, 0, 0)),
        ]
        + piece_specs(Y, C, Z)
        + [whole((devices * chunk, Z))],
        out_shape=[
            jax.ShapeDtypeStruct((S, hx, hy * hz, O), BF16),
            jax.ShapeDtypeStruct((S, X, Y, C, Z), BF16),
        ]
        + piece_shapes(S, Y, C, Z)
        + [jax.ShapeDtypeStruct((devices * chunk, Z), BF16)],
        scratch_shapes=[
            pltpu.VMEM(((X + 2) * (Y + 2), C, Z), F32),
            pltpu.VMEM((27, C, Z), F32),
            pltpu.VMEM((C, cells), F32),
            pltpu.VMEM((C, cells), BF16),
            pltpu.VMEM((Y * C, 2 * Z), BF16),
            pltpu.VMEM((8 * C, hy * hz), BF16),
            pltpu.VMEM((X * Y, C, Z), F32),
            pltpu.VMEM((27, C, Z), F32),
            pltpu.VMEM((8 * C, O), F32),
            pltpu.VMEM((C, H), F32),
            pltpu.VMEM((C, H), F32),
            pltpu.VMEM((H, C), BF16),
            pltpu.VMEM((H, C), BF16),
            pltpu.VMEM((Y // 2, H, 4 * Z), F32),
            pltpu.VMEM((Y // 2, H, 4 * Z), F32),
            pltpu.VMEM((Y // 2, H, 4 * Z), BF16),
            pltpu.VMEM((Y // 2, H, 4 * Z), BF16),
        ],
        compiler_params=params,
        cost_estimate=pl.CostEstimate(
            flops=flops, bytes_accessed=8 * S * cells * C, transcendentals=S * cells * H
        ),
        name="main",
    )(*widened, grad_down, taps, point_in.T, point_out, wd)
    reduced, grad_merged = out[:2]
    grad_pieces, packed = out[2:6], out[6]

    grad_widened = exchange_halo(grad_pieces)

    total = sum_share(packed, devices)
    total, *grad_widened = lax.optimization_barrier((total, *grad_widened))
    total = gather_shares(total, devices)

    grad_fields = pl.pallas_call(
        functools.partial(adjoint_kernel, X, Y, C, Z),
        grid=(S,),
        in_specs=widened_specs(Y, C, Z)
        + [pl.BlockSpec((1, X, Y, C, Z), lambda s: (s, 0, 0, 0, 0)), whole((C, 27))],
        out_specs=pl.BlockSpec((1, C * X * Y, Z), lambda s: (s, 0, 0)),
        out_shape=jax.ShapeDtypeStruct((S, C * X * Y, Z), BF16),
        scratch_shapes=[
            pltpu.VMEM(((X + 2) * (Y + 2), C, Z), F32),
            pltpu.VMEM((27, C, Z), F32),
            pltpu.VMEM((C * X * Y, Z), F32),
        ],
        compiler_params=params,
        cost_estimate=pl.CostEstimate(
            flops=S * cells * 2 * 27 * C, bytes_accessed=8 * S * cells * C, transcendentals=0
        ),
        name="adjoint",
    )(*grad_widened, grad_merged, taps).reshape(S, C, X, Y, Z)

    moved = swap_in_group(reduced.reshape(gx, S // gx, hx, hy * hz, O), "gx")
    moved = moved.transpose(1, 0, 2, 3, 4).reshape(gy, per_group, gx * hx, hy * hz, O)
    moved = swap_in_group(moved, "gy").transpose(1, 2, 0, 3, 4)
    coarse = moved.reshape(per_group, gx * hx, gy * hy, hz, O).transpose(0, 4, 1, 2, 3)[None, None]

    total = total * (1.0 / math.sqrt(S * cells * devices))
    at = 8 * C
    grad_down_kernel = total[:at].reshape(2, 2, 2, C, O).transpose(4, 3, 0, 1, 2)
    wide = C * (H // Z)
    halves = total[at : at + 2 * wide].reshape(2, H // Z, C, Z).transpose(0, 2, 1, 3)
    halves = halves.reshape(2, C, H)
    grad_depth_kernel = total[at + 2 * wide : rows, :27].reshape(C, 3, 3, 3)
    return (
        coarse,
        grad_fields,
        grad_depth_kernel,
        halves[1].T,
        halves[0],
        grad_down_kernel,
    )


def solution(mesh):
    placed = (
        P(None, None, "gx", "gy", None),
        P(),
        P(),
        P(),
        P(),
        P("gx", "gy", None, None, None, None, None),
    )
    return jax.shard_map(
        per_device,
        mesh=mesh,
        in_specs=placed,
        out_specs=(
            P("gx", "gy", None, None, None, None, None),
            P(None, None, "gx", "gy", None),
            P(),
            P(),
            P(),
            P(),
        ),
        check_vma=False,
    )
```

```python
import functools
import math

import jax
import jax.numpy as jnp
from jax import lax
from jax.experimental import pallas as pl
from jax.experimental.pallas import tpu as pltpu
from jax.sharding import PartitionSpec as P

GRIDC = 4
F32 = jnp.float32
BF16 = jnp.bfloat16
VMEM_LIMIT = 40 * 1024 * 1024
CT = 8
GELU_C = math.sqrt(2.0 / math.pi)
GELU_A = 0.044715


def dot(a, b, ca, cb):
    return lax.dot_general(a, b, (((ca,), (cb,)), ((), ())), preferred_element_type=F32)


def sides():
    return lax.axis_index("gx") % 2, lax.axis_index("gy") % 2


def write_pieces(row, Y, near, far, first, second):
    p, q = sides()
    for k, (x, plane) in enumerate(((1 - p, near), (p, far))):
        for y in range(Y):
            plane[0, y] = row(x, y)
        first[k, 0] = row(x, (1 - q) * (Y - 1))
        second[k, 0] = row(x, q * (Y - 1))


def piece_shapes(S, Y, C, Z):
    return [jax.ShapeDtypeStruct((S, Y, C, Z), BF16)] * 2 + [
        jax.ShapeDtypeStruct((2, S, C, Z), BF16)
    ] * 2


def piece_specs(Y, C, Z):
    return [pl.BlockSpec((1, Y, C, Z), lambda s: (s, 0, 0, 0))] * 2 + [
        pl.BlockSpec((2, 1, C, Z), lambda s: (0, s, 0, 0))
    ] * 2


def widened_specs(Y, C, Z):
    return [pl.BlockSpec((1, Y, C, Z), lambda s: (s, 0, 0, 0))] * 4 + [
        pl.BlockSpec((2, 1, C, Z), lambda s: (0, s, 0, 0))
    ] * 4


def swap_pairs(n, start):
    return [pair for i in range(start, n - 1, 2) for pair in ((i, i + 1), (i + 1, i))]


def exchange_halo(pieces):
    near, far, first, second = pieces
    nx, ny = lax.axis_size("gx"), lax.axis_size("gy")
    from_far = lax.ppermute(far, "gx", swap_pairs(nx, 1))
    first = lax.ppermute(first, "gy", swap_pairs(ny, 0))
    second = lax.ppermute(second, "gy", swap_pairs(ny, 1))
    from_near = lax.ppermute(near, "gx", swap_pairs(nx, 0))
    corners = [jnp.stack([first[k], second[k]]) for k in range(2)]
    corner_far = lax.ppermute(corners[1], "gx", swap_pairs(nx, 1))
    corner_near = lax.ppermute(corners[0], "gx", swap_pairs(nx, 0))
    return [near, far, from_near, from_far, first, second, corner_near, corner_far]


def fill_padded(pieces, Fs):
    near, far, from_near, from_far, first, second, corner_near, corner_far = pieces
    p, q = sides()
    Y = near.shape[1]
    places = (2 - p, 1 + p, 3 * (1 - p), 3 * p)
    rims = ((first, 0), (second, 0)), ((first, 1), (second, 1))
    rims += ((corner_near, 0), (corner_near, 1)), ((corner_far, 0), (corner_far, 1))
    for x, plane, ((r0, k0), (r1, k1)) in zip(places, (near, far, from_near, from_far), rims):
        for y in range(Y):
            Fs[x * (Y + 2) + y + 1] = plane[0, y].astype(F32)
        Fs[x * (Y + 2) + (1 - q) * (Y + 1)] = r0[k0, 0].astype(F32)
        Fs[x * (Y + 2) + q * (Y + 1)] = r1[k1, 0].astype(F32)


def conv_tile(Fs, wb, flip, channels, X, Y, lane, store):
    Z = Fs.shape[2]
    weights = [wb[26 - t if flip else t, channels, :] for t in range(27)]
    for x in range(X):
        for y in range(Y):
            acc = [None, None, None]
            for a in range(3):
                for b in range(3):
                    f = Fs[(x + a) * (Y + 2) + y + b, channels, :]
                    for e in range(3):
                        term = weights[(a * 3 + b) * 3 + e] * f
                        acc[e] = term if acc[e] is None else acc[e] + term
            left = jnp.where(lane == 0, 0.0, pltpu.roll(acc[0], 1, 1))
            right = jnp.where(lane == Z - 1, 0.0, pltpu.roll(acc[2], Z - 1, 1))
            store(x, y, acc[1] + left + right)


def split_kernel(X, Y, C, Z, f_ref, near, far, first, second, wide):
    wide[...] = f_ref[0].astype(F32)

    def row(x, y):
        return wide[pl.ds(x * Y + y, C, stride=X * Y), :].astype(BF16)

    write_pieces(row, Y, near, far, first, second)


def z_permutation(Z):
    fine = lax.broadcasted_iota(jnp.int32, (2 * Z, 2 * Z), 0)
    coarse = lax.broadcasted_iota(jnp.int32, (2 * Z, 2 * Z), 1)
    inner = coarse % Z
    goes = coarse // Z + (inner % (Z // 2)) * 2 + (inner // (Z // 2)) * Z
    return jnp.where(fine == goes, 1.0, 0.0).astype(BF16)


def early_kernel(dims, gd_ref, w_ref, wd_ref, gm_ref, wb, Mb):
    X, Y, C, Z, H, O = dims
    NP = Y // 4

    @pl.when(pl.program_id(0) == 0)
    def _():
        for t in range(27):
            wb[t] = jnp.broadcast_to(w_ref[:, t : t + 1], (C, Z))

    perm = z_permutation(Z)
    for X0 in range(X // 2):
        gp = dot(wd_ref[...], gd_ref[0, X0], 1, 1).astype(BF16)
        for a in range(2):
            for b in range(2):
                for p in range(NP):
                    src = ((a * 2 + b) * 2) * C
                    dst = ((a * 2 + b) * NP + p) * C
                    for e in range(2):
                        Mb[dst : dst + C, e * Z : (e + 1) * Z] = gp[
                            src + e * C : src + (e + 1) * C, p * Z : (p + 1) * Z
                        ]
        gm = dot(Mb[...], perm, 1, 1).astype(BF16)
        for a in range(2):
            for b in range(2):
                for p in range(NP):
                    src = ((a * 2 + b) * NP + p) * C
                    for q in range(2):
                        x, y = 2 * X0 + a, 2 * (2 * p + q) + b
                        gm_ref[0, x, y] = gm[src : src + C, q * Z : (q + 1) * Z]


def main_kernel(dims, *refs):
    X, Y, C, Z, H, O = dims
    hx, NP = X // 2, Y // 4
    cells = X * Y * Z
    quarter = (Y // 2) * (Z // 2)
    widened = refs[:8]
    gd_ref, gm_ref, wb, pinT_ref, pout_ref, wd_ref, red_ref = refs[8:15]
    pieces, packed_ref = refs[15:19], refs[19]
    Fs, Ds, Mb, Pt, G1, adw, adown, aout, ain, pin, poutT = refs[20:31]
    pre_s, ga_s, act_s, gp_s, rows_s = refs[31:]
    step = pl.program_id(0)

    @pl.when(step == 0)
    def _():
        adw[...] = jnp.zeros_like(adw)
        adown[...] = jnp.zeros_like(adown)
        aout[...] = jnp.zeros_like(aout)
        ain[...] = jnp.zeros_like(ain)
        pin[...] = pinT_ref[...].astype(F32).T.astype(BF16)
        poutT[...] = pout_ref[...].astype(F32).T.astype(BF16)

    fill_padded(widened, Fs)
    lane = lax.broadcasted_iota(jnp.int32, (CT, Z), 1)

    perm = z_permutation(Z)

    def conv_body(i, carry):
        channels = pl.ds(pl.multiple_of(i * CT, CT), CT)

        def store(x, y, value):
            r = x * Y + y
            Ds[channels, r * Z : (r + 1) * Z] = value

        conv_tile(Fs, wb, False, channels, X, Y, lane, store)
        return carry

    lax.fori_loop(0, C // CT, conv_body, 0)

    width = 4 * Z

    for X0 in range(hx):

        for i in range(2 * NP):
            a, p = i // NP, i % NP
            x = 2 * X0 + a
            columns = slice((x * NP + p) * width, (x * NP + p + 1) * width)
            depth = Ds[:, columns].astype(BF16)
            gm = jnp.concatenate([gm_ref[0, x, 4 * p + j] for j in range(4)], axis=1)
            pre_s[i] = dot(pin[...], depth, 1, 0)
            ga_s[i] = dot(poutT[...], gm, 1, 0)
            for h0 in range(0, H, 16):
                hs = slice(h0, h0 + 16)
                pre = pre_s[i, hs, :]
                sq = pre * pre
                t = jnp.tanh(pre * (GELU_C + (GELU_C * GELU_A) * sq))
                h = 0.5 + 0.5 * t
                act = pre * h
                slope = h + act * (1.0 - h) * (2.0 * GELU_C + (6.0 * GELU_C * GELU_A) * sq)
                act_s[i, hs, :] = act.astype(BF16)
                gp_s[i, hs, :] = (ga_s[i, hs, :] * slope).astype(BF16)
            active, grad_pre = act_s[i], gp_s[i]
            branch = dot(pout_ref[...], active, 1, 0)
            for j in range(4):
                row = (x + 1) * (Y + 2) + 4 * p + j + 1
                merged = (Fs[row] + branch[:, j * Z : (j + 1) * Z]).astype(BF16)
                start = ((a * 2 + j % 2) * NP + p) * C
                Mb[start : start + C, (j // 2) * Z : (j // 2 + 1) * Z] = merged
            grad_depth = dot(pinT_ref[...], grad_pre, 1, 0).astype(BF16).astype(F32)
            for j in range(4):
                G1[x * Y + 4 * p + j] = grad_depth[:, j * Z : (j + 1) * Z]
            aout[...] += dot(gm, active, 1, 1)
            ain[...] += dot(depth, grad_pre, 1, 1)

        pt = dot(Mb[...], perm, 1, 0).astype(BF16)
        for a in range(2):
            for b in range(2):
                for p in range(NP):
                    src = ((a * 2 + b) * NP + p) * C
                    for e in range(2):
                        dst = ((a * 2 + b) * 2 + e) * C
                        Pt[dst : dst + C, p * Z : (p + 1) * Z] = pt[
                            src : src + C, e * Z : (e + 1) * Z
                        ]
        red_ref[0, X0] = dot(Pt[...], wd_ref[...], 0, 0).astype(BF16)
        adown[...] += dot(Pt[...], gd_ref[0, X0], 1, 0)

    write_pieces(lambda x, y: G1[x * Y + y].astype(BF16), Y, *pieces)

    def tap_body(i, carry):
        channels = pl.ds(pl.multiple_of(i * CT, CT), CT)
        sums = [None] * 27
        for x in range(X):
            for y in range(Y):
                g = G1[x * Y + y, channels, :]
                gs = (
                    jnp.where(lane == Z - 1, 0.0, pltpu.roll(g, Z - 1, 1)),
                    g,
                    jnp.where(lane == 0, 0.0, pltpu.roll(g, 1, 1)),
                )
                for a in range(3):
                    for b in range(3):
                        f = Fs[(x + a) * (Y + 2) + y + b, channels, :]
                        for e in range(3):
                            t = (a * 3 + b) * 3 + e
                            term = gs[e] * f
                            sums[t] = term if sums[t] is None else sums[t] + term
        for t in range(27):
            adw[t, channels, :] += sums[t]
        return carry

    lax.fori_loop(0, C // CT, tap_body, 0)

    @pl.when(step == pl.num_programs(0) - 1)
    def _():
        ones = jnp.ones((8, Z), BF16)
        taps = []
        for t in range(27):
            high = adw[t].astype(BF16)
            low = (adw[t] - high.astype(F32)).astype(BF16)
            taps.append((dot(ones, high, 1, 1) + dot(ones, low, 1, 1))[:1])
        taps = jnp.concatenate(taps + [jnp.zeros((5, C), F32)], axis=0)
        rows_s[...] = jnp.zeros_like(rows_s)
        for k in range(8):
            rows_s[pl.ds(k, C, stride=8), :] = adown[k * C : (k + 1) * C, :]
        rows_s[8 * C + 2 * C * (H // Z) :, :C] = taps
        packed_ref[: rows_s.shape[0], :] = rows_s[...].astype(BF16)
        at = 8 * C
        for part in (aout, ain):
            for k in range(0, H, Z):
                packed_ref[at : at + C, :] = part[:, k : k + Z].astype(BF16)
                at += C
        at = rows_s.shape[0]
        if at < packed_ref.shape[0]:
            rest = packed_ref.shape[0] - at
            packed_ref[at:, :] = jnp.zeros((rest, Z), BF16)


def adjoint_kernel(X, Y, C, Z, *refs):
    widened = refs[:8]
    gm_ref, wb, out_ref, Fs, wide = refs[8:]
    fill_padded(widened, Fs)
    lane = lax.broadcasted_iota(jnp.int32, (CT, Z), 1)
    rows = X * Y

    def conv_body(i, carry):
        first = pl.multiple_of(i * CT, CT)
        channels = pl.ds(first, CT)

        def store(x, y, value):
            r = x * Y + y
            total = value + gm_ref[0, x, y, channels, :].astype(F32)
            wide[pl.ds(first * rows + r, CT, stride=rows), :] = total

        conv_tile(Fs, wb, True, channels, X, Y, lane, store)
        return carry

    lax.fori_loop(0, C // CT, conv_body, 0)
    out_ref[0] = wide[...].astype(BF16)


def finish_kernel(dims, scale, every_ref, down_ref, out_ref, in_ref, taps_ref, total):
    C, Z, H, owners, run = dims
    for half in range(2):
        for k in range(owners // 2):
            src, dst = (k * 2 + half) * run, (half * (owners // 2) + k) * run
            total[dst : dst + run, :] = every_ref[src : src + run, :].astype(F32) * scale
    down_ref[...] = total[: 8 * C, :]
    at = 8 * C
    for ref in (out_ref, in_ref):
        for k in range(0, H, Z):
            ref[:, k : k + Z] = total[at : at + C, :]
            at += C
    for a in range(3):
        for b in range(3):
            first = at + (a * 3 + b) * 3
            taps_ref[a, b] = total[first : first + 3, :C]


def swap_in_group(blocks, axis):
    g = blocks.shape[0]
    if g == 1:
        return blocks
    n = lax.axis_size(axis)
    member = lax.axis_index(axis) % g
    got = [lax.dynamic_index_in_dim(blocks, member, 0, keepdims=False)]
    for k in range(1, g):
        out = lax.dynamic_index_in_dim(blocks, (member + k) % g, 0, keepdims=False)
        pairs = [(i, i - i % g + (i + k) % g) for i in range(n)]
        got.append(lax.ppermute(out, axis, pairs))
    if g == 2:
        first = member == 0
        return jnp.stack([jnp.where(first, got[0], got[1]), jnp.where(first, got[1], got[0])])
    got = jnp.stack(got)
    return jnp.take(got, (member - jnp.arange(g, dtype=jnp.int32)) % g, axis=0)


def sum_share(packed, nx, ny):
    lanes = packed.shape[1]
    p = lax.axis_index("gx") % 2
    halves = packed.reshape(2, -1, lanes)
    kept = lax.dynamic_index_in_dim(halves, p, 0, keepdims=False)
    given = lax.dynamic_index_in_dim(halves, 1 - p, 0, keepdims=False)
    got = lax.ppermute(given, "gx", swap_pairs(nx, 0))
    pair = (kept.astype(F32) + got.astype(F32)).astype(BF16)
    groups = [[x * ny + y for x in range(c, nx, 2) for y in range(ny)] for c in range(2)]
    mine = lax.all_to_all(
        pair.reshape(nx * ny // 2, -1, lanes), ("gx", "gy"), 0, 0, axis_index_groups=groups
    )
    return jnp.sum(mine.astype(F32), axis=0).astype(BF16)


def gather_shares(share, devices):
    every = jnp.broadcast_to(share[None], (devices,) + share.shape)
    every = lax.all_to_all(every, ("gx", "gy"), 0, 0)
    return every.reshape(-1, share.shape[1])


def per_device(fields, depth_kernel, point_in, point_out, down_kernel, cotangent):
    S, C, X, Y, Z = fields.shape
    assert X == 2 and Y % 4 == 0
    H, O = point_in.shape[0], down_kernel.shape[0]
    hx, hy, hz = X // 2, Y // 2, Z // 2
    nx, ny = lax.axis_size("gx"), lax.axis_size("gy")
    devices = nx * ny
    gx, gy = nx // GRIDC, ny // GRIDC
    per_group = S // (gx * gy)
    params = pltpu.CompilerParams(
        dimension_semantics=("arbitrary",), vmem_limit_bytes=VMEM_LIMIT
    )

    pieces = pl.pallas_call(
        functools.partial(split_kernel, X, Y, C, Z),
        grid=(S,),
        in_specs=[pl.BlockSpec((1, C * X * Y, Z), lambda s: (s, 0, 0))],
        out_specs=piece_specs(Y, C, Z),
        out_shape=piece_shapes(S, Y, C, Z),
        scratch_shapes=[pltpu.VMEM((C * X * Y, Z), F32)],
        compiler_params=params,
        name="split_fields",
    )(fields.reshape(S, C * X * Y, Z))

    widened = exchange_halo(pieces)

    moved = cotangent[0, 0].transpose(0, 2, 3, 4, 1)
    moved = moved.reshape(per_group, gx * hx, gy, hy * hz, O).transpose(2, 0, 1, 3, 4)
    moved = swap_in_group(moved, "gy").reshape(gy * per_group, gx, hx, hy * hz, O)
    moved = swap_in_group(moved.transpose(1, 0, 2, 3, 4), "gx")
    grad_down = moved.reshape(S, hx, hy * hz, O)

    wd = down_kernel.transpose(2, 3, 4, 1, 0).reshape(8 * C, O)
    taps = depth_kernel.reshape(C, 27).astype(F32)

    rows = 8 * C + 2 * C * (H // Z) + 32
    chunk = -(-rows // (16 * devices)) * 16
    cells = X * Y * Z
    whole = lambda shape: pl.BlockSpec(shape, lambda s: (0,) * len(shape))
    flops = S * cells * (2 * 6 * C * H + 2 * 3 * C * O + 2 * 2 * 27 * C)
    dims = (X, Y, C, Z, H, O)
    grad_merged, spread = pl.pallas_call(
        functools.partial(early_kernel, dims),
        grid=(S,),
        in_specs=[
            pl.BlockSpec((1, hx, hy * hz, O), lambda s: (s, 0, 0, 0)),
            whole((C, 27)),
            whole((8 * C, O)),
        ],
        out_specs=[
            pl.BlockSpec((1, X, Y, C, Z), lambda s: (s, 0, 0, 0, 0)),
            whole((27, C, Z)),
        ],
        out_shape=[
            jax.ShapeDtypeStruct((S, X, Y, C, Z), BF16),
            jax.ShapeDtypeStruct((27, C, Z), F32),
        ],
        scratch_shapes=[pltpu.VMEM((Y * C, 2 * Z), BF16)],
        compiler_params=params,
        cost_estimate=pl.CostEstimate(
            flops=S * cells * (2 * C * O + 8 * C * Z),
            bytes_accessed=4 * S * cells * C + 4 * 27 * C * Z,
            transcendentals=0,
        ),
        name="early",
    )(grad_down, taps, wd)

    out = pl.pallas_call(
        functools.partial(main_kernel, dims),
        grid=(S,),
        in_specs=widened_specs(Y, C, Z)
        + [
            pl.BlockSpec((1, hx, hy * hz, O), lambda s: (s, 0, 0, 0)),
            pl.BlockSpec((1, X, Y, C, Z), lambda s: (s, 0, 0, 0, 0)),
            whole((27, C, Z)),
            whole((C, H)),
            whole((C, H)),
            whole((8 * C, O)),
        ],
        out_specs=[pl.BlockSpec((1, hx, hy * hz, O), lambda s: (s, 0, 0, 0))]
        + piece_specs(Y, C, Z)
        + [whole((devices * chunk, Z))],
        out_shape=[jax.ShapeDtypeStruct((S, hx, hy * hz, O), BF16)]
        + piece_shapes(S, Y, C, Z)
        + [jax.ShapeDtypeStruct((devices * chunk, Z), BF16)],
        scratch_shapes=[
            pltpu.VMEM(((X + 2) * (Y + 2), C, Z), F32),
            pltpu.VMEM((C, cells), F32),
            pltpu.VMEM((Y * C, 2 * Z), BF16),
            pltpu.VMEM((8 * C, hy * hz), BF16),
            pltpu.VMEM((X * Y, C, Z), F32),
            pltpu.VMEM((27, C, Z), F32),
            pltpu.VMEM((8 * C, O), F32),
            pltpu.VMEM((C, H), F32),
            pltpu.VMEM((C, H), F32),
            pltpu.VMEM((H, C), BF16),
            pltpu.VMEM((H, C), BF16),
            pltpu.VMEM((Y // 2, H, 4 * Z), F32),
            pltpu.VMEM((Y // 2, H, 4 * Z), F32),
            pltpu.VMEM((Y // 2, H, 4 * Z), BF16),
            pltpu.VMEM((Y // 2, H, 4 * Z), BF16),
            pltpu.VMEM((rows, Z), F32),
        ],
        compiler_params=params,
        cost_estimate=pl.CostEstimate(
            flops=flops, bytes_accessed=8 * S * cells * C, transcendentals=S * cells * H
        ),
        name="main",
    )(*widened, grad_down, grad_merged, spread, point_in.T, point_out, wd)
    reduced, grad_pieces, packed = out[0], out[1:5], out[5]

    grad_widened = exchange_halo(grad_pieces)

    share = sum_share(packed, nx, ny)
    share, grad_widened[0] = lax.optimization_barrier((share, grad_widened[0]))
    every = gather_shares(share, devices)

    grad_fields = pl.pallas_call(
        functools.partial(adjoint_kernel, X, Y, C, Z),
        grid=(S,),
        in_specs=widened_specs(Y, C, Z)
        + [pl.BlockSpec((1, X, Y, C, Z), lambda s: (s, 0, 0, 0, 0)), whole((27, C, Z))],
        out_specs=pl.BlockSpec((1, C * X * Y, Z), lambda s: (s, 0, 0)),
        out_shape=jax.ShapeDtypeStruct((S, C * X * Y, Z), BF16),
        scratch_shapes=[
            pltpu.VMEM(((X + 2) * (Y + 2), C, Z), F32),
            pltpu.VMEM((C * X * Y, Z), F32),
        ],
        compiler_params=params,
        cost_estimate=pl.CostEstimate(
            flops=S * cells * 2 * 27 * C, bytes_accessed=8 * S * cells * C, transcendentals=0
        ),
        name="adjoint",
    )(*grad_widened, grad_merged, spread).reshape(S, C, X, Y, Z)

    moved = swap_in_group(reduced.reshape(gx, S // gx, hx, hy * hz, O), "gx")
    moved = moved.transpose(1, 0, 2, 3, 4).reshape(gy, per_group, gx * hx, hy * hz, O)
    moved = swap_in_group(moved, "gy").transpose(1, 2, 0, 3, 4)
    coarse = moved.reshape(per_group, gx * hx, gy * hy, hz, O).transpose(0, 4, 1, 2, 3)[None, None]

    scale = 1.0 / math.sqrt(S * cells * devices)
    down, outw, inw, tapw = pl.pallas_call(
        functools.partial(finish_kernel, (C, Z, H, nx, ny * chunk), scale),
        out_shape=[
            jax.ShapeDtypeStruct((8 * C, O), F32),
            jax.ShapeDtypeStruct((C, H), F32),
            jax.ShapeDtypeStruct((C, H), F32),
            jax.ShapeDtypeStruct((3, 3, 3, C), F32),
        ],
        scratch_shapes=[pltpu.VMEM((devices * chunk, Z), F32)],
        name="finish",
    )(every)
    return (
        coarse,
        grad_fields,
        tapw.transpose(3, 0, 1, 2),
        inw.T,
        outw,
        down.reshape(C, 2, 2, 2, O).transpose(4, 0, 1, 2, 3),
    )


def solution(mesh):
    placed = (
        P(None, None, "gx", "gy", None),
        P(),
        P(),
        P(),
        P(),
        P("gx", "gy", None, None, None, None, None),
    )
    return jax.shard_map(
        per_device,
        mesh=mesh,
        in_specs=placed,
        out_specs=(
            P("gx", "gy", None, None, None, None, None),
            P(None, None, "gx", "gy", None),
            P(),
            P(),
            P(),
            P(),
        ),
        check_vma=False,
    )
```

```python
import functools
import math

import jax
import jax.numpy as jnp
from jax import lax
from jax.experimental import pallas as pl
from jax.experimental.pallas import tpu as pltpu
from jax.sharding import PartitionSpec as P

GRIDC = 4
F32 = jnp.float32
BF16 = jnp.bfloat16
VMEM_LIMIT = 40 * 1024 * 1024
CT = 8
GELU_C = math.sqrt(2.0 / math.pi)
GELU_A = 0.044715


def dot(a, b, ca, cb):
    return lax.dot_general(a, b, (((ca,), (cb,)), ((), ())), preferred_element_type=F32)


def sides():
    return lax.axis_index("gx") % 2, lax.axis_index("gy") % 2


def write_pieces(row, s, Y, near, far, first, second):
    p, q = sides()
    for k, (x, plane) in enumerate(((1 - p, near), (p, far))):
        for y in range(Y):
            plane[s, y] = row(x, y)
        first[k, s] = row(x, (1 - q) * (Y - 1))
        second[k, s] = row(x, q * (Y - 1))


def piece_shapes(S, Y, C, Z):
    return [jax.ShapeDtypeStruct((S, Y, C, Z), BF16)] * 2 + [
        jax.ShapeDtypeStruct((2, S, C, Z), BF16)
    ] * 2


def in_vmem(n):
    return [pl.BlockSpec(memory_space=pltpu.VMEM)] * n


def swap_pairs(n, start):
    return [pair for i in range(start, n - 1, 2) for pair in ((i, i + 1), (i + 1, i))]


def exchange_halo(pieces):
    near, far, first, second = pieces
    nx, ny = lax.axis_size("gx"), lax.axis_size("gy")
    from_far = lax.ppermute(far, "gx", swap_pairs(nx, 1))
    first = lax.ppermute(first, "gy", swap_pairs(ny, 0))
    second = lax.ppermute(second, "gy", swap_pairs(ny, 1))
    from_near = lax.ppermute(near, "gx", swap_pairs(nx, 0))
    corners = [jnp.stack([first[k], second[k]]) for k in range(2)]
    corner_far = lax.ppermute(corners[1], "gx", swap_pairs(nx, 1))
    corner_near = lax.ppermute(corners[0], "gx", swap_pairs(nx, 0))
    return [near, far, from_near, from_far, first, second, corner_near, corner_far]


def fill_padded(pieces, s, Fs):
    near, far, from_near, from_far, first, second, corner_near, corner_far = pieces
    p, q = sides()
    Y = near.shape[1]
    places = (2 - p, 1 + p, 3 * (1 - p), 3 * p)
    rims = ((first, 0), (second, 0)), ((first, 1), (second, 1))
    rims += ((corner_near, 0), (corner_near, 1)), ((corner_far, 0), (corner_far, 1))
    for x, plane, ((r0, k0), (r1, k1)) in zip(places, (near, far, from_near, from_far), rims):
        for y in range(Y):
            Fs[x * (Y + 2) + y + 1] = plane[s, y].astype(F32)
        Fs[x * (Y + 2) + (1 - q) * (Y + 1)] = r0[k0, s].astype(F32)
        Fs[x * (Y + 2) + q * (Y + 1)] = r1[k1, s].astype(F32)


def conv_tile(Fs, wb, flip, channels, X, Y, lane, store):
    Z = Fs.shape[2]
    weights = [wb[26 - t if flip else t, channels, :] for t in range(27)]
    for x in range(X):
        for y in range(Y):
            acc = [None, None, None]
            for a in range(3):
                for b in range(3):
                    f = Fs[(x + a) * (Y + 2) + y + b, channels, :]
                    for e in range(3):
                        term = weights[(a * 3 + b) * 3 + e] * f
                        acc[e] = term if acc[e] is None else acc[e] + term
            left = jnp.where(lane == 0, 0.0, pltpu.roll(acc[0], 1, 1))
            right = jnp.where(lane == Z - 1, 0.0, pltpu.roll(acc[2], Z - 1, 1))
            store(x, y, acc[1] + left + right)


def split_kernel(X, Y, C, Z, f_ref, near, far, first, second, wide):
    wide[...] = f_ref[0].astype(F32)

    def row(x, y):
        return wide[pl.ds(x * Y + y, C, stride=X * Y), :].astype(BF16)

    write_pieces(row, pl.program_id(0), Y, near, far, first, second)


def z_permutation(Z):
    fine = lax.broadcasted_iota(jnp.int32, (2 * Z, 2 * Z), 0)
    coarse = lax.broadcasted_iota(jnp.int32, (2 * Z, 2 * Z), 1)
    inner = coarse % Z
    goes = coarse // Z + (inner % (Z // 2)) * 2 + (inner // (Z // 2)) * Z
    return jnp.where(fine == goes, 1.0, 0.0).astype(BF16)


def early_kernel(dims, gd_ref, w_ref, wd_ref, gm_ref, wb, Mb):
    X, Y, C, Z, H, O = dims
    NP = Y // 4
    step = pl.program_id(0)

    @pl.when(step == 0)
    def _():
        for t in range(27):
            wb[t] = jnp.broadcast_to(w_ref[:, t : t + 1], (C, Z))

    perm = z_permutation(Z)
    for X0 in range(X // 2):
        gp = dot(wd_ref[...], gd_ref[step, X0], 1, 1).astype(BF16)
        for a in range(2):
            for b in range(2):
                for p in range(NP):
                    src = ((a * 2 + b) * 2) * C
                    dst = ((a * 2 + b) * NP + p) * C
                    for e in range(2):
                        Mb[dst : dst + C, e * Z : (e + 1) * Z] = gp[
                            src + e * C : src + (e + 1) * C, p * Z : (p + 1) * Z
                        ]
        gm = dot(Mb[...], perm, 1, 1).astype(BF16)
        for a in range(2):
            for b in range(2):
                for p in range(NP):
                    src = ((a * 2 + b) * NP + p) * C
                    for q in range(2):
                        x, y = 2 * X0 + a, 2 * (2 * p + q) + b
                        gm_ref[step, x, y] = gm[src : src + C, q * Z : (q + 1) * Z]


def main_kernel(dims, *refs):
    X, Y, C, Z, H, O = dims
    hx, NP = X // 2, Y // 4
    cells = X * Y * Z
    quarter = (Y // 2) * (Z // 2)
    widened = refs[:8]
    gd_ref, gm_ref, wb, pinT_ref, pout_ref, wd_ref, red_ref = refs[8:15]
    pieces, packed_ref = refs[15:19], refs[19]
    Fs, Ds, Mb, Pt, G1, adw, adown, aout, ain, pin, poutT = refs[20:31]
    pre_s, ga_s, act_s, gp_s, rows_s = refs[31:]
    step = pl.program_id(0)

    @pl.when(step == 0)
    def _():
        adw[...] = jnp.zeros_like(adw)
        adown[...] = jnp.zeros_like(adown)
        aout[...] = jnp.zeros_like(aout)
        ain[...] = jnp.zeros_like(ain)
        pin[...] = pinT_ref[...].astype(F32).T.astype(BF16)
        poutT[...] = pout_ref[...].astype(F32).T.astype(BF16)

    fill_padded(widened, step, Fs)
    lane = lax.broadcasted_iota(jnp.int32, (CT, Z), 1)

    perm = z_permutation(Z)

    def conv_body(i, carry):
        channels = pl.ds(pl.multiple_of(i * CT, CT), CT)

        def store(x, y, value):
            r = x * Y + y
            Ds[channels, r * Z : (r + 1) * Z] = value

        conv_tile(Fs, wb, False, channels, X, Y, lane, store)
        return carry

    lax.fori_loop(0, C // CT, conv_body, 0)

    width = 4 * Z

    for X0 in range(hx):

        for i in range(2 * NP):
            a, p = i // NP, i % NP
            x = 2 * X0 + a
            columns = slice((x * NP + p) * width, (x * NP + p + 1) * width)
            depth = Ds[:, columns].astype(BF16)
            gm = jnp.concatenate([gm_ref[step, x, 4 * p + j] for j in range(4)], axis=1)
            pre_s[i] = dot(pin[...], depth, 1, 0)
            ga_s[i] = dot(poutT[...], gm, 1, 0)
            for h0 in range(0, H, 16):
                hs = slice(h0, h0 + 16)
                pre = pre_s[i, hs, :]
                sq = pre * pre
                t = jnp.tanh(pre * (GELU_C + (GELU_C * GELU_A) * sq))
                h = 0.5 + 0.5 * t
                act = pre * h
                slope = h + act * (1.0 - h) * (2.0 * GELU_C + (6.0 * GELU_C * GELU_A) * sq)
                act_s[i, hs, :] = act.astype(BF16)
                gp_s[i, hs, :] = (ga_s[i, hs, :] * slope).astype(BF16)
            active, grad_pre = act_s[i], gp_s[i]
            branch = dot(pout_ref[...], active, 1, 0)
            for j in range(4):
                row = (x + 1) * (Y + 2) + 4 * p + j + 1
                merged = (Fs[row] + branch[:, j * Z : (j + 1) * Z]).astype(BF16)
                start = ((a * 2 + j % 2) * NP + p) * C
                Mb[start : start + C, (j // 2) * Z : (j // 2 + 1) * Z] = merged
            grad_depth = dot(pinT_ref[...], grad_pre, 1, 0).astype(BF16).astype(F32)
            for j in range(4):
                G1[x * Y + 4 * p + j] = grad_depth[:, j * Z : (j + 1) * Z]
            aout[...] += dot(gm, active, 1, 1)
            ain[...] += dot(depth, grad_pre, 1, 1)

        pt = dot(Mb[...], perm, 1, 0).astype(BF16)
        for a in range(2):
            for b in range(2):
                for p in range(NP):
                    src = ((a * 2 + b) * NP + p) * C
                    for e in range(2):
                        dst = ((a * 2 + b) * 2 + e) * C
                        Pt[dst : dst + C, p * Z : (p + 1) * Z] = pt[
                            src : src + C, e * Z : (e + 1) * Z
                        ]
        red_ref[step, X0] = dot(Pt[...], wd_ref[...], 0, 0).astype(BF16)
        adown[...] += dot(Pt[...], gd_ref[step, X0], 1, 0)

    write_pieces(lambda x, y: G1[x * Y + y].astype(BF16), step, Y, *pieces)

    def tap_body(i, carry):
        channels = pl.ds(pl.multiple_of(i * CT, CT), CT)
        sums = [None] * 27
        for x in range(X):
            for y in range(Y):
                g = G1[x * Y + y, channels, :]
                gs = (
                    jnp.where(lane == Z - 1, 0.0, pltpu.roll(g, Z - 1, 1)),
                    g,
                    jnp.where(lane == 0, 0.0, pltpu.roll(g, 1, 1)),
                )
                for a in range(3):
                    for b in range(3):
                        f = Fs[(x + a) * (Y + 2) + y + b, channels, :]
                        for e in range(3):
                            t = (a * 3 + b) * 3 + e
                            term = gs[e] * f
                            sums[t] = term if sums[t] is None else sums[t] + term
        for t in range(27):
            adw[t, channels, :] += sums[t]
        return carry

    lax.fori_loop(0, C // CT, tap_body, 0)

    @pl.when(step == pl.num_programs(0) - 1)
    def _():
        ones = jnp.ones((8, Z), BF16)
        taps = []
        for t in range(27):
            high = adw[t].astype(BF16)
            low = (adw[t] - high.astype(F32)).astype(BF16)
            taps.append((dot(ones, high, 1, 1) + dot(ones, low, 1, 1))[:1])
        taps = jnp.concatenate(taps + [jnp.zeros((5, C), F32)], axis=0)
        rows_s[...] = jnp.zeros_like(rows_s)
        for k in range(8):
            rows_s[pl.ds(k, C, stride=8), :] = adown[k * C : (k + 1) * C, :]
        rows_s[8 * C + 2 * C * (H // Z) :, :C] = taps
        packed_ref[: rows_s.shape[0], :] = rows_s[...].astype(BF16)
        at = 8 * C
        for part in (aout, ain):
            for k in range(0, H, Z):
                packed_ref[at : at + C, :] = part[:, k : k + Z].astype(BF16)
                at += C
        at = rows_s.shape[0]
        if at < packed_ref.shape[0]:
            rest = packed_ref.shape[0] - at
            packed_ref[at:, :] = jnp.zeros((rest, Z), BF16)


def adjoint_kernel(X, Y, C, Z, *refs):
    widened = refs[:8]
    gm_ref, wb, out_ref, Fs, wide = refs[8:]
    step = pl.program_id(0)
    fill_padded(widened, step, Fs)
    lane = lax.broadcasted_iota(jnp.int32, (CT, Z), 1)
    rows = X * Y

    def conv_body(i, carry):
        first = pl.multiple_of(i * CT, CT)
        channels = pl.ds(first, CT)

        def store(x, y, value):
            r = x * Y + y
            total = value + gm_ref[step, x, y, channels, :].astype(F32)
            wide[pl.ds(first * rows + r, CT, stride=rows), :] = total

        conv_tile(Fs, wb, True, channels, X, Y, lane, store)
        return carry

    lax.fori_loop(0, C // CT, conv_body, 0)
    out_ref[0] = wide[...].astype(BF16)


def finish_kernel(C, Z, H, scale, every_ref, down_ref, out_ref, in_ref, taps_ref):
    down_ref[...] = every_ref[: 8 * C, :].astype(F32) * scale
    at = 8 * C
    for ref in (out_ref, in_ref):
        for k in range(0, H, Z):
            ref[:, k : k + Z] = every_ref[at : at + C, :].astype(F32) * scale
            at += C
    taps = every_ref[at : at + 32, :].astype(F32) * scale
    for a in range(3):
        for b in range(3):
            first = (a * 3 + b) * 3
            taps_ref[a, b] = taps[first : first + 3, :C]


def sum_spread_kernel(parts_ref, out_ref):
    total = parts_ref[0].astype(F32)
    for i in range(1, parts_ref.shape[0]):
        total = total + parts_ref[i].astype(F32)
    total = total.astype(BF16)
    for j in range(out_ref.shape[0]):
        out_ref[j] = total


def sum_spread(parts, receivers):
    shape = (receivers,) + parts.shape[1:]
    return pl.pallas_call(
        sum_spread_kernel,
        in_specs=in_vmem(1),
        out_specs=in_vmem(1)[0],
        out_shape=jax.ShapeDtypeStruct(shape, BF16),
        name="sum_spread",
    )(parts)


def swap_in_group(blocks, axis):
    g = blocks.shape[0]
    if g == 1:
        return blocks
    n = lax.axis_size(axis)
    member = lax.axis_index(axis) % g
    got = [lax.dynamic_index_in_dim(blocks, member, 0, keepdims=False)]
    for k in range(1, g):
        out = lax.dynamic_index_in_dim(blocks, (member + k) % g, 0, keepdims=False)
        pairs = [(i, i - i % g + (i + k) % g) for i in range(n)]
        got.append(lax.ppermute(out, axis, pairs))
    if g == 2:
        first = member == 0
        return jnp.stack([jnp.where(first, got[0], got[1]), jnp.where(first, got[1], got[0])])
    got = jnp.stack(got)
    return jnp.take(got, (member - jnp.arange(g, dtype=jnp.int32)) % g, axis=0)


def per_device(fields, depth_kernel, point_in, point_out, down_kernel, cotangent):
    S, C, X, Y, Z = fields.shape
    assert X == 2 and Y % 4 == 0
    H, O = point_in.shape[0], down_kernel.shape[0]
    hx, hy, hz = X // 2, Y // 2, Z // 2
    nx, ny = lax.axis_size("gx"), lax.axis_size("gy")
    devices = nx * ny
    gx, gy = nx // GRIDC, ny // GRIDC
    per_group = S // (gx * gy)
    params = pltpu.CompilerParams(
        dimension_semantics=("arbitrary",), vmem_limit_bytes=VMEM_LIMIT
    )

    pieces = pl.pallas_call(
        functools.partial(split_kernel, X, Y, C, Z),
        grid=(S,),
        in_specs=[pl.BlockSpec((1, C * X * Y, Z), lambda s: (s, 0, 0))],
        out_specs=in_vmem(4),
        out_shape=piece_shapes(S, Y, C, Z),
        scratch_shapes=[pltpu.VMEM((C * X * Y, Z), F32)],
        compiler_params=params,
        name="split_fields",
    )(fields.reshape(S, C * X * Y, Z))

    widened = exchange_halo(pieces)

    moved = cotangent[0, 0].transpose(0, 2, 3, 4, 1)
    moved = moved.reshape(per_group, gx * hx, gy, hy * hz, O).transpose(2, 0, 1, 3, 4)
    moved = swap_in_group(moved, "gy").reshape(gy * per_group, gx, hx, hy * hz, O)
    moved = swap_in_group(moved.transpose(1, 0, 2, 3, 4), "gx")
    grad_down = moved.reshape(S, hx, hy * hz, O)

    wd = down_kernel.transpose(2, 3, 4, 1, 0).reshape(8 * C, O)
    taps = depth_kernel.reshape(C, 27).astype(F32)

    rows = 8 * C + 2 * C * (H // Z) + 32
    chunk = -(-rows // (16 * nx)) * 16
    cells = X * Y * Z
    flops = S * cells * (2 * 6 * C * H + 2 * 3 * C * O + 2 * 2 * 27 * C)
    dims = (X, Y, C, Z, H, O)
    grad_merged, spread = pl.pallas_call(
        functools.partial(early_kernel, dims),
        grid=(S,),
        in_specs=in_vmem(3),
        out_specs=in_vmem(2),
        out_shape=[
            jax.ShapeDtypeStruct((S, X, Y, C, Z), BF16),
            jax.ShapeDtypeStruct((27, C, Z), F32),
        ],
        scratch_shapes=[pltpu.VMEM((Y * C, 2 * Z), BF16)],
        compiler_params=params,
        cost_estimate=pl.CostEstimate(
            flops=S * cells * (2 * C * O + 8 * C * Z),
            bytes_accessed=4 * S * cells * C + 4 * 27 * C * Z,
            transcendentals=0,
        ),
        name="early",
    )(grad_down, taps, wd)

    out = pl.pallas_call(
        functools.partial(main_kernel, dims),
        grid=(S,),
        in_specs=in_vmem(14),
        out_specs=in_vmem(6),
        out_shape=[jax.ShapeDtypeStruct((S, hx, hy * hz, O), BF16)]
        + piece_shapes(S, Y, C, Z)
        + [jax.ShapeDtypeStruct((nx * chunk, Z), BF16)],
        scratch_shapes=[
            pltpu.VMEM(((X + 2) * (Y + 2), C, Z), F32),
            pltpu.VMEM((C, cells), F32),
            pltpu.VMEM((Y * C, 2 * Z), BF16),
            pltpu.VMEM((8 * C, hy * hz), BF16),
            pltpu.VMEM((X * Y, C, Z), F32),
            pltpu.VMEM((27, C, Z), F32),
            pltpu.VMEM((8 * C, O), F32),
            pltpu.VMEM((C, H), F32),
            pltpu.VMEM((C, H), F32),
            pltpu.VMEM((H, C), BF16),
            pltpu.VMEM((H, C), BF16),
            pltpu.VMEM((Y // 2, H, 4 * Z), F32),
            pltpu.VMEM((Y // 2, H, 4 * Z), F32),
            pltpu.VMEM((Y // 2, H, 4 * Z), BF16),
            pltpu.VMEM((Y // 2, H, 4 * Z), BF16),
            pltpu.VMEM((rows, Z), F32),
        ],
        compiler_params=params,
        cost_estimate=pl.CostEstimate(
            flops=flops, bytes_accessed=8 * S * cells * C, transcendentals=S * cells * H
        ),
        name="main",
    )(*widened, grad_down, grad_merged, spread, point_in.T, point_out, wd)
    reduced, grad_pieces, packed = out[0], out[1:5], out[5]

    grad_widened = exchange_halo(grad_pieces)

    parts = lax.all_to_all(packed.reshape(nx, chunk, Z), "gx", 0, 0)
    parts = lax.all_to_all(sum_spread(parts, ny), "gy", 0, 0)
    share = sum_spread(parts, nx)
    share, grad_widened[0] = lax.optimization_barrier((share, grad_widened[0]))
    every = lax.all_to_all(share, "gx", 0, 0).reshape(nx * chunk, Z)

    grad_fields = pl.pallas_call(
        functools.partial(adjoint_kernel, X, Y, C, Z),
        grid=(S,),
        in_specs=in_vmem(10),
        out_specs=pl.BlockSpec((1, C * X * Y, Z), lambda s: (s, 0, 0)),
        out_shape=jax.ShapeDtypeStruct((S, C * X * Y, Z), BF16),
        scratch_shapes=[
            pltpu.VMEM(((X + 2) * (Y + 2), C, Z), F32),
            pltpu.VMEM((C * X * Y, Z), F32),
        ],
        compiler_params=params,
        cost_estimate=pl.CostEstimate(
            flops=S * cells * 2 * 27 * C, bytes_accessed=8 * S * cells * C, transcendentals=0
        ),
        name="adjoint",
    )(*grad_widened, grad_merged, spread).reshape(S, C, X, Y, Z)

    moved = swap_in_group(reduced.reshape(gx, S // gx, hx, hy * hz, O), "gx")
    moved = moved.transpose(1, 0, 2, 3, 4).reshape(gy, per_group, gx * hx, hy * hz, O)
    moved = swap_in_group(moved, "gy").transpose(1, 2, 0, 3, 4)
    coarse = moved.reshape(per_group, gx * hx, gy * hy, hz, O).transpose(0, 4, 1, 2, 3)[None, None]

    scale = 1.0 / math.sqrt(S * cells * devices)
    down, outw, inw, tapw = pl.pallas_call(
        functools.partial(finish_kernel, C, Z, H, scale),
        out_shape=[
            jax.ShapeDtypeStruct((8 * C, O), F32),
            jax.ShapeDtypeStruct((C, H), F32),
            jax.ShapeDtypeStruct((C, H), F32),
            jax.ShapeDtypeStruct((3, 3, 3, C), F32),
        ],
        in_specs=in_vmem(1),
        name="finish",
    )(every)
    return (
        coarse,
        grad_fields,
        tapw.transpose(3, 0, 1, 2),
        inw.T,
        outw,
        down.reshape(C, 2, 2, 2, O).transpose(4, 0, 1, 2, 3),
    )


def solution(mesh):
    placed = (
        P(None, None, "gx", "gy", None),
        P(),
        P(),
        P(),
        P(),
        P("gx", "gy", None, None, None, None, None),
    )
    return jax.shard_map(
        per_device,
        mesh=mesh,
        in_specs=placed,
        out_specs=(
            P("gx", "gy", None, None, None, None, None),
            P(None, None, "gx", "gy", None),
            P(),
            P(),
            P(),
            P(),
        ),
        check_vma=False,
    )
```

```python
import functools
import math

import jax
import jax.numpy as jnp
from jax import lax
from jax.experimental import pallas as pl
from jax.experimental.pallas import tpu as pltpu
from jax.sharding import PartitionSpec as P

GRIDC = 4
F32 = jnp.float32
BF16 = jnp.bfloat16
MIB = 1024 * 1024
STACK = 10
GELU_C = math.sqrt(2.0 / math.pi)
GELU_A = 0.044715


def dot(a, b, ca, cb):
    return lax.dot_general(a, b, (((ca,), (cb,)), ((), ())), preferred_element_type=F32)


def sides():
    return lax.axis_index("gx") % 2, lax.axis_index("gy") % 2


def write_pieces(row, s, Y, near, far, first, second):
    p, q = sides()
    for k, (x, plane) in enumerate(((1 - p, near), (p, far))):
        for y in range(Y):
            plane[s, y] = row(x, y)
        first[k, s] = row(x, (1 - q) * (Y - 1))
        second[k, s] = row(x, q * (Y - 1))


def piece_shapes(S, Y, C, Z):
    return [jax.ShapeDtypeStruct((S, Y, C, Z), BF16)] * 2 + [
        jax.ShapeDtypeStruct((2, S, C, Z), BF16)
    ] * 2


def params(mib):
    return pltpu.CompilerParams(vmem_limit_bytes=mib * MIB)


def in_vmem(n):
    return [pl.BlockSpec(memory_space=pltpu.VMEM)] * n


def swap_pairs(n, start):
    return [pair for i in range(start, n - 1, 2) for pair in ((i, i + 1), (i + 1, i))]


def exchange_halo(pieces):
    near, far, first, second = pieces
    nx, ny = lax.axis_size("gx"), lax.axis_size("gy")
    from_far = lax.ppermute(far, "gx", swap_pairs(nx, 1))
    first = lax.ppermute(first, "gy", swap_pairs(ny, 0))
    second = lax.ppermute(second, "gy", swap_pairs(ny, 1))
    from_near = lax.ppermute(near, "gx", swap_pairs(nx, 0))
    corners = [jnp.stack([first[k], second[k]]) for k in range(2)]
    corner_far = lax.ppermute(corners[1], "gx", swap_pairs(nx, 1))
    corner_near = lax.ppermute(corners[0], "gx", swap_pairs(nx, 0))
    return [near, far, from_near, from_far, first, second, corner_near, corner_far]


def fill_stack(pieces, s, Fs, FB):
    near, far, from_near, from_far, first, second, corner_near, corner_far = pieces
    p, q = sides()
    Y, C, Z = near.shape[1:]
    places = (2 - p, 1 + p, 3 * (1 - p), 3 * p)
    rims = ((first, 0), (second, 0)), ((first, 1), (second, 1))
    rims += ((corner_near, 0), (corner_near, 1)), ((corner_far, 0), (corner_far, 1))
    for x, plane, ((r0, k0), (r1, k1)) in zip(places, (near, far, from_near, from_far), rims):
        for y in range(Y):
            Fs[x * (Y + 2) + y + 1] = plane[s, y]
        Fs[x * (Y + 2) + (1 - q) * (Y + 1)] = r0[k0, s]
        Fs[x * (Y + 2) + q * (Y + 1)] = r1[k1, s]
    for a in range(3):
        for b in range(3):
            at = (a * 3 + b) * C
            for x in range(2):
                for y in range(Y):
                    r = x * Y + y
                    FB[at : at + C, r * Z : (r + 1) * Z] = Fs[(x + a) * (Y + 2) + y + b]
    FB[9 * C :, :] = jnp.zeros((FB.shape[0] - 9 * C, FB.shape[1]), BF16)


def from_left(value, lane):
    return jnp.where(lane == 0, 0.0, pltpu.roll(value, 1, 1))


def from_right(value, lane):
    Z = value.shape[1]
    return jnp.where(lane == Z - 1, 0.0, pltpu.roll(value, Z - 1, 1))


def conv_rows(taps, stack, C, Z, lane):
    acc = dot(taps, stack, 1, 0)
    rows = []
    for k in range(0, stack.shape[1], Z):
        left, mid, right = (acc[e * C : (e + 1) * C, k : k + Z] for e in range(3))
        rows.append(mid + from_left(left, lane) + from_right(right, lane))
    return rows


def split_kernel(X, Y, C, Z, f_ref, near, far, first, second, wide):
    wide[...] = f_ref[0].astype(F32)

    def row(x, y):
        return wide[pl.ds(x * Y + y, C, stride=X * Y), :].astype(BF16)

    write_pieces(row, pl.program_id(0), Y, near, far, first, second)


def z_permutation(Z):
    fine = lax.broadcasted_iota(jnp.int32, (2 * Z, 2 * Z), 0)
    coarse = lax.broadcasted_iota(jnp.int32, (2 * Z, 2 * Z), 1)
    inner = coarse % Z
    goes = coarse // Z + (inner % (Z // 2)) * 2 + (inner // (Z // 2)) * Z
    return jnp.where(fine == goes, 1.0, 0.0).astype(BF16)


def early_kernel(dims, gd_ref, w_ref, wd_ref, gm_ref, tap_ref, flip_ref, Mb):
    X, Y, C, Z, H, O = dims
    NP = Y // 4
    step = pl.program_id(0)

    @pl.when(step == 0)
    def _():
        row = lax.broadcasted_iota(jnp.int32, (C, STACK * C), 0)
        column = lax.broadcasted_iota(jnp.int32, (C, STACK * C), 1)
        for ref, flip in ((tap_ref, False), (flip_ref, True)):
            for e in range(3):
                block = jnp.zeros((C, STACK * C), F32)
                for ab in range(9):
                    t = ab * 3 + e
                    t = 26 - t if flip else t
                    block = jnp.where(column == row + ab * C, w_ref[:, t : t + 1], block)
                ref[e * C : (e + 1) * C, :] = block.astype(BF16)

    perm = z_permutation(Z)
    for X0 in range(X // 2):
        gp = dot(wd_ref[...], gd_ref[step, X0], 1, 1).astype(BF16)
        for a in range(2):
            for b in range(2):
                for p in range(NP):
                    src = ((a * 2 + b) * 2) * C
                    dst = ((a * 2 + b) * NP + p) * C
                    for e in range(2):
                        Mb[dst : dst + C, e * Z : (e + 1) * Z] = gp[
                            src + e * C : src + (e + 1) * C, p * Z : (p + 1) * Z
                        ]
        gm = dot(Mb[...], perm, 1, 1).astype(BF16)
        for a in range(2):
            for b in range(2):
                for p in range(NP):
                    src = ((a * 2 + b) * NP + p) * C
                    for q in range(2):
                        x, y = 2 * X0 + a, 2 * (2 * p + q) + b
                        gm_ref[step, x, y] = gm[src : src + C, q * Z : (q + 1) * Z]


def main_kernel(dims, *refs):
    X, Y, C, Z, H, O = dims
    hx, NP = X // 2, Y // 4
    cells = X * Y * Z
    quarter = (Y // 2) * (Z // 2)
    widened = refs[:8]
    gd_ref, gm_ref, tap_ref, pinT_ref, pout_ref, wd_ref, red_ref = refs[8:15]
    pieces, packed_ref = refs[15:19], refs[19]
    Fs, FB, Mb, Pt, G1, Gs, atap, adown, aout, ain, pin, poutT = refs[20:32]
    pre_s, ga_s, act_s, gp_s, rows_s = refs[32:]
    step = pl.program_id(0)

    @pl.when(step == 0)
    def _():
        atap[...] = jnp.zeros_like(atap)
        adown[...] = jnp.zeros_like(adown)
        aout[...] = jnp.zeros_like(aout)
        ain[...] = jnp.zeros_like(ain)
        pin[...] = pinT_ref[...].astype(F32).T.astype(BF16)
        poutT[...] = pout_ref[...].astype(F32).T.astype(BF16)

    fill_stack(widened, step, Fs, FB)
    lane = lax.broadcasted_iota(jnp.int32, (C, Z), 1)
    perm = z_permutation(Z)

    width = 4 * Z

    for X0 in range(hx):

        for i in range(2 * NP):
            a, p = i // NP, i % NP
            x = 2 * X0 + a
            columns = slice((x * NP + p) * width, (x * NP + p + 1) * width)
            depth = conv_rows(tap_ref[...], FB[:, columns], C, Z, lane)
            depth = jnp.concatenate(depth, axis=1).astype(BF16)
            gm = jnp.concatenate([gm_ref[step, x, 4 * p + j] for j in range(4)], axis=1)
            pre_s[i] = dot(pin[...], depth, 1, 0)
            ga_s[i] = dot(poutT[...], gm, 1, 0)
            for h0 in range(0, H, 16):
                hs = slice(h0, h0 + 16)
                pre = pre_s[i, hs, :]
                sq = pre * pre
                t = jnp.tanh(pre * (GELU_C + (GELU_C * GELU_A) * sq))
                h = 0.5 + 0.5 * t
                act = pre * h
                slope = h + act * (1.0 - h) * (2.0 * GELU_C + (6.0 * GELU_C * GELU_A) * sq)
                act_s[i, hs, :] = act.astype(BF16)
                gp_s[i, hs, :] = (ga_s[i, hs, :] * slope).astype(BF16)
            active, grad_pre = act_s[i], gp_s[i]
            branch = dot(pout_ref[...], active, 1, 0)
            for j in range(4):
                row = (x + 1) * (Y + 2) + 4 * p + j + 1
                merged = (Fs[row].astype(F32) + branch[:, j * Z : (j + 1) * Z]).astype(BF16)
                start = ((a * 2 + j % 2) * NP + p) * C
                Mb[start : start + C, (j // 2) * Z : (j // 2 + 1) * Z] = merged
            grad_depth = dot(pinT_ref[...], grad_pre, 1, 0).astype(BF16).astype(F32)
            for j in range(4):
                r = x * Y + 4 * p + j
                g = grad_depth[:, j * Z : (j + 1) * Z]
                G1[r] = g.astype(BF16)
                for e, value in enumerate((from_right(g, lane), g, from_left(g, lane))):
                    Gs[e * C : (e + 1) * C, r * Z : (r + 1) * Z] = value.astype(BF16)
            aout[...] += dot(gm, active, 1, 1)
            ain[...] += dot(depth, grad_pre, 1, 1)

        pt = dot(Mb[...], perm, 1, 0).astype(BF16)
        for a in range(2):
            for b in range(2):
                for p in range(NP):
                    src = ((a * 2 + b) * NP + p) * C
                    for e in range(2):
                        dst = ((a * 2 + b) * 2 + e) * C
                        Pt[dst : dst + C, p * Z : (p + 1) * Z] = pt[
                            src : src + C, e * Z : (e + 1) * Z
                        ]
        red_ref[step, X0] = dot(Pt[...], wd_ref[...], 0, 0).astype(BF16)
        adown[...] += dot(Pt[...], gd_ref[step, X0], 1, 0)

    write_pieces(lambda x, y: G1[x * Y + y], step, Y, *pieces)
    atap[...] += dot(Gs[...], FB[...], 1, 1)

    @pl.when(step == pl.num_programs(0) - 1)
    def _():
        rows_s[...] = jnp.zeros_like(rows_s)
        for k in range(8):
            rows_s[pl.ds(k, C, stride=8), :] = adown[k * C : (k + 1) * C, :]
        row = lax.broadcasted_iota(jnp.int32, (C, STACK * C), 0)
        column = lax.broadcasted_iota(jnp.int32, (C, STACK * C), 1)
        at = 8 * C + 2 * C * (H // Z)
        for e in range(3):
            block = jnp.where(column % C == row, atap[e * C : (e + 1) * C, :], 0.0)
            line = jnp.sum(block, axis=0, keepdims=True)
            for k in range(0, STACK * C, Z):
                rows_s[at : at + 1, :] = line[:, k : k + Z]
                at += 1
        packed_ref[: rows_s.shape[0], :] = rows_s[...].astype(BF16)
        at = 8 * C
        for part in (aout, ain):
            for k in range(0, H, Z):
                packed_ref[at : at + C, :] = part[:, k : k + Z].astype(BF16)
                at += C
        at = rows_s.shape[0]
        if at < packed_ref.shape[0]:
            rest = packed_ref.shape[0] - at
            packed_ref[at:, :] = jnp.zeros((rest, Z), BF16)


def adjoint_kernel(X, Y, C, Z, *refs):
    widened = refs[:8]
    gm_ref, tap_ref, out_ref, Fs, FB, wide = refs[8:]
    step = pl.program_id(0)
    fill_stack(widened, step, Fs, FB)
    lane = lax.broadcasted_iota(jnp.int32, (C, Z), 1)
    for r0 in range(0, X * Y, 4):
        rows = conv_rows(tap_ref[...], FB[:, r0 * Z : (r0 + 4) * Z], C, Z, lane)
        for r, value in enumerate(rows, r0):
            total = value + gm_ref[step, r // Y, r % Y].astype(F32)
            wide[pl.ds(r, C, stride=X * Y), :] = total
    out_ref[0] = wide[...].astype(BF16)


def finish_kernel(C, Z, H, scale, every_ref, down_ref, out_ref, in_ref, taps_ref):
    down_ref[...] = every_ref[: 8 * C, :].astype(F32) * scale
    at = 8 * C
    for ref in (out_ref, in_ref):
        for k in range(0, H, Z):
            ref[:, k : k + Z] = every_ref[at : at + C, :].astype(F32) * scale
            at += C
    taps = every_ref[at : at + 16, :].astype(F32) * scale
    per_line = STACK * C // Z
    for a in range(3):
        for b in range(3):
            line, k = divmod((a * 3 + b) * C, Z)
            for e in range(3):
                at = e * per_line + line
                taps_ref[a, b, e : e + 1, :] = taps[at : at + 1, k : k + C]


def sum_spread_kernel(parts_ref, out_ref):
    total = parts_ref[0].astype(F32)
    for i in range(1, parts_ref.shape[0]):
        total = total + parts_ref[i].astype(F32)
    total = total.astype(BF16)
    for j in range(out_ref.shape[0]):
        out_ref[j] = total


def sum_spread(parts, receivers):
    shape = (receivers,) + parts.shape[1:]
    return pl.pallas_call(
        sum_spread_kernel,
        in_specs=in_vmem(1),
        out_specs=in_vmem(1)[0],
        out_shape=jax.ShapeDtypeStruct(shape, BF16),
        compiler_params=params(4),
        name="sum_spread",
    )(parts)


def swap_in_group(blocks, axis):
    g = blocks.shape[0]
    if g == 1:
        return blocks
    n = lax.axis_size(axis)
    member = lax.axis_index(axis) % g
    got = [lax.dynamic_index_in_dim(blocks, member, 0, keepdims=False)]
    for k in range(1, g):
        out = lax.dynamic_index_in_dim(blocks, (member + k) % g, 0, keepdims=False)
        pairs = [(i, i - i % g + (i + k) % g) for i in range(n)]
        got.append(lax.ppermute(out, axis, pairs))
    if g == 2:
        first = member == 0
        return jnp.stack([jnp.where(first, got[0], got[1]), jnp.where(first, got[1], got[0])])
    got = jnp.stack(got)
    return jnp.take(got, (member - jnp.arange(g, dtype=jnp.int32)) % g, axis=0)


def per_device(fields, depth_kernel, point_in, point_out, down_kernel, cotangent):
    S, C, X, Y, Z = fields.shape
    assert X == 2 and Y % 4 == 0
    H, O = point_in.shape[0], down_kernel.shape[0]
    hx, hy, hz = X // 2, Y // 2, Z // 2
    nx, ny = lax.axis_size("gx"), lax.axis_size("gy")
    devices = nx * ny
    gx, gy = nx // GRIDC, ny // GRIDC
    per_group = S // (gx * gy)

    pieces = pl.pallas_call(
        functools.partial(split_kernel, X, Y, C, Z),
        grid=(S,),
        in_specs=[pl.BlockSpec((1, C * X * Y, Z), lambda s: (s, 0, 0))],
        out_specs=in_vmem(4),
        out_shape=piece_shapes(S, Y, C, Z),
        scratch_shapes=[pltpu.VMEM((C * X * Y, Z), F32)],
        compiler_params=params(6),
        name="split_fields",
    )(fields.reshape(S, C * X * Y, Z))

    widened = exchange_halo(pieces)

    moved = cotangent[0, 0].transpose(0, 2, 3, 4, 1)
    moved = moved.reshape(per_group, gx * hx, gy, hy * hz, O).transpose(2, 0, 1, 3, 4)
    moved = swap_in_group(moved, "gy").reshape(gy * per_group, gx, hx, hy * hz, O)
    moved = swap_in_group(moved.transpose(1, 0, 2, 3, 4), "gx")
    grad_down = moved.reshape(S, hx, hy * hz, O)

    wd = down_kernel.transpose(2, 3, 4, 1, 0).reshape(8 * C, O)
    taps = depth_kernel.reshape(C, 27).astype(F32)

    rows = 8 * C + 2 * C * (H // Z) + 16
    chunk = -(-rows // (16 * nx)) * 16
    cells = X * Y * Z
    flops = S * cells * (2 * 6 * C * H + 2 * 3 * C * O + 2 * 2 * 27 * C)
    dims = (X, Y, C, Z, H, O)
    grad_merged, tap_matrix, flip_matrix = pl.pallas_call(
        functools.partial(early_kernel, dims),
        grid=(S,),
        in_specs=in_vmem(3),
        out_specs=in_vmem(3),
        out_shape=[
            jax.ShapeDtypeStruct((S, X, Y, C, Z), BF16),
            jax.ShapeDtypeStruct((3 * C, STACK * C), BF16),
            jax.ShapeDtypeStruct((3 * C, STACK * C), BF16),
        ],
        scratch_shapes=[pltpu.VMEM((Y * C, 2 * Z), BF16)],
        compiler_params=params(8),
        cost_estimate=pl.CostEstimate(
            flops=S * cells * (2 * C * O + 8 * C * Z),
            bytes_accessed=4 * S * cells * C + 4 * 27 * C * Z,
            transcendentals=0,
        ),
        name="early",
    )(grad_down, taps, wd)

    out = pl.pallas_call(
        functools.partial(main_kernel, dims),
        grid=(S,),
        in_specs=in_vmem(14),
        out_specs=in_vmem(6),
        out_shape=[jax.ShapeDtypeStruct((S, hx, hy * hz, O), BF16)]
        + piece_shapes(S, Y, C, Z)
        + [jax.ShapeDtypeStruct((nx * chunk, Z), BF16)],
        scratch_shapes=[
            pltpu.VMEM(((X + 2) * (Y + 2), C, Z), BF16),
            pltpu.VMEM((STACK * C, cells), BF16),
            pltpu.VMEM((Y * C, 2 * Z), BF16),
            pltpu.VMEM((8 * C, hy * hz), BF16),
            pltpu.VMEM((X * Y, C, Z), BF16),
            pltpu.VMEM((3 * C, cells), BF16),
            pltpu.VMEM((3 * C, STACK * C), F32),
            pltpu.VMEM((8 * C, O), F32),
            pltpu.VMEM((C, H), F32),
            pltpu.VMEM((C, H), F32),
            pltpu.VMEM((H, C), BF16),
            pltpu.VMEM((H, C), BF16),
            pltpu.VMEM((Y // 2, H, 4 * Z), F32),
            pltpu.VMEM((Y // 2, H, 4 * Z), F32),
            pltpu.VMEM((Y // 2, H, 4 * Z), BF16),
            pltpu.VMEM((Y // 2, H, 4 * Z), BF16),
            pltpu.VMEM((rows, Z), F32),
        ],
        compiler_params=params(24),
        cost_estimate=pl.CostEstimate(
            flops=flops, bytes_accessed=8 * S * cells * C, transcendentals=S * cells * H
        ),
        name="main",
    )(*widened, grad_down, grad_merged, tap_matrix, point_in.T, point_out, wd)
    reduced, grad_pieces, packed = out[0], out[1:5], out[5]

    grad_widened = exchange_halo(grad_pieces)

    parts = lax.all_to_all(packed.reshape(nx, chunk, Z), "gx", 0, 0)
    parts = lax.all_to_all(sum_spread(parts, ny), "gy", 0, 0)
    share = sum_spread(parts, nx)
    share, grad_widened[0] = lax.optimization_barrier((share, grad_widened[0]))
    every = lax.all_to_all(share, "gx", 0, 0).reshape(nx * chunk, Z)

    grad_fields = pl.pallas_call(
        functools.partial(adjoint_kernel, X, Y, C, Z),
        grid=(S,),
        in_specs=in_vmem(10),
        out_specs=pl.BlockSpec((1, C * X * Y, Z), lambda s: (s, 0, 0)),
        out_shape=jax.ShapeDtypeStruct((S, C * X * Y, Z), BF16),
        scratch_shapes=[
            pltpu.VMEM(((X + 2) * (Y + 2), C, Z), BF16),
            pltpu.VMEM((STACK * C, cells), BF16),
            pltpu.VMEM((C * X * Y, Z), F32),
        ],
        compiler_params=params(14),
        cost_estimate=pl.CostEstimate(
            flops=S * cells * 2 * 27 * C, bytes_accessed=8 * S * cells * C, transcendentals=0
        ),
        name="adjoint",
    )(*grad_widened, grad_merged, flip_matrix).reshape(S, C, X, Y, Z)

    moved = swap_in_group(reduced.reshape(gx, S // gx, hx, hy * hz, O), "gx")
    moved = moved.transpose(1, 0, 2, 3, 4).reshape(gy, per_group, gx * hx, hy * hz, O)
    moved = swap_in_group(moved, "gy").transpose(1, 2, 0, 3, 4)
    coarse = moved.reshape(per_group, gx * hx, gy * hy, hz, O).transpose(0, 4, 1, 2, 3)[None, None]

    scale = 1.0 / math.sqrt(S * cells * devices)
    down, outw, inw, tapw = pl.pallas_call(
        functools.partial(finish_kernel, C, Z, H, scale),
        out_shape=[
            jax.ShapeDtypeStruct((8 * C, O), F32),
            jax.ShapeDtypeStruct((C, H), F32),
            jax.ShapeDtypeStruct((C, H), F32),
            jax.ShapeDtypeStruct((3, 3, 3, C), F32),
        ],
        in_specs=in_vmem(1),
        compiler_params=params(6),
        name="finish",
    )(every)
    return (
        coarse,
        grad_fields,
        tapw.transpose(3, 0, 1, 2),
        inw.T,
        outw,
        down.reshape(C, 2, 2, 2, O).transpose(4, 0, 1, 2, 3),
    )


def solution(mesh):
    placed = (
        P(None, None, "gx", "gy", None),
        P(),
        P(),
        P(),
        P(),
        P("gx", "gy", None, None, None, None, None),
    )
    return jax.shard_map(
        per_device,
        mesh=mesh,
        in_specs=placed,
        out_specs=(
            P("gx", "gy", None, None, None, None, None),
            P(None, None, "gx", "gy", None),
            P(),
            P(),
            P(),
            P(),
        ),
        check_vma=False,
    )
```

```python
import functools
import math

import jax
import jax.numpy as jnp
from jax import lax
from jax.experimental import pallas as pl
from jax.experimental.pallas import tpu as pltpu
from jax.sharding import PartitionSpec as P

GRIDC = 4
F32 = jnp.float32
BF16 = jnp.bfloat16
MIB = 1024 * 1024
STACK = 10
GELU_C = math.sqrt(2.0 / math.pi)
GELU_A = 0.044715


def dot(a, b, ca, cb):
    return lax.dot_general(a, b, (((ca,), (cb,)), ((), ())), preferred_element_type=F32)


def sides():
    return lax.axis_index("gx") % 2, lax.axis_index("gy") % 2


def write_pieces(row, s, Y, near, far, first, second):
    p, q = sides()
    for k, (x, plane) in enumerate(((1 - p, near), (p, far))):
        for y in range(Y):
            plane[s, y] = row(x, y)
        first[k, s] = row(x, (1 - q) * (Y - 1))
        second[k, s] = row(x, q * (Y - 1))


def piece_shapes(S, Y, C, Z):
    return [jax.ShapeDtypeStruct((S, Y, C, Z), BF16)] * 2 + [
        jax.ShapeDtypeStruct((2, S, C, Z), BF16)
    ] * 2


def params(mib):
    return pltpu.CompilerParams(vmem_limit_bytes=mib * MIB)


def in_vmem(n):
    return [pl.BlockSpec(memory_space=pltpu.VMEM)] * n


def swap_pairs(n, start):
    return [pair for i in range(start, n - 1, 2) for pair in ((i, i + 1), (i + 1, i))]


def swap_x(plane, start):
    return lax.ppermute(plane, "gx", swap_pairs(lax.axis_size("gx"), start))


def swap_y(rows, start):
    return lax.ppermute(rows, "gy", swap_pairs(lax.axis_size("gy"), start))


def halo_by_corners(pieces):
    near, far, first, second = pieces
    from_near, from_far = swap_x(near, 0), swap_x(far, 1)
    first, second = swap_y(first, 0), swap_y(second, 1)
    corner_far = swap_x(jnp.stack([first[1], second[1]]), 1)
    corner_near = swap_x(jnp.stack([first[0], second[0]]), 0)
    return [near, far, from_near, from_far, first, second, corner_near, corner_far]


def halo_by_planes(pieces):
    near, far, first, second = pieces
    from_near, from_far = swap_x(near, 0), swap_x(far, 1)
    _, q = sides()
    Y = near.shape[1]
    got = []
    for own, y, start in ((first, (1 - q) * (Y - 1), 0), (second, q * (Y - 1), 1)):
        rows = [
            lax.dynamic_index_in_dim(plane, y, 1, keepdims=False) for plane in (from_near, from_far)
        ]
        got.append(swap_y(jnp.concatenate([own, jnp.stack(rows)]), start))
    return [near, far, from_near, from_far, *got]


def fill_padded(planes, rims, s, Fs):
    p, q = sides()
    Y = planes[0].shape[1]
    places = (2 - p, 1 + p, 3 * (1 - p), 3 * p)
    for x, plane, ((r0, k0), (r1, k1)) in zip(places, planes, rims):
        for y in range(Y):
            Fs[x * (Y + 2) + y + 1] = plane[s, y].astype(Fs.dtype)
        Fs[x * (Y + 2) + (1 - q) * (Y + 1)] = r0[k0, s].astype(Fs.dtype)
        Fs[x * (Y + 2) + q * (Y + 1)] = r1[k1, s].astype(Fs.dtype)


def fill_stack(Fs, FB, Y):
    C, Z = Fs.shape[1:]
    for a in range(3):
        for b in range(3):
            at = (a * 3 + b) * C
            for x in range(2):
                for y in range(Y):
                    r = x * Y + y
                    row = Fs[(x + a) * (Y + 2) + y + b].astype(BF16)
                    FB[at : at + C, r * Z : (r + 1) * Z] = row
    FB[9 * C :, :] = jnp.zeros((FB.shape[0] - 9 * C, FB.shape[1]), BF16)


def from_left(value, lane):
    return jnp.where(lane == 0, 0.0, pltpu.roll(value, 1, 1))


def from_right(value, lane):
    Z = value.shape[1]
    return jnp.where(lane == Z - 1, 0.0, pltpu.roll(value, Z - 1, 1))


def conv_rows(taps, stack, C, Z, lane):
    acc = dot(taps, stack, 1, 0)
    rows = []
    for k in range(0, stack.shape[1], Z):
        left, mid, right = (acc[e * C : (e + 1) * C, k : k + Z] for e in range(3))
        rows.append(mid + from_left(left, lane) + from_right(right, lane))
    return rows


def conv_tiles(wb, Fs, Ds, rows, Y, lane):
    C, Z = Fs.shape[1:]
    for c in range(0, C, 8):
        weights = [wb[t, c : c + 8, :] for t in range(27)]
        for r in rows:
            x, y = divmod(r, Y)
            acc = [None, None, None]
            for a in range(3):
                for b in range(3):
                    f = Fs[(x + a) * (Y + 2) + y + b, c : c + 8, :]
                    for e in range(3):
                        term = weights[(a * 3 + b) * 3 + e] * f
                        acc[e] = term if acc[e] is None else acc[e] + term
            total = acc[1] + from_left(acc[0], lane[:8]) + from_right(acc[2], lane[:8])
            Ds[c : c + 8, r * Z : (r + 1) * Z] = total


def split_kernel(X, Y, C, Z, f_ref, near, far, first, second, wide):
    wide[...] = f_ref[0].astype(F32)

    def row(x, y):
        return wide[pl.ds(x * Y + y, C, stride=X * Y), :].astype(BF16)

    write_pieces(row, pl.program_id(0), Y, near, far, first, second)


def z_permutation(Z):
    fine = lax.broadcasted_iota(jnp.int32, (2 * Z, 2 * Z), 0)
    coarse = lax.broadcasted_iota(jnp.int32, (2 * Z, 2 * Z), 1)
    inner = coarse % Z
    goes = coarse // Z + (inner % (Z // 2)) * 2 + (inner // (Z // 2)) * Z
    return jnp.where(fine == goes, 1.0, 0.0).astype(BF16)


def early_kernel(dims, gd_ref, w_ref, wd_ref, gm_ref, wb, flip_ref, Mb):
    X, Y, C, Z, H, O = dims
    NP = Y // 4
    step = pl.program_id(0)

    @pl.when(step == 0)
    def _():
        row = lax.broadcasted_iota(jnp.int32, (C, STACK * C), 0)
        column = lax.broadcasted_iota(jnp.int32, (C, STACK * C), 1)
        for e in range(3):
            block = jnp.zeros((C, STACK * C), F32)
            for ab in range(9):
                t = 26 - (ab * 3 + e)
                block = jnp.where(column == row + ab * C, w_ref[:, t : t + 1], block)
            flip_ref[e * C : (e + 1) * C, :] = block.astype(BF16)
        for t in range(27):
            wb[t] = jnp.broadcast_to(w_ref[:, t : t + 1], (C, Z))

    perm = z_permutation(Z)
    for X0 in range(X // 2):
        gp = dot(wd_ref[...], gd_ref[step, X0], 1, 1).astype(BF16)
        for a in range(2):
            for b in range(2):
                for p in range(NP):
                    src = ((a * 2 + b) * 2) * C
                    dst = ((a * 2 + b) * NP + p) * C
                    for e in range(2):
                        Mb[dst : dst + C, e * Z : (e + 1) * Z] = gp[
                            src + e * C : src + (e + 1) * C, p * Z : (p + 1) * Z
                        ]
        gm = dot(Mb[...], perm, 1, 1).astype(BF16)
        for a in range(2):
            for b in range(2):
                for p in range(NP):
                    src = ((a * 2 + b) * NP + p) * C
                    for q in range(2):
                        x, y = 2 * X0 + a, 2 * (2 * p + q) + b
                        gm_ref[step, x, y] = gm[src : src + C, q * Z : (q + 1) * Z]


def main_kernel(dims, *refs):
    X, Y, C, Z, H, O = dims
    hx, NP = X // 2, Y // 4
    cells = X * Y * Z
    quarter = (Y // 2) * (Z // 2)
    planes, (first, second, corner_near, corner_far) = refs[:4], refs[4:8]
    rims = [((first, k), (second, k)) for k in range(2)]
    rims += [((corner, 0), (corner, 1)) for corner in (corner_near, corner_far)]
    gd_ref, gm_ref, wb, pinT_ref, pout_ref, wd_ref, red_ref = refs[8:15]
    pieces, packed_ref = refs[15:19], refs[19]
    Fs, FB, Ds, Mb, Pt, G1, Gs, atap, adown, aout, ain, pin, poutT = refs[20:33]
    pre_s, ga_s, act_s, gp_s, rows_s = refs[33:]
    step = pl.program_id(0)

    @pl.when(step == 0)
    def _():
        atap[...] = jnp.zeros_like(atap)
        Gs[3 * C :, :] = jnp.zeros((C, Gs.shape[1]), BF16)
        adown[...] = jnp.zeros_like(adown)
        aout[...] = jnp.zeros_like(aout)
        ain[...] = jnp.zeros_like(ain)
        pin[...] = pinT_ref[...].astype(F32).T.astype(BF16)
        poutT[...] = pout_ref[...].astype(F32).T.astype(BF16)

    fill_padded(planes, rims, step, Fs)
    fill_stack(Fs, FB, Y)
    lane = lax.broadcasted_iota(jnp.int32, (C, Z), 1)
    perm = z_permutation(Z)

    width = 4 * Z

    for X0 in range(hx):

        for i in range(2 * NP):
            a, p = i // NP, i % NP
            x = 2 * X0 + a
            columns = slice((x * NP + p) * width, (x * NP + p + 1) * width)
            r0 = x * Y + 4 * p
            conv_tiles(wb, Fs, Ds, range(r0, r0 + 4), Y, lane)
            depth = Ds[:, columns].astype(BF16)
            gm = jnp.concatenate([gm_ref[step, x, 4 * p + j] for j in range(4)], axis=1)
            pre_s[i] = dot(pin[...], depth, 1, 0)
            ga_s[i] = dot(poutT[...], gm, 1, 0)
            for h0 in range(0, H, 16):
                hs = slice(h0, h0 + 16)
                pre = pre_s[i, hs, :]
                sq = pre * pre
                t = jnp.tanh(pre * (GELU_C + (GELU_C * GELU_A) * sq))
                h = 0.5 + 0.5 * t
                act = pre * h
                slope = h + act * (1.0 - h) * (2.0 * GELU_C + (6.0 * GELU_C * GELU_A) * sq)
                act_s[i, hs, :] = act.astype(BF16)
                gp_s[i, hs, :] = (ga_s[i, hs, :] * slope).astype(BF16)
            active, grad_pre = act_s[i], gp_s[i]
            branch = dot(pout_ref[...], active, 1, 0)
            for j in range(4):
                row = (x + 1) * (Y + 2) + 4 * p + j + 1
                merged = (Fs[row] + branch[:, j * Z : (j + 1) * Z]).astype(BF16)
                start = ((a * 2 + j % 2) * NP + p) * C
                Mb[start : start + C, (j // 2) * Z : (j // 2 + 1) * Z] = merged
            grad_depth = dot(pinT_ref[...], grad_pre, 1, 0).astype(BF16).astype(F32)
            for j in range(4):
                r = x * Y + 4 * p + j
                g = grad_depth[:, j * Z : (j + 1) * Z]
                G1[r] = g.astype(BF16)
                for e, value in enumerate((from_right(g, lane), g, from_left(g, lane))):
                    Gs[e * C : (e + 1) * C, r * Z : (r + 1) * Z] = value.astype(BF16)
            aout[...] += dot(gm, active, 1, 1)
            ain[...] += dot(depth, grad_pre, 1, 1)

        pt = dot(Mb[...], perm, 1, 0).astype(BF16)
        for a in range(2):
            for b in range(2):
                for p in range(NP):
                    src = ((a * 2 + b) * NP + p) * C
                    for e in range(2):
                        dst = ((a * 2 + b) * 2 + e) * C
                        Pt[dst : dst + C, p * Z : (p + 1) * Z] = pt[
                            src : src + C, e * Z : (e + 1) * Z
                        ]
        red_ref[step, X0] = dot(Pt[...], wd_ref[...], 0, 0).astype(BF16)
        adown[...] += dot(Pt[...], gd_ref[step, X0], 1, 0)

    write_pieces(lambda x, y: G1[x * Y + y], step, Y, *pieces)
    atap[...] += dot(FB[...], Gs[...], 1, 1)

    @pl.when(step == pl.num_programs(0) - 1)
    def _():
        rows_s[...] = jnp.zeros_like(rows_s)
        for k in range(8):
            rows_s[pl.ds(k, C, stride=8), :] = adown[k * C : (k + 1) * C, :]
        row = lax.broadcasted_iota(jnp.int32, (C, 4 * C), 0)
        column = lax.broadcasted_iota(jnp.int32, (C, 4 * C), 1)
        at = 8 * C + 2 * C * (H // Z)
        for ab in range(9):
            block = jnp.where(column % C == row, atap[ab * C : (ab + 1) * C, :], 0.0)
            line = jnp.sum(block, axis=0, keepdims=True)
            for k in range(0, 4 * C, Z):
                rows_s[at : at + 1, :] = line[:, k : k + Z]
                at += 1
        packed_ref[: rows_s.shape[0], :] = rows_s[...].astype(BF16)
        at = 8 * C
        for part in (aout, ain):
            for k in range(0, H, Z):
                packed_ref[at : at + C, :] = part[:, k : k + Z].astype(BF16)
                at += C
        at = rows_s.shape[0]
        if at < packed_ref.shape[0]:
            rest = packed_ref.shape[0] - at
            packed_ref[at:, :] = jnp.zeros((rest, Z), BF16)


def adjoint_kernel(X, Y, C, Z, *refs):
    planes, (first, second) = refs[:4], refs[4:6]
    gm_ref, tap_ref, out_ref, Fs, FB, wide = refs[6:]
    step = pl.program_id(0)
    fill_padded(planes, [((first, k), (second, k)) for k in range(4)], step, Fs)
    fill_stack(Fs, FB, Y)
    lane = lax.broadcasted_iota(jnp.int32, (C, Z), 1)
    for r0 in range(0, X * Y, 4):
        rows = conv_rows(tap_ref[...], FB[:, r0 * Z : (r0 + 4) * Z], C, Z, lane)
        for r, value in enumerate(rows, r0):
            total = value + gm_ref[step, r // Y, r % Y].astype(F32)
            wide[pl.ds(r, C, stride=X * Y), :] = total
    out_ref[0] = wide[...].astype(BF16)


def finish_kernel(C, Z, H, scale, every_ref, down_ref, out_ref, in_ref, taps_ref):
    down_ref[...] = every_ref[: 8 * C, :].astype(F32) * scale
    at = 8 * C
    for ref in (out_ref, in_ref):
        for k in range(0, H, Z):
            ref[:, k : k + Z] = every_ref[at : at + C, :].astype(F32) * scale
            at += C
    taps = every_ref[at : at + 32, :].astype(F32) * scale
    for a in range(3):
        for b in range(3):
            for e in range(3):
                line, k = divmod(e * C, Z)
                line += (a * 3 + b) * (4 * C // Z)
                taps_ref[a, b, e : e + 1, :] = taps[line : line + 1, k : k + C]


def sum_spread_kernel(parts_ref, out_ref):
    total = parts_ref[0].astype(F32)
    for i in range(1, parts_ref.shape[0]):
        total = total + parts_ref[i].astype(F32)
    total = total.astype(BF16)
    for j in range(out_ref.shape[0]):
        out_ref[j] = total


def sum_spread(parts, receivers):
    shape = (receivers,) + parts.shape[1:]
    return pl.pallas_call(
        sum_spread_kernel,
        in_specs=in_vmem(1),
        out_specs=in_vmem(1)[0],
        out_shape=jax.ShapeDtypeStruct(shape, BF16),
        compiler_params=params(4),
        name="sum_spread",
    )(parts)


def swap_in_group(blocks, axis):
    g = blocks.shape[0]
    if g == 1:
        return blocks
    n = lax.axis_size(axis)
    member = lax.axis_index(axis) % g
    got = [lax.dynamic_index_in_dim(blocks, member, 0, keepdims=False)]
    for k in range(1, g):
        out = lax.dynamic_index_in_dim(blocks, (member + k) % g, 0, keepdims=False)
        pairs = [(i, i - i % g + (i + k) % g) for i in range(n)]
        got.append(lax.ppermute(out, axis, pairs))
    if g == 2:
        first = member == 0
        return jnp.stack([jnp.where(first, got[0], got[1]), jnp.where(first, got[1], got[0])])
    got = jnp.stack(got)
    return jnp.take(got, (member - jnp.arange(g, dtype=jnp.int32)) % g, axis=0)


def per_device(fields, depth_kernel, point_in, point_out, down_kernel, cotangent):
    S, C, X, Y, Z = fields.shape
    assert X == 2 and Y % 4 == 0
    H, O = point_in.shape[0], down_kernel.shape[0]
    hx, hy, hz = X // 2, Y // 2, Z // 2
    nx, ny = lax.axis_size("gx"), lax.axis_size("gy")
    devices = nx * ny
    gx, gy = nx // GRIDC, ny // GRIDC
    per_group = S // (gx * gy)

    pieces = pl.pallas_call(
        functools.partial(split_kernel, X, Y, C, Z),
        grid=(S,),
        in_specs=[pl.BlockSpec((1, C * X * Y, Z), lambda s: (s, 0, 0))],
        out_specs=in_vmem(4),
        out_shape=piece_shapes(S, Y, C, Z),
        scratch_shapes=[pltpu.VMEM((C * X * Y, Z), F32)],
        compiler_params=params(6),
        name="split_fields",
    )(fields.reshape(S, C * X * Y, Z))


    moved = cotangent[0, 0].transpose(0, 2, 3, 4, 1)
    moved = moved.reshape(per_group, gx * hx, gy, hy * hz, O).transpose(2, 0, 1, 3, 4)
    moved = swap_in_group(moved, "gy").reshape(gy * per_group, gx, hx, hy * hz, O)
    moved = swap_in_group(moved.transpose(1, 0, 2, 3, 4), "gx")
    grad_down = moved.reshape(S, hx, hy * hz, O)

    near, far, first, second = pieces
    first, second, grad_down = lax.optimization_barrier((first, second, grad_down))
    widened = halo_by_corners((near, far, first, second))

    wd = down_kernel.transpose(2, 3, 4, 1, 0).reshape(8 * C, O)
    taps = depth_kernel.reshape(C, 27).astype(F32)

    rows = 8 * C + 2 * C * (H // Z) + 32
    chunk = -(-rows // (16 * nx)) * 16
    cells = X * Y * Z
    flops = S * cells * (2 * 6 * C * H + 2 * 3 * C * O + 2 * 2 * 27 * C)
    dims = (X, Y, C, Z, H, O)
    grad_merged, spread, flip_matrix = pl.pallas_call(
        functools.partial(early_kernel, dims),
        grid=(S,),
        in_specs=in_vmem(3),
        out_specs=in_vmem(3),
        out_shape=[
            jax.ShapeDtypeStruct((S, X, Y, C, Z), BF16),
            jax.ShapeDtypeStruct((27, C, Z), F32),
            jax.ShapeDtypeStruct((3 * C, STACK * C), BF16),
        ],
        scratch_shapes=[pltpu.VMEM((Y * C, 2 * Z), BF16)],
        compiler_params=params(8),
        cost_estimate=pl.CostEstimate(
            flops=S * cells * (2 * C * O + 8 * C * Z),
            bytes_accessed=4 * S * cells * C + 4 * 27 * C * Z,
            transcendentals=0,
        ),
        name="early",
    )(grad_down, taps, wd)

    out = pl.pallas_call(
        functools.partial(main_kernel, dims),
        grid=(S,),
        in_specs=in_vmem(14),
        out_specs=in_vmem(6),
        out_shape=[jax.ShapeDtypeStruct((S, hx, hy * hz, O), BF16)]
        + piece_shapes(S, Y, C, Z)
        + [jax.ShapeDtypeStruct((nx * chunk, Z), BF16)],
        scratch_shapes=[
            pltpu.VMEM(((X + 2) * (Y + 2), C, Z), F32),
            pltpu.VMEM((STACK * C, cells), BF16),
            pltpu.VMEM((C, cells), F32),
            pltpu.VMEM((Y * C, 2 * Z), BF16),
            pltpu.VMEM((8 * C, hy * hz), BF16),
            pltpu.VMEM((X * Y, C, Z), BF16),
            pltpu.VMEM((4 * C, cells), BF16),
            pltpu.VMEM((STACK * C, 4 * C), F32),
            pltpu.VMEM((8 * C, O), F32),
            pltpu.VMEM((C, H), F32),
            pltpu.VMEM((C, H), F32),
            pltpu.VMEM((H, C), BF16),
            pltpu.VMEM((H, C), BF16),
            pltpu.VMEM((Y // 2, H, 4 * Z), F32),
            pltpu.VMEM((Y // 2, H, 4 * Z), F32),
            pltpu.VMEM((Y // 2, H, 4 * Z), BF16),
            pltpu.VMEM((Y // 2, H, 4 * Z), BF16),
            pltpu.VMEM((rows, Z), F32),
        ],
        compiler_params=params(24),
        cost_estimate=pl.CostEstimate(
            flops=flops, bytes_accessed=8 * S * cells * C, transcendentals=S * cells * H
        ),
        name="main",
    )(*widened, grad_down, grad_merged, spread, point_in.T, point_out, wd)
    reduced, grad_pieces, packed = out[0], out[1:5], out[5]

    grad_widened = halo_by_planes(grad_pieces)

    parts = lax.all_to_all(packed.reshape(nx, chunk, Z), "gx", 0, 0)
    parts = lax.all_to_all(sum_spread(parts, ny), "gy", 0, 0)
    share = sum_spread(parts, nx)
    share, grad_widened[0] = lax.optimization_barrier((share, grad_widened[0]))
    every = lax.all_to_all(share, "gx", 0, 0).reshape(nx * chunk, Z)

    grad_fields = pl.pallas_call(
        functools.partial(adjoint_kernel, X, Y, C, Z),
        grid=(S,),
        in_specs=in_vmem(8),
        out_specs=pl.BlockSpec((1, C * X * Y, Z), lambda s: (s, 0, 0)),
        out_shape=jax.ShapeDtypeStruct((S, C * X * Y, Z), BF16),
        scratch_shapes=[
            pltpu.VMEM(((X + 2) * (Y + 2), C, Z), BF16),
            pltpu.VMEM((STACK * C, cells), BF16),
            pltpu.VMEM((C * X * Y, Z), F32),
        ],
        compiler_params=params(14),
        cost_estimate=pl.CostEstimate(
            flops=S * cells * 2 * 27 * C, bytes_accessed=8 * S * cells * C, transcendentals=0
        ),
        name="adjoint",
    )(*grad_widened, grad_merged, flip_matrix).reshape(S, C, X, Y, Z)

    moved = swap_in_group(reduced.reshape(gx, S // gx, hx, hy * hz, O), "gx")
    moved = moved.transpose(1, 0, 2, 3, 4).reshape(gy, per_group, gx * hx, hy * hz, O)
    moved = swap_in_group(moved, "gy").transpose(1, 2, 0, 3, 4)
    coarse = moved.reshape(per_group, gx * hx, gy * hy, hz, O).transpose(0, 4, 1, 2, 3)[None, None]

    scale = 1.0 / math.sqrt(S * cells * devices)
    down, outw, inw, tapw = pl.pallas_call(
        functools.partial(finish_kernel, C, Z, H, scale),
        out_shape=[
            jax.ShapeDtypeStruct((8 * C, O), F32),
            jax.ShapeDtypeStruct((C, H), F32),
            jax.ShapeDtypeStruct((C, H), F32),
            jax.ShapeDtypeStruct((3, 3, 3, C), F32),
        ],
        in_specs=in_vmem(1),
        compiler_params=params(6),
        name="finish",
    )(every)
    return (
        coarse,
        grad_fields,
        tapw.transpose(3, 0, 1, 2),
        inw.T,
        outw,
        down.reshape(C, 2, 2, 2, O).transpose(4, 0, 1, 2, 3),
    )


def solution(mesh):
    placed = (
        P(None, None, "gx", "gy", None),
        P(),
        P(),
        P(),
        P(),
        P("gx", "gy", None, None, None, None, None),
    )
    return jax.shard_map(
        per_device,
        mesh=mesh,
        in_specs=placed,
        out_specs=(
            P("gx", "gy", None, None, None, None, None),
            P(None, None, "gx", "gy", None),
            P(),
            P(),
            P(),
            P(),
        ),
        check_vma=False,
    )
```

```python
import functools
import math

import jax
import jax.numpy as jnp
from jax import lax
from jax.experimental import pallas as pl
from jax.experimental.pallas import tpu as pltpu
from jax.sharding import PartitionSpec as P

GRIDC = 4
F32 = jnp.float32
BF16 = jnp.bfloat16
MIB = 1024 * 1024
STACK = 10
GELU_C = math.sqrt(2.0 / math.pi)
GELU_A = 0.044715


def dot(a, b, ca, cb):
    return lax.dot_general(a, b, (((ca,), (cb,)), ((), ())), preferred_element_type=F32)


def sides():
    return lax.axis_index("gx") % 2, lax.axis_index("gy") % 2


def write_pieces(row, s, Y, near, far, first, second):
    p, q = sides()
    for k, (x, plane) in enumerate(((1 - p, near), (p, far))):
        for y in range(Y):
            plane[s, y] = row(x, y)
        first[k, s] = row(x, (1 - q) * (Y - 1))
        second[k, s] = row(x, q * (Y - 1))


def piece_shapes(S, Y, C, Z):
    return [jax.ShapeDtypeStruct((S, Y, C, Z), BF16)] * 2 + [
        jax.ShapeDtypeStruct((2, S, C, Z), BF16)
    ] * 2


def params(mib):
    return pltpu.CompilerParams(vmem_limit_bytes=mib * MIB)


def in_vmem(n):
    return [pl.BlockSpec(memory_space=pltpu.VMEM)] * n


def swap_pairs(n, start):
    return [pair for i in range(start, n - 1, 2) for pair in ((i, i + 1), (i + 1, i))]


def swap_x(plane, start):
    return lax.ppermute(plane, "gx", swap_pairs(lax.axis_size("gx"), start))


def swap_y(rows, start):
    return lax.ppermute(rows, "gy", swap_pairs(lax.axis_size("gy"), start))


def halo_by_corners(pieces):
    near, far, first, second = pieces
    from_near, from_far = swap_x(near, 0), swap_x(far, 1)
    first, second = swap_y(first, 0), swap_y(second, 1)
    corner_far = swap_x(jnp.stack([first[1], second[1]]), 1)
    corner_near = swap_x(jnp.stack([first[0], second[0]]), 0)
    return [near, far, from_near, from_far, first, second, corner_near, corner_far]


def halo_by_planes(pieces):
    near, far, first, second = pieces
    from_near, from_far = swap_x(near, 0), swap_x(far, 1)
    _, q = sides()
    Y = near.shape[1]
    got = []
    for own, y, start in ((first, (1 - q) * (Y - 1), 0), (second, q * (Y - 1), 1)):
        rows = [
            lax.dynamic_index_in_dim(plane, y, 1, keepdims=False) for plane in (from_near, from_far)
        ]
        got.append(swap_y(jnp.concatenate([own, jnp.stack(rows)]), start))
    return [near, far, from_near, from_far, *got]


def fill_padded(planes, rims, s, Fs):
    p, q = sides()
    Y = planes[0].shape[1]
    places = (2 - p, 1 + p, 3 * (1 - p), 3 * p)
    for x, plane in zip(places, planes):
        for y in range(Y):
            Fs[x * (Y + 2) + y + 1] = plane[s, y].astype(Fs.dtype)
    for x, ((r0, k0), (r1, k1)) in zip(places, rims):
        Fs[x * (Y + 2) + (1 - q) * (Y + 1)] = r0[k0, s].astype(Fs.dtype)
        Fs[x * (Y + 2) + q * (Y + 1)] = r1[k1, s].astype(Fs.dtype)


def fill_stack(Fs, FB, rows, Y):
    C, Z = Fs.shape[1:]
    for a in range(3):
        for b in range(3):
            at = (a * 3 + b) * C
            for r, (x, y) in enumerate(rows):
                row = Fs[(x + a) * (Y + 2) + y + b].astype(BF16)
                FB[at : at + C, r * Z : (r + 1) * Z] = row
    FB[9 * C :, :] = jnp.zeros((FB.shape[0] - 9 * C, FB.shape[1]), BF16)


def from_left(value, lane):
    return jnp.where(lane == 0, 0.0, pltpu.roll(value, 1, 1))


def from_right(value, lane):
    Z = value.shape[1]
    return jnp.where(lane == Z - 1, 0.0, pltpu.roll(value, Z - 1, 1))


def conv_rows(taps, stack, C, Z, lane):
    acc = dot(taps, stack, 1, 0)
    rows = []
    for k in range(0, stack.shape[1], Z):
        left, mid, right = (acc[e * C : (e + 1) * C, k : k + Z] for e in range(3))
        rows.append(mid + from_left(left, lane) + from_right(right, lane))
    return rows


def conv_tiles(wb, flip, Fs, rows, Y, lane, store):
    for c in range(0, Fs.shape[1], 8):
        weights = [wb[26 - t if flip else t, c : c + 8, :] for t in range(27)]
        for j, (x, y) in enumerate(rows):
            acc = [None, None, None]
            for a in range(3):
                for b in range(3):
                    f = Fs[(x + a) * (Y + 2) + y + b, c : c + 8, :]
                    for e in range(3):
                        term = weights[(a * 3 + b) * 3 + e] * f
                        acc[e] = term if acc[e] is None else acc[e] + term
            store(c, j, acc[1] + from_left(acc[0], lane[:8]) + from_right(acc[2], lane[:8]))


def split_kernel(X, Y, C, Z, f_ref, near, far, first, second, wide):
    wide[...] = f_ref[0].astype(F32)

    def row(x, y):
        return wide[pl.ds(x * Y + y, C, stride=X * Y), :].astype(BF16)

    write_pieces(row, pl.program_id(0), Y, near, far, first, second)


def z_permutation(Z):
    fine = lax.broadcasted_iota(jnp.int32, (2 * Z, 2 * Z), 0)
    coarse = lax.broadcasted_iota(jnp.int32, (2 * Z, 2 * Z), 1)
    inner = coarse % Z
    goes = coarse // Z + (inner % (Z // 2)) * 2 + (inner // (Z // 2)) * Z
    return jnp.where(fine == goes, 1.0, 0.0).astype(BF16)


def early_kernel(dims, gd_ref, w_ref, wd_ref, gm_ref, wb, flip_ref, Mb):
    X, Y, C, Z, H, O = dims
    NP = Y // 4
    step = pl.program_id(0)

    @pl.when(step == 0)
    def _():
        row = lax.broadcasted_iota(jnp.int32, (C, STACK * C), 0)
        column = lax.broadcasted_iota(jnp.int32, (C, STACK * C), 1)
        for e in range(3):
            block = jnp.zeros((C, STACK * C), F32)
            for ab in range(9):
                t = 26 - (ab * 3 + e)
                block = jnp.where(column == row + ab * C, w_ref[:, t : t + 1], block)
            flip_ref[e * C : (e + 1) * C, :] = block.astype(BF16)
        for t in range(27):
            wb[t] = jnp.broadcast_to(w_ref[:, t : t + 1], (C, Z))

    perm = z_permutation(Z)
    for X0 in range(X // 2):
        gp = dot(wd_ref[...], gd_ref[step, X0], 1, 1).astype(BF16)
        for a in range(2):
            for b in range(2):
                for p in range(NP):
                    src = ((a * 2 + b) * 2) * C
                    dst = ((a * 2 + b) * NP + p) * C
                    for e in range(2):
                        Mb[dst : dst + C, e * Z : (e + 1) * Z] = gp[
                            src + e * C : src + (e + 1) * C, p * Z : (p + 1) * Z
                        ]
        gm = dot(Mb[...], perm, 1, 1).astype(BF16)
        for a in range(2):
            for b in range(2):
                for p in range(NP):
                    src = ((a * 2 + b) * NP + p) * C
                    for q in range(2):
                        x, y = 2 * X0 + a, 2 * (2 * p + q) + b
                        gm_ref[step, x, y] = gm[src : src + C, q * Z : (q + 1) * Z]


def set_up(pinT_ref, pout_ref, pin, poutT):
    pin[...] = pinT_ref[...].astype(F32).T.astype(BF16)
    poutT[...] = pout_ref[...].astype(F32).T.astype(BF16)


def merged_place(x, y, Y, C, Z):
    start = ((x * 2 + y % 2) * (Y // 4) + y // 4) * C
    q = y // 2 % 2
    return slice(start, start + C), slice(q * Z, (q + 1) * Z)


def forward_backward(i, rows, step, dims, lane, ops, put_merged, put_grad):
    X, Y, C, Z, H, O = dims
    Fs, Ds, gm_ref, wb, pinT_ref, pout_ref, pin, poutT, pre_s, ga_s, act_s, gp_s, aout, ain = ops

    def store(c, j, value):
        Ds[i, c : c + 8, j * Z : (j + 1) * Z] = value

    conv_tiles(wb, False, Fs, rows, Y, lane, store)
    depth = Ds[i].astype(BF16)
    gm = jnp.concatenate([gm_ref[step, x, y] for x, y in rows], axis=1)
    pre_s[i] = dot(pin[...], depth, 1, 0)
    ga_s[i] = dot(poutT[...], gm, 1, 0)
    for h0 in range(0, H, 16):
        hs = slice(h0, h0 + 16)
        pre = pre_s[i, hs, :]
        sq = pre * pre
        t = jnp.tanh(pre * (GELU_C + (GELU_C * GELU_A) * sq))
        h = 0.5 + 0.5 * t
        act = pre * h
        slope = h + act * (1.0 - h) * (2.0 * GELU_C + (6.0 * GELU_C * GELU_A) * sq)
        act_s[i, hs, :] = act.astype(BF16)
        gp_s[i, hs, :] = (ga_s[i, hs, :] * slope).astype(BF16)
    active, grad_pre = act_s[i], gp_s[i]
    branch = dot(pout_ref[...], active, 1, 0)
    grad_depth = dot(pinT_ref[...], grad_pre, 1, 0).astype(BF16)
    for j, (x, y) in enumerate(rows):
        lanes = slice(j * Z, (j + 1) * Z)
        row = Fs[(x + 1) * (Y + 2) + y + 1]
        put_merged(x, y, (row + branch[:, lanes]).astype(BF16))
        put_grad(x, y, grad_depth[:, lanes])
    aout[...] += dot(gm, active, 1, 1)
    ain[...] += dot(depth, grad_pre, 1, 1)


def inner_kernel(dims, *refs):
    X, Y, C, Z, H, O = dims
    planes, (gm_ref, wb, pinT_ref, pout_ref) = refs[:4], refs[4:8]
    Mb, G, aout, ain, Fs, Ds, pin, poutT, pre_s, ga_s, act_s, gp_s = refs[8:]
    step = pl.program_id(0)

    @pl.when(step == 0)
    def _():
        aout[...] = jnp.zeros_like(aout)
        ain[...] = jnp.zeros_like(ain)
        set_up(pinT_ref, pout_ref, pin, poutT)

    fill_padded(planes, (), step, Fs)
    lane = lax.broadcasted_iota(jnp.int32, (C, Z), 1)
    ops = Fs, Ds, gm_ref, wb, pinT_ref, pout_ref, pin, poutT, pre_s, ga_s, act_s, gp_s, aout, ain

    def put_merged(x, y, value):
        rows, lanes = merged_place(x, y, Y, C, Z)
        Mb[step, rows, lanes] = value

    def put_grad(x, y, value):
        G[step, x * Y + y] = value

    rows = [(x, y) for x in range(X) for y in range(1, Y - 1)]
    for i in range(len(rows) // 4):
        chunk = rows[4 * i : 4 * i + 4]
        forward_backward(i, chunk, step, dims, lane, ops, put_merged, put_grad)


def outer_kernel(dims, *refs):
    X, Y, C, Z, H, O = dims
    NP = Y // 4
    planes, (first, second, corner_near, corner_far) = refs[:4], refs[4:8]
    rims = [((first, k), (second, k)) for k in range(2)]
    rims += [((corner, 0), (corner, 1)) for corner in (corner_near, corner_far)]
    gd_ref, gm_ref, wb, pinT_ref, pout_ref, wd_ref, Mb_ref, G_ref, aout_ref, ain_ref = refs[8:18]
    red_ref, pieces, packed_ref = refs[18], refs[19:23], refs[23]
    Fs, FB, Ds, Mb, Pt, G1, Gs, atap, adown, aout, ain, pin, poutT = refs[24:37]
    pre_s, ga_s, act_s, gp_s, rows_s = refs[37:]
    step = pl.program_id(0)

    @pl.when(step == 0)
    def _():
        atap[...] = jnp.zeros_like(atap)
        Gs[3 * C :, :] = jnp.zeros((C, Gs.shape[1]), BF16)
        adown[...] = jnp.zeros_like(adown)
        aout[...] = aout_ref[...]
        ain[...] = ain_ref[...]
        set_up(pinT_ref, pout_ref, pin, poutT)

    fill_padded(planes, rims, step, Fs)
    cells = [(x, y) for x in range(X) for y in range(Y)]
    fill_stack(Fs, FB, cells, Y)
    lane = lax.broadcasted_iota(jnp.int32, (C, Z), 1)
    perm = z_permutation(Z)
    Mb[...] = Mb_ref[step]
    G1[...] = G_ref[step]
    ops = Fs, Ds, gm_ref, wb, pinT_ref, pout_ref, pin, poutT, pre_s, ga_s, act_s, gp_s, aout, ain

    def put_merged(x, y, value):
        rows, lanes = merged_place(x, y, Y, C, Z)
        Mb[rows, lanes] = value

    def put_grad(x, y, value):
        G1[x * Y + y] = value

    rows = [(x, y) for x in range(X) for y in (0, Y - 1)]
    forward_backward(0, rows, step, dims, lane, ops, put_merged, put_grad)

    write_pieces(lambda x, y: G1[x * Y + y], step, Y, *pieces)
    for r in range(X * Y):
        g = G1[r].astype(F32)
        for e, value in enumerate((from_right(g, lane), g, from_left(g, lane))):
            Gs[e * C : (e + 1) * C, r * Z : (r + 1) * Z] = value.astype(BF16)
    atap[...] += dot(FB[...], Gs[...], 1, 1)

    pt = dot(Mb[...], perm, 1, 0).astype(BF16)
    for a in range(2):
        for b in range(2):
            for p in range(NP):
                src = ((a * 2 + b) * NP + p) * C
                for e in range(2):
                    dst = ((a * 2 + b) * 2 + e) * C
                    Pt[dst : dst + C, p * Z : (p + 1) * Z] = pt[
                        src : src + C, e * Z : (e + 1) * Z
                    ]
    red_ref[step, 0] = dot(Pt[...], wd_ref[...], 0, 0).astype(BF16)
    adown[...] += dot(Pt[...], gd_ref[step, 0], 1, 0)

    @pl.when(step == pl.num_programs(0) - 1)
    def _():
        rows_s[...] = jnp.zeros_like(rows_s)
        for k in range(8):
            rows_s[pl.ds(k, C, stride=8), :] = adown[k * C : (k + 1) * C, :]
        row = lax.broadcasted_iota(jnp.int32, (C, 4 * C), 0)
        column = lax.broadcasted_iota(jnp.int32, (C, 4 * C), 1)
        at = 8 * C + 2 * C * (H // Z)
        for ab in range(9):
            block = jnp.where(column % C == row, atap[ab * C : (ab + 1) * C, :], 0.0)
            line = jnp.sum(block, axis=0, keepdims=True)
            for k in range(0, 4 * C, Z):
                rows_s[at : at + 1, :] = line[:, k : k + Z]
                at += 1
        packed_ref[: rows_s.shape[0], :] = rows_s[...].astype(BF16)
        at = 8 * C
        for part in (aout, ain):
            for k in range(0, H, Z):
                packed_ref[at : at + C, :] = part[:, k : k + Z].astype(BF16)
                at += C
        at = rows_s.shape[0]
        if at < packed_ref.shape[0]:
            rest = packed_ref.shape[0] - at
            packed_ref[at:, :] = jnp.zeros((rest, Z), BF16)


def adjoint_kernel(X, Y, C, Z, *refs):
    planes, (first, second) = refs[:4], refs[4:6]
    gm_ref, wb, flip_ref, moved_ref, out_ref, coarse_ref, Fs, FB, wide = refs[6:]
    step = pl.program_id(0)
    coarse_ref[...] = moved_ref[...]
    fill_padded(planes, [((first, k), (second, k)) for k in range(4)], step, Fs)
    cells = [(x, y) for x in range(X) for y in range(Y)]
    products, tiles = cells[: len(cells) // 2], cells[len(cells) // 2 :]
    fill_stack(Fs, FB, products, Y)
    lane = lax.broadcasted_iota(jnp.int32, (C, Z), 1)
    for r0 in range(0, len(products), 2):
        rows = conv_rows(flip_ref[...], FB[:, r0 * Z : (r0 + 2) * Z], C, Z, lane)
        for (x, y), value in zip(products[r0 : r0 + 2], rows):
            total = value + gm_ref[step, x, y].astype(F32)
            wide[pl.ds(x * Y + y, C, stride=X * Y), :] = total

        def store(c, j, value):
            x, y = tiles[r0 + j]
            total = value + gm_ref[step, x, y, c : c + 8, :].astype(F32)
            wide[pl.ds(c * X * Y + x * Y + y, 8, stride=X * Y), :] = total

        conv_tiles(wb, True, Fs, tiles[r0 : r0 + 2], Y, lane, store)
    out_ref[0] = wide[...].astype(BF16)


def finish_kernel(C, Z, H, scale, every_ref, down_ref, out_ref, in_ref, taps_ref):
    down_ref[...] = every_ref[: 8 * C, :].astype(F32) * scale
    at = 8 * C
    for ref in (out_ref, in_ref):
        for k in range(0, H, Z):
            ref[:, k : k + Z] = every_ref[at : at + C, :].astype(F32) * scale
            at += C
    taps = every_ref[at : at + 32, :].astype(F32) * scale
    for a in range(3):
        for b in range(3):
            for e in range(3):
                line, k = divmod(e * C, Z)
                line += (a * 3 + b) * (4 * C // Z)
                taps_ref[a, b, e : e + 1, :] = taps[line : line + 1, k : k + C]


def sum_spread_kernel(parts_ref, out_ref):
    total = parts_ref[0].astype(F32)
    for i in range(1, parts_ref.shape[0]):
        total = total + parts_ref[i].astype(F32)
    total = total.astype(BF16)
    for j in range(out_ref.shape[0]):
        out_ref[j] = total


def sum_spread(parts, receivers):
    shape = (receivers,) + parts.shape[1:]
    return pl.pallas_call(
        sum_spread_kernel,
        in_specs=in_vmem(1),
        out_specs=in_vmem(1)[0],
        out_shape=jax.ShapeDtypeStruct(shape, BF16),
        compiler_params=params(4),
        name="sum_spread",
    )(parts)


def swap_in_group(blocks, axis):
    g = blocks.shape[0]
    if g == 1:
        return blocks
    n = lax.axis_size(axis)
    member = lax.axis_index(axis) % g
    got = [lax.dynamic_index_in_dim(blocks, member, 0, keepdims=False)]
    for k in range(1, g):
        out = lax.dynamic_index_in_dim(blocks, (member + k) % g, 0, keepdims=False)
        pairs = [(i, i - i % g + (i + k) % g) for i in range(n)]
        got.append(lax.ppermute(out, axis, pairs))
    if g == 2:
        first = member == 0
        return jnp.stack([jnp.where(first, got[0], got[1]), jnp.where(first, got[1], got[0])])
    got = jnp.stack(got)
    return jnp.take(got, (member - jnp.arange(g, dtype=jnp.int32)) % g, axis=0)


def per_device(fields, depth_kernel, point_in, point_out, down_kernel, cotangent):
    S, C, X, Y, Z = fields.shape
    assert X == 2 and Y % 4 == 0
    H, O = point_in.shape[0], down_kernel.shape[0]
    hx, hy, hz = X // 2, Y // 2, Z // 2
    nx, ny = lax.axis_size("gx"), lax.axis_size("gy")
    devices = nx * ny
    gx, gy = nx // GRIDC, ny // GRIDC
    per_group = S // (gx * gy)

    pieces = pl.pallas_call(
        functools.partial(split_kernel, X, Y, C, Z),
        grid=(S,),
        in_specs=[pl.BlockSpec((1, C * X * Y, Z), lambda s: (s, 0, 0))],
        out_specs=in_vmem(4),
        out_shape=piece_shapes(S, Y, C, Z),
        scratch_shapes=[pltpu.VMEM((C * X * Y, Z), F32)],
        compiler_params=params(6),
        name="split_fields",
    )(fields.reshape(S, C * X * Y, Z))


    moved = cotangent[0, 0].transpose(0, 2, 3, 4, 1)
    moved = moved.reshape(per_group, gx * hx, gy, hy * hz, O).transpose(2, 0, 1, 3, 4)
    moved = swap_in_group(moved, "gy").reshape(gy * per_group, gx, hx, hy * hz, O)
    moved = swap_in_group(moved.transpose(1, 0, 2, 3, 4), "gx")
    grad_down = moved.reshape(S, hx, hy * hz, O)

    widened = halo_by_corners(pieces)

    wd = down_kernel.transpose(2, 3, 4, 1, 0).reshape(8 * C, O)
    taps = depth_kernel.reshape(C, 27).astype(F32)

    rows = 8 * C + 2 * C * (H // Z) + 32
    chunk = -(-rows // (16 * nx)) * 16
    cells = X * Y * Z
    dims = (X, Y, C, Z, H, O)
    grad_merged, spread, flip_matrix = pl.pallas_call(
        functools.partial(early_kernel, dims),
        grid=(S,),
        in_specs=in_vmem(3),
        out_specs=in_vmem(3),
        out_shape=[
            jax.ShapeDtypeStruct((S, X, Y, C, Z), BF16),
            jax.ShapeDtypeStruct((27, C, Z), F32),
            jax.ShapeDtypeStruct((3 * C, STACK * C), BF16),
        ],
        scratch_shapes=[pltpu.VMEM((Y * C, 2 * Z), BF16)],
        compiler_params=params(8),
        cost_estimate=pl.CostEstimate(
            flops=S * cells * (2 * C * O + 8 * C * Z),
            bytes_accessed=4 * S * cells * C + 4 * 27 * C * Z,
            transcendentals=0,
        ),
        name="early",
    )(grad_down, taps, wd)

    def work(rows):
        return pl.CostEstimate(
            flops=S * rows * Z * (2 * 6 * C * H + 2 * 27 * C),
            bytes_accessed=8 * S * rows * Z * C,
            transcendentals=S * rows * Z * H,
        )

    def chunk_scratch(n):
        return [
            pltpu.VMEM((H, C), BF16),
            pltpu.VMEM((H, C), BF16),
            pltpu.VMEM((n, H, 4 * Z), F32),
            pltpu.VMEM((n, H, 4 * Z), F32),
            pltpu.VMEM((n, H, 4 * Z), BF16),
            pltpu.VMEM((n, H, 4 * Z), BF16),
        ]

    chunks = X * (Y - 2) // 4
    inner = pl.pallas_call(
        functools.partial(inner_kernel, dims),
        grid=(S,),
        in_specs=in_vmem(8),
        out_specs=in_vmem(4),
        out_shape=[
            jax.ShapeDtypeStruct((S, Y * C, 2 * Z), BF16),
            jax.ShapeDtypeStruct((S, X * Y, C, Z), BF16),
            jax.ShapeDtypeStruct((C, H), F32),
            jax.ShapeDtypeStruct((C, H), F32),
        ],
        scratch_shapes=[
            pltpu.VMEM(((X + 2) * (Y + 2), C, Z), F32),
            pltpu.VMEM((chunks, C, 4 * Z), F32),
        ]
        + chunk_scratch(chunks),
        compiler_params=params(16),
        cost_estimate=work(X * (Y - 2)),
        name="inner",
    )(*widened[:4], grad_merged, spread, point_in.T, point_out)
    out = pl.pallas_call(
        functools.partial(outer_kernel, dims),
        grid=(S,),
        in_specs=in_vmem(18),
        out_specs=in_vmem(6),
        out_shape=[jax.ShapeDtypeStruct((S, hx, hy * hz, O), BF16)]
        + piece_shapes(S, Y, C, Z)
        + [jax.ShapeDtypeStruct((nx * chunk, Z), BF16)],
        scratch_shapes=[
            pltpu.VMEM(((X + 2) * (Y + 2), C, Z), F32),
            pltpu.VMEM((STACK * C, cells), BF16),
            pltpu.VMEM((1, C, 4 * Z), F32),
            pltpu.VMEM((Y * C, 2 * Z), BF16),
            pltpu.VMEM((8 * C, hy * hz), BF16),
            pltpu.VMEM((X * Y, C, Z), BF16),
            pltpu.VMEM((4 * C, cells), BF16),
            pltpu.VMEM((STACK * C, 4 * C), F32),
            pltpu.VMEM((8 * C, O), F32),
            pltpu.VMEM((C, H), F32),
            pltpu.VMEM((C, H), F32),
        ]
        + chunk_scratch(1)
        + [pltpu.VMEM((rows, Z), F32)],
        compiler_params=params(16),
        cost_estimate=work(2 * X),
        name="outer",
    )(*widened, grad_down, grad_merged, spread, point_in.T, point_out, wd, *inner)
    reduced, grad_pieces, packed = out[0], out[1:5], out[5]

    grad_widened = halo_by_planes(grad_pieces)

    parts = lax.all_to_all(packed.reshape(nx, chunk, Z), "gx", 0, 0)
    parts = lax.all_to_all(sum_spread(parts, ny), "gy", 0, 0)
    share = sum_spread(parts, nx)
    share, grad_widened[0] = lax.optimization_barrier((share, grad_widened[0]))
    every = lax.all_to_all(share, "gx", 0, 0).reshape(nx * chunk, Z)

    moved = swap_in_group(reduced.reshape(gx, S // gx, hx, hy * hz, O), "gx")
    moved = moved.transpose(1, 0, 2, 3, 4).reshape(gy, per_group, gx * hx, hy * hz, O)
    moved = swap_in_group(moved, "gy").transpose(1, 2, 0, 3, 4)
    moved = moved.reshape(per_group, gx * hx, gy * hy * hz, O)

    grad_fields, coarse = pl.pallas_call(
        functools.partial(adjoint_kernel, X, Y, C, Z),
        grid=(S,),
        in_specs=in_vmem(10),
        out_specs=[
            pl.BlockSpec((1, C * X * Y, Z), lambda s: (s, 0, 0)),
            pl.BlockSpec(moved.shape, lambda s: (0, 0, 0, 0)),
        ],
        out_shape=[
            jax.ShapeDtypeStruct((S, C * X * Y, Z), BF16),
            jax.ShapeDtypeStruct(moved.shape, BF16),
        ],
        scratch_shapes=[
            pltpu.VMEM(((X + 2) * (Y + 2), C, Z), F32),
            pltpu.VMEM((STACK * C, cells // 2), BF16),
            pltpu.VMEM((C * X * Y, Z), F32),
        ],
        compiler_params=params(14),
        cost_estimate=pl.CostEstimate(
            flops=S * cells * 2 * 27 * C, bytes_accessed=8 * S * cells * C, transcendentals=0
        ),
        name="adjoint",
    )(*grad_widened, grad_merged, spread, flip_matrix, moved)
    grad_fields = grad_fields.reshape(S, C, X, Y, Z)
    coarse = coarse.reshape(per_group, gx * hx, gy * hy, hz, O)
    coarse = coarse.transpose(0, 4, 1, 2, 3)[None, None]

    scale = 1.0 / math.sqrt(S * cells * devices)
    down, outw, inw, tapw = pl.pallas_call(
        functools.partial(finish_kernel, C, Z, H, scale),
        out_shape=[
            jax.ShapeDtypeStruct((8 * C, O), F32),
            jax.ShapeDtypeStruct((C, H), F32),
            jax.ShapeDtypeStruct((C, H), F32),
            jax.ShapeDtypeStruct((3, 3, 3, C), F32),
        ],
        in_specs=in_vmem(1),
        compiler_params=params(6),
        name="finish",
    )(every)
    return (
        coarse,
        grad_fields,
        tapw.transpose(3, 0, 1, 2),
        inw.T,
        outw,
        down.reshape(C, 2, 2, 2, O).transpose(4, 0, 1, 2, 3),
    )


def solution(mesh):
    placed = (
        P(None, None, "gx", "gy", None),
        P(),
        P(),
        P(),
        P(),
        P("gx", "gy", None, None, None, None, None),
    )
    return jax.shard_map(
        per_device,
        mesh=mesh,
        in_specs=placed,
        out_specs=(
            P("gx", "gy", None, None, None, None, None),
            P(None, None, "gx", "gy", None),
            P(),
            P(),
            P(),
            P(),
        ),
        check_vma=False,
    )
```

```python
import functools
import math

import jax
import jax.numpy as jnp
from jax import lax
from jax.experimental import pallas as pl
from jax.experimental.pallas import tpu as pltpu
from jax.sharding import PartitionSpec as P

GRIDC = 4
F32 = jnp.float32
BF16 = jnp.bfloat16
MIB = 1024 * 1024
STACK = 10
GELU_C = math.sqrt(2.0 / math.pi)
GELU_A = 0.044715


def dot(a, b, ca, cb):
    return lax.dot_general(a, b, (((ca,), (cb,)), ((), ())), preferred_element_type=F32)


def sides():
    return lax.axis_index("gx") % 2, lax.axis_index("gy") % 2


def write_pieces(row, s, Y, near, far, first, second):
    p, q = sides()
    for k, (x, plane) in enumerate(((1 - p, near), (p, far))):
        for y in range(Y):
            plane[s, y] = row(x, y)
        first[k, s] = row(x, (1 - q) * (Y - 1))
        second[k, s] = row(x, q * (Y - 1))


def piece_shapes(S, Y, C, Z):
    return [jax.ShapeDtypeStruct((S, Y, C, Z), BF16)] * 2 + [
        jax.ShapeDtypeStruct((2, S, C, Z), BF16)
    ] * 2


def params(mib):
    return pltpu.CompilerParams(vmem_limit_bytes=mib * MIB)


def in_vmem(n):
    return [pl.BlockSpec(memory_space=pltpu.VMEM)] * n


def swap_pairs(n, start):
    return [pair for i in range(start, n - 1, 2) for pair in ((i, i + 1), (i + 1, i))]


def swap_x(plane, start):
    return lax.ppermute(plane, "gx", swap_pairs(lax.axis_size("gx"), start))


def swap_y(rows, start):
    return lax.ppermute(rows, "gy", swap_pairs(lax.axis_size("gy"), start))


def halo_by_corners(pieces):
    near, far, first, second = pieces
    from_near, from_far = swap_x(near, 0), swap_x(far, 1)
    first, second = swap_y(first, 0), swap_y(second, 1)
    corner_far = swap_x(jnp.stack([first[1], second[1]]), 1)
    corner_near = swap_x(jnp.stack([first[0], second[0]]), 0)
    return [near, far, from_near, from_far, first, second, corner_near, corner_far]


def halo_by_planes(pieces):
    near, far, first, second = pieces
    from_near, from_far = swap_x(near, 0), swap_x(far, 1)
    _, q = sides()
    Y = near.shape[1]
    got = []
    for own, y, start in ((first, (1 - q) * (Y - 1), 0), (second, q * (Y - 1), 1)):
        rows = [
            lax.dynamic_index_in_dim(plane, y, 1, keepdims=False) for plane in (from_near, from_far)
        ]
        got.append(swap_y(jnp.concatenate([own, jnp.stack(rows)]), start))
    return [near, far, from_near, from_far, *got]


def fill_padded(planes, rims, s, Fs):
    p, q = sides()
    Y = planes[0].shape[1]
    places = (2 - p, 1 + p, 3 * (1 - p), 3 * p)
    for x, plane, ((r0, k0), (r1, k1)) in zip(places, planes, rims):
        for y in range(Y):
            Fs[x * (Y + 2) + y + 1] = plane[s, y].astype(Fs.dtype)
        Fs[x * (Y + 2) + (1 - q) * (Y + 1)] = r0[k0, s].astype(Fs.dtype)
        Fs[x * (Y + 2) + q * (Y + 1)] = r1[k1, s].astype(Fs.dtype)


def fill_stack(Fs, FB, Y):
    C, Z = Fs.shape[1:]
    for a in range(3):
        for b in range(3):
            at = (a * 3 + b) * C
            for x in range(2):
                for y in range(Y):
                    r = x * Y + y
                    row = Fs[(x + a) * (Y + 2) + y + b].astype(BF16)
                    FB[at : at + C, r * Z : (r + 1) * Z] = row
    FB[9 * C :, :] = jnp.zeros((FB.shape[0] - 9 * C, FB.shape[1]), BF16)


def from_left(value, lane):
    return jnp.where(lane == 0, 0.0, pltpu.roll(value, 1, 1))


def from_right(value, lane):
    Z = value.shape[1]
    return jnp.where(lane == Z - 1, 0.0, pltpu.roll(value, Z - 1, 1))


def conv_rows(taps, stack, C, Z, lane):
    acc = dot(taps, stack, 1, 0)
    rows = []
    for k in range(0, stack.shape[1], Z):
        left, mid, right = (acc[e * C : (e + 1) * C, k : k + Z] for e in range(3))
        rows.append(mid + from_left(left, lane) + from_right(right, lane))
    return rows


def conv_tiles(wb, Fs, Ds, rows, Y, lane):
    C, Z = Fs.shape[1:]
    for c in range(0, C, 8):
        weights = [wb[t, c : c + 8, :] for t in range(27)]
        for r in rows:
            x, y = divmod(r, Y)
            acc = [None, None, None]
            for a in range(3):
                for b in range(3):
                    f = Fs[(x + a) * (Y + 2) + y + b, c : c + 8, :]
                    for e in range(3):
                        term = weights[(a * 3 + b) * 3 + e] * f
                        acc[e] = term if acc[e] is None else acc[e] + term
            total = acc[1] + from_left(acc[0], lane[:8]) + from_right(acc[2], lane[:8])
            Ds[c : c + 8, r * Z : (r + 1) * Z] = total


def split_kernel(X, Y, C, Z, f_ref, near, far, first, second, wide):
    wide[...] = f_ref[0].astype(F32)

    def row(x, y):
        return wide[pl.ds(x * Y + y, C, stride=X * Y), :].astype(BF16)

    write_pieces(row, pl.program_id(0), Y, near, far, first, second)


def z_permutation(Z):
    fine = lax.broadcasted_iota(jnp.int32, (2 * Z, 2 * Z), 0)
    coarse = lax.broadcasted_iota(jnp.int32, (2 * Z, 2 * Z), 1)
    inner = coarse % Z
    goes = coarse // Z + (inner % (Z // 2)) * 2 + (inner // (Z // 2)) * Z
    return jnp.where(fine == goes, 1.0, 0.0).astype(BF16)


def early_kernel(dims, gd_ref, w_ref, wd_ref, gm_ref, wb, flip_ref, Mb):
    X, Y, C, Z, H, O = dims
    NP = Y // 4
    step = pl.program_id(0)

    @pl.when(step == 0)
    def _():
        row = lax.broadcasted_iota(jnp.int32, (C, STACK * C), 0)
        column = lax.broadcasted_iota(jnp.int32, (C, STACK * C), 1)
        for e in range(3):
            block = jnp.zeros((C, STACK * C), F32)
            for ab in range(9):
                t = 26 - (ab * 3 + e)
                block = jnp.where(column == row + ab * C, w_ref[:, t : t + 1], block)
            flip_ref[e * C : (e + 1) * C, :] = block.astype(BF16)
        for t in range(27):
            wb[t] = jnp.broadcast_to(w_ref[:, t : t + 1], (C, Z))

    perm = z_permutation(Z)
    for X0 in range(X // 2):
        gp = dot(wd_ref[...], gd_ref[step, X0], 1, 1).astype(BF16)
        for a in range(2):
            for b in range(2):
                for p in range(NP):
                    src = ((a * 2 + b) * 2) * C
                    dst = ((a * 2 + b) * NP + p) * C
                    for e in range(2):
                        Mb[dst : dst + C, e * Z : (e + 1) * Z] = gp[
                            src + e * C : src + (e + 1) * C, p * Z : (p + 1) * Z
                        ]
        gm = dot(Mb[...], perm, 1, 1).astype(BF16)
        for a in range(2):
            for b in range(2):
                for p in range(NP):
                    src = ((a * 2 + b) * NP + p) * C
                    for q in range(2):
                        x, y = 2 * X0 + a, 2 * (2 * p + q) + b
                        gm_ref[step, x, y] = gm[src : src + C, q * Z : (q + 1) * Z]


def main_kernel(dims, *refs):
    X, Y, C, Z, H, O = dims
    hx, NP = X // 2, Y // 4
    cells = X * Y * Z
    quarter = (Y // 2) * (Z // 2)
    planes, (first, second, corner_near, corner_far) = refs[:4], refs[4:8]
    rims = [((first, k), (second, k)) for k in range(2)]
    rims += [((corner, 0), (corner, 1)) for corner in (corner_near, corner_far)]
    gd_ref, gm_ref, wb, pinT_ref, pout_ref, wd_ref, red_ref = refs[8:15]
    pieces, packed_ref = refs[15:19], refs[19]
    Fs, FB, Ds, Mb, Pt, G1, Gs, atap, adown, aout, ain, pin, poutT = refs[20:33]
    pre_s, ga_s, act_s, gp_s, rows_s = refs[33:]
    step = pl.program_id(0)

    @pl.when(step == 0)
    def _():
        atap[...] = jnp.zeros_like(atap)
        Gs[3 * C :, :] = jnp.zeros((C, Gs.shape[1]), BF16)
        adown[...] = jnp.zeros_like(adown)
        aout[...] = jnp.zeros_like(aout)
        ain[...] = jnp.zeros_like(ain)
        pin[...] = pinT_ref[...].astype(F32).T.astype(BF16)
        poutT[...] = pout_ref[...].astype(F32).T.astype(BF16)

    fill_padded(planes, rims, step, Fs)
    fill_stack(Fs, FB, Y)
    lane = lax.broadcasted_iota(jnp.int32, (C, Z), 1)
    perm = z_permutation(Z)

    width = 4 * Z

    for X0 in range(hx):

        for i in range(2 * NP):
            a, p = i // NP, i % NP
            x = 2 * X0 + a
            columns = slice((x * NP + p) * width, (x * NP + p + 1) * width)
            r0 = x * Y + 4 * p
            conv_tiles(wb, Fs, Ds, range(r0, r0 + 4), Y, lane)
            depth = Ds[:, columns].astype(BF16)
            gm = jnp.concatenate([gm_ref[step, x, 4 * p + j] for j in range(4)], axis=1)
            pre_s[i] = dot(pin[...], depth, 1, 0)
            ga_s[i] = dot(poutT[...], gm, 1, 0)
            for h0 in range(0, H, 16):
                hs = slice(h0, h0 + 16)
                pre = pre_s[i, hs, :]
                sq = pre * pre
                t = jnp.tanh(pre * (GELU_C + (GELU_C * GELU_A) * sq))
                h = 0.5 + 0.5 * t
                act = pre * h
                slope = h + act * (1.0 - h) * (2.0 * GELU_C + (6.0 * GELU_C * GELU_A) * sq)
                act_s[i, hs, :] = act.astype(BF16)
                gp_s[i, hs, :] = (ga_s[i, hs, :] * slope).astype(BF16)
            active, grad_pre = act_s[i], gp_s[i]
            branch = dot(pout_ref[...], active, 1, 0)
            for j in range(4):
                row = (x + 1) * (Y + 2) + 4 * p + j + 1
                merged = (Fs[row] + branch[:, j * Z : (j + 1) * Z]).astype(BF16)
                start = ((a * 2 + j % 2) * NP + p) * C
                Mb[start : start + C, (j // 2) * Z : (j // 2 + 1) * Z] = merged
            grad_depth = dot(pinT_ref[...], grad_pre, 1, 0).astype(BF16).astype(F32)
            for j in range(4):
                r = x * Y + 4 * p + j
                g = grad_depth[:, j * Z : (j + 1) * Z]
                G1[r] = g.astype(BF16)
                for e, value in enumerate((from_right(g, lane), g, from_left(g, lane))):
                    Gs[e * C : (e + 1) * C, r * Z : (r + 1) * Z] = value.astype(BF16)
            aout[...] += dot(gm, active, 1, 1)
            ain[...] += dot(depth, grad_pre, 1, 1)

        pt = dot(Mb[...], perm, 1, 0).astype(BF16)
        for a in range(2):
            for b in range(2):
                for p in range(NP):
                    src = ((a * 2 + b) * NP + p) * C
                    for e in range(2):
                        dst = ((a * 2 + b) * 2 + e) * C
                        Pt[dst : dst + C, p * Z : (p + 1) * Z] = pt[
                            src : src + C, e * Z : (e + 1) * Z
                        ]
        red_ref[step, X0] = dot(Pt[...], wd_ref[...], 0, 0).astype(BF16)
        adown[...] += dot(Pt[...], gd_ref[step, X0], 1, 0)

    write_pieces(lambda x, y: G1[x * Y + y], step, Y, *pieces)
    atap[...] += dot(FB[...], Gs[...], 1, 1)

    @pl.when(step == pl.num_programs(0) - 1)
    def _():
        rows_s[...] = jnp.zeros_like(rows_s)
        for k in range(8):
            rows_s[pl.ds(k, C, stride=8), :] = adown[k * C : (k + 1) * C, :]
        row = lax.broadcasted_iota(jnp.int32, (C, 4 * C), 0)
        column = lax.broadcasted_iota(jnp.int32, (C, 4 * C), 1)
        at = 8 * C + 2 * C * (H // Z)
        for ab in range(9):
            block = jnp.where(column % C == row, atap[ab * C : (ab + 1) * C, :], 0.0)
            line = jnp.sum(block, axis=0, keepdims=True)
            for k in range(0, 4 * C, Z):
                rows_s[at : at + 1, :] = line[:, k : k + Z]
                at += 1
        packed_ref[: rows_s.shape[0], :] = rows_s[...].astype(BF16)
        at = 8 * C
        for part in (aout, ain):
            for k in range(0, H, Z):
                packed_ref[at : at + C, :] = part[:, k : k + Z].astype(BF16)
                at += C
        at = rows_s.shape[0]
        if at < packed_ref.shape[0]:
            rest = packed_ref.shape[0] - at
            packed_ref[at:, :] = jnp.zeros((rest, Z), BF16)


def adjoint_kernel(X, Y, C, Z, *refs):
    planes, (first, second) = refs[:4], refs[4:6]
    gm_ref, tap_ref, out_ref, Fs, FB, wide = refs[6:]
    step = pl.program_id(0)
    fill_padded(planes, [((first, k), (second, k)) for k in range(4)], step, Fs)
    fill_stack(Fs, FB, Y)
    lane = lax.broadcasted_iota(jnp.int32, (C, Z), 1)
    for r0 in range(0, X * Y, 4):
        rows = conv_rows(tap_ref[...], FB[:, r0 * Z : (r0 + 4) * Z], C, Z, lane)
        for r, value in enumerate(rows, r0):
            total = value + gm_ref[step, r // Y, r % Y].astype(F32)
            wide[pl.ds(r, C, stride=X * Y), :] = total
    out_ref[0] = wide[...].astype(BF16)


def finish_kernel(C, Z, H, scale, every_ref, down_ref, out_ref, in_ref, taps_ref):
    down_ref[...] = every_ref[: 8 * C, :].astype(F32) * scale
    at = 8 * C
    for ref in (out_ref, in_ref):
        for k in range(0, H, Z):
            ref[:, k : k + Z] = every_ref[at : at + C, :].astype(F32) * scale
            at += C
    taps = every_ref[at : at + 32, :].astype(F32) * scale
    for a in range(3):
        for b in range(3):
            for e in range(3):
                line, k = divmod(e * C, Z)
                line += (a * 3 + b) * (4 * C // Z)
                taps_ref[a, b, e : e + 1, :] = taps[line : line + 1, k : k + C]


def sum_spread_kernel(parts_ref, out_ref):
    total = parts_ref[0].astype(F32)
    for i in range(1, parts_ref.shape[0]):
        total = total + parts_ref[i].astype(F32)
    total = total.astype(BF16)
    for j in range(out_ref.shape[0]):
        out_ref[j] = total


def sum_spread(parts, receivers):
    shape = (receivers,) + parts.shape[1:]
    return pl.pallas_call(
        sum_spread_kernel,
        in_specs=in_vmem(1),
        out_specs=in_vmem(1)[0],
        out_shape=jax.ShapeDtypeStruct(shape, BF16),
        compiler_params=params(4),
        name="sum_spread",
    )(parts)


def swap_in_group(blocks, axis):
    g = blocks.shape[0]
    if g == 1:
        return blocks
    n = lax.axis_size(axis)
    member = lax.axis_index(axis) % g
    got = [lax.dynamic_index_in_dim(blocks, member, 0, keepdims=False)]
    for k in range(1, g):
        out = lax.dynamic_index_in_dim(blocks, (member + k) % g, 0, keepdims=False)
        pairs = [(i, i - i % g + (i + k) % g) for i in range(n)]
        got.append(lax.ppermute(out, axis, pairs))
    if g == 2:
        first = member == 0
        return jnp.stack([jnp.where(first, got[0], got[1]), jnp.where(first, got[1], got[0])])
    got = jnp.stack(got)
    return jnp.take(got, (member - jnp.arange(g, dtype=jnp.int32)) % g, axis=0)


def per_device(fields, depth_kernel, point_in, point_out, down_kernel, cotangent):
    S, C, X, Y, Z = fields.shape
    assert X == 2 and Y % 4 == 0
    H, O = point_in.shape[0], down_kernel.shape[0]
    hx, hy, hz = X // 2, Y // 2, Z // 2
    nx, ny = lax.axis_size("gx"), lax.axis_size("gy")
    devices = nx * ny
    gx, gy = nx // GRIDC, ny // GRIDC
    per_group = S // (gx * gy)

    pieces = pl.pallas_call(
        functools.partial(split_kernel, X, Y, C, Z),
        grid=(S,),
        in_specs=[pl.BlockSpec((1, C * X * Y, Z), lambda s: (s, 0, 0))],
        out_specs=in_vmem(4),
        out_shape=piece_shapes(S, Y, C, Z),
        scratch_shapes=[pltpu.VMEM((C * X * Y, Z), F32)],
        compiler_params=params(6),
        name="split_fields",
    )(fields.reshape(S, C * X * Y, Z))


    moved = cotangent[0, 0].transpose(0, 2, 3, 4, 1)
    moved = moved.reshape(per_group, gx * hx, gy, hy * hz, O).transpose(2, 0, 1, 3, 4)
    moved = swap_in_group(moved, "gy").reshape(gy * per_group, gx, hx, hy * hz, O)
    moved = swap_in_group(moved.transpose(1, 0, 2, 3, 4), "gx")
    grad_down = moved.reshape(S, hx, hy * hz, O)

    widened = halo_by_corners(pieces)

    wd = down_kernel.transpose(2, 3, 4, 1, 0).reshape(8 * C, O)
    taps = depth_kernel.reshape(C, 27).astype(F32)

    rows = 8 * C + 2 * C * (H // Z) + 32
    chunk = -(-rows // (8 * nx)) * 8
    cells = X * Y * Z
    flops = S * cells * (2 * 6 * C * H + 2 * 3 * C * O + 2 * 2 * 27 * C)
    dims = (X, Y, C, Z, H, O)
    grad_merged, spread, flip_matrix = pl.pallas_call(
        functools.partial(early_kernel, dims),
        grid=(S,),
        in_specs=in_vmem(3),
        out_specs=in_vmem(3),
        out_shape=[
            jax.ShapeDtypeStruct((S, X, Y, C, Z), BF16),
            jax.ShapeDtypeStruct((27, C, Z), F32),
            jax.ShapeDtypeStruct((3 * C, STACK * C), BF16),
        ],
        scratch_shapes=[pltpu.VMEM((Y * C, 2 * Z), BF16)],
        compiler_params=params(8),
        cost_estimate=pl.CostEstimate(
            flops=S * cells * (2 * C * O + 8 * C * Z),
            bytes_accessed=4 * S * cells * C + 4 * 27 * C * Z,
            transcendentals=0,
        ),
        name="early",
    )(grad_down, taps, wd)

    out = pl.pallas_call(
        functools.partial(main_kernel, dims),
        grid=(S,),
        in_specs=in_vmem(14),
        out_specs=in_vmem(6),
        out_shape=[jax.ShapeDtypeStruct((S, hx, hy * hz, O), BF16)]
        + piece_shapes(S, Y, C, Z)
        + [jax.ShapeDtypeStruct((nx * chunk, Z), BF16)],
        scratch_shapes=[
            pltpu.VMEM(((X + 2) * (Y + 2), C, Z), F32),
            pltpu.VMEM((STACK * C, cells), BF16),
            pltpu.VMEM((C, cells), F32),
            pltpu.VMEM((Y * C, 2 * Z), BF16),
            pltpu.VMEM((8 * C, hy * hz), BF16),
            pltpu.VMEM((X * Y, C, Z), BF16),
            pltpu.VMEM((4 * C, cells), BF16),
            pltpu.VMEM((STACK * C, 4 * C), F32),
            pltpu.VMEM((8 * C, O), F32),
            pltpu.VMEM((C, H), F32),
            pltpu.VMEM((C, H), F32),
            pltpu.VMEM((H, C), BF16),
            pltpu.VMEM((H, C), BF16),
            pltpu.VMEM((Y // 2, H, 4 * Z), F32),
            pltpu.VMEM((Y // 2, H, 4 * Z), F32),
            pltpu.VMEM((Y // 2, H, 4 * Z), BF16),
            pltpu.VMEM((Y // 2, H, 4 * Z), BF16),
            pltpu.VMEM((rows, Z), F32),
        ],
        compiler_params=params(24),
        cost_estimate=pl.CostEstimate(
            flops=flops, bytes_accessed=8 * S * cells * C, transcendentals=S * cells * H
        ),
        name="main",
    )(*widened, grad_down, grad_merged, spread, point_in.T, point_out, wd)
    reduced, grad_pieces, packed = out[0], out[1:5], out[5]

    grad_widened = halo_by_planes(grad_pieces)

    parts = lax.all_to_all(packed.reshape(nx, chunk, Z), "gx", 0, 0)
    parts = lax.all_to_all(sum_spread(parts, ny), "gy", 0, 0)
    share = sum_spread(parts, nx)
    share, grad_widened[0] = lax.optimization_barrier((share, grad_widened[0]))
    every = lax.all_to_all(share, "gx", 0, 0).reshape(nx * chunk, Z)

    grad_fields = pl.pallas_call(
        functools.partial(adjoint_kernel, X, Y, C, Z),
        grid=(S,),
        in_specs=in_vmem(8),
        out_specs=pl.BlockSpec((1, C * X * Y, Z), lambda s: (s, 0, 0)),
        out_shape=jax.ShapeDtypeStruct((S, C * X * Y, Z), BF16),
        scratch_shapes=[
            pltpu.VMEM(((X + 2) * (Y + 2), C, Z), BF16),
            pltpu.VMEM((STACK * C, cells), BF16),
            pltpu.VMEM((C * X * Y, Z), F32),
        ],
        compiler_params=params(14),
        cost_estimate=pl.CostEstimate(
            flops=S * cells * 2 * 27 * C, bytes_accessed=8 * S * cells * C, transcendentals=0
        ),
        name="adjoint",
    )(*grad_widened, grad_merged, flip_matrix).reshape(S, C, X, Y, Z)

    moved = swap_in_group(reduced.reshape(gx, S // gx, hx, hy * hz, O), "gx")
    moved = moved.transpose(1, 0, 2, 3, 4).reshape(gy, per_group, gx * hx, hy * hz, O)
    moved = swap_in_group(moved, "gy").transpose(1, 2, 0, 3, 4)
    coarse = moved.reshape(per_group, gx * hx, gy * hy, hz, O).transpose(0, 4, 1, 2, 3)[None, None]

    scale = 1.0 / math.sqrt(S * cells * devices)
    down, outw, inw, tapw = pl.pallas_call(
        functools.partial(finish_kernel, C, Z, H, scale),
        out_shape=[
            jax.ShapeDtypeStruct((8 * C, O), F32),
            jax.ShapeDtypeStruct((C, H), F32),
            jax.ShapeDtypeStruct((C, H), F32),
            jax.ShapeDtypeStruct((3, 3, 3, C), F32),
        ],
        in_specs=in_vmem(1),
        compiler_params=params(6),
        name="finish",
    )(every)
    return (
        coarse,
        grad_fields,
        tapw.transpose(3, 0, 1, 2),
        inw.T,
        outw,
        down.reshape(C, 2, 2, 2, O).transpose(4, 0, 1, 2, 3),
    )


def solution(mesh):
    placed = (
        P(None, None, "gx", "gy", None),
        P(),
        P(),
        P(),
        P(),
        P("gx", "gy", None, None, None, None, None),
    )
    return jax.shard_map(
        per_device,
        mesh=mesh,
        in_specs=placed,
        out_specs=(
            P("gx", "gy", None, None, None, None, None),
            P(None, None, "gx", "gy", None),
            P(),
            P(),
            P(),
            P(),
        ),
        check_vma=False,
    )
```

```python
import functools
import math

import jax
import jax.numpy as jnp
from jax import lax
from jax.experimental import pallas as pl
from jax.experimental.pallas import tpu as pltpu
from jax.sharding import PartitionSpec as P

GRIDC = 4
F32 = jnp.float32
BF16 = jnp.bfloat16
MIB = 1024 * 1024
STACK = 10
GELU_C = math.sqrt(2.0 / math.pi)
GELU_A = 0.044715


def dot(a, b, ca, cb):
    return lax.dot_general(a, b, (((ca,), (cb,)), ((), ())), preferred_element_type=F32)


def sides():
    return lax.axis_index("gx") % 2, lax.axis_index("gy") % 2


def write_pieces(row, s, Y, near, far, first, second):
    p, q = sides()
    for k, (x, plane) in enumerate(((1 - p, near), (p, far))):
        for y in range(Y):
            plane[s, y] = row(x, y)
        first[k, s] = row(x, (1 - q) * (Y - 1))
        second[k, s] = row(x, q * (Y - 1))


def piece_shapes(S, Y, C, Z):
    return [jax.ShapeDtypeStruct((S, Y, C, Z), BF16)] * 2 + [
        jax.ShapeDtypeStruct((2, S, C, Z), BF16)
    ] * 2


def params(mib):
    return pltpu.CompilerParams(vmem_limit_bytes=mib * MIB)


def in_vmem(n):
    return [pl.BlockSpec(memory_space=pltpu.VMEM)] * n


def swap_pairs(n, start):
    return [pair for i in range(start, n - 1, 2) for pair in ((i, i + 1), (i + 1, i))]


def swap_x(plane, start):
    return lax.ppermute(plane, "gx", swap_pairs(lax.axis_size("gx"), start))


def swap_y(rows, start):
    return lax.ppermute(rows, "gy", swap_pairs(lax.axis_size("gy"), start))


def halo_by_corners(pieces):
    near, far, first, second = pieces
    from_near, from_far = swap_x(near, 0), swap_x(far, 1)
    first, second = swap_y(first, 0), swap_y(second, 1)
    corner_far = swap_x(jnp.stack([first[1], second[1]]), 1)
    corner_near = swap_x(jnp.stack([first[0], second[0]]), 0)
    return [near, far, from_near, from_far, first, second, corner_near, corner_far]


def halo_by_planes(pieces):
    near, far, first, second = pieces
    from_near, from_far = swap_x(near, 0), swap_x(far, 1)
    _, q = sides()
    Y = near.shape[1]
    got = []
    for own, y, start in ((first, (1 - q) * (Y - 1), 0), (second, q * (Y - 1), 1)):
        rows = [
            lax.dynamic_index_in_dim(plane, y, 1, keepdims=False) for plane in (from_near, from_far)
        ]
        got.append(swap_y(jnp.concatenate([own, jnp.stack(rows)]), start))
    return [near, far, from_near, from_far, *got]


def fill_padded(planes, rims, s, Fs):
    p, q = sides()
    Y = planes[0].shape[1]
    places = (2 - p, 1 + p, 3 * (1 - p), 3 * p)
    for x, plane, ((r0, k0), (r1, k1)) in zip(places, planes, rims):
        for y in range(Y):
            Fs[x * (Y + 2) + y + 1] = plane[s, y].astype(Fs.dtype)
        Fs[x * (Y + 2) + (1 - q) * (Y + 1)] = r0[k0, s].astype(Fs.dtype)
        Fs[x * (Y + 2) + q * (Y + 1)] = r1[k1, s].astype(Fs.dtype)


def fill_stack(Fs, FB, Y):
    C, Z = Fs.shape[1:]
    for a in range(3):
        for b in range(3):
            at = (a * 3 + b) * C
            for x in range(2):
                for y in range(Y):
                    r = x * Y + y
                    row = Fs[(x + a) * (Y + 2) + y + b].astype(BF16)
                    FB[at : at + C, r * Z : (r + 1) * Z] = row
    if FB.shape[0] > 9 * C:
        FB[9 * C :, :] = jnp.zeros((FB.shape[0] - 9 * C, FB.shape[1]), BF16)


def from_left(value, lane):
    return jnp.where(lane == 0, 0.0, pltpu.roll(value, 1, 1))


def from_right(value, lane):
    Z = value.shape[1]
    return jnp.where(lane == Z - 1, 0.0, pltpu.roll(value, Z - 1, 1))


def conv_rows(taps, stack, C, Z, lane):
    acc = dot(taps, stack, 1, 0)
    rows = []
    for k in range(0, stack.shape[1], Z):
        left, mid, right = (acc[e * C : (e + 1) * C, k : k + Z] for e in range(3))
        rows.append(mid + from_left(left, lane) + from_right(right, lane))
    return rows


def conv_tiles(wb, Fs, Ds, rows, Y, lane):
    C, Z = Fs.shape[1:]
    for c in range(0, C, 8):
        weights = [wb[t, c : c + 8, :] for t in range(27)]
        for r in rows:
            x, y = divmod(r, Y)
            acc = [None, None, None]
            for a in range(3):
                for b in range(3):
                    f = Fs[(x + a) * (Y + 2) + y + b, c : c + 8, :]
                    for e in range(3):
                        term = weights[(a * 3 + b) * 3 + e] * f
                        acc[e] = term if acc[e] is None else acc[e] + term
            total = acc[1] + from_left(acc[0], lane[:8]) + from_right(acc[2], lane[:8])
            Ds[c : c + 8, r * Z : (r + 1) * Z] = total


def split_kernel(X, Y, C, Z, f_ref, near, far, first, second, wide):
    wide[...] = f_ref[0].astype(F32)

    def row(x, y):
        return wide[pl.ds(x * Y + y, C, stride=X * Y), :].astype(BF16)

    write_pieces(row, pl.program_id(0), Y, near, far, first, second)


def z_permutation(Z):
    fine = lax.broadcasted_iota(jnp.int32, (2 * Z, 2 * Z), 0)
    coarse = lax.broadcasted_iota(jnp.int32, (2 * Z, 2 * Z), 1)
    inner = coarse % Z
    goes = coarse // Z + (inner % (Z // 2)) * 2 + (inner // (Z // 2)) * Z
    return jnp.where(fine == goes, 1.0, 0.0).astype(BF16)


def early_kernel(dims, gd_ref, w_ref, wd_ref, gm_ref, wb, flip_ref, Mb):
    X, Y, C, Z, H, O = dims
    NP = Y // 4
    step = pl.program_id(0)

    @pl.when(step == 0)
    def _():
        row = lax.broadcasted_iota(jnp.int32, (C, STACK * C), 0)
        column = lax.broadcasted_iota(jnp.int32, (C, STACK * C), 1)
        for e in range(3):
            block = jnp.zeros((C, STACK * C), F32)
            for ab in range(9):
                t = 26 - (ab * 3 + e)
                block = jnp.where(column == row + ab * C, w_ref[:, t : t + 1], block)
            flip_ref[e * C : (e + 1) * C, :] = block.astype(BF16)
        for t in range(27):
            wb[t] = jnp.broadcast_to(w_ref[:, t : t + 1], (C, Z))

    perm = z_permutation(Z)
    for X0 in range(X // 2):
        gp = dot(wd_ref[...], gd_ref[step, X0], 1, 1).astype(BF16)
        for a in range(2):
            for b in range(2):
                for p in range(NP):
                    src = ((a * 2 + b) * 2) * C
                    dst = ((a * 2 + b) * NP + p) * C
                    for e in range(2):
                        Mb[dst : dst + C, e * Z : (e + 1) * Z] = gp[
                            src + e * C : src + (e + 1) * C, p * Z : (p + 1) * Z
                        ]
        gm = dot(Mb[...], perm, 1, 1).astype(BF16)
        for a in range(2):
            for b in range(2):
                for p in range(NP):
                    src = ((a * 2 + b) * NP + p) * C
                    for q in range(2):
                        x, y = 2 * X0 + a, 2 * (2 * p + q) + b
                        gm_ref[step, x, y] = gm[src : src + C, q * Z : (q + 1) * Z]


def main_kernel(dims, *refs):
    X, Y, C, Z, H, O = dims
    hx, NP = X // 2, Y // 4
    cells = X * Y * Z
    quarter = (Y // 2) * (Z // 2)
    planes, (first, second, corner_near, corner_far) = refs[:4], refs[4:8]
    rims = [((first, k), (second, k)) for k in range(2)]
    rims += [((corner, 0), (corner, 1)) for corner in (corner_near, corner_far)]
    gd_ref, gm_ref, wb, pinT_ref, pout_ref, wd_ref, red_ref = refs[8:15]
    pieces, packed_ref = refs[15:19], refs[19]
    Fs, FB, Ds, Mb, Pt, G1, Gs, atap, adown, aout, ain, pin, poutT = refs[20:33]
    pre_s, ga_s, act_s, gp_s, rows_s = refs[33:]
    step = pl.program_id(0)

    @pl.when(step == 0)
    def _():
        atap[...] = jnp.zeros_like(atap)
        Gs[3 * C :, :] = jnp.zeros((C, Gs.shape[1]), BF16)
        adown[...] = jnp.zeros_like(adown)
        aout[...] = jnp.zeros_like(aout)
        ain[...] = jnp.zeros_like(ain)
        pin[...] = pinT_ref[...].astype(F32).T.astype(BF16)
        poutT[...] = pout_ref[...].astype(F32).T.astype(BF16)

    fill_padded(planes, rims, step, Fs)
    fill_stack(Fs, FB, Y)
    lane = lax.broadcasted_iota(jnp.int32, (C, Z), 1)
    perm = z_permutation(Z)

    chunks = [[(x, 4 * p + j) for j in range(4)] for x in range(X) for p in range(NP)]

    def columns(i):
        return slice(4 * i * Z, 4 * (i + 1) * Z)

    def convolve(i):
        first = 4 * i
        conv_tiles(wb, Fs, Ds, range(first, first + 4), Y, lane)

    def enter(i):
        gm = jnp.concatenate([gm_ref[step, x, y] for x, y in chunks[i]], axis=1)
        pre_s[i] = dot(pin[...], Ds[:, columns(i)].astype(BF16), 1, 0)
        ga_s[i] = dot(poutT[...], gm, 1, 0)

    def activate(i):
        for h0 in range(0, H, 16):
            hs = slice(h0, h0 + 16)
            pre = pre_s[i, hs, :]
            sq = pre * pre
            t = jnp.tanh(pre * (GELU_C + (GELU_C * GELU_A) * sq))
            h = 0.5 + 0.5 * t
            act = pre * h
            slope = h + act * (1.0 - h) * (2.0 * GELU_C + (6.0 * GELU_C * GELU_A) * sq)
            act_s[i, hs, :] = act.astype(BF16)
            gp_s[i, hs, :] = (ga_s[i, hs, :] * slope).astype(BF16)

    def leave(i):
        grad_depth = dot(pinT_ref[...], gp_s[i], 1, 0).astype(BF16)
        branch = dot(pout_ref[...], act_s[i], 1, 0)
        for j, (x, y) in enumerate(chunks[i]):
            r = x * Y + y
            row = Fs[(x + 1) * (Y + 2) + y + 1]
            merged = (row + branch[:, j * Z : (j + 1) * Z]).astype(BF16)
            start = ((x * 2 + y % 2) * NP + y // 4) * C
            q = y // 2 % 2
            Mb[start : start + C, q * Z : (q + 1) * Z] = merged
            G1[r] = grad_depth[:, j * Z : (j + 1) * Z]
            g = G1[r].astype(F32)
            for e, value in enumerate((from_right(g, lane), g, from_left(g, lane))):
                Gs[e * C : (e + 1) * C, r * Z : (r + 1) * Z] = value.astype(BF16)
        gm = jnp.concatenate([gm_ref[step, x, y] for x, y in chunks[i]], axis=1)
        aout[...] += dot(gm, act_s[i], 1, 1)
        ain[...] += dot(Ds[:, columns(i)].astype(BF16), gp_s[i], 1, 1)
        atap[...] += dot(FB[:, columns(i)], Gs[:, columns(i)], 1, 1)

    last = len(chunks) - 1
    convolve(0)
    enter(0)
    convolve(1)
    activate(0)
    for i in range(last + 1):
        if i < last:
            enter(i + 1)
        leave(i)
        if i + 2 <= last:
            convolve(i + 2)
        if i < last:
            activate(i + 1)

    for X0 in range(hx):
        pt = dot(Mb[...], perm, 1, 0).astype(BF16)
        for a in range(2):
            for b in range(2):
                for p in range(NP):
                    src = ((a * 2 + b) * NP + p) * C
                    for e in range(2):
                        dst = ((a * 2 + b) * 2 + e) * C
                        Pt[dst : dst + C, p * Z : (p + 1) * Z] = pt[
                            src : src + C, e * Z : (e + 1) * Z
                        ]
        red_ref[step, X0] = dot(Pt[...], wd_ref[...], 0, 0).astype(BF16)
        adown[...] += dot(Pt[...], gd_ref[step, X0], 1, 0)

    write_pieces(lambda x, y: G1[x * Y + y], step, Y, *pieces)

    @pl.when(step == pl.num_programs(0) - 1)
    def _():
        rows_s[...] = jnp.zeros_like(rows_s)
        for k in range(8):
            rows_s[pl.ds(k, C, stride=8), :] = adown[k * C : (k + 1) * C, :]
        row = lax.broadcasted_iota(jnp.int32, (C, 4 * C), 0)
        column = lax.broadcasted_iota(jnp.int32, (C, 4 * C), 1)
        at = 8 * C + 2 * C * (H // Z)
        for ab in range(9):
            block = jnp.where(column % C == row, atap[ab * C : (ab + 1) * C, :], 0.0)
            line = jnp.sum(block, axis=0, keepdims=True)
            for k in range(0, 4 * C, Z):
                rows_s[at : at + 1, :] = line[:, k : k + Z]
                at += 1
        packed_ref[: rows_s.shape[0], :] = rows_s[...].astype(BF16)
        at = 8 * C
        for part in (aout, ain):
            for k in range(0, H, Z):
                packed_ref[at : at + C, :] = part[:, k : k + Z].astype(BF16)
                at += C
        at = rows_s.shape[0]
        if at < packed_ref.shape[0]:
            rest = packed_ref.shape[0] - at
            packed_ref[at:, :] = jnp.zeros((rest, Z), BF16)


def adjoint_kernel(X, Y, C, Z, *refs):
    planes, (first, second) = refs[:4], refs[4:6]
    gm_ref, tap_ref, out_ref, Fs, FB, wide = refs[6:]
    step = pl.program_id(0)
    fill_padded(planes, [((first, k), (second, k)) for k in range(4)], step, Fs)
    fill_stack(Fs, FB, Y)
    lane = lax.broadcasted_iota(jnp.int32, (C, Z), 1)
    for r0 in range(0, X * Y, 4):
        rows = conv_rows(tap_ref[...], FB[:, r0 * Z : (r0 + 4) * Z], C, Z, lane)
        for r, value in enumerate(rows, r0):
            total = value + gm_ref[step, r // Y, r % Y].astype(F32)
            wide[pl.ds(r, C, stride=X * Y), :] = total
    out_ref[0] = wide[...].astype(BF16)


def finish_kernel(C, Z, H, scale, every_ref, down_ref, out_ref, in_ref, taps_ref):
    down_ref[...] = every_ref[: 8 * C, :].astype(F32) * scale
    at = 8 * C
    for ref in (out_ref, in_ref):
        for k in range(0, H, Z):
            ref[:, k : k + Z] = every_ref[at : at + C, :].astype(F32) * scale
            at += C
    taps = every_ref[at : at + 32, :].astype(F32) * scale
    for a in range(3):
        for b in range(3):
            for e in range(3):
                line, k = divmod(e * C, Z)
                line += (a * 3 + b) * (4 * C // Z)
                taps_ref[a, b, e : e + 1, :] = taps[line : line + 1, k : k + C]


def sum_spread_kernel(parts_ref, out_ref):
    total = parts_ref[0].astype(F32)
    for i in range(1, parts_ref.shape[0]):
        total = total + parts_ref[i].astype(F32)
    total = total.astype(BF16)
    for j in range(out_ref.shape[0]):
        out_ref[j] = total


def sum_spread(parts, receivers):
    shape = (receivers,) + parts.shape[1:]
    return pl.pallas_call(
        sum_spread_kernel,
        in_specs=in_vmem(1),
        out_specs=in_vmem(1)[0],
        out_shape=jax.ShapeDtypeStruct(shape, BF16),
        compiler_params=params(4),
        name="sum_spread",
    )(parts)


def swap_in_group(blocks, axis):
    g = blocks.shape[0]
    if g == 1:
        return blocks
    n = lax.axis_size(axis)
    member = lax.axis_index(axis) % g
    got = [lax.dynamic_index_in_dim(blocks, member, 0, keepdims=False)]
    for k in range(1, g):
        out = lax.dynamic_index_in_dim(blocks, (member + k) % g, 0, keepdims=False)
        pairs = [(i, i - i % g + (i + k) % g) for i in range(n)]
        got.append(lax.ppermute(out, axis, pairs))
    if g == 2:
        first = member == 0
        return jnp.stack([jnp.where(first, got[0], got[1]), jnp.where(first, got[1], got[0])])
    got = jnp.stack(got)
    return jnp.take(got, (member - jnp.arange(g, dtype=jnp.int32)) % g, axis=0)


def per_device(fields, depth_kernel, point_in, point_out, down_kernel, cotangent):
    S, C, X, Y, Z = fields.shape
    assert X == 2 and Y % 4 == 0
    H, O = point_in.shape[0], down_kernel.shape[0]
    hx, hy, hz = X // 2, Y // 2, Z // 2
    nx, ny = lax.axis_size("gx"), lax.axis_size("gy")
    devices = nx * ny
    gx, gy = nx // GRIDC, ny // GRIDC
    per_group = S // (gx * gy)

    pieces = pl.pallas_call(
        functools.partial(split_kernel, X, Y, C, Z),
        grid=(S,),
        in_specs=[pl.BlockSpec((1, C * X * Y, Z), lambda s: (s, 0, 0))],
        out_specs=in_vmem(4),
        out_shape=piece_shapes(S, Y, C, Z),
        scratch_shapes=[pltpu.VMEM((C * X * Y, Z), F32)],
        compiler_params=params(6),
        name="split_fields",
    )(fields.reshape(S, C * X * Y, Z))


    moved = cotangent[0, 0].transpose(0, 2, 3, 4, 1)
    moved = moved.reshape(per_group, gx * hx, gy, hy * hz, O).transpose(2, 0, 1, 3, 4)
    moved = swap_in_group(moved, "gy").reshape(gy * per_group, gx, hx, hy * hz, O)
    moved = swap_in_group(moved.transpose(1, 0, 2, 3, 4), "gx")
    grad_down = moved.reshape(S, hx, hy * hz, O)

    widened = halo_by_corners(pieces)

    wd = down_kernel.transpose(2, 3, 4, 1, 0).reshape(8 * C, O)
    taps = depth_kernel.reshape(C, 27).astype(F32)

    rows = 8 * C + 2 * C * (H // Z) + 32
    chunk = -(-rows // (8 * nx)) * 8
    cells = X * Y * Z
    flops = S * cells * (2 * 6 * C * H + 2 * 3 * C * O + 2 * 2 * 27 * C)
    dims = (X, Y, C, Z, H, O)
    grad_merged, spread, flip_matrix = pl.pallas_call(
        functools.partial(early_kernel, dims),
        grid=(S,),
        in_specs=in_vmem(3),
        out_specs=in_vmem(3),
        out_shape=[
            jax.ShapeDtypeStruct((S, X, Y, C, Z), BF16),
            jax.ShapeDtypeStruct((27, C, Z), F32),
            jax.ShapeDtypeStruct((3 * C, STACK * C), BF16),
        ],
        scratch_shapes=[pltpu.VMEM((Y * C, 2 * Z), BF16)],
        compiler_params=params(8),
        cost_estimate=pl.CostEstimate(
            flops=S * cells * (2 * C * O + 8 * C * Z),
            bytes_accessed=4 * S * cells * C + 4 * 27 * C * Z,
            transcendentals=0,
        ),
        name="early",
    )(grad_down, taps, wd)

    out = pl.pallas_call(
        functools.partial(main_kernel, dims),
        grid=(S,),
        in_specs=in_vmem(14),
        out_specs=in_vmem(6),
        out_shape=[jax.ShapeDtypeStruct((S, hx, hy * hz, O), BF16)]
        + piece_shapes(S, Y, C, Z)
        + [jax.ShapeDtypeStruct((nx * chunk, Z), BF16)],
        scratch_shapes=[
            pltpu.VMEM(((X + 2) * (Y + 2), C, Z), F32),
            pltpu.VMEM((9 * C, cells), BF16),
            pltpu.VMEM((C, cells), F32),
            pltpu.VMEM((Y * C, 2 * Z), BF16),
            pltpu.VMEM((8 * C, hy * hz), BF16),
            pltpu.VMEM((X * Y, C, Z), BF16),
            pltpu.VMEM((4 * C, cells), BF16),
            pltpu.VMEM((9 * C, 4 * C), F32),
            pltpu.VMEM((8 * C, O), F32),
            pltpu.VMEM((C, H), F32),
            pltpu.VMEM((C, H), F32),
            pltpu.VMEM((H, C), BF16),
            pltpu.VMEM((H, C), BF16),
            pltpu.VMEM((Y // 2, H, 4 * Z), F32),
            pltpu.VMEM((Y // 2, H, 4 * Z), F32),
            pltpu.VMEM((Y // 2, H, 4 * Z), BF16),
            pltpu.VMEM((Y // 2, H, 4 * Z), BF16),
            pltpu.VMEM((rows, Z), F32),
        ],
        compiler_params=params(24),
        cost_estimate=pl.CostEstimate(
            flops=flops, bytes_accessed=8 * S * cells * C, transcendentals=S * cells * H
        ),
        name="main",
    )(*widened, grad_down, grad_merged, spread, point_in.T, point_out, wd)
    reduced, grad_pieces, packed = out[0], out[1:5], out[5]

    grad_widened = halo_by_planes(grad_pieces)

    parts = lax.all_to_all(packed.reshape(nx, chunk, Z), "gx", 0, 0)
    parts = lax.all_to_all(sum_spread(parts, ny), "gy", 0, 0)
    share = sum_spread(parts, nx)
    share, grad_widened[0] = lax.optimization_barrier((share, grad_widened[0]))
    every = lax.all_to_all(share, "gx", 0, 0).reshape(nx * chunk, Z)

    grad_fields = pl.pallas_call(
        functools.partial(adjoint_kernel, X, Y, C, Z),
        grid=(S,),
        in_specs=in_vmem(8),
        out_specs=pl.BlockSpec((1, C * X * Y, Z), lambda s: (s, 0, 0)),
        out_shape=jax.ShapeDtypeStruct((S, C * X * Y, Z), BF16),
        scratch_shapes=[
            pltpu.VMEM(((X + 2) * (Y + 2), C, Z), BF16),
            pltpu.VMEM((STACK * C, cells), BF16),
            pltpu.VMEM((C * X * Y, Z), F32),
        ],
        compiler_params=params(14),
        cost_estimate=pl.CostEstimate(
            flops=S * cells * 2 * 27 * C, bytes_accessed=8 * S * cells * C, transcendentals=0
        ),
        name="adjoint",
    )(*grad_widened, grad_merged, flip_matrix).reshape(S, C, X, Y, Z)

    moved = swap_in_group(reduced.reshape(gx, S // gx, hx, hy * hz, O), "gx")
    moved = moved.transpose(1, 0, 2, 3, 4).reshape(gy, per_group, gx * hx, hy * hz, O)
    moved = swap_in_group(moved, "gy").transpose(1, 2, 0, 3, 4)
    coarse = moved.reshape(per_group, gx * hx, gy * hy, hz, O).transpose(0, 4, 1, 2, 3)[None, None]

    scale = 1.0 / math.sqrt(S * cells * devices)
    down, outw, inw, tapw = pl.pallas_call(
        functools.partial(finish_kernel, C, Z, H, scale),
        out_shape=[
            jax.ShapeDtypeStruct((8 * C, O), F32),
            jax.ShapeDtypeStruct((C, H), F32),
            jax.ShapeDtypeStruct((C, H), F32),
            jax.ShapeDtypeStruct((3, 3, 3, C), F32),
        ],
        in_specs=in_vmem(1),
        compiler_params=params(6),
        name="finish",
    )(every)
    return (
        coarse,
        grad_fields,
        tapw.transpose(3, 0, 1, 2),
        inw.T,
        outw,
        down.reshape(C, 2, 2, 2, O).transpose(4, 0, 1, 2, 3),
    )


def solution(mesh):
    placed = (
        P(None, None, "gx", "gy", None),
        P(),
        P(),
        P(),
        P(),
        P("gx", "gy", None, None, None, None, None),
    )
    return jax.shard_map(
        per_device,
        mesh=mesh,
        in_specs=placed,
        out_specs=(
            P("gx", "gy", None, None, None, None, None),
            P(None, None, "gx", "gy", None),
            P(),
            P(),
            P(),
            P(),
        ),
        check_vma=False,
    )
```

```python
import functools
import math

import jax
import jax.numpy as jnp
from jax import lax
from jax.experimental import pallas as pl
from jax.experimental.pallas import tpu as pltpu
from jax.sharding import PartitionSpec as P

GRIDC = 4
F32 = jnp.float32
BF16 = jnp.bfloat16
MIB = 1024 * 1024
STACK = 10
GELU_C = math.sqrt(2.0 / math.pi)
GELU_A = 0.044715


def dot(a, b, ca, cb):
    return lax.dot_general(a, b, (((ca,), (cb,)), ((), ())), preferred_element_type=F32)


def sides():
    return lax.axis_index("gx") % 2, lax.axis_index("gy") % 2


def write_pieces(row, s, Y, near, far, first, second):
    p, q = sides()
    for k, (x, plane) in enumerate(((1 - p, near), (p, far))):
        for y in range(Y):
            plane[s, y] = row(x, y)
        first[k, s] = row(x, (1 - q) * (Y - 1))
        second[k, s] = row(x, q * (Y - 1))


def piece_shapes(S, Y, C, Z):
    return [jax.ShapeDtypeStruct((S, Y, C, Z), BF16)] * 2 + [
        jax.ShapeDtypeStruct((2, S, C, Z), BF16)
    ] * 2


def params(mib):
    return pltpu.CompilerParams(vmem_limit_bytes=mib * MIB)


def in_vmem(n):
    return [pl.BlockSpec(memory_space=pltpu.VMEM)] * n


def swap_pairs(n, start):
    return [pair for i in range(start, n - 1, 2) for pair in ((i, i + 1), (i + 1, i))]


def swap_x(plane, start):
    return lax.ppermute(plane, "gx", swap_pairs(lax.axis_size("gx"), start))


def swap_y(rows, start):
    return lax.ppermute(rows, "gy", swap_pairs(lax.axis_size("gy"), start))


def halo_by_corners(pieces):
    near, far, first, second = pieces
    from_near, from_far = swap_x(near, 0), swap_x(far, 1)
    first, second = swap_y(first, 0), swap_y(second, 1)
    corner_far = swap_x(jnp.stack([first[1], second[1]]), 1)
    corner_near = swap_x(jnp.stack([first[0], second[0]]), 0)
    return [near, far, from_near, from_far, first, second, corner_near, corner_far]


def halo_by_planes(pieces):
    near, far, first, second = pieces
    from_near, from_far = swap_x(near, 0), swap_x(far, 1)
    _, q = sides()
    Y = near.shape[1]
    got = []
    for own, y, start in ((first, (1 - q) * (Y - 1), 0), (second, q * (Y - 1), 1)):
        rows = [
            lax.dynamic_index_in_dim(plane, y, 1, keepdims=False) for plane in (from_near, from_far)
        ]
        got.append(swap_y(jnp.concatenate([own, jnp.stack(rows)]), start))
    return [near, far, from_near, from_far, *got]


def fill_padded(planes, rims, s, Fs):
    p, q = sides()
    Y = planes[0].shape[1]
    places = (2 - p, 1 + p, 3 * (1 - p), 3 * p)
    for x, plane, ((r0, k0), (r1, k1)) in zip(places, planes, rims):
        for y in range(Y):
            Fs[x * (Y + 2) + y + 1] = plane[s, y].astype(Fs.dtype)
        Fs[x * (Y + 2) + (1 - q) * (Y + 1)] = r0[k0, s].astype(Fs.dtype)
        Fs[x * (Y + 2) + q * (Y + 1)] = r1[k1, s].astype(Fs.dtype)


def fill_stack(Fs, FB, Y):
    C, Z = Fs.shape[1:]
    for a in range(3):
        for b in range(3):
            at = (a * 3 + b) * C
            for x in range(2):
                for y in range(Y):
                    r = x * Y + y
                    row = Fs[(x + a) * (Y + 2) + y + b].astype(BF16)
                    FB[at : at + C, r * Z : (r + 1) * Z] = row
    if FB.shape[0] > 9 * C:
        FB[9 * C :, :] = jnp.zeros((FB.shape[0] - 9 * C, FB.shape[1]), BF16)


def from_left(value, lane):
    return jnp.where(lane == 0, 0.0, pltpu.roll(value, 1, 1))


def from_right(value, lane):
    Z = value.shape[1]
    return jnp.where(lane == Z - 1, 0.0, pltpu.roll(value, Z - 1, 1))


def conv_rows(taps, stack, C, Z, lane):
    acc = dot(taps, stack, 1, 0)
    rows = []
    for k in range(0, stack.shape[1], Z):
        left, mid, right = (acc[e * C : (e + 1) * C, k : k + Z] for e in range(3))
        rows.append(mid + from_left(left, lane) + from_right(right, lane))
    return rows


def conv_tiles(wb, Fs, Ds, rows, Y, lane):
    C, Z = Fs.shape[1:]
    for c in range(0, C, 8):
        weights = [wb[t, c : c + 8, :] for t in range(27)]
        for r in rows:
            x, y = divmod(r, Y)
            acc = [None, None, None]
            for a in range(3):
                for b in range(3):
                    f = Fs[(x + a) * (Y + 2) + y + b, c : c + 8, :]
                    for e in range(3):
                        term = weights[(a * 3 + b) * 3 + e] * f
                        acc[e] = term if acc[e] is None else acc[e] + term
            total = acc[1] + from_left(acc[0], lane[:8]) + from_right(acc[2], lane[:8])
            Ds[c : c + 8, r * Z : (r + 1) * Z] = total


def split_kernel(X, Y, C, Z, f_ref, near, far, first, second, raw, wide, arrived):
    S = near.shape[0]
    part = raw.shape[2]
    copies = [
        [
            pltpu.make_async_copy(
                f_ref.at[s, pl.ds(k * part, part)], raw.at[s, k], arrived.at[2 * s + k]
            )
            for k in range(2)
        ]
        for s in range(S)
    ]
    for s in range(S):
        for copy in copies[s]:
            copy.start()
    for s in range(S):
        for k in range(2):
            copies[s][k].wait()
            wide[k * part : (k + 1) * part, :] = raw[s, k].astype(F32)

        def row(x, y):
            return wide[pl.ds(x * Y + y, C, stride=X * Y), :].astype(BF16)

        write_pieces(row, s, Y, near, far, first, second)


def z_permutation(Z):
    fine = lax.broadcasted_iota(jnp.int32, (2 * Z, 2 * Z), 0)
    coarse = lax.broadcasted_iota(jnp.int32, (2 * Z, 2 * Z), 1)
    inner = coarse % Z
    goes = coarse // Z + (inner % (Z // 2)) * 2 + (inner // (Z // 2)) * Z
    return jnp.where(fine == goes, 1.0, 0.0).astype(BF16)


def early_kernel(dims, gd_ref, w_ref, wd_ref, gm_ref, wb, flip_ref, Mb):
    X, Y, C, Z, H, O = dims
    NP = Y // 4
    step = pl.program_id(0)

    @pl.when(step == 0)
    def _():
        row = lax.broadcasted_iota(jnp.int32, (C, STACK * C), 0)
        column = lax.broadcasted_iota(jnp.int32, (C, STACK * C), 1)
        for e in range(3):
            block = jnp.zeros((C, STACK * C), F32)
            for ab in range(9):
                t = 26 - (ab * 3 + e)
                block = jnp.where(column == row + ab * C, w_ref[:, t : t + 1], block)
            flip_ref[e * C : (e + 1) * C, :] = block.astype(BF16)
        for t in range(27):
            wb[t] = jnp.broadcast_to(w_ref[:, t : t + 1], (C, Z))

    perm = z_permutation(Z)
    for X0 in range(X // 2):
        gp = dot(wd_ref[...], gd_ref[step, X0], 1, 1).astype(BF16)
        for a in range(2):
            for b in range(2):
                for p in range(NP):
                    src = ((a * 2 + b) * 2) * C
                    dst = ((a * 2 + b) * NP + p) * C
                    for e in range(2):
                        Mb[dst : dst + C, e * Z : (e + 1) * Z] = gp[
                            src + e * C : src + (e + 1) * C, p * Z : (p + 1) * Z
                        ]
        gm = dot(Mb[...], perm, 1, 1).astype(BF16)
        for a in range(2):
            for b in range(2):
                for p in range(NP):
                    src = ((a * 2 + b) * NP + p) * C
                    for q in range(2):
                        x, y = 2 * X0 + a, 2 * (2 * p + q) + b
                        gm_ref[step, x, y] = gm[src : src + C, q * Z : (q + 1) * Z]


def main_kernel(dims, *refs):
    X, Y, C, Z, H, O = dims
    hx, NP = X // 2, Y // 4
    cells = X * Y * Z
    quarter = (Y // 2) * (Z // 2)
    planes, (first, second, corner_near, corner_far) = refs[:4], refs[4:8]
    rims = [((first, k), (second, k)) for k in range(2)]
    rims += [((corner, 0), (corner, 1)) for corner in (corner_near, corner_far)]
    gd_ref, gm_ref, wb, pinT_ref, pout_ref, wd_ref, red_ref = refs[8:15]
    pieces, kept_ref, given_ref = refs[15:19], refs[19], refs[20]
    Fs, FB, Ds, Mb, Pt, G1, Gs, atap, adown, aout, ain, pin, poutT = refs[21:34]
    pre_s, ga_s, act_s, gp_s, rows_s, packed = refs[34:]
    step = pl.program_id(0)

    @pl.when(step == 0)
    def _():
        atap[...] = jnp.zeros_like(atap)
        Gs[3 * C :, :] = jnp.zeros((C, Gs.shape[1]), BF16)
        adown[...] = jnp.zeros_like(adown)
        aout[...] = jnp.zeros_like(aout)
        ain[...] = jnp.zeros_like(ain)
        pin[...] = pinT_ref[...].astype(F32).T.astype(BF16)
        poutT[...] = pout_ref[...].astype(F32).T.astype(BF16)

    fill_padded(planes, rims, step, Fs)
    fill_stack(Fs, FB, Y)
    lane = lax.broadcasted_iota(jnp.int32, (C, Z), 1)
    perm = z_permutation(Z)

    chunks = [[(x, 4 * p + j) for j in range(4)] for x in range(X) for p in range(NP)]

    def columns(i):
        return slice(4 * i * Z, 4 * (i + 1) * Z)

    def convolve(i):
        first = 4 * i
        conv_tiles(wb, Fs, Ds, range(first, first + 4), Y, lane)

    def enter(i):
        gm = jnp.concatenate([gm_ref[step, x, y] for x, y in chunks[i]], axis=1)
        pre_s[i] = dot(pin[...], Ds[:, columns(i)].astype(BF16), 1, 0)
        ga_s[i] = dot(poutT[...], gm, 1, 0)

    def activate(i):
        for h0 in range(0, H, 16):
            hs = slice(h0, h0 + 16)
            pre = pre_s[i, hs, :]
            sq = pre * pre
            t = jnp.tanh(pre * (GELU_C + (GELU_C * GELU_A) * sq))
            h = 0.5 + 0.5 * t
            act = pre * h
            slope = h + act * (1.0 - h) * (2.0 * GELU_C + (6.0 * GELU_C * GELU_A) * sq)
            act_s[i, hs, :] = act.astype(BF16)
            gp_s[i, hs, :] = (ga_s[i, hs, :] * slope).astype(BF16)

    def leave(i):
        grad_depth = dot(pinT_ref[...], gp_s[i], 1, 0).astype(BF16)
        branch = dot(pout_ref[...], act_s[i], 1, 0)
        for j, (x, y) in enumerate(chunks[i]):
            r = x * Y + y
            row = Fs[(x + 1) * (Y + 2) + y + 1]
            merged = (row + branch[:, j * Z : (j + 1) * Z]).astype(BF16)
            start = ((x * 2 + y % 2) * NP + y // 4) * C
            q = y // 2 % 2
            Mb[start : start + C, q * Z : (q + 1) * Z] = merged
            G1[r] = grad_depth[:, j * Z : (j + 1) * Z]
            g = G1[r].astype(F32)
            for e, value in enumerate((from_right(g, lane), g, from_left(g, lane))):
                Gs[e * C : (e + 1) * C, r * Z : (r + 1) * Z] = value.astype(BF16)
        gm = jnp.concatenate([gm_ref[step, x, y] for x, y in chunks[i]], axis=1)
        aout[...] += dot(gm, act_s[i], 1, 1)
        ain[...] += dot(Ds[:, columns(i)].astype(BF16), gp_s[i], 1, 1)
        atap[...] += dot(FB[:, columns(i)], Gs[:, columns(i)], 1, 1)

    last = len(chunks) - 1
    convolve(0)
    enter(0)
    convolve(1)
    activate(0)
    for i in range(last + 1):
        if i < last:
            enter(i + 1)
        leave(i)
        if i + 2 <= last:
            convolve(i + 2)
        if i < last:
            activate(i + 1)

    for X0 in range(hx):
        pt = dot(Mb[...], perm, 1, 0).astype(BF16)
        for a in range(2):
            for b in range(2):
                for p in range(NP):
                    src = ((a * 2 + b) * NP + p) * C
                    for e in range(2):
                        dst = ((a * 2 + b) * 2 + e) * C
                        Pt[dst : dst + C, p * Z : (p + 1) * Z] = pt[
                            src : src + C, e * Z : (e + 1) * Z
                        ]
        red_ref[step, X0] = dot(Pt[...], wd_ref[...], 0, 0).astype(BF16)
        adown[...] += dot(Pt[...], gd_ref[step, X0], 1, 0)

    write_pieces(lambda x, y: G1[x * Y + y], step, Y, *pieces)

    @pl.when(step == pl.num_programs(0) - 1)
    def _():
        rows_s[...] = jnp.zeros_like(rows_s)
        for k in range(8):
            rows_s[pl.ds(k, C, stride=8), :] = adown[k * C : (k + 1) * C, :]
        row = lax.broadcasted_iota(jnp.int32, (C, 4 * C), 0)
        column = lax.broadcasted_iota(jnp.int32, (C, 4 * C), 1)
        at = 8 * C + 2 * C * (H // Z)
        for ab in range(9):
            block = jnp.where(column % C == row, atap[ab * C : (ab + 1) * C, :], 0.0)
            line = jnp.sum(block, axis=0, keepdims=True)
            for k in range(0, 4 * C, Z):
                rows_s[at : at + 1, :] = line[:, k : k + Z]
                at += 1
        packed[: rows_s.shape[0], :] = rows_s[...].astype(BF16)
        at = 8 * C
        for part in (aout, ain):
            for k in range(0, H, Z):
                packed[at : at + C, :] = part[:, k : k + Z].astype(BF16)
                at += C
        at = rows_s.shape[0]
        if at < packed.shape[0]:
            packed[at:, :] = jnp.zeros((packed.shape[0] - at, Z), BF16)
        half = kept_ref.shape[0]
        mine, _ = sides()
        kept_ref[...] = packed[pl.ds(pl.multiple_of(mine * half, half), half), :]
        given_ref[...] = packed[pl.ds(pl.multiple_of((1 - mine) * half, half), half), :]


def adjoint_kernel(X, Y, C, Z, *refs):
    planes, (first, second) = refs[:4], refs[4:6]
    gm_ref, tap_ref, out_ref, Fs, FB, wide = refs[6:]
    step = pl.program_id(0)
    fill_padded(planes, [((first, k), (second, k)) for k in range(4)], step, Fs)
    fill_stack(Fs, FB, Y)
    lane = lax.broadcasted_iota(jnp.int32, (C, Z), 1)
    for r0 in range(0, X * Y, 4):
        rows = conv_rows(tap_ref[...], FB[:, r0 * Z : (r0 + 4) * Z], C, Z, lane)
        for r, value in enumerate(rows, r0):
            total = value + gm_ref[step, r // Y, r % Y].astype(F32)
            wide[pl.ds(r, C, stride=X * Y), :] = total
    out_ref[0] = wide[...].astype(BF16)


def finish_kernel(C, Z, H, scale, kept, got, down_ref, out_ref, in_ref, taps_ref, every_ref):
    half = kept.shape[0]
    mine, _ = sides()
    every_ref[pl.ds(pl.multiple_of(mine * half, half), half), :] = kept[...]
    every_ref[pl.ds(pl.multiple_of((1 - mine) * half, half), half), :] = got[...]
    down_ref[...] = every_ref[: 8 * C, :].astype(F32) * scale
    at = 8 * C
    for ref in (out_ref, in_ref):
        for k in range(0, H, Z):
            ref[:, k : k + Z] = every_ref[at : at + C, :].astype(F32) * scale
            at += C
    taps = every_ref[at : at + 32, :].astype(F32) * scale
    for a in range(3):
        for b in range(3):
            for e in range(3):
                line, k = divmod(e * C, Z)
                line += (a * 3 + b) * (4 * C // Z)
                taps_ref[a, b, e : e + 1, :] = taps[line : line + 1, k : k + C]


def add_kernel(kept, got, out_ref):
    out_ref[...] = (kept[...].astype(F32) + got[...].astype(F32)).astype(BF16)


def sum_spread_kernel(parts_ref, out_ref):
    total = parts_ref[0].astype(F32)
    for i in range(1, parts_ref.shape[0]):
        total = total + parts_ref[i].astype(F32)
    total = total.astype(BF16)
    for j in range(out_ref.shape[0]):
        out_ref[j] = total


def sum_spread(parts, receivers):
    shape = (receivers,) + parts.shape[1:]
    return pl.pallas_call(
        sum_spread_kernel,
        in_specs=in_vmem(1),
        out_specs=in_vmem(1)[0],
        out_shape=jax.ShapeDtypeStruct(shape, BF16),
        compiler_params=params(4),
        name="sum_spread",
    )(parts)


def swap_in_group(blocks, axis):
    g = blocks.shape[0]
    if g == 1:
        return blocks
    n = lax.axis_size(axis)
    member = lax.axis_index(axis) % g
    got = [lax.dynamic_index_in_dim(blocks, member, 0, keepdims=False)]
    for k in range(1, g):
        out = lax.dynamic_index_in_dim(blocks, (member + k) % g, 0, keepdims=False)
        pairs = [(i, i - i % g + (i + k) % g) for i in range(n)]
        got.append(lax.ppermute(out, axis, pairs))
    if g == 2:
        first = member == 0
        return jnp.stack([jnp.where(first, got[0], got[1]), jnp.where(first, got[1], got[0])])
    got = jnp.stack(got)
    return jnp.take(got, (member - jnp.arange(g, dtype=jnp.int32)) % g, axis=0)


def per_device(fields, depth_kernel, point_in, point_out, down_kernel, cotangent):
    S, C, X, Y, Z = fields.shape
    assert X == 2 and Y % 4 == 0
    H, O = point_in.shape[0], down_kernel.shape[0]
    hx, hy, hz = X // 2, Y // 2, Z // 2
    nx, ny = lax.axis_size("gx"), lax.axis_size("gy")
    devices = nx * ny
    gx, gy = nx // GRIDC, ny // GRIDC
    per_group = S // (gx * gy)

    pieces = pl.pallas_call(
        functools.partial(split_kernel, X, Y, C, Z),
        in_specs=[pl.BlockSpec(memory_space=pltpu.HBM)],
        out_specs=in_vmem(4),
        out_shape=piece_shapes(S, Y, C, Z),
        scratch_shapes=[
            pltpu.VMEM((S, 2, C * X * Y // 2, Z), BF16),
            pltpu.VMEM((C * X * Y, Z), F32),
            pltpu.SemaphoreType.DMA((2 * S,)),
        ],
        compiler_params=params(8),
        name="split_fields",
    )(fields.reshape(S, C * X * Y, Z))


    moved = cotangent[0, 0].transpose(0, 2, 3, 4, 1)
    moved = moved.reshape(per_group, gx * hx, gy, hy * hz, O).transpose(2, 0, 1, 3, 4)
    moved = swap_in_group(moved, "gy").reshape(gy * per_group, gx, hx, hy * hz, O)
    moved = swap_in_group(moved.transpose(1, 0, 2, 3, 4), "gx")
    grad_down = moved.reshape(S, hx, hy * hz, O)

    widened = halo_by_corners(pieces)

    wd = down_kernel.transpose(2, 3, 4, 1, 0).reshape(8 * C, O)
    taps = depth_kernel.reshape(C, 27).astype(F32)

    rows = 8 * C + 2 * C * (H // Z) + 32
    chunk = -(-rows // (8 * devices)) * 8
    half = chunk * devices // 2
    cells = X * Y * Z
    flops = S * cells * (2 * 6 * C * H + 2 * 3 * C * O + 2 * 2 * 27 * C)
    dims = (X, Y, C, Z, H, O)
    grad_merged, spread, flip_matrix = pl.pallas_call(
        functools.partial(early_kernel, dims),
        grid=(S,),
        in_specs=in_vmem(3),
        out_specs=in_vmem(3),
        out_shape=[
            jax.ShapeDtypeStruct((S, X, Y, C, Z), BF16),
            jax.ShapeDtypeStruct((27, C, Z), F32),
            jax.ShapeDtypeStruct((3 * C, STACK * C), BF16),
        ],
        scratch_shapes=[pltpu.VMEM((Y * C, 2 * Z), BF16)],
        compiler_params=params(8),
        cost_estimate=pl.CostEstimate(
            flops=S * cells * (2 * C * O + 8 * C * Z),
            bytes_accessed=4 * S * cells * C + 4 * 27 * C * Z,
            transcendentals=0,
        ),
        name="early",
    )(grad_down, taps, wd)

    out = pl.pallas_call(
        functools.partial(main_kernel, dims),
        grid=(S,),
        in_specs=in_vmem(14),
        out_specs=in_vmem(7),
        out_shape=[jax.ShapeDtypeStruct((S, hx, hy * hz, O), BF16)]
        + piece_shapes(S, Y, C, Z)
        + [jax.ShapeDtypeStruct((half, Z), BF16)] * 2,
        scratch_shapes=[
            pltpu.VMEM(((X + 2) * (Y + 2), C, Z), F32),
            pltpu.VMEM((9 * C, cells), BF16),
            pltpu.VMEM((C, cells), F32),
            pltpu.VMEM((Y * C, 2 * Z), BF16),
            pltpu.VMEM((8 * C, hy * hz), BF16),
            pltpu.VMEM((X * Y, C, Z), BF16),
            pltpu.VMEM((4 * C, cells), BF16),
            pltpu.VMEM((9 * C, 4 * C), F32),
            pltpu.VMEM((8 * C, O), F32),
            pltpu.VMEM((C, H), F32),
            pltpu.VMEM((C, H), F32),
            pltpu.VMEM((H, C), BF16),
            pltpu.VMEM((H, C), BF16),
            pltpu.VMEM((Y // 2, H, 4 * Z), F32),
            pltpu.VMEM((Y // 2, H, 4 * Z), F32),
            pltpu.VMEM((Y // 2, H, 4 * Z), BF16),
            pltpu.VMEM((Y // 2, H, 4 * Z), BF16),
            pltpu.VMEM((rows, Z), F32),
            pltpu.VMEM((2 * half, Z), BF16),
        ],
        compiler_params=params(24),
        cost_estimate=pl.CostEstimate(
            flops=flops, bytes_accessed=8 * S * cells * C, transcendentals=S * cells * H
        ),
        name="main",
    )(*widened, grad_down, grad_merged, spread, point_in.T, point_out, wd)
    reduced, grad_pieces, (kept, given) = out[0], out[1:5], out[5:]

    grad_widened = halo_by_planes(grad_pieces)

    groups = [[x * ny + y for x in range(c, nx, 2) for y in range(ny)] for c in range(2)]

    def among_chips(blocks):
        return lax.all_to_all(blocks, ("gx", "gy"), 0, 0, axis_index_groups=groups)

    chip_sum = pl.pallas_call(
        add_kernel,
        in_specs=in_vmem(2),
        out_specs=in_vmem(1)[0],
        out_shape=jax.ShapeDtypeStruct((half, Z), BF16),
        compiler_params=params(4),
        name="chip_sum",
    )(kept, swap_x(given, 0))
    parts = among_chips(chip_sum.reshape(devices // 2, chunk, Z))
    share = sum_spread(parts, devices // 2)
    share, grad_widened[0] = lax.optimization_barrier((share, grad_widened[0]))
    kept = among_chips(share).reshape(half, Z)
    got = swap_x(kept, 0)

    grad_fields = pl.pallas_call(
        functools.partial(adjoint_kernel, X, Y, C, Z),
        grid=(S,),
        in_specs=in_vmem(8),
        out_specs=pl.BlockSpec((1, C * X * Y, Z), lambda s: (s, 0, 0)),
        out_shape=jax.ShapeDtypeStruct((S, C * X * Y, Z), BF16),
        scratch_shapes=[
            pltpu.VMEM(((X + 2) * (Y + 2), C, Z), BF16),
            pltpu.VMEM((STACK * C, cells), BF16),
            pltpu.VMEM((C * X * Y, Z), F32),
        ],
        compiler_params=params(14),
        cost_estimate=pl.CostEstimate(
            flops=S * cells * 2 * 27 * C, bytes_accessed=8 * S * cells * C, transcendentals=0
        ),
        name="adjoint",
    )(*grad_widened, grad_merged, flip_matrix).reshape(S, C, X, Y, Z)

    moved = swap_in_group(reduced.reshape(gx, S // gx, hx, hy * hz, O), "gx")
    moved = moved.transpose(1, 0, 2, 3, 4).reshape(gy, per_group, gx * hx, hy * hz, O)
    moved = swap_in_group(moved, "gy").transpose(1, 2, 0, 3, 4)
    coarse = moved.reshape(per_group, gx * hx, gy * hy, hz, O).transpose(0, 4, 1, 2, 3)[None, None]

    scale = 1.0 / math.sqrt(S * cells * devices)
    down, outw, inw, tapw = pl.pallas_call(
        functools.partial(finish_kernel, C, Z, H, scale),
        out_shape=[
            jax.ShapeDtypeStruct((8 * C, O), F32),
            jax.ShapeDtypeStruct((C, H), F32),
            jax.ShapeDtypeStruct((C, H), F32),
            jax.ShapeDtypeStruct((3, 3, 3, C), F32),
        ],
        in_specs=in_vmem(2),
        scratch_shapes=[pltpu.VMEM((2 * half, Z), BF16)],
        compiler_params=params(6),
        name="finish",
    )(kept, got)
    return (
        coarse,
        grad_fields,
        tapw.transpose(3, 0, 1, 2),
        inw.T,
        outw,
        down.reshape(C, 2, 2, 2, O).transpose(4, 0, 1, 2, 3),
    )


def solution(mesh):
    placed = (
        P(None, None, "gx", "gy", None),
        P(),
        P(),
        P(),
        P(),
        P("gx", "gy", None, None, None, None, None),
    )
    return jax.shard_map(
        per_device,
        mesh=mesh,
        in_specs=placed,
        out_specs=(
            P("gx", "gy", None, None, None, None, None),
            P(None, None, "gx", "gy", None),
            P(),
            P(),
            P(),
            P(),
        ),
        check_vma=False,
    )
```

```python
import functools
import math

import jax
import jax.numpy as jnp
from jax import lax
from jax.experimental import pallas as pl
from jax.experimental.pallas import tpu as pltpu
from jax.sharding import PartitionSpec as P

GRIDC = 4
F32 = jnp.float32
BF16 = jnp.bfloat16
MIB = 1024 * 1024
STACK = 10
GELU_C = math.sqrt(2.0 / math.pi)
GELU_A = 0.044715


def dot(a, b, ca, cb):
    return lax.dot_general(a, b, (((ca,), (cb,)), ((), ())), preferred_element_type=F32)


def sides():
    return lax.axis_index("gx") % 2, lax.axis_index("gy") % 2


def write_pieces(row, s, Y, near, far, first, second):
    p, q = sides()
    for k, (x, plane) in enumerate(((1 - p, near), (p, far))):
        for y in range(Y):
            plane[s, y] = row(x, y)
        first[k, s] = row(x, (1 - q) * (Y - 1))
        second[k, s] = row(x, q * (Y - 1))


def piece_shapes(S, Y, C, Z):
    return [jax.ShapeDtypeStruct((S, Y, C, Z), BF16)] * 2 + [
        jax.ShapeDtypeStruct((2, S, C, Z), BF16)
    ] * 2


def params(mib):
    return pltpu.CompilerParams(vmem_limit_bytes=mib * MIB)


def in_vmem(n):
    return [pl.BlockSpec(memory_space=pltpu.VMEM)] * n


def swap_pairs(n, start):
    return [pair for i in range(start, n - 1, 2) for pair in ((i, i + 1), (i + 1, i))]


def swap_x(plane, start):
    return lax.ppermute(plane, "gx", swap_pairs(lax.axis_size("gx"), start))


def swap_y(rows, start):
    return lax.ppermute(rows, "gy", swap_pairs(lax.axis_size("gy"), start))


def halo_by_corners(pieces):
    near, far, first, second = pieces
    from_near, from_far = swap_x(near, 0), swap_x(far, 1)
    first, second = swap_y(first, 0), swap_y(second, 1)
    corner_far = swap_x(jnp.stack([first[1], second[1]]), 1)
    corner_near = swap_x(jnp.stack([first[0], second[0]]), 0)
    return [near, far, from_near, from_far, first, second, corner_near, corner_far]


def halo_by_planes(near, far):
    from_near, from_far = swap_x(near, 0), swap_x(far, 1)
    _, q = sides()
    Y = near.shape[1]
    got = []
    for y, start in (((1 - q) * (Y - 1), 0), (q * (Y - 1), 1)):
        rows = [
            lax.dynamic_index_in_dim(plane, y, 1, keepdims=False)
            for plane in (from_near, near, far, from_far)
        ]
        got.append(swap_y(jnp.stack(rows), start))
    return [from_near, near, far, from_far, *got]


def fill_padded(planes, s, Fs):
    _, q = sides()
    for u, plane, (r0, k0), (r1, k1) in planes:
        Y = plane.shape[1]
        for y in range(Y):
            Fs[u * (Y + 2) + y + 1] = plane[s, y].astype(Fs.dtype)
        Fs[u * (Y + 2) + (1 - q) * (Y + 1)] = r0[k0, s].astype(Fs.dtype)
        Fs[u * (Y + 2) + q * (Y + 1)] = r1[k1, s].astype(Fs.dtype)


def fill_stack(Fs, FB, rows, Y):
    C, Z = Fs.shape[1:]
    for a in range(3):
        for b in range(3):
            at = (a * 3 + b) * C
            for r, (x, y) in enumerate(rows):
                row = Fs[(x + a) * (Y + 2) + y + b].astype(BF16)
                FB[at : at + C, r * Z : (r + 1) * Z] = row
    if FB.shape[0] > 9 * C:
        FB[9 * C :, :] = jnp.zeros((FB.shape[0] - 9 * C, FB.shape[1]), BF16)


def in_grid(x):
    p, _ = sides()
    return p if x else 1 - p


def from_left(value, lane):
    return jnp.where(lane == 0, 0.0, pltpu.roll(value, 1, 1))


def from_right(value, lane):
    Z = value.shape[1]
    return jnp.where(lane == Z - 1, 0.0, pltpu.roll(value, Z - 1, 1))


def conv_rows(taps, stack, C, Z, lane):
    acc = dot(taps, stack, 1, 0)
    rows = []
    for k in range(0, stack.shape[1], Z):
        left, mid, right = (acc[e * C : (e + 1) * C, k : k + Z] for e in range(3))
        rows.append(mid + from_left(left, lane) + from_right(right, lane))
    return rows


def conv_tiles(wb, Fs, Ds, rows, Y, lane):
    C, Z = Fs.shape[1:]
    for c in range(0, C, 8):
        weights = [wb[t, c : c + 8, :] for t in range(27)]
        for x, y in rows:
            acc = [None, None, None]
            for a in range(3):
                for b in range(3):
                    f = Fs[(x + a) * (Y + 2) + y + b, c : c + 8, :]
                    for e in range(3):
                        term = weights[(a * 3 + b) * 3 + e] * f
                        acc[e] = term if acc[e] is None else acc[e] + term
            total = acc[1] + from_left(acc[0], lane[:8]) + from_right(acc[2], lane[:8])
            Ds[c : c + 8, y * Z : (y + 1) * Z] = total


def split_kernel(X, Y, C, Z, f_ref, near, far, first, second, wide):
    wide[...] = f_ref[0].astype(F32)

    def row(x, y):
        return wide[pl.ds(x * Y + y, C, stride=X * Y), :].astype(BF16)

    write_pieces(row, pl.program_id(0), Y, near, far, first, second)


def z_permutation(Z):
    fine = lax.broadcasted_iota(jnp.int32, (2 * Z, 2 * Z), 0)
    coarse = lax.broadcasted_iota(jnp.int32, (2 * Z, 2 * Z), 1)
    inner = coarse % Z
    goes = coarse // Z + (inner % (Z // 2)) * 2 + (inner // (Z // 2)) * Z
    return jnp.where(fine == goes, 1.0, 0.0).astype(BF16)


def early_kernel(dims, gd_ref, w_ref, wd_ref, gm_ref, wb, flip_ref, Mb):
    X, Y, C, Z, H, O = dims
    NP = Y // 4
    step = pl.program_id(0)

    @pl.when(step == 0)
    def _():
        row = lax.broadcasted_iota(jnp.int32, (C, STACK * C), 0)
        column = lax.broadcasted_iota(jnp.int32, (C, STACK * C), 1)
        p, _ = sides()

        def tap(a, b, e):
            here, mirrored = (a * 3 + b) * 3 + e, ((2 - a) * 3 + b) * 3 + e
            return jnp.where(
                p == 1, w_ref[:, here : here + 1], w_ref[:, mirrored : mirrored + 1]
            )

        for e in range(3):
            block = jnp.zeros((C, STACK * C), F32)
            for ab in range(9):
                flipped = tap(2 - ab // 3, 2 - ab % 3, 2 - e)
                block = jnp.where(column == row + ab * C, flipped, block)
            flip_ref[e * C : (e + 1) * C, :] = block.astype(BF16)
        for t in range(27):
            wb[t] = jnp.broadcast_to(tap(t // 9, t // 3 % 3, t % 3), (C, Z))

    perm = z_permutation(Z)
    for X0 in range(X // 2):
        gp = dot(wd_ref[...], gd_ref[step, X0], 1, 1).astype(BF16)
        for a in range(2):
            for b in range(2):
                for p in range(NP):
                    src = ((a * 2 + b) * 2) * C
                    dst = ((a * 2 + b) * NP + p) * C
                    for e in range(2):
                        Mb[dst : dst + C, e * Z : (e + 1) * Z] = gp[
                            src + e * C : src + (e + 1) * C, p * Z : (p + 1) * Z
                        ]
        gm = dot(Mb[...], perm, 1, 1).astype(BF16)
        for a in range(2):
            for b in range(2):
                for p in range(NP):
                    src = ((a * 2 + b) * NP + p) * C
                    for q in range(2):
                        y = 2 * (2 * p + q) + b
                        gm_ref[step, in_grid(a), y] = gm[src : src + C, q * Z : (q + 1) * Z]


def plane_work(x, step, dims, ops, put_merged):
    X, Y, C, Z, H, O = dims
    gm_ref, wb, pinT_ref, pout_ref, grad_ref, aout, ain, atap = ops[:8]
    Fs, FB, Ds, Gs, pre_s, ga_s, act_s, gp_s, pin, poutT = ops[8:]
    lane = lax.broadcasted_iota(jnp.int32, (C, Z), 1)
    fill_stack(Fs, FB, [(x, y) for y in range(Y)], Y)
    Gs[3 * C :, :] = jnp.zeros((C, Gs.shape[1]), BF16)

    def columns(i):
        return slice(4 * i * Z, 4 * (i + 1) * Z)

    def convolve(i):
        conv_tiles(wb, Fs, Ds, [(x, y) for y in range(4 * i, 4 * i + 4)], Y, lane)

    def grad_merged(i):
        return jnp.concatenate([gm_ref[step, x, y] for y in range(4 * i, 4 * i + 4)], axis=1)

    def enter(i):
        pre_s[i] = dot(pin[...], Ds[:, columns(i)].astype(BF16), 1, 0)
        ga_s[i] = dot(poutT[...], grad_merged(i), 1, 0)

    def activate(i):
        for h0 in range(0, H, 16):
            hs = slice(h0, h0 + 16)
            pre = pre_s[i, hs, :]
            sq = pre * pre
            t = jnp.tanh(pre * (GELU_C + (GELU_C * GELU_A) * sq))
            h = 0.5 + 0.5 * t
            act = pre * h
            slope = h + act * (1.0 - h) * (2.0 * GELU_C + (6.0 * GELU_C * GELU_A) * sq)
            act_s[i, hs, :] = act.astype(BF16)
            gp_s[i, hs, :] = (ga_s[i, hs, :] * slope).astype(BF16)

    def leave(i):
        grad_depth = dot(pinT_ref[...], gp_s[i], 1, 0).astype(BF16)
        branch = dot(pout_ref[...], act_s[i], 1, 0)
        for j in range(4):
            y = 4 * i + j
            row = Fs[(x + 1) * (Y + 2) + y + 1]
            put_merged(y, (row + branch[:, j * Z : (j + 1) * Z]).astype(BF16))
            grad_ref[step, y] = grad_depth[:, j * Z : (j + 1) * Z]
            g = grad_depth[:, j * Z : (j + 1) * Z].astype(F32)
            for e, value in enumerate((from_right(g, lane), g, from_left(g, lane))):
                Gs[e * C : (e + 1) * C, y * Z : (y + 1) * Z] = value.astype(BF16)
        aout[...] += dot(grad_merged(i), act_s[i], 1, 1)
        ain[...] += dot(Ds[:, columns(i)].astype(BF16), gp_s[i], 1, 1)
        atap[...] += dot(FB[:, columns(i)], Gs[:, columns(i)], 1, 1)

    last = Y // 4 - 1
    convolve(0)
    enter(0)
    convolve(1)
    activate(0)
    for i in range(last + 1):
        if i < last:
            enter(i + 1)
        leave(i)
        if i + 2 <= last:
            convolve(i + 2)
        if i < last:
            activate(i + 1)


def merged_place(x, y, Y, C, Z):
    start = ((in_grid(x) * 2 + y % 2) * (Y // 4) + y // 4) * C
    q = y // 2 % 2
    return pl.ds(pl.multiple_of(start, C), C), slice(q * Z, (q + 1) * Z)


def set_up(pinT_ref, pout_ref, pin, poutT):
    pin[...] = pinT_ref[...].astype(F32).T.astype(BF16)
    poutT[...] = pout_ref[...].astype(F32).T.astype(BF16)


def near_kernel(dims, *refs):
    X, Y, C, Z, H, O = dims
    from_near, near, far, first, second, corner, gm_ref, wb, pinT_ref, pout_ref = refs[:10]
    grad_ref, Mb, aout, ain, atap = refs[10:15]
    Fs, FB, Ds, Gs, pre_s, ga_s, act_s, gp_s, pin, poutT = refs[15:]
    step = pl.program_id(0)

    @pl.when(step == 0)
    def _():
        aout[...] = jnp.zeros_like(aout)
        ain[...] = jnp.zeros_like(ain)
        atap[...] = jnp.zeros_like(atap)
        set_up(pinT_ref, pout_ref, pin, poutT)

    planes = [
        (0, from_near, (corner, 0), (corner, 1)),
        (1, near, (first, 0), (second, 0)),
        (2, far, (first, 1), (second, 1)),
    ]
    fill_padded(planes, step, Fs)

    def put_merged(y, value):
        rows, lanes = merged_place(0, y, Y, C, Z)
        Mb[step, rows, lanes] = value

    ops = gm_ref, wb, pinT_ref, pout_ref, grad_ref, aout, ain, atap
    ops += Fs, FB, Ds, Gs, pre_s, ga_s, act_s, gp_s, pin, poutT
    plane_work(0, step, dims, ops, put_merged)


def far_kernel(dims, *refs):
    X, Y, C, Z, H, O = dims
    NP = Y // 4
    near, far, from_far, first, second, corner, gm_ref, wb, pinT_ref, pout_ref = refs[:10]
    gd_ref, wd_ref, Mb_ref, aout_ref, ain_ref, atap_ref = refs[10:16]
    grad_ref, red_ref, packed_ref = refs[16:19]
    Fs, FB, Ds, Gs, pre_s, ga_s, act_s, gp_s, pin, poutT = refs[19:29]
    Mb, Pt, atap, adown, aout, ain, rows_s = refs[29:]
    step = pl.program_id(0)

    @pl.when(step == 0)
    def _():
        aout[...] = aout_ref[...]
        ain[...] = ain_ref[...]
        atap[...] = atap_ref[...]
        adown[...] = jnp.zeros_like(adown)
        set_up(pinT_ref, pout_ref, pin, poutT)

    planes = [
        (1, near, (first, 0), (second, 0)),
        (2, far, (first, 1), (second, 1)),
        (3, from_far, (corner, 0), (corner, 1)),
    ]
    fill_padded(planes, step, Fs)
    Mb[...] = Mb_ref[step]

    def put_merged(y, value):
        rows, lanes = merged_place(1, y, Y, C, Z)
        Mb[rows, lanes] = value

    ops = gm_ref, wb, pinT_ref, pout_ref, grad_ref, aout, ain, atap
    ops += Fs, FB, Ds, Gs, pre_s, ga_s, act_s, gp_s, pin, poutT
    plane_work(1, step, dims, ops, put_merged)

    pt = dot(Mb[...], z_permutation(Z), 1, 0).astype(BF16)
    for a in range(2):
        for b in range(2):
            for p in range(NP):
                src = ((a * 2 + b) * NP + p) * C
                for e in range(2):
                    dst = ((a * 2 + b) * 2 + e) * C
                    Pt[dst : dst + C, p * Z : (p + 1) * Z] = pt[
                        src : src + C, e * Z : (e + 1) * Z
                    ]
    red_ref[step, 0] = dot(Pt[...], wd_ref[...], 0, 0).astype(BF16)
    adown[...] += dot(Pt[...], gd_ref[step, 0], 1, 0)

    @pl.when(step == pl.num_programs(0) - 1)
    def _():
        rows_s[...] = jnp.zeros_like(rows_s)
        for k in range(8):
            rows_s[pl.ds(k, C, stride=8), :] = adown[k * C : (k + 1) * C, :]
        row = lax.broadcasted_iota(jnp.int32, (C, 4 * C), 0)
        column = lax.broadcasted_iota(jnp.int32, (C, 4 * C), 1)
        lines = []
        for ab in range(9):
            block = jnp.where(column % C == row, atap[ab * C : (ab + 1) * C, :], 0.0)
            lines.append(jnp.sum(block, axis=0, keepdims=True))
        p, _ = sides()
        at = 8 * C + 2 * C * (H // Z)
        for a in range(3):
            for b in range(3):
                line = jnp.where(p == 1, lines[a * 3 + b], lines[(2 - a) * 3 + b])
                for k in range(0, 4 * C, Z):
                    rows_s[at : at + 1, :] = line[:, k : k + Z]
                    at += 1
        packed_ref[: rows_s.shape[0], :] = rows_s[...].astype(BF16)
        at = 8 * C
        for part in (aout, ain):
            for k in range(0, H, Z):
                packed_ref[at : at + C, :] = part[:, k : k + Z].astype(BF16)
                at += C
        at = rows_s.shape[0]
        if at < packed_ref.shape[0]:
            rest = packed_ref.shape[0] - at
            packed_ref[at:, :] = jnp.zeros((rest, Z), BF16)


def adjoint_kernel(X, Y, C, Z, *refs):
    planes, (first, second) = refs[:4], refs[4:6]
    gm_ref, tap_ref, out_ref, Fs, FB, wide = refs[6:]
    step = pl.program_id(0)
    fill_padded([(u, planes[u], (first, u), (second, u)) for u in range(4)], step, Fs)
    cells = [(x, y) for x in range(X) for y in range(Y)]
    fill_stack(Fs, FB, cells, Y)
    lane = lax.broadcasted_iota(jnp.int32, (C, Z), 1)
    for r0 in range(0, X * Y, 4):
        rows = conv_rows(tap_ref[...], FB[:, r0 * Z : (r0 + 4) * Z], C, Z, lane)
        for (x, y), value in zip(cells[r0 : r0 + 4], rows):
            total = value + gm_ref[step, x, y].astype(F32)
            wide[pl.ds(in_grid(x) * Y + y, C, stride=X * Y), :] = total
    out_ref[0] = wide[...].astype(BF16)


def finish_kernel(C, Z, H, scale, every_ref, down_ref, out_ref, in_ref, taps_ref):
    down_ref[...] = every_ref[: 8 * C, :].astype(F32) * scale
    at = 8 * C
    for ref in (out_ref, in_ref):
        for k in range(0, H, Z):
            ref[:, k : k + Z] = every_ref[at : at + C, :].astype(F32) * scale
            at += C
    taps = every_ref[at : at + 32, :].astype(F32) * scale
    for a in range(3):
        for b in range(3):
            for e in range(3):
                line, k = divmod(e * C, Z)
                line += (a * 3 + b) * (4 * C // Z)
                taps_ref[a, b, e : e + 1, :] = taps[line : line + 1, k : k + C]


def sum_spread_kernel(parts_ref, out_ref):
    total = parts_ref[0].astype(F32)
    for i in range(1, parts_ref.shape[0]):
        total = total + parts_ref[i].astype(F32)
    total = total.astype(BF16)
    for j in range(out_ref.shape[0]):
        out_ref[j] = total


def sum_spread(parts, receivers):
    shape = (receivers,) + parts.shape[1:]
    return pl.pallas_call(
        sum_spread_kernel,
        in_specs=in_vmem(1),
        out_specs=in_vmem(1)[0],
        out_shape=jax.ShapeDtypeStruct(shape, BF16),
        compiler_params=params(4),
        name="sum_spread",
    )(parts)


def swap_in_group(blocks, axis):
    g = blocks.shape[0]
    if g == 1:
        return blocks
    n = lax.axis_size(axis)
    member = lax.axis_index(axis) % g
    got = [lax.dynamic_index_in_dim(blocks, member, 0, keepdims=False)]
    for k in range(1, g):
        out = lax.dynamic_index_in_dim(blocks, (member + k) % g, 0, keepdims=False)
        pairs = [(i, i - i % g + (i + k) % g) for i in range(n)]
        got.append(lax.ppermute(out, axis, pairs))
    if g == 2:
        first = member == 0
        return jnp.stack([jnp.where(first, got[0], got[1]), jnp.where(first, got[1], got[0])])
    got = jnp.stack(got)
    return jnp.take(got, (member - jnp.arange(g, dtype=jnp.int32)) % g, axis=0)


def per_device(fields, depth_kernel, point_in, point_out, down_kernel, cotangent):
    S, C, X, Y, Z = fields.shape
    assert X == 2 and Y % 4 == 0
    H, O = point_in.shape[0], down_kernel.shape[0]
    hx, hy, hz = X // 2, Y // 2, Z // 2
    nx, ny = lax.axis_size("gx"), lax.axis_size("gy")
    devices = nx * ny
    gx, gy = nx // GRIDC, ny // GRIDC
    per_group = S // (gx * gy)

    pieces = pl.pallas_call(
        functools.partial(split_kernel, X, Y, C, Z),
        grid=(S,),
        in_specs=[pl.BlockSpec((1, C * X * Y, Z), lambda s: (s, 0, 0))],
        out_specs=in_vmem(4),
        out_shape=piece_shapes(S, Y, C, Z),
        scratch_shapes=[pltpu.VMEM((C * X * Y, Z), F32)],
        compiler_params=params(6),
        name="split_fields",
    )(fields.reshape(S, C * X * Y, Z))


    moved = cotangent[0, 0].transpose(0, 2, 3, 4, 1)
    moved = moved.reshape(per_group, gx * hx, gy, hy * hz, O).transpose(2, 0, 1, 3, 4)
    moved = swap_in_group(moved, "gy").reshape(gy * per_group, gx, hx, hy * hz, O)
    moved = swap_in_group(moved.transpose(1, 0, 2, 3, 4), "gx")
    grad_down = moved.reshape(S, hx, hy * hz, O)

    widened = halo_by_corners(pieces)

    wd = down_kernel.transpose(2, 3, 4, 1, 0).reshape(8 * C, O)
    taps = depth_kernel.reshape(C, 27).astype(F32)

    rows = 8 * C + 2 * C * (H // Z) + 32
    chunk = -(-rows // (8 * nx)) * 8
    cells = X * Y * Z
    dims = (X, Y, C, Z, H, O)
    grad_merged, spread, flip_matrix = pl.pallas_call(
        functools.partial(early_kernel, dims),
        grid=(S,),
        in_specs=in_vmem(3),
        out_specs=in_vmem(3),
        out_shape=[
            jax.ShapeDtypeStruct((S, X, Y, C, Z), BF16),
            jax.ShapeDtypeStruct((27, C, Z), F32),
            jax.ShapeDtypeStruct((3 * C, STACK * C), BF16),
        ],
        scratch_shapes=[pltpu.VMEM((Y * C, 2 * Z), BF16)],
        compiler_params=params(8),
        cost_estimate=pl.CostEstimate(
            flops=S * cells * (2 * C * O + 8 * C * Z),
            bytes_accessed=4 * S * cells * C + 4 * 27 * C * Z,
            transcendentals=0,
        ),
        name="early",
    )(grad_down, taps, wd)

    scratch = [
        pltpu.VMEM(((X + 2) * (Y + 2), C, Z), F32),
        pltpu.VMEM((9 * C, Y * Z), BF16),
        pltpu.VMEM((C, Y * Z), F32),
        pltpu.VMEM((4 * C, Y * Z), BF16),
        pltpu.VMEM((Y // 4, H, 4 * Z), F32),
        pltpu.VMEM((Y // 4, H, 4 * Z), F32),
        pltpu.VMEM((Y // 4, H, 4 * Z), BF16),
        pltpu.VMEM((Y // 4, H, 4 * Z), BF16),
        pltpu.VMEM((H, C), BF16),
        pltpu.VMEM((H, C), BF16),
    ]
    sums = [(C, H), (C, H), (9 * C, 4 * C)]
    cost = pl.CostEstimate(
        flops=S * cells * (6 * C * H + 27 * C * 4 * C),
        bytes_accessed=8 * S * cells * C,
        transcendentals=S * cells * H // 2,
    )
    near, far, from_near, from_far, first, second, corner_near, corner_far = widened
    common = (first, second), (grad_merged, spread, point_in.T, point_out)
    grad_near, merged, *partial_sums = pl.pallas_call(
        functools.partial(near_kernel, dims),
        grid=(S,),
        in_specs=in_vmem(10),
        out_specs=in_vmem(5),
        out_shape=[
            jax.ShapeDtypeStruct((S, Y, C, Z), BF16),
            jax.ShapeDtypeStruct((S, Y * C, 2 * Z), BF16),
        ]
        + [jax.ShapeDtypeStruct(shape, F32) for shape in sums],
        scratch_shapes=scratch,
        compiler_params=params(14),
        cost_estimate=cost,
        name="near_side",
    )(from_near, near, far, *common[0], corner_near, *common[1])
    grad_far, reduced, packed = pl.pallas_call(
        functools.partial(far_kernel, dims),
        grid=(S,),
        in_specs=in_vmem(16),
        out_specs=in_vmem(3),
        out_shape=[
            jax.ShapeDtypeStruct((S, Y, C, Z), BF16),
            jax.ShapeDtypeStruct((S, hx, hy * hz, O), BF16),
            jax.ShapeDtypeStruct((nx * chunk, Z), BF16),
        ],
        scratch_shapes=scratch
        + [
            pltpu.VMEM((Y * C, 2 * Z), BF16),
            pltpu.VMEM((8 * C, hy * hz), BF16),
            pltpu.VMEM((9 * C, 4 * C), F32),
            pltpu.VMEM((8 * C, O), F32),
            pltpu.VMEM((C, H), F32),
            pltpu.VMEM((C, H), F32),
            pltpu.VMEM((rows, Z), F32),
        ],
        compiler_params=params(16),
        cost_estimate=cost,
        name="far_side",
    )(near, far, from_far, *common[0], corner_far, *common[1], grad_down, wd, merged, *partial_sums)

    grad_widened = halo_by_planes(grad_near, grad_far)

    parts = lax.all_to_all(packed.reshape(nx, chunk, Z), "gx", 0, 0)
    parts = lax.all_to_all(sum_spread(parts, ny), "gy", 0, 0)
    share = sum_spread(parts, nx)
    share, grad_widened[1] = lax.optimization_barrier((share, grad_widened[1]))
    every = lax.all_to_all(share, "gx", 0, 0).reshape(nx * chunk, Z)

    grad_fields = pl.pallas_call(
        functools.partial(adjoint_kernel, X, Y, C, Z),
        grid=(S,),
        in_specs=in_vmem(8),
        out_specs=pl.BlockSpec((1, C * X * Y, Z), lambda s: (s, 0, 0)),
        out_shape=jax.ShapeDtypeStruct((S, C * X * Y, Z), BF16),
        scratch_shapes=[
            pltpu.VMEM(((X + 2) * (Y + 2), C, Z), BF16),
            pltpu.VMEM((STACK * C, cells), BF16),
            pltpu.VMEM((C * X * Y, Z), F32),
        ],
        compiler_params=params(14),
        cost_estimate=pl.CostEstimate(
            flops=S * cells * 2 * 27 * C, bytes_accessed=8 * S * cells * C, transcendentals=0
        ),
        name="adjoint",
    )(*grad_widened, grad_merged, flip_matrix).reshape(S, C, X, Y, Z)

    moved = swap_in_group(reduced.reshape(gx, S // gx, hx, hy * hz, O), "gx")
    moved = moved.transpose(1, 0, 2, 3, 4).reshape(gy, per_group, gx * hx, hy * hz, O)
    moved = swap_in_group(moved, "gy").transpose(1, 2, 0, 3, 4)
    coarse = moved.reshape(per_group, gx * hx, gy * hy, hz, O).transpose(0, 4, 1, 2, 3)[None, None]

    scale = 1.0 / math.sqrt(S * cells * devices)
    down, outw, inw, tapw = pl.pallas_call(
        functools.partial(finish_kernel, C, Z, H, scale),
        out_shape=[
            jax.ShapeDtypeStruct((8 * C, O), F32),
            jax.ShapeDtypeStruct((C, H), F32),
            jax.ShapeDtypeStruct((C, H), F32),
            jax.ShapeDtypeStruct((3, 3, 3, C), F32),
        ],
        in_specs=in_vmem(1),
        compiler_params=params(6),
        name="finish",
    )(every)
    return (
        coarse,
        grad_fields,
        tapw.transpose(3, 0, 1, 2),
        inw.T,
        outw,
        down.reshape(C, 2, 2, 2, O).transpose(4, 0, 1, 2, 3),
    )


def solution(mesh):
    placed = (
        P(None, None, "gx", "gy", None),
        P(),
        P(),
        P(),
        P(),
        P("gx", "gy", None, None, None, None, None),
    )
    return jax.shard_map(
        per_device,
        mesh=mesh,
        in_specs=placed,
        out_specs=(
            P("gx", "gy", None, None, None, None, None),
            P(None, None, "gx", "gy", None),
            P(),
            P(),
            P(),
            P(),
        ),
        check_vma=False,
    )
```

```python
import functools
import math

import jax
import jax.numpy as jnp
from jax import lax
from jax.experimental import pallas as pl
from jax.experimental.pallas import tpu as pltpu
from jax.sharding import PartitionSpec as P

GRIDC = 4
F32 = jnp.float32
BF16 = jnp.bfloat16
MIB = 1024 * 1024
STACK = 10
GELU_C = math.sqrt(2.0 / math.pi)
GELU_A = 0.044715


def dot(a, b, ca, cb):
    return lax.dot_general(a, b, (((ca,), (cb,)), ((), ())), preferred_element_type=F32)


def sides():
    return lax.axis_index("gx") % 2, lax.axis_index("gy") % 2


def write_pieces(row, s, Y, near, far, first, second):
    p, q = sides()
    for k, (x, plane) in enumerate(((1 - p, near), (p, far))):
        for y in range(Y):
            plane[s, y] = row(x, y)
        first[k, s] = row(x, (1 - q) * (Y - 1))
        second[k, s] = row(x, q * (Y - 1))


def piece_shapes(S, Y, C, Z):
    return [jax.ShapeDtypeStruct((S, Y, C, Z), BF16)] * 2 + [
        jax.ShapeDtypeStruct((2, S, C, Z), BF16)
    ] * 2


def params(mib):
    return pltpu.CompilerParams(vmem_limit_bytes=mib * MIB)


def in_vmem(n):
    return [pl.BlockSpec(memory_space=pltpu.VMEM)] * n


def swap_pairs(n, start):
    return [pair for i in range(start, n - 1, 2) for pair in ((i, i + 1), (i + 1, i))]


def swap_x(plane, start):
    return lax.ppermute(plane, "gx", swap_pairs(lax.axis_size("gx"), start))


def swap_y(rows, start):
    return lax.ppermute(rows, "gy", swap_pairs(lax.axis_size("gy"), start))


def halo_by_corners(pieces):
    near, far, first, second = pieces
    from_near, from_far = swap_x(near, 0), swap_x(far, 1)
    first, second = swap_y(first, 0), swap_y(second, 1)
    corner_far = swap_x(jnp.stack([first[1], second[1]]), 1)
    corner_near = swap_x(jnp.stack([first[0], second[0]]), 0)
    return [near, far, from_near, from_far, first, second, corner_near, corner_far]


def halo_by_planes(near, far):
    from_near, from_far = swap_x(near, 0), swap_x(far, 1)
    _, q = sides()
    Y = near.shape[1]
    got = []
    for y, start in (((1 - q) * (Y - 1), 0), (q * (Y - 1), 1)):
        rows = [
            lax.dynamic_index_in_dim(plane, y, 1, keepdims=False)
            for plane in (from_near, near, far, from_far)
        ]
        got.append(swap_y(jnp.stack(rows), start))
    return [from_near, near, far, from_far, *got]


def fill_padded(planes, s, Fs):
    _, q = sides()
    for u, plane, (r0, k0), (r1, k1) in planes:
        Y = plane.shape[1]
        for y in range(Y):
            Fs[u * (Y + 2) + y + 1] = plane[s, y].astype(Fs.dtype)
        Fs[u * (Y + 2) + (1 - q) * (Y + 1)] = r0[k0, s].astype(Fs.dtype)
        Fs[u * (Y + 2) + q * (Y + 1)] = r1[k1, s].astype(Fs.dtype)


def fill_stack(Fs, FB, rows, Y):
    C, Z = Fs.shape[1:]
    for a in range(3):
        for b in range(3):
            at = (a * 3 + b) * C
            for r, (x, y) in enumerate(rows):
                row = Fs[(x + a) * (Y + 2) + y + b].astype(BF16)
                FB[at : at + C, r * Z : (r + 1) * Z] = row
    if FB.shape[0] > 9 * C:
        FB[9 * C :, :] = jnp.zeros((FB.shape[0] - 9 * C, FB.shape[1]), BF16)


def in_grid(x):
    p, _ = sides()
    return p if x else 1 - p


def from_left(value, lane):
    return jnp.where(lane == 0, 0.0, pltpu.roll(value, 1, 1))


def from_right(value, lane):
    Z = value.shape[1]
    return jnp.where(lane == Z - 1, 0.0, pltpu.roll(value, Z - 1, 1))


def conv_rows(taps, stack, C, Z, lane):
    acc = dot(taps, stack, 1, 0)
    rows = []
    for k in range(0, stack.shape[1], Z):
        left, mid, right = (acc[e * C : (e + 1) * C, k : k + Z] for e in range(3))
        rows.append(mid + from_left(left, lane) + from_right(right, lane))
    return rows


def conv_tiles(wb, Fs, Ds, rows, Y, lane):
    C, Z = Fs.shape[1:]
    for c in range(0, C, 8):
        weights = [wb[t, c : c + 8, :] for t in range(27)]
        for x, y in rows:
            acc = [None, None, None]
            for a in range(3):
                for b in range(3):
                    f = Fs[(x + a) * (Y + 2) + y + b, c : c + 8, :]
                    for e in range(3):
                        term = weights[(a * 3 + b) * 3 + e] * f
                        acc[e] = term if acc[e] is None else acc[e] + term
            total = acc[1] + from_left(acc[0], lane[:8]) + from_right(acc[2], lane[:8])
            Ds[c : c + 8, y * Z : (y + 1) * Z] = total


def split_kernel(X, Y, C, Z, f_ref, near, far, first, second, wide):
    wide[...] = f_ref[0].astype(F32)

    def row(x, y):
        return wide[pl.ds(x * Y + y, C, stride=X * Y), :].astype(BF16)

    write_pieces(row, pl.program_id(0), Y, near, far, first, second)


def z_permutation(Z):
    fine = lax.broadcasted_iota(jnp.int32, (2 * Z, 2 * Z), 0)
    coarse = lax.broadcasted_iota(jnp.int32, (2 * Z, 2 * Z), 1)
    inner = coarse % Z
    goes = coarse // Z + (inner % (Z // 2)) * 2 + (inner // (Z // 2)) * Z
    return jnp.where(fine == goes, 1.0, 0.0).astype(BF16)


def outward_taps(w_ref):
    p, _ = sides()
    mirrored = jnp.concatenate([w_ref[:, 18:27], w_ref[:, 9:18], w_ref[:, 0:9]], axis=1)
    return jnp.where(p == 1, w_ref[...], mirrored)


def early_kernel(dims, gd_ref, w_ref, wd_ref, gm_ref, wb, Mb):
    X, Y, C, Z, H, O = dims
    NP = Y // 4
    step = pl.program_id(0)

    @pl.when(step == 0)
    def _():
        taps = outward_taps(w_ref)
        for t in range(27):
            wb[t] = jnp.broadcast_to(taps[:, t : t + 1], (C, Z))

    perm = z_permutation(Z)
    for X0 in range(X // 2):
        gp = dot(wd_ref[...], gd_ref[step, X0], 1, 1).astype(BF16)
        for a in range(2):
            for b in range(2):
                for p in range(NP):
                    src = ((a * 2 + b) * 2) * C
                    dst = ((a * 2 + b) * NP + p) * C
                    for e in range(2):
                        Mb[dst : dst + C, e * Z : (e + 1) * Z] = gp[
                            src + e * C : src + (e + 1) * C, p * Z : (p + 1) * Z
                        ]
        gm = dot(Mb[...], perm, 1, 1).astype(BF16)
        for a in range(2):
            for b in range(2):
                for p in range(NP):
                    src = ((a * 2 + b) * NP + p) * C
                    for q in range(2):
                        y = 2 * (2 * p + q) + b
                        gm_ref[step, in_grid(a), y] = gm[src : src + C, q * Z : (q + 1) * Z]


def plane_work(x, step, dims, ops, put_merged):
    X, Y, C, Z, H, O = dims
    gm_ref, wb, pinT_ref, pout_ref, grad_ref, aout, ain, atap = ops[:8]
    Fs, FB, Ds, Gs, pre_s, ga_s, act_s, gp_s, pin, poutT = ops[8:]
    lane = lax.broadcasted_iota(jnp.int32, (C, Z), 1)
    fill_stack(Fs, FB, [(x, y) for y in range(Y)], Y)
    Gs[3 * C :, :] = jnp.zeros((C, Gs.shape[1]), BF16)

    def columns(i):
        return slice(4 * i * Z, 4 * (i + 1) * Z)

    def convolve(i):
        conv_tiles(wb, Fs, Ds, [(x, y) for y in range(4 * i, 4 * i + 4)], Y, lane)

    def grad_merged(i):
        return jnp.concatenate([gm_ref[step, x, y] for y in range(4 * i, 4 * i + 4)], axis=1)

    def enter(i):
        pre_s[i] = dot(pin[...], Ds[:, columns(i)].astype(BF16), 1, 0)
        ga_s[i] = dot(poutT[...], grad_merged(i), 1, 0)

    def activate(i):
        for h0 in range(0, H, 16):
            hs = slice(h0, h0 + 16)
            pre = pre_s[i, hs, :]
            sq = pre * pre
            t = jnp.tanh(pre * (GELU_C + (GELU_C * GELU_A) * sq))
            h = 0.5 + 0.5 * t
            act = pre * h
            slope = h + act * (1.0 - h) * (2.0 * GELU_C + (6.0 * GELU_C * GELU_A) * sq)
            act_s[i, hs, :] = act.astype(BF16)
            gp_s[i, hs, :] = (ga_s[i, hs, :] * slope).astype(BF16)

    def leave(i):
        grad_depth = dot(pinT_ref[...], gp_s[i], 1, 0).astype(BF16)
        branch = dot(pout_ref[...], act_s[i], 1, 0)
        for j in range(4):
            y = 4 * i + j
            row = Fs[(x + 1) * (Y + 2) + y + 1]
            put_merged(y, (row + branch[:, j * Z : (j + 1) * Z]).astype(BF16))
            grad_ref[step, y] = grad_depth[:, j * Z : (j + 1) * Z]
            g = grad_depth[:, j * Z : (j + 1) * Z].astype(F32)
            for e, value in enumerate((from_right(g, lane), g, from_left(g, lane))):
                Gs[e * C : (e + 1) * C, y * Z : (y + 1) * Z] = value.astype(BF16)
        aout[...] += dot(grad_merged(i), act_s[i], 1, 1)
        ain[...] += dot(Ds[:, columns(i)].astype(BF16), gp_s[i], 1, 1)
        atap[...] += dot(FB[:, columns(i)], Gs[:, columns(i)], 1, 1)

    last = Y // 4 - 1
    convolve(0)
    enter(0)
    convolve(1)
    activate(0)
    for i in range(last + 1):
        if i < last:
            enter(i + 1)
        leave(i)
        if i + 2 <= last:
            convolve(i + 2)
        if i < last:
            activate(i + 1)


def merged_place(x, y, Y, C, Z):
    start = ((in_grid(x) * 2 + y % 2) * (Y // 4) + y // 4) * C
    q = y // 2 % 2
    return pl.ds(pl.multiple_of(start, C), C), slice(q * Z, (q + 1) * Z)


def set_up(pinT_ref, pout_ref, pin, poutT):
    pin[...] = pinT_ref[...].astype(F32).T.astype(BF16)
    poutT[...] = pout_ref[...].astype(F32).T.astype(BF16)


def near_kernel(dims, *refs):
    X, Y, C, Z, H, O = dims
    from_near, near, far, first, second, corner, gm_ref, wb, pinT_ref, pout_ref = refs[:10]
    grad_ref, Mb, aout, ain, atap = refs[10:15]
    Fs, FB, Ds, Gs, pre_s, ga_s, act_s, gp_s, pin, poutT = refs[15:]
    step = pl.program_id(0)

    @pl.when(step == 0)
    def _():
        aout[...] = jnp.zeros_like(aout)
        ain[...] = jnp.zeros_like(ain)
        atap[...] = jnp.zeros_like(atap)
        set_up(pinT_ref, pout_ref, pin, poutT)

    planes = [
        (0, from_near, (corner, 0), (corner, 1)),
        (1, near, (first, 0), (second, 0)),
        (2, far, (first, 1), (second, 1)),
    ]
    fill_padded(planes, step, Fs)

    def put_merged(y, value):
        rows, lanes = merged_place(0, y, Y, C, Z)
        Mb[step, rows, lanes] = value

    ops = gm_ref, wb, pinT_ref, pout_ref, grad_ref, aout, ain, atap
    ops += Fs, FB, Ds, Gs, pre_s, ga_s, act_s, gp_s, pin, poutT
    plane_work(0, step, dims, ops, put_merged)


def far_kernel(dims, *refs):
    X, Y, C, Z, H, O = dims
    NP = Y // 4
    near, far, from_far, first, second, corner, gm_ref, wb, pinT_ref, pout_ref = refs[:10]
    gd_ref, wd_ref, Mb_ref, aout_ref, ain_ref, atap_ref = refs[10:16]
    grad_ref, red_ref, packed_ref = refs[16:19]
    Fs, FB, Ds, Gs, pre_s, ga_s, act_s, gp_s, pin, poutT = refs[19:29]
    Mb, Pt, atap, adown, aout, ain, rows_s = refs[29:]
    step = pl.program_id(0)

    @pl.when(step == 0)
    def _():
        aout[...] = aout_ref[...]
        ain[...] = ain_ref[...]
        atap[...] = atap_ref[...]
        adown[...] = jnp.zeros_like(adown)
        set_up(pinT_ref, pout_ref, pin, poutT)

    planes = [
        (1, near, (first, 0), (second, 0)),
        (2, far, (first, 1), (second, 1)),
        (3, from_far, (corner, 0), (corner, 1)),
    ]
    fill_padded(planes, step, Fs)
    Mb[...] = Mb_ref[step]

    def put_merged(y, value):
        rows, lanes = merged_place(1, y, Y, C, Z)
        Mb[rows, lanes] = value

    ops = gm_ref, wb, pinT_ref, pout_ref, grad_ref, aout, ain, atap
    ops += Fs, FB, Ds, Gs, pre_s, ga_s, act_s, gp_s, pin, poutT
    plane_work(1, step, dims, ops, put_merged)

    pt = dot(Mb[...], z_permutation(Z), 1, 0).astype(BF16)
    for a in range(2):
        for b in range(2):
            for p in range(NP):
                src = ((a * 2 + b) * NP + p) * C
                for e in range(2):
                    dst = ((a * 2 + b) * 2 + e) * C
                    Pt[dst : dst + C, p * Z : (p + 1) * Z] = pt[
                        src : src + C, e * Z : (e + 1) * Z
                    ]
    red_ref[step, 0] = dot(Pt[...], wd_ref[...], 0, 0).astype(BF16)
    adown[...] += dot(Pt[...], gd_ref[step, 0], 1, 0)

    @pl.when(step == pl.num_programs(0) - 1)
    def _():
        rows_s[...] = jnp.zeros_like(rows_s)
        for k in range(8):
            rows_s[pl.ds(k, C, stride=8), :] = adown[k * C : (k + 1) * C, :]
        row = lax.broadcasted_iota(jnp.int32, (C, 4 * C), 0)
        column = lax.broadcasted_iota(jnp.int32, (C, 4 * C), 1)
        lines = []
        for ab in range(9):
            block = jnp.where(column % C == row, atap[ab * C : (ab + 1) * C, :], 0.0)
            lines.append(jnp.sum(block, axis=0, keepdims=True))
        p, _ = sides()
        at = 8 * C + 2 * C * (H // Z)
        for a in range(3):
            for b in range(3):
                line = jnp.where(p == 1, lines[a * 3 + b], lines[(2 - a) * 3 + b])
                for k in range(0, 4 * C, Z):
                    rows_s[at : at + 1, :] = line[:, k : k + Z]
                    at += 1
        packed_ref[: rows_s.shape[0], :] = rows_s[...].astype(BF16)
        at = 8 * C
        for part in (aout, ain):
            for k in range(0, H, Z):
                packed_ref[at : at + C, :] = part[:, k : k + Z].astype(BF16)
                at += C
        at = rows_s.shape[0]
        if at < packed_ref.shape[0]:
            rest = packed_ref.shape[0] - at
            packed_ref[at:, :] = jnp.zeros((rest, Z), BF16)


def adjoint_kernel(X, Y, C, Z, *refs):
    planes, (first, second) = refs[:4], refs[4:6]
    gm_ref, w_ref, out_ref, Fs, FB, wide, tap_ref = refs[6:]
    step = pl.program_id(0)

    @pl.when(step == 0)
    def _():
        taps = outward_taps(w_ref)
        row = lax.broadcasted_iota(jnp.int32, (C, STACK * C), 0)
        column = lax.broadcasted_iota(jnp.int32, (C, STACK * C), 1)
        for e in range(3):
            block = jnp.zeros((C, STACK * C), F32)
            for ab in range(9):
                t = 26 - (ab * 3 + e)
                block = jnp.where(column == row + ab * C, taps[:, t : t + 1], block)
            tap_ref[e * C : (e + 1) * C, :] = block.astype(BF16)

    fill_padded([(u, planes[u], (first, u), (second, u)) for u in range(4)], step, Fs)
    cells = [(x, y) for x in range(X) for y in range(Y)]
    fill_stack(Fs, FB, cells, Y)
    lane = lax.broadcasted_iota(jnp.int32, (C, Z), 1)
    for r0 in range(0, X * Y, 4):
        rows = conv_rows(tap_ref[...], FB[:, r0 * Z : (r0 + 4) * Z], C, Z, lane)
        for (x, y), value in zip(cells[r0 : r0 + 4], rows):
            total = value + gm_ref[step, x, y].astype(F32)
            wide[pl.ds(in_grid(x) * Y + y, C, stride=X * Y), :] = total
    out_ref[0] = wide[...].astype(BF16)


def finish_kernel(C, Z, H, scale, every_ref, down_ref, out_ref, in_ref, taps_ref):
    down_ref[...] = every_ref[: 8 * C, :].astype(F32) * scale
    at = 8 * C
    for ref in (out_ref, in_ref):
        for k in range(0, H, Z):
            ref[:, k : k + Z] = every_ref[at : at + C, :].astype(F32) * scale
            at += C
    taps = every_ref[at : at + 32, :].astype(F32) * scale
    for a in range(3):
        for b in range(3):
            for e in range(3):
                line, k = divmod(e * C, Z)
                line += (a * 3 + b) * (4 * C // Z)
                taps_ref[a, b, e : e + 1, :] = taps[line : line + 1, k : k + C]


def sum_spread_kernel(parts_ref, out_ref):
    total = parts_ref[0].astype(F32)
    for i in range(1, parts_ref.shape[0]):
        total = total + parts_ref[i].astype(F32)
    total = total.astype(BF16)
    for j in range(out_ref.shape[0]):
        out_ref[j] = total


def sum_spread(parts, receivers):
    shape = (receivers,) + parts.shape[1:]
    return pl.pallas_call(
        sum_spread_kernel,
        in_specs=in_vmem(1),
        out_specs=in_vmem(1)[0],
        out_shape=jax.ShapeDtypeStruct(shape, BF16),
        compiler_params=params(4),
        name="sum_spread",
    )(parts)


def swap_in_group(blocks, axis):
    g = blocks.shape[0]
    if g == 1:
        return blocks
    n = lax.axis_size(axis)
    member = lax.axis_index(axis) % g
    got = [lax.dynamic_index_in_dim(blocks, member, 0, keepdims=False)]
    for k in range(1, g):
        out = lax.dynamic_index_in_dim(blocks, (member + k) % g, 0, keepdims=False)
        pairs = [(i, i - i % g + (i + k) % g) for i in range(n)]
        got.append(lax.ppermute(out, axis, pairs))
    if g == 2:
        first = member == 0
        return jnp.stack([jnp.where(first, got[0], got[1]), jnp.where(first, got[1], got[0])])
    got = jnp.stack(got)
    return jnp.take(got, (member - jnp.arange(g, dtype=jnp.int32)) % g, axis=0)


def per_device(fields, depth_kernel, point_in, point_out, down_kernel, cotangent):
    S, C, X, Y, Z = fields.shape
    assert X == 2 and Y % 4 == 0
    H, O = point_in.shape[0], down_kernel.shape[0]
    hx, hy, hz = X // 2, Y // 2, Z // 2
    nx, ny = lax.axis_size("gx"), lax.axis_size("gy")
    devices = nx * ny
    gx, gy = nx // GRIDC, ny // GRIDC
    per_group = S // (gx * gy)

    pieces = pl.pallas_call(
        functools.partial(split_kernel, X, Y, C, Z),
        grid=(S,),
        in_specs=[pl.BlockSpec((1, C * X * Y, Z), lambda s: (s, 0, 0))],
        out_specs=in_vmem(4),
        out_shape=piece_shapes(S, Y, C, Z),
        scratch_shapes=[pltpu.VMEM((C * X * Y, Z), F32)],
        compiler_params=params(6),
        name="split_fields",
    )(fields.reshape(S, C * X * Y, Z))


    moved = cotangent[0, 0].transpose(0, 2, 3, 4, 1)
    moved = moved.reshape(per_group, gx * hx, gy, hy * hz, O).transpose(2, 0, 1, 3, 4)
    moved = swap_in_group(moved, "gy").reshape(gy * per_group, gx, hx, hy * hz, O)
    moved = swap_in_group(moved.transpose(1, 0, 2, 3, 4), "gx")
    grad_down = moved.reshape(S, hx, hy * hz, O)

    widened = halo_by_corners(pieces)

    wd = down_kernel.transpose(2, 3, 4, 1, 0).reshape(8 * C, O)
    taps = depth_kernel.reshape(C, 27).astype(F32)

    rows = 8 * C + 2 * C * (H // Z) + 32
    chunk = -(-rows // (8 * nx)) * 8
    cells = X * Y * Z
    dims = (X, Y, C, Z, H, O)
    grad_merged, spread = pl.pallas_call(
        functools.partial(early_kernel, dims),
        grid=(S,),
        in_specs=in_vmem(3),
        out_specs=in_vmem(2),
        out_shape=[
            jax.ShapeDtypeStruct((S, X, Y, C, Z), BF16),
            jax.ShapeDtypeStruct((27, C, Z), F32),
        ],
        scratch_shapes=[pltpu.VMEM((Y * C, 2 * Z), BF16)],
        compiler_params=params(8),
        cost_estimate=pl.CostEstimate(
            flops=S * cells * (2 * C * O + 8 * C * Z),
            bytes_accessed=4 * S * cells * C + 4 * 27 * C * Z,
            transcendentals=0,
        ),
        name="early",
    )(grad_down, taps, wd)

    scratch = [
        pltpu.VMEM(((X + 2) * (Y + 2), C, Z), F32),
        pltpu.VMEM((9 * C, Y * Z), BF16),
        pltpu.VMEM((C, Y * Z), F32),
        pltpu.VMEM((4 * C, Y * Z), BF16),
        pltpu.VMEM((Y // 4, H, 4 * Z), F32),
        pltpu.VMEM((Y // 4, H, 4 * Z), F32),
        pltpu.VMEM((Y // 4, H, 4 * Z), BF16),
        pltpu.VMEM((Y // 4, H, 4 * Z), BF16),
        pltpu.VMEM((H, C), BF16),
        pltpu.VMEM((H, C), BF16),
    ]
    sums = [(C, H), (C, H), (9 * C, 4 * C)]
    cost = pl.CostEstimate(
        flops=S * cells * (6 * C * H + 27 * C * 4 * C),
        bytes_accessed=8 * S * cells * C,
        transcendentals=S * cells * H // 2,
    )
    near, far, from_near, from_far, first, second, corner_near, corner_far = widened
    common = (first, second), (grad_merged, spread, point_in.T, point_out)
    grad_near, merged, *partial_sums = pl.pallas_call(
        functools.partial(near_kernel, dims),
        grid=(S,),
        in_specs=in_vmem(10),
        out_specs=in_vmem(5),
        out_shape=[
            jax.ShapeDtypeStruct((S, Y, C, Z), BF16),
            jax.ShapeDtypeStruct((S, Y * C, 2 * Z), BF16),
        ]
        + [jax.ShapeDtypeStruct(shape, F32) for shape in sums],
        scratch_shapes=scratch,
        compiler_params=params(14),
        cost_estimate=cost,
        name="near_side",
    )(from_near, near, far, *common[0], corner_near, *common[1])
    grad_far, reduced, packed = pl.pallas_call(
        functools.partial(far_kernel, dims),
        grid=(S,),
        in_specs=in_vmem(16),
        out_specs=in_vmem(3),
        out_shape=[
            jax.ShapeDtypeStruct((S, Y, C, Z), BF16),
            jax.ShapeDtypeStruct((S, hx, hy * hz, O), BF16),
            jax.ShapeDtypeStruct((nx * chunk, Z), BF16),
        ],
        scratch_shapes=scratch
        + [
            pltpu.VMEM((Y * C, 2 * Z), BF16),
            pltpu.VMEM((8 * C, hy * hz), BF16),
            pltpu.VMEM((9 * C, 4 * C), F32),
            pltpu.VMEM((8 * C, O), F32),
            pltpu.VMEM((C, H), F32),
            pltpu.VMEM((C, H), F32),
            pltpu.VMEM((rows, Z), F32),
        ],
        compiler_params=params(16),
        cost_estimate=cost,
        name="far_side",
    )(near, far, from_far, *common[0], corner_far, *common[1], grad_down, wd, merged, *partial_sums)

    moved = swap_in_group(reduced.reshape(gx, S // gx, hx, hy * hz, O), "gx")
    moved = moved.transpose(1, 0, 2, 3, 4).reshape(gy, per_group, gx * hx, hy * hz, O)
    moved = swap_in_group(moved, "gy").transpose(1, 2, 0, 3, 4)
    grad_near, grad_far, moved = lax.optimization_barrier((grad_near, grad_far, moved))
    coarse = moved.reshape(per_group, gx * hx, gy * hy, hz, O).transpose(0, 4, 1, 2, 3)[None, None]
    grad_widened = halo_by_planes(grad_near, grad_far)

    parts = lax.all_to_all(packed.reshape(nx, chunk, Z), "gx", 0, 0)
    parts = lax.all_to_all(sum_spread(parts, ny), "gy", 0, 0)
    share = sum_spread(parts, nx)
    share, grad_widened[1] = lax.optimization_barrier((share, grad_widened[1]))
    every = lax.all_to_all(share, "gx", 0, 0).reshape(nx * chunk, Z)

    grad_fields = pl.pallas_call(
        functools.partial(adjoint_kernel, X, Y, C, Z),
        grid=(S,),
        in_specs=in_vmem(8),
        out_specs=pl.BlockSpec((1, C * X * Y, Z), lambda s: (s, 0, 0)),
        out_shape=jax.ShapeDtypeStruct((S, C * X * Y, Z), BF16),
        scratch_shapes=[
            pltpu.VMEM(((X + 2) * (Y + 2), C, Z), BF16),
            pltpu.VMEM((STACK * C, cells), BF16),
            pltpu.VMEM((C * X * Y, Z), F32),
            pltpu.VMEM((3 * C, STACK * C), BF16),
        ],
        compiler_params=params(14),
        cost_estimate=pl.CostEstimate(
            flops=S * cells * 2 * 27 * C, bytes_accessed=8 * S * cells * C, transcendentals=0
        ),
        name="adjoint",
    )(*grad_widened, grad_merged, taps).reshape(S, C, X, Y, Z)

    scale = 1.0 / math.sqrt(S * cells * devices)
    down, outw, inw, tapw = pl.pallas_call(
        functools.partial(finish_kernel, C, Z, H, scale),
        out_shape=[
            jax.ShapeDtypeStruct((8 * C, O), F32),
            jax.ShapeDtypeStruct((C, H), F32),
            jax.ShapeDtypeStruct((C, H), F32),
            jax.ShapeDtypeStruct((3, 3, 3, C), F32),
        ],
        in_specs=in_vmem(1),
        compiler_params=params(6),
        name="finish",
    )(every)
    return (
        coarse,
        grad_fields,
        tapw.transpose(3, 0, 1, 2),
        inw.T,
        outw,
        down.reshape(C, 2, 2, 2, O).transpose(4, 0, 1, 2, 3),
    )


def solution(mesh):
    placed = (
        P(None, None, "gx", "gy", None),
        P(),
        P(),
        P(),
        P(),
        P("gx", "gy", None, None, None, None, None),
    )
    return jax.shard_map(
        per_device,
        mesh=mesh,
        in_specs=placed,
        out_specs=(
            P("gx", "gy", None, None, None, None, None),
            P(None, None, "gx", "gy", None),
            P(),
            P(),
            P(),
            P(),
        ),
        check_vma=False,
    )
```

```python
import functools
import math

import jax
import jax.numpy as jnp
from jax import lax
from jax.experimental import pallas as pl
from jax.experimental.pallas import tpu as pltpu
from jax.sharding import PartitionSpec as P

GRIDC = 4
F32 = jnp.float32
BF16 = jnp.bfloat16
MIB = 1024 * 1024
STACK = 10
GELU_C = math.sqrt(2.0 / math.pi)
GELU_A = 0.044715


def dot(a, b, ca, cb):
    return lax.dot_general(a, b, (((ca,), (cb,)), ((), ())), preferred_element_type=F32)


def sides():
    return lax.axis_index("gx") % 2, lax.axis_index("gy") % 2


def write_pieces(row, s, Y, near, far, first, second):
    p, q = sides()
    for k, (x, plane) in enumerate(((1 - p, near), (p, far))):
        for y in range(Y):
            plane[s, y] = row(x, y)
        first[k, s] = row(x, (1 - q) * (Y - 1))
        second[k, s] = row(x, q * (Y - 1))


def piece_shapes(S, Y, C, Z):
    return [jax.ShapeDtypeStruct((S, Y, C, Z), BF16)] * 2 + [
        jax.ShapeDtypeStruct((2, S, C, Z), BF16)
    ] * 2


def params(mib):
    return pltpu.CompilerParams(vmem_limit_bytes=mib * MIB)


def in_vmem(n):
    return [pl.BlockSpec(memory_space=pltpu.VMEM)] * n


def swap_pairs(n, start):
    return [pair for i in range(start, n - 1, 2) for pair in ((i, i + 1), (i + 1, i))]


def swap_x(plane, start):
    return lax.ppermute(plane, "gx", swap_pairs(lax.axis_size("gx"), start))


def swap_y(rows, start):
    return lax.ppermute(rows, "gy", swap_pairs(lax.axis_size("gy"), start))


def halo_by_corners(pieces):
    near, far, first, second = pieces
    from_near, from_far = swap_x(near, 0), swap_x(far, 1)
    first, second = swap_y(first, 0), swap_y(second, 1)
    corner_far = swap_x(jnp.stack([first[1], second[1]]), 1)
    corner_near = swap_x(jnp.stack([first[0], second[0]]), 0)
    return [near, far, from_near, from_far, first, second, corner_near, corner_far]


def halo_by_planes(pieces):
    near, far, first, second = pieces
    from_near, from_far = swap_x(near, 0), swap_x(far, 1)
    _, q = sides()
    Y = near.shape[1]
    got = []
    for own, y, start in ((first, (1 - q) * (Y - 1), 0), (second, q * (Y - 1), 1)):
        rows = [
            lax.dynamic_index_in_dim(plane, y, 1, keepdims=False) for plane in (from_near, from_far)
        ]
        got.append(swap_y(jnp.concatenate([own, jnp.stack(rows)]), start))
    return [near, far, from_near, from_far, *got]


def fill_padded(planes, s, Fs):
    _, q = sides()
    for u, plane, (r0, k0), (r1, k1) in planes:
        Y = plane.shape[1]
        for y in range(Y):
            Fs[u * (Y + 2) + y + 1] = plane[s, y].astype(Fs.dtype)
        Fs[u * (Y + 2) + (1 - q) * (Y + 1)] = r0[k0, s].astype(Fs.dtype)
        Fs[u * (Y + 2) + q * (Y + 1)] = r1[k1, s].astype(Fs.dtype)


def fill_stack(Fs, FB, rows, Y):
    C, Z = Fs.shape[1:]
    for a in range(3):
        for b in range(3):
            at = (a * 3 + b) * C
            for r, (x, y) in enumerate(rows):
                row = Fs[(x + a) * (Y + 2) + y + b].astype(BF16)
                FB[at : at + C, r * Z : (r + 1) * Z] = row
    if FB.shape[0] > 9 * C:
        FB[9 * C :, :] = jnp.zeros((FB.shape[0] - 9 * C, FB.shape[1]), BF16)


def in_grid(x):
    p, _ = sides()
    return p if x else 1 - p


def from_left(value, lane):
    return jnp.where(lane == 0, 0.0, pltpu.roll(value, 1, 1))


def from_right(value, lane):
    Z = value.shape[1]
    return jnp.where(lane == Z - 1, 0.0, pltpu.roll(value, Z - 1, 1))


def conv_rows(taps, stack, C, Z, lane):
    acc = dot(taps, stack, 1, 0)
    rows = []
    for k in range(0, stack.shape[1], Z):
        left, mid, right = (acc[e * C : (e + 1) * C, k : k + Z] for e in range(3))
        rows.append(mid + from_left(left, lane) + from_right(right, lane))
    return rows


def conv_tiles(wb, Fs, Ds, rows, Y, lane):
    C, Z = Fs.shape[1:]
    for c in range(0, C, 8):
        weights = [wb[t, c : c + 8, :] for t in range(27)]
        for x, y in rows:
            acc = [None, None, None]
            for a in range(3):
                for b in range(3):
                    f = Fs[(x + a) * (Y + 2) + y + b, c : c + 8, :]
                    for e in range(3):
                        term = weights[(a * 3 + b) * 3 + e] * f
                        acc[e] = term if acc[e] is None else acc[e] + term
            total = acc[1] + from_left(acc[0], lane[:8]) + from_right(acc[2], lane[:8])
            Ds[c : c + 8, y * Z : (y + 1) * Z] = total


def split_kernel(X, Y, C, Z, f_ref, near, far, first, second, wide):
    wide[...] = f_ref[0].astype(F32)

    def row(x, y):
        return wide[pl.ds(x * Y + y, C, stride=X * Y), :].astype(BF16)

    write_pieces(row, pl.program_id(0), Y, near, far, first, second)


def z_permutation(Z):
    fine = lax.broadcasted_iota(jnp.int32, (2 * Z, 2 * Z), 0)
    coarse = lax.broadcasted_iota(jnp.int32, (2 * Z, 2 * Z), 1)
    inner = coarse % Z
    goes = coarse // Z + (inner % (Z // 2)) * 2 + (inner // (Z // 2)) * Z
    return jnp.where(fine == goes, 1.0, 0.0).astype(BF16)


def outward_taps(w_ref):
    p, _ = sides()
    mirrored = jnp.concatenate([w_ref[:, 18:27], w_ref[:, 9:18], w_ref[:, 0:9]], axis=1)
    return jnp.where(p == 1, w_ref[...], mirrored)


def early_kernel(dims, gd_ref, w_ref, wd_ref, gm_ref, wb, Mb):
    X, Y, C, Z, H, O = dims
    NP = Y // 4
    step = pl.program_id(0)

    @pl.when(step == 0)
    def _():
        taps = outward_taps(w_ref)
        for t in range(27):
            wb[t] = jnp.broadcast_to(taps[:, t : t + 1], (C, Z))

    perm = z_permutation(Z)
    for X0 in range(X // 2):
        gp = dot(wd_ref[...], gd_ref[step, X0], 1, 1).astype(BF16)
        for a in range(2):
            for b in range(2):
                for p in range(NP):
                    src = ((a * 2 + b) * 2) * C
                    dst = ((a * 2 + b) * NP + p) * C
                    for e in range(2):
                        Mb[dst : dst + C, e * Z : (e + 1) * Z] = gp[
                            src + e * C : src + (e + 1) * C, p * Z : (p + 1) * Z
                        ]
        gm = dot(Mb[...], perm, 1, 1).astype(BF16)
        for a in range(2):
            for b in range(2):
                for p in range(NP):
                    src = ((a * 2 + b) * NP + p) * C
                    for q in range(2):
                        y = 2 * (2 * p + q) + b
                        gm_ref[step, in_grid(a), y] = gm[src : src + C, q * Z : (q + 1) * Z]


def plane_work(x, samples, dims, ops, put_merged):
    X, Y, C, Z, H, O = dims
    gm_ref, wb, pinT_ref, pout_ref, grad_ref, aout, ain, atap = ops[:8]
    Fs, FB, Ds, Gs, pre_s, ga_s, act_s, gp_s, pin, poutT = ops[8:]
    lane = lax.broadcasted_iota(jnp.int32, (C, Z), 1)
    for g in range(len(samples)):
        fill_stack(Fs.at[g], FB.at[g], [(x, y) for y in range(Y)], Y)
        Gs[g, 3 * C :, :] = jnp.zeros((C, Gs.shape[2]), BF16)
    chunks = [(g, range(4 * i, 4 * i + 4)) for g in range(len(samples)) for i in range(Y // 4)]

    def columns(i):
        rows = chunks[i][1]
        return slice(rows[0] * Z, (rows[-1] + 1) * Z)

    def convolve(i):
        g, rows = chunks[i]
        conv_tiles(wb, Fs.at[g], Ds.at[g], [(x, y) for y in rows], Y, lane)

    def grad_merged(i):
        g, rows = chunks[i]
        return jnp.concatenate([gm_ref[samples[g], x, y] for y in rows], axis=1)

    def depth(i):
        return Ds[chunks[i][0], :, columns(i)].astype(BF16)

    def enter(i):
        pre_s[i] = dot(pin[...], depth(i), 1, 0)
        ga_s[i] = dot(poutT[...], grad_merged(i), 1, 0)

    def activate(i):
        for h0 in range(0, H, 16):
            hs = slice(h0, h0 + 16)
            pre = pre_s[i, hs, :]
            sq = pre * pre
            t = jnp.tanh(pre * (GELU_C + (GELU_C * GELU_A) * sq))
            h = 0.5 + 0.5 * t
            act = pre * h
            slope = h + act * (1.0 - h) * (2.0 * GELU_C + (6.0 * GELU_C * GELU_A) * sq)
            act_s[i, hs, :] = act.astype(BF16)
            gp_s[i, hs, :] = (ga_s[i, hs, :] * slope).astype(BF16)

    def leave(i):
        g, rows = chunks[i]
        grad_depth = dot(pinT_ref[...], gp_s[i], 1, 0).astype(BF16)
        branch = dot(pout_ref[...], act_s[i], 1, 0)
        for j, y in enumerate(rows):
            lanes = slice(j * Z, (j + 1) * Z)
            row = Fs[g, (x + 1) * (Y + 2) + y + 1]
            put_merged(g, y, (row + branch[:, lanes]).astype(BF16))
            grad_ref[samples[g], y] = grad_depth[:, lanes]
            value = grad_depth[:, lanes].astype(F32)
            shifted = from_right(value, lane), value, from_left(value, lane)
            for e, moved in enumerate(shifted):
                Gs[g, e * C : (e + 1) * C, y * Z : (y + 1) * Z] = moved.astype(BF16)
        aout[...] += dot(grad_merged(i), act_s[i], 1, 1)
        ain[...] += dot(depth(i), gp_s[i], 1, 1)
        atap[...] += dot(FB[g, :, columns(i)], Gs[g, :, columns(i)], 1, 1)

    last = len(chunks) - 1
    convolve(0)
    enter(0)
    convolve(1)
    activate(0)
    for i in range(last + 1):
        if i < last:
            enter(i + 1)
        leave(i)
        if i + 2 <= last:
            convolve(i + 2)
        if i < last:
            activate(i + 1)


def merged_place(x, y, Y, C, Z):
    start = ((in_grid(x) * 2 + y % 2) * (Y // 4) + y // 4) * C
    q = y // 2 % 2
    return pl.ds(pl.multiple_of(start, C), C), slice(q * Z, (q + 1) * Z)


def set_up(pinT_ref, pout_ref, pin, poutT):
    pin[...] = pinT_ref[...].astype(F32).T.astype(BF16)
    poutT[...] = pout_ref[...].astype(F32).T.astype(BF16)


def near_kernel(dims, *refs):
    X, Y, C, Z, H, O = dims
    from_near, near, far, first, second, corner, gm_ref, wb, pinT_ref, pout_ref = refs[:10]
    grad_ref, Mb, aout, ain, atap = refs[10:15]
    Fs, FB, Ds, Gs, pre_s, ga_s, act_s, gp_s, pin, poutT = refs[15:]
    step = pl.program_id(0)

    @pl.when(step == 0)
    def _():
        aout[...] = jnp.zeros_like(aout)
        ain[...] = jnp.zeros_like(ain)
        atap[...] = jnp.zeros_like(atap)
        set_up(pinT_ref, pout_ref, pin, poutT)

    planes = [
        (0, from_near, (corner, 0), (corner, 1)),
        (1, near, (first, 0), (second, 0)),
        (2, far, (first, 1), (second, 1)),
    ]
    samples = [step * Fs.shape[0] + g for g in range(Fs.shape[0])]
    for g, sample in enumerate(samples):
        fill_padded(planes, sample, Fs.at[g])

    def put_merged(g, y, value):
        rows, lanes = merged_place(0, y, Y, C, Z)
        Mb[samples[g], rows, lanes] = value

    ops = gm_ref, wb, pinT_ref, pout_ref, grad_ref, aout, ain, atap
    ops += Fs, FB, Ds, Gs, pre_s, ga_s, act_s, gp_s, pin, poutT
    plane_work(0, samples, dims, ops, put_merged)


def far_kernel(dims, *refs):
    X, Y, C, Z, H, O = dims
    NP = Y // 4
    near, far, from_far, first, second, corner, gm_ref, wb, pinT_ref, pout_ref = refs[:10]
    gd_ref, wd_ref, grad_near_ref, Mb_ref, aout_ref, ain_ref, atap_ref = refs[10:17]
    red_ref, near_ref, grad_ref, first_ref, second_ref, packed_ref = refs[17:23]
    Fs, FB, Ds, Gs, pre_s, ga_s, act_s, gp_s, pin, poutT = refs[23:33]
    Mb, Pt, atap, adown, aout, ain, rows_s = refs[33:]
    step = pl.program_id(0)

    @pl.when(step == 0)
    def _():
        aout[...] = aout_ref[...]
        ain[...] = ain_ref[...]
        atap[...] = atap_ref[...]
        adown[...] = jnp.zeros_like(adown)
        set_up(pinT_ref, pout_ref, pin, poutT)

    planes = [
        (1, near, (first, 0), (second, 0)),
        (2, far, (first, 1), (second, 1)),
        (3, from_far, (corner, 0), (corner, 1)),
    ]
    samples = [step * Fs.shape[0] + g for g in range(Fs.shape[0])]
    for g, sample in enumerate(samples):
        fill_padded(planes, sample, Fs.at[g])
        Mb[g] = Mb_ref[sample]
        near_ref[sample] = grad_near_ref[sample]

    def put_merged(g, y, value):
        rows, lanes = merged_place(1, y, Y, C, Z)
        Mb[g, rows, lanes] = value

    ops = gm_ref, wb, pinT_ref, pout_ref, grad_ref, aout, ain, atap
    ops += Fs, FB, Ds, Gs, pre_s, ga_s, act_s, gp_s, pin, poutT
    plane_work(1, samples, dims, ops, put_merged)

    _, q = sides()
    for g, sample in enumerate(samples):
        for k, plane in enumerate((grad_near_ref, grad_ref)):
            first_ref[k, sample] = plane[sample, (1 - q) * (Y - 1)]
            second_ref[k, sample] = plane[sample, q * (Y - 1)]
        pt = dot(Mb[g], z_permutation(Z), 1, 0).astype(BF16)
        for a in range(2):
            for b in range(2):
                for p in range(NP):
                    src = ((a * 2 + b) * NP + p) * C
                    for e in range(2):
                        dst = ((a * 2 + b) * 2 + e) * C
                        Pt[g, dst : dst + C, p * Z : (p + 1) * Z] = pt[
                            src : src + C, e * Z : (e + 1) * Z
                        ]
        red_ref[sample, 0] = dot(Pt[g], wd_ref[...], 0, 0).astype(BF16)
        adown[...] += dot(Pt[g], gd_ref[sample, 0], 1, 0)

    @pl.when(step == pl.num_programs(0) - 1)
    def _():
        rows_s[...] = jnp.zeros_like(rows_s)
        for k in range(8):
            rows_s[pl.ds(k, C, stride=8), :] = adown[k * C : (k + 1) * C, :]
        row = lax.broadcasted_iota(jnp.int32, (C, 4 * C), 0)
        column = lax.broadcasted_iota(jnp.int32, (C, 4 * C), 1)
        lines = []
        for ab in range(9):
            block = jnp.where(column % C == row, atap[ab * C : (ab + 1) * C, :], 0.0)
            lines.append(jnp.sum(block, axis=0, keepdims=True))
        p, _ = sides()
        at = 8 * C + 2 * C * (H // Z)
        for a in range(3):
            for b in range(3):
                line = jnp.where(p == 1, lines[a * 3 + b], lines[(2 - a) * 3 + b])
                for k in range(0, 4 * C, Z):
                    rows_s[at : at + 1, :] = line[:, k : k + Z]
                    at += 1
        packed_ref[: rows_s.shape[0], :] = rows_s[...].astype(BF16)
        at = 8 * C
        for part in (aout, ain):
            for k in range(0, H, Z):
                packed_ref[at : at + C, :] = part[:, k : k + Z].astype(BF16)
                at += C
        at = rows_s.shape[0]
        if at < packed_ref.shape[0]:
            rest = packed_ref.shape[0] - at
            packed_ref[at:, :] = jnp.zeros((rest, Z), BF16)


def adjoint_kernel(X, Y, C, Z, *refs):
    planes, (first, second) = refs[:4], refs[4:6]
    gm_ref, w_ref, out_ref, Fs, FB, wide, tap_ref = refs[6:]
    step = pl.program_id(0)

    @pl.when(step == 0)
    def _():
        taps = outward_taps(w_ref)
        row = lax.broadcasted_iota(jnp.int32, (C, STACK * C), 0)
        column = lax.broadcasted_iota(jnp.int32, (C, STACK * C), 1)
        for e in range(3):
            block = jnp.zeros((C, STACK * C), F32)
            for ab in range(9):
                t = 26 - (ab * 3 + e)
                block = jnp.where(column == row + ab * C, taps[:, t : t + 1], block)
            tap_ref[e * C : (e + 1) * C, :] = block.astype(BF16)

    places = (1, 2, 0, 3)
    widened = [(places[k], planes[k], (first, k), (second, k)) for k in range(4)]
    fill_padded(widened, step, Fs)
    cells = [(x, y) for x in range(X) for y in range(Y)]
    fill_stack(Fs, FB, cells, Y)
    lane = lax.broadcasted_iota(jnp.int32, (C, Z), 1)
    for r0 in range(0, X * Y, 4):
        rows = conv_rows(tap_ref[...], FB[:, r0 * Z : (r0 + 4) * Z], C, Z, lane)
        for (x, y), value in zip(cells[r0 : r0 + 4], rows):
            total = value + gm_ref[step, x, y].astype(F32)
            wide[pl.ds(in_grid(x) * Y + y, C, stride=X * Y), :] = total
    out_ref[0] = wide[...].astype(BF16)


def finish_kernel(C, Z, H, scale, every_ref, down_ref, out_ref, in_ref, taps_ref):
    down_ref[...] = every_ref[: 8 * C, :].astype(F32) * scale
    at = 8 * C
    for ref in (out_ref, in_ref):
        for k in range(0, H, Z):
            ref[:, k : k + Z] = every_ref[at : at + C, :].astype(F32) * scale
            at += C
    taps = every_ref[at : at + 32, :].astype(F32) * scale
    for a in range(3):
        for b in range(3):
            for e in range(3):
                line, k = divmod(e * C, Z)
                line += (a * 3 + b) * (4 * C // Z)
                taps_ref[a, b, e : e + 1, :] = taps[line : line + 1, k : k + C]


def sum_spread_kernel(parts_ref, out_ref):
    total = parts_ref[0].astype(F32)
    for i in range(1, parts_ref.shape[0]):
        total = total + parts_ref[i].astype(F32)
    total = total.astype(BF16)
    for j in range(out_ref.shape[0]):
        out_ref[j] = total


def sum_spread(parts, receivers):
    shape = (receivers,) + parts.shape[1:]
    return pl.pallas_call(
        sum_spread_kernel,
        in_specs=in_vmem(1),
        out_specs=in_vmem(1)[0],
        out_shape=jax.ShapeDtypeStruct(shape, BF16),
        compiler_params=params(4),
        name="sum_spread",
    )(parts)


def swap_in_group(blocks, axis):
    g = blocks.shape[0]
    if g == 1:
        return blocks
    n = lax.axis_size(axis)
    member = lax.axis_index(axis) % g
    got = [lax.dynamic_index_in_dim(blocks, member, 0, keepdims=False)]
    for k in range(1, g):
        out = lax.dynamic_index_in_dim(blocks, (member + k) % g, 0, keepdims=False)
        pairs = [(i, i - i % g + (i + k) % g) for i in range(n)]
        got.append(lax.ppermute(out, axis, pairs))
    if g == 2:
        first = member == 0
        return jnp.stack([jnp.where(first, got[0], got[1]), jnp.where(first, got[1], got[0])])
    got = jnp.stack(got)
    return jnp.take(got, (member - jnp.arange(g, dtype=jnp.int32)) % g, axis=0)


def per_device(fields, depth_kernel, point_in, point_out, down_kernel, cotangent):
    S, C, X, Y, Z = fields.shape
    assert X == 2 and Y % 4 == 0
    H, O = point_in.shape[0], down_kernel.shape[0]
    hx, hy, hz = X // 2, Y // 2, Z // 2
    nx, ny = lax.axis_size("gx"), lax.axis_size("gy")
    devices = nx * ny
    gx, gy = nx // GRIDC, ny // GRIDC
    per_group = S // (gx * gy)

    pieces = pl.pallas_call(
        functools.partial(split_kernel, X, Y, C, Z),
        grid=(S,),
        in_specs=[pl.BlockSpec((1, C * X * Y, Z), lambda s: (s, 0, 0))],
        out_specs=in_vmem(4),
        out_shape=piece_shapes(S, Y, C, Z),
        scratch_shapes=[pltpu.VMEM((C * X * Y, Z), F32)],
        compiler_params=params(6),
        name="split_fields",
    )(fields.reshape(S, C * X * Y, Z))


    moved = cotangent[0, 0].transpose(0, 2, 3, 4, 1)
    moved = moved.reshape(per_group, gx * hx, gy, hy * hz, O).transpose(2, 0, 1, 3, 4)
    moved = swap_in_group(moved, "gy").reshape(gy * per_group, gx, hx, hy * hz, O)
    moved = swap_in_group(moved.transpose(1, 0, 2, 3, 4), "gx")
    grad_down = moved.reshape(S, hx, hy * hz, O)

    widened = halo_by_corners(pieces)

    wd = down_kernel.transpose(2, 3, 4, 1, 0).reshape(8 * C, O)
    taps = depth_kernel.reshape(C, 27).astype(F32)

    rows = 8 * C + 2 * C * (H // Z) + 32
    chunk = -(-rows // (8 * nx)) * 8
    cells = X * Y * Z
    dims = (X, Y, C, Z, H, O)
    grad_merged, spread = pl.pallas_call(
        functools.partial(early_kernel, dims),
        grid=(S,),
        in_specs=in_vmem(3),
        out_specs=in_vmem(2),
        out_shape=[
            jax.ShapeDtypeStruct((S, X, Y, C, Z), BF16),
            jax.ShapeDtypeStruct((27, C, Z), F32),
        ],
        scratch_shapes=[pltpu.VMEM((Y * C, 2 * Z), BF16)],
        compiler_params=params(8),
        cost_estimate=pl.CostEstimate(
            flops=S * cells * (2 * C * O + 8 * C * Z),
            bytes_accessed=4 * S * cells * C + 4 * 27 * C * Z,
            transcendentals=0,
        ),
        name="early",
    )(grad_down, taps, wd)

    G = 2 if S % 2 == 0 else 1
    chunks = G * Y // 4
    scratch = [
        pltpu.VMEM((G, (X + 2) * (Y + 2), C, Z), F32),
        pltpu.VMEM((G, 9 * C, Y * Z), BF16),
        pltpu.VMEM((G, C, Y * Z), F32),
        pltpu.VMEM((G, 4 * C, Y * Z), BF16),
        pltpu.VMEM((chunks, H, 4 * Z), F32),
        pltpu.VMEM((chunks, H, 4 * Z), F32),
        pltpu.VMEM((chunks, H, 4 * Z), BF16),
        pltpu.VMEM((chunks, H, 4 * Z), BF16),
        pltpu.VMEM((H, C), BF16),
        pltpu.VMEM((H, C), BF16),
    ]
    sums = [(C, H), (C, H), (9 * C, 4 * C)]
    cost = pl.CostEstimate(
        flops=S * cells * (6 * C * H + 27 * C * 4 * C),
        bytes_accessed=8 * S * cells * C,
        transcendentals=S * cells * H // 2,
    )
    near, far, from_near, from_far, first, second, corner_near, corner_far = widened
    common = (first, second), (grad_merged, spread, point_in.T, point_out)
    grad_near, merged, *partial_sums = pl.pallas_call(
        functools.partial(near_kernel, dims),
        grid=(S // G,),
        in_specs=in_vmem(10),
        out_specs=in_vmem(5),
        out_shape=[
            jax.ShapeDtypeStruct((S, Y, C, Z), BF16),
            jax.ShapeDtypeStruct((S, Y * C, 2 * Z), BF16),
        ]
        + [jax.ShapeDtypeStruct(shape, F32) for shape in sums],
        scratch_shapes=scratch,
        compiler_params=params(17),
        cost_estimate=cost,
        name="near_side",
    )(from_near, near, far, *common[0], corner_near, *common[1])
    reduced, *grad_pieces, packed = pl.pallas_call(
        functools.partial(far_kernel, dims),
        grid=(S // G,),
        in_specs=in_vmem(17),
        out_specs=in_vmem(6),
        out_shape=[jax.ShapeDtypeStruct((S, hx, hy * hz, O), BF16)]
        + piece_shapes(S, Y, C, Z)
        + [jax.ShapeDtypeStruct((nx * chunk, Z), BF16)],
        scratch_shapes=scratch
        + [
            pltpu.VMEM((G, Y * C, 2 * Z), BF16),
            pltpu.VMEM((G, 8 * C, hy * hz), BF16),
            pltpu.VMEM((9 * C, 4 * C), F32),
            pltpu.VMEM((8 * C, O), F32),
            pltpu.VMEM((C, H), F32),
            pltpu.VMEM((C, H), F32),
            pltpu.VMEM((rows, Z), F32),
        ],
        compiler_params=params(21),
        cost_estimate=cost,
        name="far_side",
    )(
        *(near, far, from_far, first, second, corner_far, *common[1]),
        *(grad_down, wd, grad_near, merged, *partial_sums),
    )

    grad_widened = halo_by_planes(grad_pieces)

    parts = lax.all_to_all(packed.reshape(nx, chunk, Z), "gx", 0, 0)
    parts = lax.all_to_all(sum_spread(parts, ny), "gy", 0, 0)
    share = sum_spread(parts, nx)
    share, grad_widened[0] = lax.optimization_barrier((share, grad_widened[0]))
    every = lax.all_to_all(share, "gx", 0, 0).reshape(nx * chunk, Z)

    grad_fields = pl.pallas_call(
        functools.partial(adjoint_kernel, X, Y, C, Z),
        grid=(S,),
        in_specs=in_vmem(8),
        out_specs=pl.BlockSpec((1, C * X * Y, Z), lambda s: (s, 0, 0)),
        out_shape=jax.ShapeDtypeStruct((S, C * X * Y, Z), BF16),
        scratch_shapes=[
            pltpu.VMEM(((X + 2) * (Y + 2), C, Z), BF16),
            pltpu.VMEM((STACK * C, cells), BF16),
            pltpu.VMEM((C * X * Y, Z), F32),
            pltpu.VMEM((3 * C, STACK * C), BF16),
        ],
        compiler_params=params(14),
        cost_estimate=pl.CostEstimate(
            flops=S * cells * 2 * 27 * C, bytes_accessed=8 * S * cells * C, transcendentals=0
        ),
        name="adjoint",
    )(*grad_widened, grad_merged, taps).reshape(S, C, X, Y, Z)

    moved = swap_in_group(reduced.reshape(gx, S // gx, hx, hy * hz, O), "gx")
    moved = moved.transpose(1, 0, 2, 3, 4).reshape(gy, per_group, gx * hx, hy * hz, O)
    moved = swap_in_group(moved, "gy").transpose(1, 2, 0, 3, 4)
    coarse = moved.reshape(per_group, gx * hx, gy * hy, hz, O).transpose(0, 4, 1, 2, 3)[None, None]
    scale = 1.0 / math.sqrt(S * cells * devices)
    down, outw, inw, tapw = pl.pallas_call(
        functools.partial(finish_kernel, C, Z, H, scale),
        out_shape=[
            jax.ShapeDtypeStruct((8 * C, O), F32),
            jax.ShapeDtypeStruct((C, H), F32),
            jax.ShapeDtypeStruct((C, H), F32),
            jax.ShapeDtypeStruct((3, 3, 3, C), F32),
        ],
        in_specs=in_vmem(1),
        compiler_params=params(6),
        name="finish",
    )(every)
    return (
        coarse,
        grad_fields,
        tapw.transpose(3, 0, 1, 2),
        inw.T,
        outw,
        down.reshape(C, 2, 2, 2, O).transpose(4, 0, 1, 2, 3),
    )


def solution(mesh):
    placed = (
        P(None, None, "gx", "gy", None),
        P(),
        P(),
        P(),
        P(),
        P("gx", "gy", None, None, None, None, None),
    )
    return jax.shard_map(
        per_device,
        mesh=mesh,
        in_specs=placed,
        out_specs=(
            P("gx", "gy", None, None, None, None, None),
            P(None, None, "gx", "gy", None),
            P(),
            P(),
            P(),
            P(),
        ),
        check_vma=False,
    )
```

```python
import functools
import math

import jax
import jax.numpy as jnp
from jax import lax
from jax.experimental import pallas as pl
from jax.experimental.pallas import tpu as pltpu
from jax.sharding import PartitionSpec as P

GRIDC = 4
F32 = jnp.float32
BF16 = jnp.bfloat16
MIB = 1024 * 1024
STACK = 10
GELU_C = math.sqrt(2.0 / math.pi)
GELU_A = 0.044715


def dot(a, b, ca, cb):
    return lax.dot_general(a, b, (((ca,), (cb,)), ((), ())), preferred_element_type=F32)


def sides():
    return lax.axis_index("gx") % 2, lax.axis_index("gy") % 2


def write_pieces(row, s, Y, near, far, first, second):
    p, q = sides()
    for k, (x, plane) in enumerate(((1 - p, near), (p, far))):
        for y in range(Y):
            plane[s, y] = row(x, y)
        first[k, s] = row(x, (1 - q) * (Y - 1))
        second[k, s] = row(x, q * (Y - 1))


def piece_shapes(S, Y, C, Z):
    return [jax.ShapeDtypeStruct((S, Y, C, Z), BF16)] * 2 + [
        jax.ShapeDtypeStruct((2, S, C, Z), BF16)
    ] * 2


def params(mib):
    return pltpu.CompilerParams(vmem_limit_bytes=mib * MIB)


def in_vmem(n):
    return [pl.BlockSpec(memory_space=pltpu.VMEM)] * n


def swap_pairs(n, start):
    return [pair for i in range(start, n - 1, 2) for pair in ((i, i + 1), (i + 1, i))]


def swap_x(plane, start):
    return lax.ppermute(plane, "gx", swap_pairs(lax.axis_size("gx"), start))


def swap_y(rows, start):
    return lax.ppermute(rows, "gy", swap_pairs(lax.axis_size("gy"), start))


def halo_by_corners(pieces):
    near, far, first, second = pieces
    from_near, from_far = swap_x(near, 0), swap_x(far, 1)
    first, second = swap_y(first, 0), swap_y(second, 1)
    corner_far = swap_x(jnp.stack([first[1], second[1]]), 1)
    corner_near = swap_x(jnp.stack([first[0], second[0]]), 0)
    return [near, far, from_near, from_far, first, second, corner_near, corner_far]


def halo_by_planes(pieces):
    near, far, first, second = pieces
    from_near, from_far = swap_x(near, 0), swap_x(far, 1)
    _, q = sides()
    Y = near.shape[1]
    got = []
    for own, y, start in ((first, (1 - q) * (Y - 1), 0), (second, q * (Y - 1), 1)):
        rows = [
            lax.dynamic_index_in_dim(plane, y, 1, keepdims=False) for plane in (from_near, from_far)
        ]
        got.append(swap_y(jnp.concatenate([own, jnp.stack(rows)]), start))
    return [near, far, from_near, from_far, *got]


def fill_padded(planes, s, Fs):
    _, q = sides()
    for u, plane, (r0, k0), (r1, k1) in planes:
        Y = plane.shape[1]
        for y in range(Y):
            Fs[u * (Y + 2) + y + 1] = plane[s, y].astype(Fs.dtype)
        Fs[u * (Y + 2) + (1 - q) * (Y + 1)] = r0[k0, s].astype(Fs.dtype)
        Fs[u * (Y + 2) + q * (Y + 1)] = r1[k1, s].astype(Fs.dtype)


def fill_stack(Fs, FB, rows, Y):
    C, Z = Fs.shape[1:]
    for a in range(3):
        for b in range(3):
            at = (a * 3 + b) * C
            for r, (x, y) in enumerate(rows):
                row = Fs[(x + a) * (Y + 2) + y + b].astype(BF16)
                FB[at : at + C, r * Z : (r + 1) * Z] = row
    if FB.shape[0] > 9 * C:
        FB[9 * C :, :] = jnp.zeros((FB.shape[0] - 9 * C, FB.shape[1]), BF16)


def in_grid(x):
    p, _ = sides()
    return p if x else 1 - p


def from_left(value, lane):
    return jnp.where(lane == 0, 0.0, pltpu.roll(value, 1, 1))


def from_right(value, lane):
    Z = value.shape[1]
    return jnp.where(lane == Z - 1, 0.0, pltpu.roll(value, Z - 1, 1))


def conv_rows(taps, stack, C, Z, lane):
    acc = dot(taps, stack, 1, 0)
    rows = []
    for k in range(0, stack.shape[1], Z):
        left, mid, right = (acc[e * C : (e + 1) * C, k : k + Z] for e in range(3))
        rows.append(mid + from_left(left, lane) + from_right(right, lane))
    return rows


def conv_tile(wb, Fs, Ds, rows, Y, lane, c):
    Z = Fs.shape[2]
    weights = [wb[t, c : c + 8, :] for t in range(27)]
    for x, y in rows:
        acc = [None, None, None]
        for a in range(3):
            for b in range(3):
                f = Fs[(x + a) * (Y + 2) + y + b, c : c + 8, :]
                for e in range(3):
                    term = weights[(a * 3 + b) * 3 + e] * f
                    acc[e] = term if acc[e] is None else acc[e] + term
        total = acc[1] + from_left(acc[0], lane[:8]) + from_right(acc[2], lane[:8])
        Ds[c : c + 8, y * Z : (y + 1) * Z] = total


def split_kernel(X, Y, C, Z, f_ref, w_ref, near, far, first, second, taps_ref, wide):
    taps_ref[...] = outward_taps(w_ref)
    wide[...] = f_ref[0].astype(F32)

    def row(x, y):
        return wide[pl.ds(x * Y + y, C, stride=X * Y), :].astype(BF16)

    write_pieces(row, pl.program_id(0), Y, near, far, first, second)


def z_permutation(Z):
    fine = lax.broadcasted_iota(jnp.int32, (2 * Z, 2 * Z), 0)
    coarse = lax.broadcasted_iota(jnp.int32, (2 * Z, 2 * Z), 1)
    inner = coarse % Z
    goes = coarse // Z + (inner % (Z // 2)) * 2 + (inner // (Z // 2)) * Z
    return jnp.where(fine == goes, 1.0, 0.0).astype(BF16)


def outward_taps(w_ref):
    p, _ = sides()
    mirrored = jnp.concatenate([w_ref[:, 18:27], w_ref[:, 9:18], w_ref[:, 0:9]], axis=1)
    return jnp.where(p == 1, w_ref[...], mirrored)


def early_kernel(dims, gd_ref, w_ref, wd_ref, gm_ref, wb, Mb):
    X, Y, C, Z, H, O = dims
    NP = Y // 4
    step = pl.program_id(0)

    @pl.when(step == 0)
    def _():
        for t in range(27):
            wb[t] = jnp.broadcast_to(w_ref[:, t : t + 1], (C, Z))

    perm = z_permutation(Z)
    for X0 in range(X // 2):
        gp = dot(wd_ref[...], gd_ref[step, X0], 1, 1).astype(BF16)
        for a in range(2):
            for b in range(2):
                for p in range(NP):
                    src = ((a * 2 + b) * 2) * C
                    dst = ((a * 2 + b) * NP + p) * C
                    for e in range(2):
                        Mb[dst : dst + C, e * Z : (e + 1) * Z] = gp[
                            src + e * C : src + (e + 1) * C, p * Z : (p + 1) * Z
                        ]
        gm = dot(Mb[...], perm, 1, 1).astype(BF16)
        for a in range(2):
            for b in range(2):
                for p in range(NP):
                    src = ((a * 2 + b) * NP + p) * C
                    for q in range(2):
                        y = 2 * (2 * p + q) + b
                        gm_ref[step, in_grid(a), y] = gm[src : src + C, q * Z : (q + 1) * Z]


def plane_work(x, samples, dims, ops, put_merged):
    X, Y, C, Z, H, O = dims
    gm_ref, wb, pinT_ref, pout_ref, grad_ref, aout, ain, atap = ops[:8]
    Fs, FB, Ds, Gs, pre_s, ga_s, act_s, gp_s, pin, poutT = ops[8:]
    lane = lax.broadcasted_iota(jnp.int32, (C, Z), 1)
    for g in range(len(samples)):
        fill_stack(Fs.at[g], FB.at[g], [(x, y) for y in range(Y)], Y)
        Gs[g, 3 * C :, :] = jnp.zeros((C, Gs.shape[2]), BF16)
    chunks = [(g, range(4 * i, 4 * i + 4)) for g in range(len(samples)) for i in range(Y // 4)]

    def convolve(i):
        g, rows = chunks[i]
        cells = [(x, y) for y in rows]

        def tile(c):
            conv_tile(wb, Fs.at[g], Ds.at[g], cells, Y, lane, c)

        return [functools.partial(tile, c) for c in range(0, C, 8)]

    def grad_merged(i, part=slice(None)):
        g, rows = chunks[i]
        return jnp.concatenate([gm_ref[samples[g], x, y] for y in rows[part]], axis=1)

    def depth(i, lanes):
        g, rows = chunks[i]
        first = rows[0] * Z
        return Ds[g, :, first + lanes.start : first + lanes.stop].astype(BF16)

    halves = [(slice(0, 2), slice(0, 2 * Z)), (slice(2, 4), slice(2 * Z, 4 * Z))]

    def enter(i):
        def pre(lanes):
            pre_s[i, :, lanes] = dot(pin[...], depth(i, lanes), 1, 0)

        def ga(part, lanes):
            ga_s[i, :, lanes] = dot(poutT[...], grad_merged(i, part), 1, 0)

        steps = []
        for part, lanes in halves:
            steps += [functools.partial(pre, lanes), functools.partial(ga, part, lanes)]
        return steps

    def activate(i):
        def block(h0):
            hs = slice(h0, h0 + 16)
            pre = pre_s[i, hs, :]
            sq = pre * pre
            t = jnp.tanh(pre * (GELU_C + (GELU_C * GELU_A) * sq))
            h = 0.5 + 0.5 * t
            act = pre * h
            slope = h + act * (1.0 - h) * (2.0 * GELU_C + (6.0 * GELU_C * GELU_A) * sq)
            act_s[i, hs, :] = act.astype(BF16)
            gp_s[i, hs, :] = (ga_s[i, hs, :] * slope).astype(BF16)

        return [functools.partial(block, h0) for h0 in range(0, H, 16)]

    def leave(i):
        g, rows = chunks[i]

        def backward(part, lanes):
            grad_depth = dot(pinT_ref[...], gp_s[i, :, lanes], 1, 0).astype(BF16)
            for j, y in enumerate(rows[part]):
                row = grad_depth[:, j * Z : (j + 1) * Z]
                grad_ref[samples[g], y] = row
                value = row.astype(F32)
                shifted = from_right(value, lane), value, from_left(value, lane)
                for e, moved in enumerate(shifted):
                    Gs[g, e * C : (e + 1) * C, y * Z : (y + 1) * Z] = moved.astype(BF16)

        def forward(part, lanes):
            branch = dot(pout_ref[...], act_s[i, :, lanes], 1, 0)
            for j, y in enumerate(rows[part]):
                row = Fs[g, (x + 1) * (Y + 2) + y + 1]
                put_merged(g, y, (row + branch[:, j * Z : (j + 1) * Z]).astype(BF16))

        def out_sum():
            aout[...] += dot(grad_merged(i), act_s[i], 1, 1)

        def in_sum():
            ain[...] += dot(depth(i, slice(0, 4 * Z)), gp_s[i], 1, 1)

        def tap_sum():
            columns = slice(rows[0] * Z, (rows[-1] + 1) * Z)
            atap[...] += dot(FB[g, :, columns], Gs[g, :, columns], 1, 1)

        steps = [functools.partial(backward, *half) for half in halves]
        steps += [functools.partial(forward, *half) for half in halves]
        return steps + [out_sum, in_sum, tap_sum]

    def alternate(products, others):
        order = [((k + 0.5) / len(part), n, step) for n, part in enumerate((products, others))
                 for k, step in enumerate(part)]
        for _, _, step in sorted(order, key=lambda entry: entry[:2]):
            step()

    last = len(chunks) - 1
    alternate([], convolve(0))
    alternate(enter(0), convolve(1))
    alternate([], activate(0))
    for i in range(last + 1):
        alternate(enter(i + 1) if i < last else [], convolve(i + 2) if i + 2 <= last else [])
        alternate(leave(i), activate(i + 1) if i < last else [])


def merged_place(x, y, Y, C, Z):
    start = ((in_grid(x) * 2 + y % 2) * (Y // 4) + y // 4) * C
    q = y // 2 % 2
    return pl.ds(pl.multiple_of(start, C), C), slice(q * Z, (q + 1) * Z)


def set_up(pinT_ref, pout_ref, pin, poutT):
    pin[...] = pinT_ref[...].astype(F32).T.astype(BF16)
    poutT[...] = pout_ref[...].astype(F32).T.astype(BF16)


def near_kernel(dims, *refs):
    X, Y, C, Z, H, O = dims
    from_near, near, far, first, second, corner, gm_ref, wb, pinT_ref, pout_ref = refs[:10]
    grad_ref, Mb, aout, ain, atap = refs[10:15]
    Fs, FB, Ds, Gs, pre_s, ga_s, act_s, gp_s, pin, poutT = refs[15:]
    step = pl.program_id(0)

    @pl.when(step == 0)
    def _():
        aout[...] = jnp.zeros_like(aout)
        ain[...] = jnp.zeros_like(ain)
        atap[...] = jnp.zeros_like(atap)
        set_up(pinT_ref, pout_ref, pin, poutT)

    planes = [
        (0, from_near, (corner, 0), (corner, 1)),
        (1, near, (first, 0), (second, 0)),
        (2, far, (first, 1), (second, 1)),
    ]
    samples = [step * Fs.shape[0] + g for g in range(Fs.shape[0])]
    for g, sample in enumerate(samples):
        fill_padded(planes, sample, Fs.at[g])

    def put_merged(g, y, value):
        rows, lanes = merged_place(0, y, Y, C, Z)
        Mb[samples[g], rows, lanes] = value

    ops = gm_ref, wb, pinT_ref, pout_ref, grad_ref, aout, ain, atap
    ops += Fs, FB, Ds, Gs, pre_s, ga_s, act_s, gp_s, pin, poutT
    plane_work(0, samples, dims, ops, put_merged)


def far_kernel(dims, *refs):
    X, Y, C, Z, H, O = dims
    NP = Y // 4
    near, far, from_far, first, second, corner, gm_ref, wb, pinT_ref, pout_ref = refs[:10]
    gd_ref, wd_ref, grad_near_ref, Mb_ref, aout_ref, ain_ref, atap_ref = refs[10:17]
    red_ref, near_ref, grad_ref, first_ref, second_ref, packed_ref = refs[17:23]
    Fs, FB, Ds, Gs, pre_s, ga_s, act_s, gp_s, pin, poutT = refs[23:33]
    Mb, Pt, atap, adown, aout, ain, rows_s = refs[33:]
    step = pl.program_id(0)

    @pl.when(step == 0)
    def _():
        aout[...] = aout_ref[...]
        ain[...] = ain_ref[...]
        atap[...] = atap_ref[...]
        adown[...] = jnp.zeros_like(adown)
        set_up(pinT_ref, pout_ref, pin, poutT)

    planes = [
        (1, near, (first, 0), (second, 0)),
        (2, far, (first, 1), (second, 1)),
        (3, from_far, (corner, 0), (corner, 1)),
    ]
    samples = [step * Fs.shape[0] + g for g in range(Fs.shape[0])]
    for g, sample in enumerate(samples):
        fill_padded(planes, sample, Fs.at[g])
        Mb[g] = Mb_ref[sample]
        near_ref[sample] = grad_near_ref[sample]

    def put_merged(g, y, value):
        rows, lanes = merged_place(1, y, Y, C, Z)
        Mb[g, rows, lanes] = value

    ops = gm_ref, wb, pinT_ref, pout_ref, grad_ref, aout, ain, atap
    ops += Fs, FB, Ds, Gs, pre_s, ga_s, act_s, gp_s, pin, poutT
    plane_work(1, samples, dims, ops, put_merged)

    _, q = sides()
    for g, sample in enumerate(samples):
        for k, plane in enumerate((grad_near_ref, grad_ref)):
            first_ref[k, sample] = plane[sample, (1 - q) * (Y - 1)]
            second_ref[k, sample] = plane[sample, q * (Y - 1)]
        pt = dot(Mb[g], z_permutation(Z), 1, 0).astype(BF16)
        for a in range(2):
            for b in range(2):
                for p in range(NP):
                    src = ((a * 2 + b) * NP + p) * C
                    for e in range(2):
                        dst = ((a * 2 + b) * 2 + e) * C
                        Pt[g, dst : dst + C, p * Z : (p + 1) * Z] = pt[
                            src : src + C, e * Z : (e + 1) * Z
                        ]
        red_ref[sample, 0] = dot(Pt[g], wd_ref[...], 0, 0).astype(BF16)
        adown[...] += dot(Pt[g], gd_ref[sample, 0], 1, 0)

    @pl.when(step == pl.num_programs(0) - 1)
    def _():
        rows_s[...] = jnp.zeros_like(rows_s)
        for k in range(8):
            rows_s[pl.ds(k, C, stride=8), :] = adown[k * C : (k + 1) * C, :]
        row = lax.broadcasted_iota(jnp.int32, (C, 4 * C), 0)
        column = lax.broadcasted_iota(jnp.int32, (C, 4 * C), 1)
        lines = []
        for ab in range(9):
            block = jnp.where(column % C == row, atap[ab * C : (ab + 1) * C, :], 0.0)
            lines.append(jnp.sum(block, axis=0, keepdims=True))
        p, _ = sides()
        at = 8 * C + 2 * C * (H // Z)
        for a in range(3):
            for b in range(3):
                line = jnp.where(p == 1, lines[a * 3 + b], lines[(2 - a) * 3 + b])
                for k in range(0, 4 * C, Z):
                    rows_s[at : at + 1, :] = line[:, k : k + Z]
                    at += 1
        packed_ref[: rows_s.shape[0], :] = rows_s[...].astype(BF16)
        at = 8 * C
        for part in (aout, ain):
            for k in range(0, H, Z):
                packed_ref[at : at + C, :] = part[:, k : k + Z].astype(BF16)
                at += C
        at = rows_s.shape[0]
        if at < packed_ref.shape[0]:
            rest = packed_ref.shape[0] - at
            packed_ref[at:, :] = jnp.zeros((rest, Z), BF16)


def adjoint_kernel(X, Y, C, Z, *refs):
    planes, (first, second) = refs[:4], refs[4:6]
    gm_ref, w_ref, out_ref, Fs, FB, wide, tap_ref = refs[6:]
    step = pl.program_id(0)

    @pl.when(step == 0)
    def _():
        row = lax.broadcasted_iota(jnp.int32, (C, STACK * C), 0)
        column = lax.broadcasted_iota(jnp.int32, (C, STACK * C), 1)
        for e in range(3):
            block = jnp.zeros((C, STACK * C), F32)
            for ab in range(9):
                t = 26 - (ab * 3 + e)
                block = jnp.where(column == row + ab * C, w_ref[:, t : t + 1], block)
            tap_ref[e * C : (e + 1) * C, :] = block.astype(BF16)

    places = (1, 2, 0, 3)
    widened = [(places[k], planes[k], (first, k), (second, k)) for k in range(4)]
    fill_padded(widened, step, Fs)
    cells = [(x, y) for x in range(X) for y in range(Y)]
    fill_stack(Fs, FB, cells, Y)
    lane = lax.broadcasted_iota(jnp.int32, (C, Z), 1)
    for r0 in range(0, X * Y, 4):
        rows = conv_rows(tap_ref[...], FB[:, r0 * Z : (r0 + 4) * Z], C, Z, lane)
        for (x, y), value in zip(cells[r0 : r0 + 4], rows):
            total = value + gm_ref[step, x, y].astype(F32)
            wide[pl.ds(in_grid(x) * Y + y, C, stride=X * Y), :] = total
    out_ref[0] = wide[...].astype(BF16)


def finish_kernel(C, Z, H, scale, every_ref, down_ref, out_ref, in_ref, taps_ref):
    down_ref[...] = every_ref[: 8 * C, :].astype(F32) * scale
    at = 8 * C
    for ref in (out_ref, in_ref):
        for k in range(0, H, Z):
            ref[:, k : k + Z] = every_ref[at : at + C, :].astype(F32) * scale
            at += C
    taps = every_ref[at : at + 32, :].astype(F32) * scale
    for a in range(3):
        for b in range(3):
            for e in range(3):
                line, k = divmod(e * C, Z)
                line += (a * 3 + b) * (4 * C // Z)
                taps_ref[a, b, e : e + 1, :] = taps[line : line + 1, k : k + C]


def sum_spread_kernel(parts_ref, out_ref):
    total = parts_ref[0].astype(F32)
    for i in range(1, parts_ref.shape[0]):
        total = total + parts_ref[i].astype(F32)
    total = total.astype(BF16)
    for j in range(out_ref.shape[0]):
        out_ref[j] = total


def sum_spread(parts, receivers):
    shape = (receivers,) + parts.shape[1:]
    return pl.pallas_call(
        sum_spread_kernel,
        in_specs=in_vmem(1),
        out_specs=in_vmem(1)[0],
        out_shape=jax.ShapeDtypeStruct(shape, BF16),
        compiler_params=params(4),
        name="sum_spread",
    )(parts)


def swap_in_group(blocks, axis):
    g = blocks.shape[0]
    if g == 1:
        return blocks
    n = lax.axis_size(axis)
    member = lax.axis_index(axis) % g
    got = [lax.dynamic_index_in_dim(blocks, member, 0, keepdims=False)]
    for k in range(1, g):
        out = lax.dynamic_index_in_dim(blocks, (member + k) % g, 0, keepdims=False)
        pairs = [(i, i - i % g + (i + k) % g) for i in range(n)]
        got.append(lax.ppermute(out, axis, pairs))
    if g == 2:
        first = member == 0
        return jnp.stack([jnp.where(first, got[0], got[1]), jnp.where(first, got[1], got[0])])
    got = jnp.stack(got)
    return jnp.take(got, (member - jnp.arange(g, dtype=jnp.int32)) % g, axis=0)


def per_device(fields, depth_kernel, point_in, point_out, down_kernel, cotangent):
    S, C, X, Y, Z = fields.shape
    assert X == 2 and Y % 4 == 0
    H, O = point_in.shape[0], down_kernel.shape[0]
    hx, hy, hz = X // 2, Y // 2, Z // 2
    nx, ny = lax.axis_size("gx"), lax.axis_size("gy")
    devices = nx * ny
    gx, gy = nx // GRIDC, ny // GRIDC
    per_group = S // (gx * gy)

    *pieces, taps = pl.pallas_call(
        functools.partial(split_kernel, X, Y, C, Z),
        grid=(S,),
        in_specs=[pl.BlockSpec((1, C * X * Y, Z), lambda s: (s, 0, 0)), *in_vmem(1)],
        out_specs=in_vmem(5),
        out_shape=piece_shapes(S, Y, C, Z) + [jax.ShapeDtypeStruct((C, 27), F32)],
        scratch_shapes=[pltpu.VMEM((C * X * Y, Z), F32)],
        compiler_params=params(6),
        name="split_fields",
    )(fields.reshape(S, C * X * Y, Z), depth_kernel.reshape(C, 27).astype(F32))


    moved = cotangent[0, 0].transpose(0, 2, 3, 4, 1)
    moved = moved.reshape(per_group, gx * hx, gy, hy * hz, O).transpose(2, 0, 1, 3, 4)
    moved = swap_in_group(moved, "gy").reshape(gy * per_group, gx, hx, hy * hz, O)
    moved = swap_in_group(moved.transpose(1, 0, 2, 3, 4), "gx")
    grad_down = moved.reshape(S, hx, hy * hz, O)

    widened = halo_by_corners(pieces)

    wd = down_kernel.transpose(2, 3, 4, 1, 0).reshape(8 * C, O)

    rows = 8 * C + 2 * C * (H // Z) + 32
    chunk = -(-rows // (8 * nx)) * 8
    cells = X * Y * Z
    dims = (X, Y, C, Z, H, O)
    grad_merged, spread = pl.pallas_call(
        functools.partial(early_kernel, dims),
        grid=(S,),
        in_specs=in_vmem(3),
        out_specs=in_vmem(2),
        out_shape=[
            jax.ShapeDtypeStruct((S, X, Y, C, Z), BF16),
            jax.ShapeDtypeStruct((27, C, Z), F32),
        ],
        scratch_shapes=[pltpu.VMEM((Y * C, 2 * Z), BF16)],
        compiler_params=params(8),
        cost_estimate=pl.CostEstimate(
            flops=S * cells * (2 * C * O + 8 * C * Z),
            bytes_accessed=4 * S * cells * C + 4 * 27 * C * Z,
            transcendentals=0,
        ),
        name="early",
    )(grad_down, taps, wd)

    G = 2 if S % 2 == 0 else 1
    chunks = G * Y // 4
    scratch = [
        pltpu.VMEM((G, (X + 2) * (Y + 2), C, Z), F32),
        pltpu.VMEM((G, 9 * C, Y * Z), BF16),
        pltpu.VMEM((G, C, Y * Z), F32),
        pltpu.VMEM((G, 4 * C, Y * Z), BF16),
        pltpu.VMEM((chunks, H, 4 * Z), F32),
        pltpu.VMEM((chunks, H, 4 * Z), F32),
        pltpu.VMEM((chunks, H, 4 * Z), BF16),
        pltpu.VMEM((chunks, H, 4 * Z), BF16),
        pltpu.VMEM((H, C), BF16),
        pltpu.VMEM((H, C), BF16),
    ]
    sums = [(C, H), (C, H), (9 * C, 4 * C)]
    cost = pl.CostEstimate(
        flops=S * cells * (6 * C * H + 27 * C * 4 * C),
        bytes_accessed=8 * S * cells * C,
        transcendentals=S * cells * H // 2,
    )
    near, far, from_near, from_far, first, second, corner_near, corner_far = widened
    common = (first, second), (grad_merged, spread, point_in.T, point_out)
    grad_near, merged, *partial_sums = pl.pallas_call(
        functools.partial(near_kernel, dims),
        grid=(S // G,),
        in_specs=in_vmem(10),
        out_specs=in_vmem(5),
        out_shape=[
            jax.ShapeDtypeStruct((S, Y, C, Z), BF16),
            jax.ShapeDtypeStruct((S, Y * C, 2 * Z), BF16),
        ]
        + [jax.ShapeDtypeStruct(shape, F32) for shape in sums],
        scratch_shapes=scratch,
        compiler_params=params(17),
        cost_estimate=cost,
        name="near_side",
    )(from_near, near, far, *common[0], corner_near, *common[1])
    reduced, *grad_pieces, packed = pl.pallas_call(
        functools.partial(far_kernel, dims),
        grid=(S // G,),
        in_specs=in_vmem(17),
        out_specs=in_vmem(6),
        out_shape=[jax.ShapeDtypeStruct((S, hx, hy * hz, O), BF16)]
        + piece_shapes(S, Y, C, Z)
        + [jax.ShapeDtypeStruct((nx * chunk, Z), BF16)],
        scratch_shapes=scratch
        + [
            pltpu.VMEM((G, Y * C, 2 * Z), BF16),
            pltpu.VMEM((G, 8 * C, hy * hz), BF16),
            pltpu.VMEM((9 * C, 4 * C), F32),
            pltpu.VMEM((8 * C, O), F32),
            pltpu.VMEM((C, H), F32),
            pltpu.VMEM((C, H), F32),
            pltpu.VMEM((rows, Z), F32),
        ],
        compiler_params=params(21),
        cost_estimate=cost,
        name="far_side",
    )(
        *(near, far, from_far, first, second, corner_far, *common[1]),
        *(grad_down, wd, grad_near, merged, *partial_sums),
    )

    grad_widened = halo_by_planes(grad_pieces)

    parts = lax.all_to_all(packed.reshape(nx, chunk, Z), "gx", 0, 0)
    parts = lax.all_to_all(sum_spread(parts, ny), "gy", 0, 0)
    share = sum_spread(parts, nx)
    share, grad_widened[0] = lax.optimization_barrier((share, grad_widened[0]))
    every = lax.all_to_all(share, "gx", 0, 0).reshape(nx * chunk, Z)

    grad_fields = pl.pallas_call(
        functools.partial(adjoint_kernel, X, Y, C, Z),
        grid=(S,),
        in_specs=in_vmem(8),
        out_specs=pl.BlockSpec((1, C * X * Y, Z), lambda s: (s, 0, 0)),
        out_shape=jax.ShapeDtypeStruct((S, C * X * Y, Z), BF16),
        scratch_shapes=[
            pltpu.VMEM(((X + 2) * (Y + 2), C, Z), BF16),
            pltpu.VMEM((STACK * C, cells), BF16),
            pltpu.VMEM((C * X * Y, Z), F32),
            pltpu.VMEM((3 * C, STACK * C), BF16),
        ],
        compiler_params=params(14),
        cost_estimate=pl.CostEstimate(
            flops=S * cells * 2 * 27 * C, bytes_accessed=8 * S * cells * C, transcendentals=0
        ),
        name="adjoint",
    )(*grad_widened, grad_merged, taps).reshape(S, C, X, Y, Z)

    moved = swap_in_group(reduced.reshape(gx, S // gx, hx, hy * hz, O), "gx")
    moved = moved.transpose(1, 0, 2, 3, 4).reshape(gy, per_group, gx * hx, hy * hz, O)
    moved = swap_in_group(moved, "gy").transpose(1, 2, 0, 3, 4)
    coarse = moved.reshape(per_group, gx * hx, gy * hy, hz, O).transpose(0, 4, 1, 2, 3)[None, None]
    scale = 1.0 / math.sqrt(S * cells * devices)
    down, outw, inw, tapw = pl.pallas_call(
        functools.partial(finish_kernel, C, Z, H, scale),
        out_shape=[
            jax.ShapeDtypeStruct((8 * C, O), F32),
            jax.ShapeDtypeStruct((C, H), F32),
            jax.ShapeDtypeStruct((C, H), F32),
            jax.ShapeDtypeStruct((3, 3, 3, C), F32),
        ],
        in_specs=in_vmem(1),
        compiler_params=params(6),
        name="finish",
    )(every)
    return (
        coarse,
        grad_fields,
        tapw.transpose(3, 0, 1, 2),
        inw.T,
        outw,
        down.reshape(C, 2, 2, 2, O).transpose(4, 0, 1, 2, 3),
    )


def solution(mesh):
    placed = (
        P(None, None, "gx", "gy", None),
        P(),
        P(),
        P(),
        P(),
        P("gx", "gy", None, None, None, None, None),
    )
    return jax.shard_map(
        per_device,
        mesh=mesh,
        in_specs=placed,
        out_specs=(
            P("gx", "gy", None, None, None, None, None),
            P(None, None, "gx", "gy", None),
            P(),
            P(),
            P(),
            P(),
        ),
        check_vma=False,
    )
```

```python
import functools
import math

import jax
import jax.numpy as jnp
from jax import lax
from jax.experimental import pallas as pl
from jax.experimental.pallas import tpu as pltpu
from jax.sharding import PartitionSpec as P

GRIDC = 4
F32 = jnp.float32
BF16 = jnp.bfloat16
MIB = 1024 * 1024
STACK = 10
GELU_C = math.sqrt(2.0 / math.pi)
GELU_A = 0.044715


def dot(a, b, ca, cb):
    return lax.dot_general(a, b, (((ca,), (cb,)), ((), ())), preferred_element_type=F32)


def sides():
    return lax.axis_index("gx") % 2, lax.axis_index("gy") % 2


def write_pieces(row, s, Y, near, far, first, second):
    p, q = sides()
    for k, (x, plane) in enumerate(((1 - p, near), (p, far))):
        for y in range(Y):
            plane[s, y] = row(x, y)
        first[k, s] = row(x, (1 - q) * (Y - 1))
        second[k, s] = row(x, q * (Y - 1))


def piece_shapes(S, Y, C, Z):
    return [jax.ShapeDtypeStruct((S, Y, C, Z), BF16)] * 2 + [
        jax.ShapeDtypeStruct((2, S, C, Z), BF16)
    ] * 2


def params(mib):
    return pltpu.CompilerParams(vmem_limit_bytes=mib * MIB)


def in_vmem(n):
    return [pl.BlockSpec(memory_space=pltpu.VMEM)] * n


def swap_pairs(n, start):
    return [pair for i in range(start, n - 1, 2) for pair in ((i, i + 1), (i + 1, i))]


def swap_x(plane, start):
    return lax.ppermute(plane, "gx", swap_pairs(lax.axis_size("gx"), start))


def swap_y(rows, start):
    return lax.ppermute(rows, "gy", swap_pairs(lax.axis_size("gy"), start))


def halo_by_corners(pieces):
    near, far, first, second = pieces
    from_near, from_far = swap_x(near, 0), swap_x(far, 1)
    first, second = swap_y(first, 0), swap_y(second, 1)
    corner_far = swap_x(jnp.stack([first[1], second[1]]), 1)
    corner_near = swap_x(jnp.stack([first[0], second[0]]), 0)
    return [near, far, from_near, from_far, first, second, corner_near, corner_far]


def halo_by_planes(pieces):
    near, far, first, second = pieces
    from_near, from_far = swap_x(near, 0), swap_x(far, 1)
    _, q = sides()
    Y = near.shape[1]
    got = []
    for own, y, start in ((first, (1 - q) * (Y - 1), 0), (second, q * (Y - 1), 1)):
        rows = [
            lax.dynamic_index_in_dim(plane, y, 1, keepdims=False) for plane in (from_near, from_far)
        ]
        got.append(swap_y(jnp.concatenate([own, jnp.stack(rows)]), start))
    return [near, far, from_near, from_far, *got]


def fill_padded(planes, s, Fs):
    _, q = sides()
    for u, plane, (r0, k0), (r1, k1) in planes:
        Y = plane.shape[1]
        for y in range(Y):
            Fs[u * (Y + 2) + y + 1] = plane[s, y].astype(Fs.dtype)
        Fs[u * (Y + 2) + (1 - q) * (Y + 1)] = r0[k0, s].astype(Fs.dtype)
        Fs[u * (Y + 2) + q * (Y + 1)] = r1[k1, s].astype(Fs.dtype)


def fill_stack(Fs, FB, rows, Y):
    C, Z = Fs.shape[1:]
    for a in range(3):
        for b in range(3):
            at = (a * 3 + b) * C
            for r, (x, y) in enumerate(rows):
                row = Fs[(x + a) * (Y + 2) + y + b].astype(BF16)
                FB[at : at + C, r * Z : (r + 1) * Z] = row
    if FB.shape[0] > 9 * C:
        FB[9 * C :, :] = jnp.zeros((FB.shape[0] - 9 * C, FB.shape[1]), BF16)


def in_grid(x):
    p, _ = sides()
    return p if x else 1 - p


def from_left(value, lane):
    return jnp.where(lane == 0, 0.0, pltpu.roll(value, 1, 1))


def from_right(value, lane):
    Z = value.shape[1]
    return jnp.where(lane == Z - 1, 0.0, pltpu.roll(value, Z - 1, 1))


def conv_rows(taps, stack, C, Z, lane):
    acc = dot(taps, stack, 1, 0)
    rows = []
    for k in range(0, stack.shape[1], Z):
        left, mid, right = (acc[e * C : (e + 1) * C, k : k + Z] for e in range(3))
        rows.append(mid + from_left(left, lane) + from_right(right, lane))
    return rows


def conv_tile(wb, Fs, Ds, rows, Y, lane, c):
    Z = Fs.shape[2]
    weights = [wb[t, c : c + 8, :] for t in range(27)]
    for x, y in rows:
        acc = [None, None, None]
        for a in range(3):
            for b in range(3):
                f = Fs[(x + a) * (Y + 2) + y + b, c : c + 8, :]
                for e in range(3):
                    term = weights[(a * 3 + b) * 3 + e] * f
                    acc[e] = term if acc[e] is None else acc[e] + term
        total = acc[1] + from_left(acc[0], lane[:8]) + from_right(acc[2], lane[:8])
        Ds[c : c + 8, y * Z : (y + 1) * Z] = total


def split_kernel(X, Y, C, Z, f_ref, near, far, first, second, wide):
    wide[...] = f_ref[0].astype(F32)

    def row(x, y):
        return wide[pl.ds(x * Y + y, C, stride=X * Y), :].astype(BF16)

    write_pieces(row, pl.program_id(0), Y, near, far, first, second)


def z_permutation(Z):
    fine = lax.broadcasted_iota(jnp.int32, (2 * Z, 2 * Z), 0)
    coarse = lax.broadcasted_iota(jnp.int32, (2 * Z, 2 * Z), 1)
    inner = coarse % Z
    goes = coarse // Z + (inner % (Z // 2)) * 2 + (inner // (Z // 2)) * Z
    return jnp.where(fine == goes, 1.0, 0.0).astype(BF16)


def outward_tap(w_ref, a, b, e):
    p, _ = sides()
    here, mirrored = (w_ref[x, b, e : e + 1, :].astype(F32) for x in (a, 2 - a))
    return jnp.where(p == 1, here, mirrored)


def early_kernel(dims, gd_ref, w_ref, wd_ref, gm_ref, wb, Mb):
    X, Y, C, Z, H, O = dims
    NP = Y // 4
    step = pl.program_id(0)

    @pl.when(step == 0)
    def _():
        diagonal = lax.broadcasted_iota(jnp.int32, (C, C), 0) == lax.broadcasted_iota(
            jnp.int32, (C, C), 1
        )
        ones = jnp.ones((C, Z), BF16)
        for t in range(27):
            tap = outward_tap(w_ref, t // 9, t // 3 % 3, t % 3)
            wb[t] = dot(jnp.where(diagonal, tap, 0.0).astype(BF16), ones, 1, 0)

    perm = z_permutation(Z)
    for X0 in range(X // 2):
        gp = dot(wd_ref[...], gd_ref[step, X0], 1, 1).astype(BF16)
        for a in range(2):
            for b in range(2):
                for p in range(NP):
                    src = ((a * 2 + b) * 2) * C
                    dst = ((a * 2 + b) * NP + p) * C
                    for e in range(2):
                        Mb[dst : dst + C, e * Z : (e + 1) * Z] = gp[
                            src + e * C : src + (e + 1) * C, p * Z : (p + 1) * Z
                        ]
        gm = dot(Mb[...], perm, 1, 1).astype(BF16)
        for a in range(2):
            for b in range(2):
                for p in range(NP):
                    src = ((a * 2 + b) * NP + p) * C
                    for q in range(2):
                        y = 2 * (2 * p + q) + b
                        gm_ref[step, in_grid(a), y] = gm[src : src + C, q * Z : (q + 1) * Z]


def plane_work(x, samples, dims, ops, put_merged):
    X, Y, C, Z, H, O = dims
    gm_ref, wb, pinT_ref, pout_ref, grad_ref, aout, ain, atap = ops[:8]
    Fs, FB, Ds, Gs, pre_s, ga_s, act_s, gp_s, pin, poutT = ops[8:]
    lane = lax.broadcasted_iota(jnp.int32, (C, Z), 1)
    for g in range(len(samples)):
        fill_stack(Fs.at[g], FB.at[g], [(x, y) for y in range(Y)], Y)
        Gs[g, 3 * C :, :] = jnp.zeros((C, Gs.shape[2]), BF16)
    chunks = [(g, range(4 * i, 4 * i + 4)) for g in range(len(samples)) for i in range(Y // 4)]

    def convolve(i):
        g, rows = chunks[i]
        cells = [(x, y) for y in rows]

        def tile(c):
            conv_tile(wb, Fs.at[g], Ds.at[g], cells, Y, lane, c)

        return [functools.partial(tile, c) for c in range(0, C, 8)]

    def grad_merged(i, part=slice(None)):
        g, rows = chunks[i]
        return jnp.concatenate([gm_ref[samples[g], x, y] for y in rows[part]], axis=1)

    def depth(i, lanes):
        g, rows = chunks[i]
        first = rows[0] * Z
        return Ds[g, :, first + lanes.start : first + lanes.stop].astype(BF16)

    halves = [(slice(0, 2), slice(0, 2 * Z)), (slice(2, 4), slice(2 * Z, 4 * Z))]

    def enter(i):
        def pre(lanes):
            pre_s[i, :, lanes] = dot(pin[...], depth(i, lanes), 1, 0)

        def ga(part, lanes):
            ga_s[i, :, lanes] = dot(poutT[...], grad_merged(i, part), 1, 0)

        steps = []
        for part, lanes in halves:
            steps += [functools.partial(pre, lanes), functools.partial(ga, part, lanes)]
        return steps

    def activate(i):
        def block(h0):
            hs = slice(h0, h0 + 16)
            pre = pre_s[i, hs, :]
            sq = pre * pre
            t = jnp.tanh(pre * (GELU_C + (GELU_C * GELU_A) * sq))
            h = 0.5 + 0.5 * t
            act = pre * h
            slope = h + act * (1.0 - h) * (2.0 * GELU_C + (6.0 * GELU_C * GELU_A) * sq)
            act_s[i, hs, :] = act.astype(BF16)
            gp_s[i, hs, :] = (ga_s[i, hs, :] * slope).astype(BF16)

        return [functools.partial(block, h0) for h0 in range(0, H, 16)]

    def leave(i):
        g, rows = chunks[i]

        def backward(part, lanes):
            grad_depth = dot(pinT_ref[...], gp_s[i, :, lanes], 1, 0).astype(BF16)
            for j, y in enumerate(rows[part]):
                row = grad_depth[:, j * Z : (j + 1) * Z]
                grad_ref[samples[g], y] = row
                value = row.astype(F32)
                shifted = from_right(value, lane), value, from_left(value, lane)
                for e, moved in enumerate(shifted):
                    Gs[g, e * C : (e + 1) * C, y * Z : (y + 1) * Z] = moved.astype(BF16)

        def forward(part, lanes):
            branch = dot(pout_ref[...], act_s[i, :, lanes], 1, 0)
            for j, y in enumerate(rows[part]):
                row = Fs[g, (x + 1) * (Y + 2) + y + 1]
                put_merged(g, y, (row + branch[:, j * Z : (j + 1) * Z]).astype(BF16))

        def out_sum():
            aout[...] += dot(grad_merged(i), act_s[i], 1, 1)

        def in_sum():
            ain[...] += dot(depth(i, slice(0, 4 * Z)), gp_s[i], 1, 1)

        def tap_sum():
            columns = slice(rows[0] * Z, (rows[-1] + 1) * Z)
            atap[...] += dot(FB[g, :, columns], Gs[g, :, columns], 1, 1)

        steps = [functools.partial(backward, *half) for half in halves]
        steps += [functools.partial(forward, *half) for half in halves]
        return steps + [out_sum, in_sum, tap_sum]

    def alternate(products, others):
        order = [((k + 0.5) / len(part), n, step) for n, part in enumerate((products, others))
                 for k, step in enumerate(part)]
        for _, _, step in sorted(order, key=lambda entry: entry[:2]):
            step()

    last = len(chunks) - 1
    alternate([], convolve(0))
    alternate(enter(0), convolve(1))
    alternate([], activate(0))
    for i in range(last + 1):
        alternate(enter(i + 1) if i < last else [], convolve(i + 2) if i + 2 <= last else [])
        alternate(leave(i), activate(i + 1) if i < last else [])


def merged_place(x, y, Y, C, Z):
    start = ((in_grid(x) * 2 + y % 2) * (Y // 4) + y // 4) * C
    q = y // 2 % 2
    return pl.ds(pl.multiple_of(start, C), C), slice(q * Z, (q + 1) * Z)


def set_up(pinT_ref, pout_ref, pin, poutT):
    pin[...] = pinT_ref[...].astype(F32).T.astype(BF16)
    poutT[...] = pout_ref[...].astype(F32).T.astype(BF16)


def near_kernel(dims, *refs):
    X, Y, C, Z, H, O = dims
    from_near, near, far, first, second, corner, gm_ref, wb, pinT_ref, pout_ref = refs[:10]
    grad_ref, Mb, aout, ain, atap = refs[10:15]
    Fs, FB, Ds, Gs, pre_s, ga_s, act_s, gp_s, pin, poutT = refs[15:]
    step = pl.program_id(0)

    @pl.when(step == 0)
    def _():
        aout[...] = jnp.zeros_like(aout)
        ain[...] = jnp.zeros_like(ain)
        atap[...] = jnp.zeros_like(atap)
        set_up(pinT_ref, pout_ref, pin, poutT)

    planes = [
        (0, from_near, (corner, 0), (corner, 1)),
        (1, near, (first, 0), (second, 0)),
        (2, far, (first, 1), (second, 1)),
    ]
    samples = [step * Fs.shape[0] + g for g in range(Fs.shape[0])]
    for g, sample in enumerate(samples):
        fill_padded(planes, sample, Fs.at[g])

    def put_merged(g, y, value):
        rows, lanes = merged_place(0, y, Y, C, Z)
        Mb[samples[g], rows, lanes] = value

    ops = gm_ref, wb, pinT_ref, pout_ref, grad_ref, aout, ain, atap
    ops += Fs, FB, Ds, Gs, pre_s, ga_s, act_s, gp_s, pin, poutT
    plane_work(0, samples, dims, ops, put_merged)


def far_kernel(dims, *refs):
    X, Y, C, Z, H, O = dims
    NP = Y // 4
    near, far, from_far, first, second, corner, gm_ref, wb, pinT_ref, pout_ref = refs[:10]
    gd_ref, wd_ref, grad_near_ref, Mb_ref, aout_ref, ain_ref, atap_ref = refs[10:17]
    red_ref, near_ref, grad_ref, first_ref, second_ref, packed_ref = refs[17:23]
    Fs, FB, Ds, Gs, pre_s, ga_s, act_s, gp_s, pin, poutT = refs[23:33]
    Mb, Pt, atap, adown, aout, ain, rows_s = refs[33:]
    step = pl.program_id(0)

    @pl.when(step == 0)
    def _():
        aout[...] = aout_ref[...]
        ain[...] = ain_ref[...]
        atap[...] = atap_ref[...]
        adown[...] = jnp.zeros_like(adown)
        set_up(pinT_ref, pout_ref, pin, poutT)

    planes = [
        (1, near, (first, 0), (second, 0)),
        (2, far, (first, 1), (second, 1)),
        (3, from_far, (corner, 0), (corner, 1)),
    ]
    samples = [step * Fs.shape[0] + g for g in range(Fs.shape[0])]
    for g, sample in enumerate(samples):
        fill_padded(planes, sample, Fs.at[g])
        Mb[g] = Mb_ref[sample]
        near_ref[sample] = grad_near_ref[sample]

    def put_merged(g, y, value):
        rows, lanes = merged_place(1, y, Y, C, Z)
        Mb[g, rows, lanes] = value

    ops = gm_ref, wb, pinT_ref, pout_ref, grad_ref, aout, ain, atap
    ops += Fs, FB, Ds, Gs, pre_s, ga_s, act_s, gp_s, pin, poutT
    plane_work(1, samples, dims, ops, put_merged)

    _, q = sides()
    for g, sample in enumerate(samples):
        for k, plane in enumerate((grad_near_ref, grad_ref)):
            first_ref[k, sample] = plane[sample, (1 - q) * (Y - 1)]
            second_ref[k, sample] = plane[sample, q * (Y - 1)]
        pt = dot(Mb[g], z_permutation(Z), 1, 0).astype(BF16)
        for a in range(2):
            for b in range(2):
                for p in range(NP):
                    src = ((a * 2 + b) * NP + p) * C
                    for e in range(2):
                        dst = ((a * 2 + b) * 2 + e) * C
                        Pt[g, dst : dst + C, p * Z : (p + 1) * Z] = pt[
                            src : src + C, e * Z : (e + 1) * Z
                        ]
        red_ref[sample, 0] = dot(Pt[g], wd_ref[...], 0, 0).astype(BF16)
        adown[...] += dot(Pt[g], gd_ref[sample, 0], 1, 0)

    @pl.when(step == pl.num_programs(0) - 1)
    def _():
        rows_s[...] = jnp.zeros_like(rows_s)
        for k in range(8):
            rows_s[pl.ds(k, C, stride=8), :] = adown[k * C : (k + 1) * C, :]
        row = lax.broadcasted_iota(jnp.int32, (C, 4 * C), 0)
        column = lax.broadcasted_iota(jnp.int32, (C, 4 * C), 1)
        lines = []
        for ab in range(9):
            block = jnp.where(column % C == row, atap[ab * C : (ab + 1) * C, :], 0.0)
            lines.append(jnp.sum(block, axis=0, keepdims=True))
        p, _ = sides()
        at = 8 * C + 2 * C * (H // Z)
        for a in range(3):
            for b in range(3):
                line = jnp.where(p == 1, lines[a * 3 + b], lines[(2 - a) * 3 + b])
                for k in range(0, 4 * C, Z):
                    rows_s[at : at + 1, :] = line[:, k : k + Z]
                    at += 1
        packed_ref[: rows_s.shape[0], :] = rows_s[...].astype(BF16)
        at = 8 * C
        for part in (aout, ain):
            for k in range(0, H, Z):
                packed_ref[at : at + C, :] = part[:, k : k + Z].astype(BF16)
                at += C
        at = rows_s.shape[0]
        if at < packed_ref.shape[0]:
            rest = packed_ref.shape[0] - at
            packed_ref[at:, :] = jnp.zeros((rest, Z), BF16)


def adjoint_kernel(X, Y, C, Z, *refs):
    planes, (first, second) = refs[:4], refs[4:6]
    gm_ref, w_ref, out_ref, Fs, FB, wide, tap_ref = refs[6:]
    step = pl.program_id(0)

    @pl.when(step == 0)
    def _():
        row = lax.broadcasted_iota(jnp.int32, (C, STACK * C), 0)
        column = lax.broadcasted_iota(jnp.int32, (C, STACK * C), 1)
        for e in range(3):
            taps = [outward_tap(w_ref, 2 - k // 3, 2 - k % 3, 2 - e) for k in range(9)]
            line = jnp.concatenate(taps + [jnp.zeros((1, C), F32)], axis=1)
            block = jnp.where(column % C == row, line, 0.0)
            tap_ref[e * C : (e + 1) * C, :] = block.astype(BF16)

    places = (1, 2, 0, 3)
    widened = [(places[k], planes[k], (first, k), (second, k)) for k in range(4)]
    fill_padded(widened, step, Fs)
    cells = [(x, y) for x in range(X) for y in range(Y)]
    fill_stack(Fs, FB, cells, Y)
    lane = lax.broadcasted_iota(jnp.int32, (C, Z), 1)
    for r0 in range(0, X * Y, 4):
        rows = conv_rows(tap_ref[...], FB[:, r0 * Z : (r0 + 4) * Z], C, Z, lane)
        for (x, y), value in zip(cells[r0 : r0 + 4], rows):
            total = value + gm_ref[step, x, y].astype(F32)
            wide[pl.ds(in_grid(x) * Y + y, C, stride=X * Y), :] = total
    out_ref[0] = wide[...].astype(BF16)


def finish_kernel(C, Z, H, scale, every_ref, down_ref, out_ref, in_ref, taps_ref):
    down_ref[...] = every_ref[: 8 * C, :].astype(F32) * scale
    at = 8 * C
    for ref in (out_ref, in_ref):
        for k in range(0, H, Z):
            ref[:, k : k + Z] = every_ref[at : at + C, :].astype(F32) * scale
            at += C
    taps = every_ref[at : at + 32, :].astype(F32) * scale
    for a in range(3):
        for b in range(3):
            for e in range(3):
                line, k = divmod(e * C, Z)
                line += (a * 3 + b) * (4 * C // Z)
                taps_ref[a, b, e : e + 1, :] = taps[line : line + 1, k : k + C]


def sum_spread_kernel(parts_ref, out_ref):
    total = parts_ref[0].astype(F32)
    for i in range(1, parts_ref.shape[0]):
        total = total + parts_ref[i].astype(F32)
    total = total.astype(BF16)
    for j in range(out_ref.shape[0]):
        out_ref[j] = total


def sum_spread(parts, receivers):
    shape = (receivers,) + parts.shape[1:]
    return pl.pallas_call(
        sum_spread_kernel,
        in_specs=in_vmem(1),
        out_specs=in_vmem(1)[0],
        out_shape=jax.ShapeDtypeStruct(shape, BF16),
        compiler_params=params(4),
        name="sum_spread",
    )(parts)


def swap_in_group(blocks, axis):
    g = blocks.shape[0]
    if g == 1:
        return blocks
    n = lax.axis_size(axis)
    member = lax.axis_index(axis) % g
    got = [lax.dynamic_index_in_dim(blocks, member, 0, keepdims=False)]
    for k in range(1, g):
        out = lax.dynamic_index_in_dim(blocks, (member + k) % g, 0, keepdims=False)
        pairs = [(i, i - i % g + (i + k) % g) for i in range(n)]
        got.append(lax.ppermute(out, axis, pairs))
    if g == 2:
        first = member == 0
        return jnp.stack([jnp.where(first, got[0], got[1]), jnp.where(first, got[1], got[0])])
    got = jnp.stack(got)
    return jnp.take(got, (member - jnp.arange(g, dtype=jnp.int32)) % g, axis=0)


def per_device(fields, depth_kernel, point_in, point_out, down_kernel, cotangent):
    S, C, X, Y, Z = fields.shape
    assert X == 2 and Y % 4 == 0
    H, O = point_in.shape[0], down_kernel.shape[0]
    hx, hy, hz = X // 2, Y // 2, Z // 2
    nx, ny = lax.axis_size("gx"), lax.axis_size("gy")
    devices = nx * ny
    gx, gy = nx // GRIDC, ny // GRIDC
    per_group = S // (gx * gy)

    pieces = pl.pallas_call(
        functools.partial(split_kernel, X, Y, C, Z),
        grid=(S,),
        in_specs=[pl.BlockSpec((1, C * X * Y, Z), lambda s: (s, 0, 0))],
        out_specs=in_vmem(4),
        out_shape=piece_shapes(S, Y, C, Z),
        scratch_shapes=[pltpu.VMEM((C * X * Y, Z), F32)],
        compiler_params=params(6),
        name="split_fields",
    )(fields.reshape(S, C * X * Y, Z))


    moved = cotangent[0, 0].transpose(0, 2, 3, 4, 1)
    moved = moved.reshape(per_group, gx * hx, gy, hy * hz, O).transpose(2, 0, 1, 3, 4)
    moved = swap_in_group(moved, "gy").reshape(gy * per_group, gx, hx, hy * hz, O)
    moved = swap_in_group(moved.transpose(1, 0, 2, 3, 4), "gx")
    grad_down = moved.reshape(S, hx, hy * hz, O)

    widened = halo_by_corners(pieces)

    taps = depth_kernel.transpose(1, 2, 3, 0)
    wd = down_kernel.transpose(2, 3, 4, 1, 0).reshape(8 * C, O)

    rows = 8 * C + 2 * C * (H // Z) + 32
    chunk = -(-rows // (8 * nx)) * 8
    cells = X * Y * Z
    dims = (X, Y, C, Z, H, O)
    grad_merged, spread = pl.pallas_call(
        functools.partial(early_kernel, dims),
        grid=(S,),
        in_specs=in_vmem(3),
        out_specs=in_vmem(2),
        out_shape=[
            jax.ShapeDtypeStruct((S, X, Y, C, Z), BF16),
            jax.ShapeDtypeStruct((27, C, Z), F32),
        ],
        scratch_shapes=[pltpu.VMEM((Y * C, 2 * Z), BF16)],
        compiler_params=params(8),
        cost_estimate=pl.CostEstimate(
            flops=S * cells * (2 * C * O + 8 * C * Z),
            bytes_accessed=4 * S * cells * C + 4 * 27 * C * Z,
            transcendentals=0,
        ),
        name="early",
    )(grad_down, taps, wd)

    G = 2 if S % 2 == 0 else 1
    chunks = G * Y // 4
    scratch = [
        pltpu.VMEM((G, (X + 2) * (Y + 2), C, Z), F32),
        pltpu.VMEM((G, 9 * C, Y * Z), BF16),
        pltpu.VMEM((G, C, Y * Z), F32),
        pltpu.VMEM((G, 4 * C, Y * Z), BF16),
        pltpu.VMEM((chunks, H, 4 * Z), F32),
        pltpu.VMEM((chunks, H, 4 * Z), F32),
        pltpu.VMEM((chunks, H, 4 * Z), BF16),
        pltpu.VMEM((chunks, H, 4 * Z), BF16),
        pltpu.VMEM((H, C), BF16),
        pltpu.VMEM((H, C), BF16),
    ]
    sums = [(C, H), (C, H), (9 * C, 4 * C)]
    cost = pl.CostEstimate(
        flops=S * cells * (6 * C * H + 27 * C * 4 * C),
        bytes_accessed=8 * S * cells * C,
        transcendentals=S * cells * H // 2,
    )
    near, far, from_near, from_far, first, second, corner_near, corner_far = widened
    common = (first, second), (grad_merged, spread, point_in.T, point_out)
    grad_near, merged, *partial_sums = pl.pallas_call(
        functools.partial(near_kernel, dims),
        grid=(S // G,),
        in_specs=in_vmem(10),
        out_specs=in_vmem(5),
        out_shape=[
            jax.ShapeDtypeStruct((S, Y, C, Z), BF16),
            jax.ShapeDtypeStruct((S, Y * C, 2 * Z), BF16),
        ]
        + [jax.ShapeDtypeStruct(shape, F32) for shape in sums],
        scratch_shapes=scratch,
        compiler_params=params(17),
        cost_estimate=cost,
        name="near_side",
    )(from_near, near, far, *common[0], corner_near, *common[1])
    reduced, *grad_pieces, packed = pl.pallas_call(
        functools.partial(far_kernel, dims),
        grid=(S // G,),
        in_specs=in_vmem(17),
        out_specs=in_vmem(6),
        out_shape=[jax.ShapeDtypeStruct((S, hx, hy * hz, O), BF16)]
        + piece_shapes(S, Y, C, Z)
        + [jax.ShapeDtypeStruct((nx * chunk, Z), BF16)],
        scratch_shapes=scratch
        + [
            pltpu.VMEM((G, Y * C, 2 * Z), BF16),
            pltpu.VMEM((G, 8 * C, hy * hz), BF16),
            pltpu.VMEM((9 * C, 4 * C), F32),
            pltpu.VMEM((8 * C, O), F32),
            pltpu.VMEM((C, H), F32),
            pltpu.VMEM((C, H), F32),
            pltpu.VMEM((rows, Z), F32),
        ],
        compiler_params=params(21),
        cost_estimate=cost,
        name="far_side",
    )(
        *(near, far, from_far, first, second, corner_far, *common[1]),
        *(grad_down, wd, grad_near, merged, *partial_sums),
    )

    grad_widened = halo_by_planes(grad_pieces)

    parts = lax.all_to_all(packed.reshape(nx, chunk, Z), "gx", 0, 0)
    parts = lax.all_to_all(sum_spread(parts, ny), "gy", 0, 0)
    share = sum_spread(parts, nx)
    share, grad_widened[0] = lax.optimization_barrier((share, grad_widened[0]))
    every = lax.all_to_all(share, "gx", 0, 0).reshape(nx * chunk, Z)

    grad_fields = pl.pallas_call(
        functools.partial(adjoint_kernel, X, Y, C, Z),
        grid=(S,),
        in_specs=in_vmem(8),
        out_specs=pl.BlockSpec((1, C * X * Y, Z), lambda s: (s, 0, 0)),
        out_shape=jax.ShapeDtypeStruct((S, C * X * Y, Z), BF16),
        scratch_shapes=[
            pltpu.VMEM(((X + 2) * (Y + 2), C, Z), BF16),
            pltpu.VMEM((STACK * C, cells), BF16),
            pltpu.VMEM((C * X * Y, Z), F32),
            pltpu.VMEM((3 * C, STACK * C), BF16),
        ],
        compiler_params=params(14),
        cost_estimate=pl.CostEstimate(
            flops=S * cells * 2 * 27 * C, bytes_accessed=8 * S * cells * C, transcendentals=0
        ),
        name="adjoint",
    )(*grad_widened, grad_merged, taps).reshape(S, C, X, Y, Z)

    moved = swap_in_group(reduced.reshape(gx, S // gx, hx, hy * hz, O), "gx")
    moved = moved.transpose(1, 0, 2, 3, 4).reshape(gy, per_group, gx * hx, hy * hz, O)
    moved = swap_in_group(moved, "gy").transpose(1, 2, 0, 3, 4)
    coarse = moved.reshape(per_group, gx * hx, gy * hy, hz, O).transpose(0, 4, 1, 2, 3)[None, None]
    scale = 1.0 / math.sqrt(S * cells * devices)
    down, outw, inw, tapw = pl.pallas_call(
        functools.partial(finish_kernel, C, Z, H, scale),
        out_shape=[
            jax.ShapeDtypeStruct((8 * C, O), F32),
            jax.ShapeDtypeStruct((C, H), F32),
            jax.ShapeDtypeStruct((C, H), F32),
            jax.ShapeDtypeStruct((3, 3, 3, C), F32),
        ],
        in_specs=in_vmem(1),
        compiler_params=params(6),
        name="finish",
    )(every)
    return (
        coarse,
        grad_fields,
        tapw.transpose(3, 0, 1, 2),
        inw.T,
        outw,
        down.reshape(C, 2, 2, 2, O).transpose(4, 0, 1, 2, 3),
    )


def solution(mesh):
    placed = (
        P(None, None, "gx", "gy", None),
        P(),
        P(),
        P(),
        P(),
        P("gx", "gy", None, None, None, None, None),
    )
    return jax.shard_map(
        per_device,
        mesh=mesh,
        in_specs=placed,
        out_specs=(
            P("gx", "gy", None, None, None, None, None),
            P(None, None, "gx", "gy", None),
            P(),
            P(),
            P(),
            P(),
        ),
        check_vma=False,
    )
```

```python
import functools
import math

import jax
import jax.numpy as jnp
from jax import lax
from jax.experimental import pallas as pl
from jax.experimental.pallas import tpu as pltpu
from jax.sharding import PartitionSpec as P

GRIDC = 4
F32 = jnp.float32
BF16 = jnp.bfloat16
MIB = 1024 * 1024
STACK = 10
GELU_C = math.sqrt(2.0 / math.pi)
GELU_A = 0.044715


def dot(a, b, ca, cb):
    return lax.dot_general(a, b, (((ca,), (cb,)), ((), ())), preferred_element_type=F32)


def sides():
    return lax.axis_index("gx") % 2, lax.axis_index("gy") % 2


def write_pieces(row, s, Y, near, far, first, second):
    p, q = sides()
    for k, (x, plane) in enumerate(((1 - p, near), (p, far))):
        for y in range(Y):
            plane[s, y] = row(x, y)
        first[k, s] = row(x, (1 - q) * (Y - 1))
        second[k, s] = row(x, q * (Y - 1))


def piece_shapes(S, Y, C, Z):
    return [jax.ShapeDtypeStruct((S, Y, C, Z), BF16)] * 2 + [
        jax.ShapeDtypeStruct((2, S, C, Z), BF16)
    ] * 2


def params(mib):
    return pltpu.CompilerParams(vmem_limit_bytes=mib * MIB)


def in_vmem(n):
    return [pl.BlockSpec(memory_space=pltpu.VMEM)] * n


def swap_pairs(n, start):
    return [pair for i in range(start, n - 1, 2) for pair in ((i, i + 1), (i + 1, i))]


def swap_x(plane, start):
    return lax.ppermute(plane, "gx", swap_pairs(lax.axis_size("gx"), start))


def swap_y(rows, start):
    return lax.ppermute(rows, "gy", swap_pairs(lax.axis_size("gy"), start))


def halo_by_corners(pieces):
    near, far, first, second = pieces
    from_near, from_far = swap_x(near, 0), swap_x(far, 1)
    first, second = swap_y(first, 0), swap_y(second, 1)
    corner_far = swap_x(jnp.stack([first[1], second[1]]), 1)
    corner_near = swap_x(jnp.stack([first[0], second[0]]), 0)
    return [near, far, from_near, from_far, first, second, corner_near, corner_far]


def halo_by_planes(pieces):
    near, far, first, second = pieces
    from_near, from_far = swap_x(near, 0), swap_x(far, 1)
    _, q = sides()
    Y = near.shape[1]
    got = []
    for own, y, start in ((first, (1 - q) * (Y - 1), 0), (second, q * (Y - 1), 1)):
        rows = [
            lax.dynamic_index_in_dim(plane, y, 1, keepdims=False) for plane in (from_near, from_far)
        ]
        got.append(swap_y(jnp.concatenate([own, jnp.stack(rows)]), start))
    return [near, far, from_near, from_far, *got]


def fill_padded(planes, s, Fs):
    _, q = sides()
    for u, plane, (r0, k0), (r1, k1) in planes:
        Y = plane.shape[1]
        for y in range(Y):
            Fs[u * (Y + 2) + y + 1] = plane[s, y].astype(Fs.dtype)
        Fs[u * (Y + 2) + (1 - q) * (Y + 1)] = r0[k0, s].astype(Fs.dtype)
        Fs[u * (Y + 2) + q * (Y + 1)] = r1[k1, s].astype(Fs.dtype)


def fill_stack(Fs, FB, rows, Y):
    C, Z = Fs.shape[1:]
    for a in range(3):
        for b in range(3):
            at = (a * 3 + b) * C
            for r, (x, y) in enumerate(rows):
                row = Fs[(x + a) * (Y + 2) + y + b].astype(BF16)
                FB[at : at + C, r * Z : (r + 1) * Z] = row
    if FB.shape[0] > 9 * C:
        FB[9 * C :, :] = jnp.zeros((FB.shape[0] - 9 * C, FB.shape[1]), BF16)


def in_grid(x):
    p, _ = sides()
    return p if x else 1 - p


def from_left(value, lane):
    return jnp.where(lane == 0, 0.0, pltpu.roll(value, 1, 1))


def from_right(value, lane):
    Z = value.shape[1]
    return jnp.where(lane == Z - 1, 0.0, pltpu.roll(value, Z - 1, 1))


def conv_rows(taps, stack, C, Z, lane):
    acc = dot(taps, stack, 1, 0)
    rows = []
    for k in range(0, stack.shape[1], Z):
        left, mid, right = (acc[e * C : (e + 1) * C, k : k + Z] for e in range(3))
        rows.append(mid + from_left(left, lane) + from_right(right, lane))
    return rows


def conv_tile(wb, Fs, Ds, rows, Y, lane, c):
    Z = Fs.shape[2]
    weights = [wb[t, c : c + 8, :] for t in range(27)]
    for x, y in rows:
        acc = [None, None, None]
        for a in range(3):
            for b in range(3):
                f = Fs[(x + a) * (Y + 2) + y + b, c : c + 8, :]
                for e in range(3):
                    term = weights[(a * 3 + b) * 3 + e] * f
                    acc[e] = term if acc[e] is None else acc[e] + term
        total = acc[1] + from_left(acc[0], lane[:8]) + from_right(acc[2], lane[:8])
        Ds[c : c + 8, y * Z : (y + 1) * Z] = total


def split_kernel(X, Y, C, Z, f_ref, w_ref, near, far, first, second, taps_ref, wide):
    taps_ref[...] = w_ref[...]
    wide[...] = f_ref[0].astype(F32)

    def row(x, y):
        return wide[pl.ds(x * Y + y, C, stride=X * Y), :].astype(BF16)

    write_pieces(row, pl.program_id(0), Y, near, far, first, second)


def z_permutation(Z):
    fine = lax.broadcasted_iota(jnp.int32, (2 * Z, 2 * Z), 0)
    coarse = lax.broadcasted_iota(jnp.int32, (2 * Z, 2 * Z), 1)
    inner = coarse % Z
    goes = coarse // Z + (inner % (Z // 2)) * 2 + (inner // (Z // 2)) * Z
    return jnp.where(fine == goes, 1.0, 0.0).astype(BF16)


def outward_tap(w_ref, a, b, e):
    p, _ = sides()
    here, mirrored = (w_ref[x, b, e : e + 1, :].astype(F32) for x in (a, 2 - a))
    return jnp.where(p == 1, here, mirrored)


def early_kernel(dims, gd_ref, w_ref, wd_ref, gm_ref, wb, Mb):
    X, Y, C, Z, H, O = dims
    NP = Y // 4
    step = pl.program_id(0)

    @pl.when(step == 0)
    def _():
        diagonal = lax.broadcasted_iota(jnp.int32, (C, C), 0) == lax.broadcasted_iota(
            jnp.int32, (C, C), 1
        )
        ones = jnp.ones((C, Z), BF16)
        for t in range(27):
            tap = outward_tap(w_ref, t // 9, t // 3 % 3, t % 3)
            wb[t] = dot(jnp.where(diagonal, tap, 0.0).astype(BF16), ones, 1, 0)

    perm = z_permutation(Z)
    for X0 in range(X // 2):
        gp = dot(wd_ref[...], gd_ref[step, X0], 1, 1).astype(BF16)
        for a in range(2):
            for b in range(2):
                for p in range(NP):
                    src = ((a * 2 + b) * 2) * C
                    dst = ((a * 2 + b) * NP + p) * C
                    for e in range(2):
                        Mb[dst : dst + C, e * Z : (e + 1) * Z] = gp[
                            src + e * C : src + (e + 1) * C, p * Z : (p + 1) * Z
                        ]
        gm = dot(Mb[...], perm, 1, 1).astype(BF16)
        for a in range(2):
            for b in range(2):
                for p in range(NP):
                    src = ((a * 2 + b) * NP + p) * C
                    for q in range(2):
                        y = 2 * (2 * p + q) + b
                        gm_ref[step, in_grid(a), y] = gm[src : src + C, q * Z : (q + 1) * Z]


def plane_work(x, samples, dims, ops, put_merged):
    X, Y, C, Z, H, O = dims
    gm_ref, wb, pinT_ref, pout_ref, grad_ref, aout, ain, atap = ops[:8]
    Fs, FB, Ds, Gs, pre_s, ga_s, act_s, gp_s, pin, poutT = ops[8:]
    lane = lax.broadcasted_iota(jnp.int32, (C, Z), 1)
    for g in range(len(samples)):
        fill_stack(Fs.at[g], FB.at[g], [(x, y) for y in range(Y)], Y)
        Gs[g, 3 * C :, :] = jnp.zeros((C, Gs.shape[2]), BF16)
    chunks = [(g, range(4 * i, 4 * i + 4)) for g in range(len(samples)) for i in range(Y // 4)]

    def convolve(i):
        g, rows = chunks[i]
        cells = [(x, y) for y in rows]

        def tile(c):
            conv_tile(wb, Fs.at[g], Ds.at[g], cells, Y, lane, c)

        return [functools.partial(tile, c) for c in range(0, C, 8)]

    def grad_merged(i, part=slice(None)):
        g, rows = chunks[i]
        return jnp.concatenate([gm_ref[samples[g], x, y] for y in rows[part]], axis=1)

    def depth(i, lanes):
        g, rows = chunks[i]
        first = rows[0] * Z
        return Ds[g, :, first + lanes.start : first + lanes.stop].astype(BF16)

    halves = [(slice(0, 2), slice(0, 2 * Z)), (slice(2, 4), slice(2 * Z, 4 * Z))]

    def enter(i):
        def pre(lanes):
            pre_s[i, :, lanes] = dot(pin[...], depth(i, lanes), 1, 0)

        def ga(part, lanes):
            ga_s[i, :, lanes] = dot(poutT[...], grad_merged(i, part), 1, 0)

        steps = []
        for part, lanes in halves:
            steps += [functools.partial(pre, lanes), functools.partial(ga, part, lanes)]
        return steps

    def activate(i):
        def block(h0):
            hs = slice(h0, h0 + 16)
            pre = pre_s[i, hs, :]
            sq = pre * pre
            t = jnp.tanh(pre * (GELU_C + (GELU_C * GELU_A) * sq))
            h = 0.5 + 0.5 * t
            act = pre * h
            slope = h + act * (1.0 - h) * (2.0 * GELU_C + (6.0 * GELU_C * GELU_A) * sq)
            act_s[i, hs, :] = act.astype(BF16)
            gp_s[i, hs, :] = (ga_s[i, hs, :] * slope).astype(BF16)

        return [functools.partial(block, h0) for h0 in range(0, H, 16)]

    def leave(i):
        g, rows = chunks[i]

        def backward(part, lanes):
            grad_depth = dot(pinT_ref[...], gp_s[i, :, lanes], 1, 0).astype(BF16)
            for j, y in enumerate(rows[part]):
                row = grad_depth[:, j * Z : (j + 1) * Z]
                grad_ref[samples[g], y] = row
                value = row.astype(F32)
                shifted = from_right(value, lane), value, from_left(value, lane)
                for e, moved in enumerate(shifted):
                    Gs[g, e * C : (e + 1) * C, y * Z : (y + 1) * Z] = moved.astype(BF16)

        def forward(part, lanes):
            branch = dot(pout_ref[...], act_s[i, :, lanes], 1, 0)
            for j, y in enumerate(rows[part]):
                row = Fs[g, (x + 1) * (Y + 2) + y + 1]
                put_merged(g, y, (row + branch[:, j * Z : (j + 1) * Z]).astype(BF16))

        def out_sum():
            aout[...] += dot(grad_merged(i), act_s[i], 1, 1)

        def in_sum():
            ain[...] += dot(depth(i, slice(0, 4 * Z)), gp_s[i], 1, 1)

        def tap_sum():
            columns = slice(rows[0] * Z, (rows[-1] + 1) * Z)
            atap[...] += dot(FB[g, :, columns], Gs[g, :, columns], 1, 1)

        steps = [functools.partial(backward, *half) for half in halves]
        steps += [functools.partial(forward, *half) for half in halves]
        return steps + [out_sum, in_sum, tap_sum]

    def alternate(products, others):
        order = [((k + 0.5) / len(part), n, step) for n, part in enumerate((products, others))
                 for k, step in enumerate(part)]
        for _, _, step in sorted(order, key=lambda entry: entry[:2]):
            step()

    last = len(chunks) - 1
    alternate([], convolve(0))
    alternate(enter(0), convolve(1))
    alternate([], activate(0))
    for i in range(last + 1):
        alternate(enter(i + 1) if i < last else [], convolve(i + 2) if i + 2 <= last else [])
        alternate(leave(i), activate(i + 1) if i < last else [])


def merged_place(x, y, Y, C, Z):
    start = ((in_grid(x) * 2 + y % 2) * (Y // 4) + y // 4) * C
    q = y // 2 % 2
    return pl.ds(pl.multiple_of(start, C), C), slice(q * Z, (q + 1) * Z)


def set_up(pinT_ref, pout_ref, pin, poutT):
    pin[...] = pinT_ref[...].astype(F32).T.astype(BF16)
    poutT[...] = pout_ref[...].astype(F32).T.astype(BF16)


def near_kernel(dims, *refs):
    X, Y, C, Z, H, O = dims
    from_near, near, far, first, second, corner, gm_ref, wb, pinT_ref, pout_ref = refs[:10]
    grad_ref, Mb, aout, ain, atap = refs[10:15]
    Fs, FB, Ds, Gs, pre_s, ga_s, act_s, gp_s, pin, poutT = refs[15:]
    step = pl.program_id(0)

    @pl.when(step == 0)
    def _():
        aout[...] = jnp.zeros_like(aout)
        ain[...] = jnp.zeros_like(ain)
        atap[...] = jnp.zeros_like(atap)
        set_up(pinT_ref, pout_ref, pin, poutT)

    planes = [
        (0, from_near, (corner, 0), (corner, 1)),
        (1, near, (first, 0), (second, 0)),
        (2, far, (first, 1), (second, 1)),
    ]
    samples = [step * Fs.shape[0] + g for g in range(Fs.shape[0])]
    for g, sample in enumerate(samples):
        fill_padded(planes, sample, Fs.at[g])

    def put_merged(g, y, value):
        rows, lanes = merged_place(0, y, Y, C, Z)
        Mb[samples[g], rows, lanes] = value

    ops = gm_ref, wb, pinT_ref, pout_ref, grad_ref, aout, ain, atap
    ops += Fs, FB, Ds, Gs, pre_s, ga_s, act_s, gp_s, pin, poutT
    plane_work(0, samples, dims, ops, put_merged)


def far_kernel(dims, *refs):
    X, Y, C, Z, H, O = dims
    NP = Y // 4
    near, far, from_far, first, second, corner, gm_ref, wb, pinT_ref, pout_ref = refs[:10]
    gd_ref, wd_ref, grad_near_ref, Mb_ref, aout_ref, ain_ref, atap_ref = refs[10:17]
    red_ref, near_ref, grad_ref, first_ref, second_ref, packed_ref = refs[17:23]
    Fs, FB, Ds, Gs, pre_s, ga_s, act_s, gp_s, pin, poutT = refs[23:33]
    Mb, Pt, atap, adown, aout, ain, rows_s = refs[33:]
    step = pl.program_id(0)

    @pl.when(step == 0)
    def _():
        aout[...] = aout_ref[...]
        ain[...] = ain_ref[...]
        atap[...] = atap_ref[...]
        adown[...] = jnp.zeros_like(adown)
        set_up(pinT_ref, pout_ref, pin, poutT)

    planes = [
        (1, near, (first, 0), (second, 0)),
        (2, far, (first, 1), (second, 1)),
        (3, from_far, (corner, 0), (corner, 1)),
    ]
    samples = [step * Fs.shape[0] + g for g in range(Fs.shape[0])]
    for g, sample in enumerate(samples):
        fill_padded(planes, sample, Fs.at[g])
        Mb[g] = Mb_ref[sample]
        near_ref[sample] = grad_near_ref[sample]

    def put_merged(g, y, value):
        rows, lanes = merged_place(1, y, Y, C, Z)
        Mb[g, rows, lanes] = value

    ops = gm_ref, wb, pinT_ref, pout_ref, grad_ref, aout, ain, atap
    ops += Fs, FB, Ds, Gs, pre_s, ga_s, act_s, gp_s, pin, poutT
    plane_work(1, samples, dims, ops, put_merged)

    _, q = sides()
    for g, sample in enumerate(samples):
        for k, plane in enumerate((grad_near_ref, grad_ref)):
            first_ref[k, sample] = plane[sample, (1 - q) * (Y - 1)]
            second_ref[k, sample] = plane[sample, q * (Y - 1)]
        pt = dot(Mb[g], z_permutation(Z), 1, 0).astype(BF16)
        for a in range(2):
            for b in range(2):
                for p in range(NP):
                    src = ((a * 2 + b) * NP + p) * C
                    for e in range(2):
                        dst = ((a * 2 + b) * 2 + e) * C
                        Pt[g, dst : dst + C, p * Z : (p + 1) * Z] = pt[
                            src : src + C, e * Z : (e + 1) * Z
                        ]
        red_ref[sample, 0] = dot(Pt[g], wd_ref[...], 0, 0).astype(BF16)
        adown[...] += dot(Pt[g], gd_ref[sample, 0], 1, 0)

    @pl.when(step == pl.num_programs(0) - 1)
    def _():
        rows_s[...] = jnp.zeros_like(rows_s)
        for k in range(8):
            rows_s[pl.ds(k, C, stride=8), :] = adown[k * C : (k + 1) * C, :]
        row = lax.broadcasted_iota(jnp.int32, (C, 4 * C), 0)
        column = lax.broadcasted_iota(jnp.int32, (C, 4 * C), 1)
        lines = []
        for ab in range(9):
            block = jnp.where(column % C == row, atap[ab * C : (ab + 1) * C, :], 0.0)
            lines.append(jnp.sum(block, axis=0, keepdims=True))
        p, _ = sides()
        at = 8 * C + 2 * C * (H // Z)
        for a in range(3):
            for b in range(3):
                line = jnp.where(p == 1, lines[a * 3 + b], lines[(2 - a) * 3 + b])
                for k in range(0, 4 * C, Z):
                    rows_s[at : at + 1, :] = line[:, k : k + Z]
                    at += 1
        packed_ref[: rows_s.shape[0], :] = rows_s[...].astype(BF16)
        at = 8 * C
        for part in (aout, ain):
            for k in range(0, H, Z):
                packed_ref[at : at + C, :] = part[:, k : k + Z].astype(BF16)
                at += C
        at = rows_s.shape[0]
        if at < packed_ref.shape[0]:
            rest = packed_ref.shape[0] - at
            packed_ref[at:, :] = jnp.zeros((rest, Z), BF16)


def adjoint_kernel(X, Y, C, Z, *refs):
    planes, (first, second) = refs[:4], refs[4:6]
    gm_ref, w_ref, out_ref, Fs, FB, wide, tap_ref = refs[6:]
    step = pl.program_id(0)

    @pl.when(step == 0)
    def _():
        row = lax.broadcasted_iota(jnp.int32, (C, STACK * C), 0)
        column = lax.broadcasted_iota(jnp.int32, (C, STACK * C), 1)
        for e in range(3):
            taps = [outward_tap(w_ref, 2 - k // 3, 2 - k % 3, 2 - e) for k in range(9)]
            line = jnp.concatenate(taps + [jnp.zeros((1, C), F32)], axis=1)
            block = jnp.where(column % C == row, line, 0.0)
            tap_ref[e * C : (e + 1) * C, :] = block.astype(BF16)

    places = (1, 2, 0, 3)
    widened = [(places[k], planes[k], (first, k), (second, k)) for k in range(4)]
    fill_padded(widened, step, Fs)
    cells = [(x, y) for x in range(X) for y in range(Y)]
    fill_stack(Fs, FB, cells, Y)
    lane = lax.broadcasted_iota(jnp.int32, (C, Z), 1)
    for r0 in range(0, X * Y, 4):
        rows = conv_rows(tap_ref[...], FB[:, r0 * Z : (r0 + 4) * Z], C, Z, lane)
        for (x, y), value in zip(cells[r0 : r0 + 4], rows):
            total = value + gm_ref[step, x, y].astype(F32)
            wide[pl.ds(in_grid(x) * Y + y, C, stride=X * Y), :] = total
    out_ref[0] = wide[...].astype(BF16)


def finish_kernel(C, Z, H, scale, every_ref, down_ref, out_ref, in_ref, taps_ref):
    down_ref[...] = every_ref[: 8 * C, :].astype(F32) * scale
    at = 8 * C
    for ref in (out_ref, in_ref):
        for k in range(0, H, Z):
            ref[:, k : k + Z] = every_ref[at : at + C, :].astype(F32) * scale
            at += C
    taps = every_ref[at : at + 32, :].astype(F32) * scale
    for a in range(3):
        for b in range(3):
            for e in range(3):
                line, k = divmod(e * C, Z)
                line += (a * 3 + b) * (4 * C // Z)
                taps_ref[a, b, e : e + 1, :] = taps[line : line + 1, k : k + C]


def sum_spread_kernel(parts_ref, out_ref):
    total = parts_ref[0].astype(F32)
    for i in range(1, parts_ref.shape[0]):
        total = total + parts_ref[i].astype(F32)
    total = total.astype(BF16)
    for j in range(out_ref.shape[0]):
        out_ref[j] = total


def sum_spread(parts, receivers):
    shape = (receivers,) + parts.shape[1:]
    return pl.pallas_call(
        sum_spread_kernel,
        in_specs=in_vmem(1),
        out_specs=in_vmem(1)[0],
        out_shape=jax.ShapeDtypeStruct(shape, BF16),
        compiler_params=params(4),
        name="sum_spread",
    )(parts)


def swap_in_group(blocks, axis):
    g = blocks.shape[0]
    if g == 1:
        return blocks
    n = lax.axis_size(axis)
    member = lax.axis_index(axis) % g
    got = [lax.dynamic_index_in_dim(blocks, member, 0, keepdims=False)]
    for k in range(1, g):
        out = lax.dynamic_index_in_dim(blocks, (member + k) % g, 0, keepdims=False)
        pairs = [(i, i - i % g + (i + k) % g) for i in range(n)]
        got.append(lax.ppermute(out, axis, pairs))
    if g == 2:
        first = member == 0
        return jnp.stack([jnp.where(first, got[0], got[1]), jnp.where(first, got[1], got[0])])
    got = jnp.stack(got)
    return jnp.take(got, (member - jnp.arange(g, dtype=jnp.int32)) % g, axis=0)


def per_device(fields, depth_kernel, point_in, point_out, down_kernel, cotangent):
    S, C, X, Y, Z = fields.shape
    assert X == 2 and Y % 4 == 0
    H, O = point_in.shape[0], down_kernel.shape[0]
    hx, hy, hz = X // 2, Y // 2, Z // 2
    nx, ny = lax.axis_size("gx"), lax.axis_size("gy")
    devices = nx * ny
    gx, gy = nx // GRIDC, ny // GRIDC
    per_group = S // (gx * gy)

    *pieces, taps = pl.pallas_call(
        functools.partial(split_kernel, X, Y, C, Z),
        grid=(S,),
        in_specs=[pl.BlockSpec((1, C * X * Y, Z), lambda s: (s, 0, 0)), *in_vmem(1)],
        out_specs=in_vmem(5),
        out_shape=piece_shapes(S, Y, C, Z) + [jax.ShapeDtypeStruct((3, 3, 3, C), BF16)],
        scratch_shapes=[pltpu.VMEM((C * X * Y, Z), F32)],
        compiler_params=params(6),
        name="split_fields",
    )(fields.reshape(S, C * X * Y, Z), depth_kernel.transpose(1, 2, 3, 0))


    moved = cotangent[0, 0].transpose(0, 2, 3, 4, 1)
    moved = moved.reshape(per_group, gx * hx, gy, hy * hz, O).transpose(2, 0, 1, 3, 4)
    moved = swap_in_group(moved, "gy").reshape(gy * per_group, gx, hx, hy * hz, O)
    moved = swap_in_group(moved.transpose(1, 0, 2, 3, 4), "gx")
    grad_down = moved.reshape(S, hx, hy * hz, O)

    widened = halo_by_corners(pieces)

    wd = down_kernel.transpose(2, 3, 4, 1, 0).reshape(8 * C, O)

    rows = 8 * C + 2 * C * (H // Z) + 32
    chunk = -(-rows // (8 * nx)) * 8
    cells = X * Y * Z
    dims = (X, Y, C, Z, H, O)
    grad_merged, spread = pl.pallas_call(
        functools.partial(early_kernel, dims),
        grid=(S,),
        in_specs=in_vmem(3),
        out_specs=in_vmem(2),
        out_shape=[
            jax.ShapeDtypeStruct((S, X, Y, C, Z), BF16),
            jax.ShapeDtypeStruct((27, C, Z), F32),
        ],
        scratch_shapes=[pltpu.VMEM((Y * C, 2 * Z), BF16)],
        compiler_params=params(8),
        cost_estimate=pl.CostEstimate(
            flops=S * cells * (2 * C * O + 8 * C * Z),
            bytes_accessed=4 * S * cells * C + 4 * 27 * C * Z,
            transcendentals=0,
        ),
        name="early",
    )(grad_down, taps, wd)

    G = 2 if S % 2 == 0 else 1
    chunks = G * Y // 4
    scratch = [
        pltpu.VMEM((G, (X + 2) * (Y + 2), C, Z), F32),
        pltpu.VMEM((G, 9 * C, Y * Z), BF16),
        pltpu.VMEM((G, C, Y * Z), F32),
        pltpu.VMEM((G, 4 * C, Y * Z), BF16),
        pltpu.VMEM((chunks, H, 4 * Z), F32),
        pltpu.VMEM((chunks, H, 4 * Z), F32),
        pltpu.VMEM((chunks, H, 4 * Z), BF16),
        pltpu.VMEM((chunks, H, 4 * Z), BF16),
        pltpu.VMEM((H, C), BF16),
        pltpu.VMEM((H, C), BF16),
    ]
    sums = [(C, H), (C, H), (9 * C, 4 * C)]
    cost = pl.CostEstimate(
        flops=S * cells * (6 * C * H + 27 * C * 4 * C),
        bytes_accessed=8 * S * cells * C,
        transcendentals=S * cells * H // 2,
    )
    near, far, from_near, from_far, first, second, corner_near, corner_far = widened
    common = (first, second), (grad_merged, spread, point_in.T, point_out)
    grad_near, merged, *partial_sums = pl.pallas_call(
        functools.partial(near_kernel, dims),
        grid=(S // G,),
        in_specs=in_vmem(10),
        out_specs=in_vmem(5),
        out_shape=[
            jax.ShapeDtypeStruct((S, Y, C, Z), BF16),
            jax.ShapeDtypeStruct((S, Y * C, 2 * Z), BF16),
        ]
        + [jax.ShapeDtypeStruct(shape, F32) for shape in sums],
        scratch_shapes=scratch,
        compiler_params=params(17),
        cost_estimate=cost,
        name="near_side",
    )(from_near, near, far, *common[0], corner_near, *common[1])
    reduced, *grad_pieces, packed = pl.pallas_call(
        functools.partial(far_kernel, dims),
        grid=(S // G,),
        in_specs=in_vmem(17),
        out_specs=in_vmem(6),
        out_shape=[jax.ShapeDtypeStruct((S, hx, hy * hz, O), BF16)]
        + piece_shapes(S, Y, C, Z)
        + [jax.ShapeDtypeStruct((nx * chunk, Z), BF16)],
        scratch_shapes=scratch
        + [
            pltpu.VMEM((G, Y * C, 2 * Z), BF16),
            pltpu.VMEM((G, 8 * C, hy * hz), BF16),
            pltpu.VMEM((9 * C, 4 * C), F32),
            pltpu.VMEM((8 * C, O), F32),
            pltpu.VMEM((C, H), F32),
            pltpu.VMEM((C, H), F32),
            pltpu.VMEM((rows, Z), F32),
        ],
        compiler_params=params(21),
        cost_estimate=cost,
        name="far_side",
    )(
        *(near, far, from_far, first, second, corner_far, *common[1]),
        *(grad_down, wd, grad_near, merged, *partial_sums),
    )

    grad_widened = halo_by_planes(grad_pieces)

    parts = lax.all_to_all(packed.reshape(nx, chunk, Z), "gx", 0, 0)
    parts = lax.all_to_all(sum_spread(parts, ny), "gy", 0, 0)
    share = sum_spread(parts, nx)
    share, grad_widened[0] = lax.optimization_barrier((share, grad_widened[0]))
    every = lax.all_to_all(share, "gx", 0, 0).reshape(nx * chunk, Z)

    grad_fields = pl.pallas_call(
        functools.partial(adjoint_kernel, X, Y, C, Z),
        grid=(S,),
        in_specs=in_vmem(8),
        out_specs=pl.BlockSpec((1, C * X * Y, Z), lambda s: (s, 0, 0)),
        out_shape=jax.ShapeDtypeStruct((S, C * X * Y, Z), BF16),
        scratch_shapes=[
            pltpu.VMEM(((X + 2) * (Y + 2), C, Z), BF16),
            pltpu.VMEM((STACK * C, cells), BF16),
            pltpu.VMEM((C * X * Y, Z), F32),
            pltpu.VMEM((3 * C, STACK * C), BF16),
        ],
        compiler_params=params(14),
        cost_estimate=pl.CostEstimate(
            flops=S * cells * 2 * 27 * C, bytes_accessed=8 * S * cells * C, transcendentals=0
        ),
        name="adjoint",
    )(*grad_widened, grad_merged, taps).reshape(S, C, X, Y, Z)

    moved = swap_in_group(reduced.reshape(gx, S // gx, hx, hy * hz, O), "gx")
    moved = moved.transpose(1, 0, 2, 3, 4).reshape(gy, per_group, gx * hx, hy * hz, O)
    moved = swap_in_group(moved, "gy").transpose(1, 2, 0, 3, 4)
    coarse = moved.reshape(per_group, gx * hx, gy * hy, hz, O).transpose(0, 4, 1, 2, 3)[None, None]
    scale = 1.0 / math.sqrt(S * cells * devices)
    down, outw, inw, tapw = pl.pallas_call(
        functools.partial(finish_kernel, C, Z, H, scale),
        out_shape=[
            jax.ShapeDtypeStruct((8 * C, O), F32),
            jax.ShapeDtypeStruct((C, H), F32),
            jax.ShapeDtypeStruct((C, H), F32),
            jax.ShapeDtypeStruct((3, 3, 3, C), F32),
        ],
        in_specs=in_vmem(1),
        compiler_params=params(6),
        name="finish",
    )(every)
    return (
        coarse,
        grad_fields,
        tapw.transpose(3, 0, 1, 2),
        inw.T,
        outw,
        down.reshape(C, 2, 2, 2, O).transpose(4, 0, 1, 2, 3),
    )


def solution(mesh):
    placed = (
        P(None, None, "gx", "gy", None),
        P(),
        P(),
        P(),
        P(),
        P("gx", "gy", None, None, None, None, None),
    )
    return jax.shard_map(
        per_device,
        mesh=mesh,
        in_specs=placed,
        out_specs=(
            P("gx", "gy", None, None, None, None, None),
            P(None, None, "gx", "gy", None),
            P(),
            P(),
            P(),
            P(),
        ),
        check_vma=False,
    )
```
